32 devices in a mesh: dp: 8 (over z, x), expert: 4 (over y, core).
Axes of the slice: x: 2, y: 2, z: 4, core: 2. Of those that a mesh axis runs over, the one named last changes fastest.
Arguments:
- tokens: bfloat16 [32, 256, 768], P(('dp', 'expert')), may hold values from -6 to 6
- conditioning: bfloat16 [32, 768], P(('dp', 'expert')), may hold values from -6 to 6
- routes: int32 [32, 256, 2], P(('dp', 'expert')), may hold values from 0 to 7, all different within a row
- cotangent: bfloat16 [32, 256, 768], P(('dp', 'expert')), may hold values from -6 to 6
- ada_weight: bfloat16 [768, 4608], P('dp'), may hold values from -0.21875 to 0.21875
- ada_bias: bfloat16 [4608], P('dp'), may hold values from -2.5 to 2.5
- qkv_weight: bfloat16 [768, 2304], P('dp'), may hold values from -0.21875 to 0.21875
- qv_bias: bfloat16 [2, 768], P(None, 'dp'), may hold values from -2.5 to 2.5
- out_weight: bfloat16 [768, 768], P('dp'), may hold values from -1.75 to 1.75
- out_bias: bfloat16 [768], P('dp'), may hold values from -2.5 to 2.5
- shared_in: bfloat16 [768, 3072], P('dp'), may hold values from -0.21875 to 0.21875
- shared_in_bias: bfloat16 [3072], P('dp'), may hold values from -2.5 to 2.5
- shared_out: bfloat16 [3072, 768], P('dp'), may hold values from -0.109375 to 0.109375
- shared_out_bias: bfloat16 [768], P('dp'), may hold values from -2.5 to 2.5
- router: bfloat16 [768, 8], P('dp'), may hold values from -0.15625 to 0.15625
- expert_in: bfloat16 [8, 768, 3072], P('expert'), may hold values from -0.21875 to 0.21875
- expert_in_bias: bfloat16 [8, 3072], P('expert'), may hold values from -2.5 to 2.5
- expert_out: bfloat16 [8, 3072, 768], P('expert'), may hold values from -0.109375 to 0.109375
- expert_out_bias: bfloat16 [8, 768], P('expert'), may hold values from -2.5 to 2.5
Outputs:
- output: bfloat16 [32, 256, 768], P(('dp', 'expert'))
- tokens_grad: float32 [32, 256, 768], P(('dp', 'expert'))
- conditioning_grad: float32 [32, 768], P(('dp', 'expert'))
- ada_weight_grad: float32 [768, 4608], P('dp')
- ada_bias_grad: float32 [4608], P('dp')
- qkv_weight_grad: float32 [768, 2304], P('dp')
- qv_bias_grad: float32 [2, 768], P(None, 'dp')
- out_weight_grad: float32 [768, 768], P('dp')
- out_bias_grad: float32 [768], P('dp')
- shared_in_grad: float32 [768, 3072], P('dp')
- shared_in_bias_grad: float32 [3072], P('dp')
- shared_out_grad: float32 [3072, 768], P('dp')
- shared_out_bias_grad: float32 [768], P('dp')
- router_grad: float32 [768, 8], P('dp')
- expert_in_grad: float32 [8, 768, 3072], P('expert', 'dp')
- expert_in_bias_grad: float32 [8, 3072], P('expert', 'dp')
- expert_out_grad: float32 [8, 3072, 768], P('expert', 'dp')
- expert_out_bias_grad: float32 [8, 768], P('expert', 'dp')
The draws below stay inside these ranges and needn't reach their ends.
Inputs may be any that keep to these rules, and one draw needn't show every extreme that they name: `routes`: each patch names two different experts.
All inputs are finite; a program needn't handle non-finite values.
Results may differ from the reference program's by a relative error of at most 0.018.
The reference program's roundings to bfloat16 on the way count: a program that leaves them out, or rounds other values in their place, can miss the bound.
Values may be sent and summed in bfloat16 or wider, within the bound.
A program may use at most 256 MiB of HBM per device.

```python
import math
import jax
import jax.numpy as jnp
from jax import lax

D = 768
HEADS = 12
HEAD_DIM = 64
FF = 3072
E = 8
SEQ = 256
TOK_DEV = 256
IMAGES = 32
CAP = 80
N_DP = 8
N_EXPERT = 4


def shard_levels(stream_key, dims, shards, smallest, high):
    factor_of, own = 1.0, jax.random.fold_in(stream_key, 6)
    for dim, blocks in shards:
        draws = jnp.exp(jax.random.uniform(jax.random.fold_in(own, dim), (blocks,), jnp.float32, smallest / len(shards), high / len(shards)))
        factor_of = factor_of * jnp.repeat(draws, dims[dim] // blocks).reshape([-1 if axis == dim else 1 for axis in range(len(dims))])
    return factor_of


def choose_distinct(key, rows, number_of, top, lift):
    ranking = jax.random.permutation(jax.random.fold_in(key, 1), number_of)
    boost = ranking
    for power in range(3):
        boost = boost * boost // number_of
    boost = boost * lift // number_of
    tickets = jax.random.randint(jax.random.fold_in(key, 2), (rows, number_of), 0, 4096) + boost
    fixed_rows = jax.random.permutation(jax.random.fold_in(key, 3), rows)[jnp.arange(number_of) % rows]
    tickets = jnp.where(jnp.arange(rows)[:, None] == fixed_rows[None, :], 1 << 14, tickets)
    score = tickets * number_of + jnp.arange(number_of)
    return lax.top_k(score.astype(jnp.int32), top)[1].astype(jnp.int32)


def normal_values(stream_key, extent, scale, bound, shards=(), kind=jnp.bfloat16):
    result = scale * jax.random.normal(stream_key, extent, jnp.float32)
    if shards:
        result = result * shard_levels(stream_key, extent, shards, -0.22, 0.18)
    return jnp.clip(result, -bound, bound).astype(kind)


def setup_inputs(seed: int = 0) -> dict:
    streams_of = jax.random.split(jax.random.key(seed), 20)
    tokens = normal_values(streams_of[0], (IMAGES, SEQ, D), 1.0, 6.0, ((0, 32),))
    conditioning = normal_values(streams_of[1], (IMAGES, D), 1.0, 6.0, ((0, 32),))
    routes = choose_distinct(streams_of[2], IMAGES * SEQ, E, 2, 2048).reshape((IMAGES, SEQ, 2))
    cotangent = normal_values(streams_of[3], (IMAGES, SEQ, D), 1.0, 6.0, ((0, 32),))
    ada_weight = normal_values(streams_of[4], (D, 6 * D), D ** -0.5, 0.21875, ((0, 8),))
    ada_bias = normal_values(streams_of[5], (6 * D,), 0.5, 2.5, ((0, 8),))
    qkv_weight = normal_values(streams_of[6], (D, 3 * D), D ** -0.5, 0.21875, ((0, 8),))
    qv_bias = normal_values(streams_of[7], (2, D), 0.5, 2.5, ((1, 8),))
    out_weight = normal_values(streams_of[8], (D, D), (D // 64) ** -0.5, 1.75, ((0, 8),))
    out_bias = normal_values(streams_of[9], (D,), 0.5, 2.5, ((0, 8),))
    shared_in = normal_values(streams_of[10], (D, FF), D ** -0.5, 0.21875, ((0, 8),))
    shared_in_bias = normal_values(streams_of[11], (FF,), 0.5, 2.5, ((0, 8),))
    shared_out = normal_values(streams_of[12], (FF, D), FF ** -0.5, 0.109375, ((0, 8),))
    shared_out_bias = normal_values(streams_of[13], (D,), 0.5, 2.5, ((0, 8),))
    router = normal_values(streams_of[14], (D, E), (2 * D) ** -0.5, 0.15625, ((0, 8),))
    expert_in = normal_values(streams_of[15], (E, D, FF), D ** -0.5, 0.21875, ((0, 4),))
    expert_in_bias = normal_values(streams_of[16], (E, FF), 0.5, 2.5, ((0, 4),))
    expert_out = normal_values(streams_of[17], (E, FF, D), FF ** -0.5, 0.109375, ((0, 4),))
    expert_out_bias = normal_values(streams_of[18], (E, D), 0.5, 2.5, ((0, 4),))
    return dict(tokens=tokens, conditioning=conditioning, routes=routes, cotangent=cotangent, ada_weight=ada_weight, ada_bias=ada_bias, qkv_weight=qkv_weight, qv_bias=qv_bias, out_weight=out_weight, out_bias=out_bias, shared_in=shared_in, shared_in_bias=shared_in_bias, shared_out=shared_out, shared_out_bias=shared_out_bias, router=router, expert_in=expert_in, expert_in_bias=expert_in_bias, expert_out=expert_out, expert_out_bias=expert_out_bias)


@jax.custom_vjp
def low(v):
    return lax.optimization_barrier(v.astype(jnp.bfloat16)).astype(jnp.float32)

@jax.custom_vjp
def low_back(v):
    return v

def low_keep(v):
    return (low(v), None)

def low_pass(kept, grad):
    return (grad,)

def back_keep(v):
    return (v, None)

def back_low(kept, grad):
    return (low(grad),)
low.defvjp(low_keep, low_pass)
low_back.defvjp(back_keep, back_low)
precise = lax.Precision.HIGHEST

def layer_norm(rows):
    centred = rows - lax.optimization_barrier(jnp.mean(rows, axis=-1, keepdims=True))
    return centred * lax.rsqrt(lax.optimization_barrier(jnp.mean(centred * centred, axis=-1, keepdims=True)) + 1e-06)

def matmul(left, right):
    return jnp.dot(left, right, precision=precise)

def front(images, modulation, qkv_weight, qv_bias, out_weight, out_bias, shared_in, shared_in_bias, shared_out, shared_out_bias, router):
    count, length, width = images.shape
    pieces = [modulation[:, None, index * width:(index + 1) * width] for index in range(6)]
    normed = low(layer_norm(images) * (1.0 + pieces[1]) + pieces[0])
    projected = matmul(normed, qkv_weight)
    query = low_back(low(projected[..., :width] + qv_bias[0]))
    keys = low_back(low(projected[..., width:2 * width]))
    values = low_back(low(projected[..., 2 * width:] + qv_bias[1]))
    head_shape = (count, length, HEADS, HEAD_DIM)
    scores = jnp.einsum('gqhc,gkhc->ghqk', query.reshape(head_shape), keys.reshape(head_shape), precision=precise) * HEAD_DIM ** (-0.5)
    scores = low_back(scores)
    probs = low(jax.nn.softmax(scores, axis=-1))
    mixed = jnp.einsum('ghqk,gkhc->gqhc', probs, values.reshape(head_shape), precision=precise).reshape(count, length, width)
    mixed = low_back(low(mixed))
    attended = low_back(matmul(mixed, out_weight) + out_bias)
    resid = images + pieces[2] * attended
    second = low(layer_norm(resid) * (1.0 + pieces[4]) + pieces[3])
    shared_pre = low_back(matmul(second, shared_in) + shared_in_bias)
    shared = matmul(low(jax.nn.gelu(shared_pre, approximate=True)), shared_out) + shared_out_bias
    logits = low_back(matmul(second, router))
    return (resid, second, shared, logits)

def reference(tokens, conditioning, routes, cotangent, ada_weight, ada_bias, qkv_weight, qv_bias, out_weight, out_bias, shared_in, shared_in_bias, shared_out, shared_out_bias, router, expert_in, expert_in_bias, expert_out, expert_out_bias):
    blocks = N_DP * N_EXPERT
    group = math.gcd(IMAGES, max(1, 4096 // SEQ))
    group_count = IMAGES // group
    route_rows = routes.reshape(blocks, 2 * TOK_DEV).astype(jnp.int32)
    one_hot = (route_rows[..., None] == jnp.arange(E, dtype=jnp.int32)).astype(jnp.int32)
    rank = jnp.cumsum(one_hot, axis=1, dtype=jnp.int32) - one_hot
    slot_index = lax.optimization_barrier(jnp.sum(rank * one_hot, axis=-1, dtype=jnp.int32))
    block_index = jnp.arange(blocks, dtype=jnp.int32)[:, None]
    position = jnp.where(slot_index < CAP, route_rows * (blocks * CAP) + block_index * CAP + slot_index, E * blocks * CAP).astype(jnp.int32).reshape(-1)
    pair_mask = one_hot.reshape(blocks, TOK_DEV, 2, E)

    def forward(tokens, conditioning, ada_weight, ada_bias, qkv_weight, qv_bias, out_weight, out_bias, shared_in, shared_in_bias, shared_out, shared_out_bias, router, expert_in, expert_in_bias, expert_out, expert_out_bias):
        modulation = low_back(matmul(low(jax.nn.silu(conditioning)), ada_weight) + ada_bias)

        def one_group(pair):
            return front(pair[0], pair[1], qkv_weight, qv_bias, out_weight, out_bias, shared_in, shared_in_bias, shared_out, shared_out_bias, router)
        resid, second, shared, logits = lax.map(jax.checkpoint(one_group), (tokens.reshape(group_count, group, SEQ, D), modulation.reshape(group_count, group, 6 * D)))
        second_rows = second.reshape(blocks, TOK_DEV, D)
        pair_rows = jnp.repeat(second_rows, 2, axis=1).reshape(-1, D)
        buffer = jnp.zeros((E * blocks * CAP, D), jnp.float32).at[position].add(pair_rows, mode='drop')
        dispatched = low_back(buffer).reshape(E, blocks * CAP, D)

        def one_expert(items):
            rows_in, first, first_bias, last, last_bias = items
            hidden = low_back(matmul(rows_in, first) + first_bias)
            return low_back(low(matmul(low(jax.nn.gelu(hidden, approximate=True)), last) + last_bias))
        results = lax.map(jax.checkpoint(one_expert), (dispatched, expert_in, expert_in_bias, expert_out, expert_out_bias))
        gathered = results.reshape(-1, D).at[position].get(mode='fill', fill_value=0.0).reshape(blocks, TOK_DEV, 2, D)
        chosen = lax.optimization_barrier(jnp.sum(logits.reshape(blocks, TOK_DEV, 1, E) * pair_mask, axis=-1))
        gates = jax.nn.softmax(chosen, axis=-1)
        expert_sum = lax.optimization_barrier(jnp.sum(gates[..., None] * gathered, axis=2))
        moe = low_back(shared.reshape(blocks, TOK_DEV, D) + expert_sum).reshape(IMAGES, SEQ, D)
        return resid.reshape(IMAGES, SEQ, D) + modulation[:, None, 5 * D:] * moe
    floats = [item.astype(jnp.float32) for item in (tokens, conditioning, ada_weight, ada_bias, qkv_weight, qv_bias, out_weight, out_bias, shared_in, shared_in_bias, shared_out, shared_out_bias, router, expert_in, expert_in_bias, expert_out, expert_out_bias)]
    output, pullback = jax.vjp(forward, *floats)
    grads = pullback(cotangent.astype(jnp.float32))
    return (output.astype(jnp.bfloat16), grads[0], grads[1], grads[2], grads[3], grads[4], grads[5], grads[6], grads[7], grads[8], grads[9], grads[10], grads[11], grads[12], grads[13], grads[14], grads[15], grads[16])
```

```python
import functools

import jax
import jax.numpy as jnp
from jax import lax
from jax.experimental import pallas as pl
from jax.experimental.pallas import tpu as pltpu
from jax.sharding import PartitionSpec as P

HEADS = 12
HEAD_DIM = 64
E = 8
CAP = 80
MESH = pl.DeviceIdType.MESH
F32 = jnp.float32
B16 = jnp.bfloat16
VMEM_LIMIT = 60 * 1024 * 1024
SCALE = HEAD_DIM ** (-0.5)
GELU_C = 0.7978845608028654
NZ, NX = 4, 2


def coords():
    dp = lax.axis_index("dp")
    ex = lax.axis_index("expert")
    return lax.div(dp, NX), lax.rem(dp, NX), lax.div(ex, 2), lax.rem(ex, 2)


def dev(z, x, y, c):
    return (NX * z + x, 2 * y + c)


def dot(a, b):
    return jnp.dot(a, b, preferred_element_type=F32)


def dot_nt(a, b):
    return lax.dot_general(a, b, (((1,), (1,)), ((), ())), preferred_element_type=F32)


def dot_tn(a, b):
    return lax.dot_general(a, b, (((0,), (0,)), ((), ())), preferred_element_type=F32)


def gelu_parts(v):
    v2 = v * v
    t = jnp.tanh(GELU_C * v * (1.0 + 0.044715 * v2))
    h = 0.5 * (1.0 + t)
    return v * h, h + 0.5 * v * (1.0 - t * t) * (GELU_C * (1.0 + 0.134145 * v2))


def norm_parts(v):
    centred = v - jnp.mean(v, axis=-1, keepdims=True)
    r = lax.rsqrt(jnp.mean(centred * centred, axis=-1, keepdims=True) + 1e-06)
    return centred * r, r


def norm_back(u, n, r):
    return r * (
        u - jnp.mean(u, axis=-1, keepdims=True) - n * jnp.mean(u * n, axis=-1, keepdims=True)
    )


def remote(src, dst, send, recv, to):
    return pltpu.make_async_remote_copy(
        src_ref=src,
        dst_ref=dst,
        send_sem=send,
        recv_sem=recv,
        device_id=to,
        device_id_type=MESH,
    )


def greet(barrier, to):
    pl.semaphore_signal(barrier, inc=1, device_id=to, device_id_type=MESH)


def params(collective_id=None):
    if collective_id is None:
        return pltpu.CompilerParams(vmem_limit_bytes=VMEM_LIMIT)
    return pltpu.CompilerParams(
        vmem_limit_bytes=VMEM_LIMIT, collective_id=collective_id, has_side_effects=True
    )


VM = pl.BlockSpec(memory_space=pltpu.VMEM)
HB = pl.BlockSpec(memory_space=pl.ANY)


def sds(shape, dtype):
    return jax.ShapeDtypeStruct(shape, dtype)


class Gather:
    def __init__(self, shards, fulls, splits, sems):
        self.z, self.x, self.y, self.c = coords()
        self.mats = list(zip(shards, fulls, splits))
        (self.zs, self.zr, self.xs, self.xr, self.ys, self.yr, self.cs, self.cr, self.loc) = sems

    @staticmethod
    def semaphores(count):
        dma = pltpu.SemaphoreType.DMA
        return [
            dma((count, 2, NZ)),
            dma((count, NZ)),
            dma((count, NZ)),
            dma((count, NZ)),
            dma((count, NZ, NX)),
            dma((count, NZ, NX)),
            dma((count, NZ, NX, 2)),
            dma((count, NZ, NX, 2)),
            dma((count,)),
        ]

    def region(self, m, zb, xb, yh, ch):
        shard, full, split = self.mats[m]
        rows, width = shard.shape[0], shard.shape[1] // 2
        start = (NX * zb + xb) * rows
        if split:
            rows = rows // 2
            start = start + yh * rows
        return full.at[
            pl.ds(pl.multiple_of(start, 16), rows), pl.ds(pl.multiple_of(ch * width, 128), width)
        ]

    def own(self, m):
        shard, full, split = self.mats[m]
        rows, width = shard.shape[0], shard.shape[1] // 2
        start = 0
        if split:
            rows = rows // 2
            start = self.y * rows
        return shard.at[
            pl.ds(pl.multiple_of(start, 16), rows),
            pl.ds(pl.multiple_of(self.c * width, 128), width),
        ]

    def zcopy(self, m, zb, side, mine=False):
        here = self.region(m, zb, self.x, self.y, self.c)
        step = 1 if side else -1
        return remote(
            self.own(m) if mine else here,
            here,
            self.zs.at[m, side, zb],
            self.zr.at[m, zb],
            dev(lax.rem(self.z + step + NZ, NZ), self.x, self.y, self.c),
        )

    def xcopy(self, m, zb, mine=False, xb=None):
        here = self.region(m, zb, self.x if xb is None else xb, self.y, self.c)
        return remote(
            self.own(m) if mine else here,
            here,
            self.xs.at[m, zb],
            self.xr.at[m, zb],
            dev(self.z, 1 - self.x, self.y, self.c),
        )

    def ycopy(self, m, zb, xb, yh=None):
        here = self.region(m, zb, xb, self.y if yh is None else yh, self.c)
        return remote(
            here,
            here,
            self.ys.at[m, zb, xb],
            self.yr.at[m, zb, xb],
            dev(self.z, self.x, 1 - self.y, self.c),
        )

    def ccopy(self, m, zb, xb, yh, ch=None):
        here = self.region(m, zb, xb, yh, self.c if ch is None else ch)
        slot = yh if self.mats[m][2] else 0
        return remote(
            here,
            here,
            self.cs.at[m, zb, xb, slot],
            self.cr.at[m, zb, xb, slot],
            dev(self.z, self.x, self.y, 1 - self.c),
        )

    def local(self, m):
        shard, full, _ = self.mats[m]
        rows = shard.shape[0]
        start = (NX * self.z + self.x) * rows
        return pltpu.make_async_copy(
            shard, full.at[pl.ds(pl.multiple_of(start, 16), rows), :], self.loc.at[m]
        )

    def blocks(self, step):
        if step == 0:
            return [(self.z, None, None)]
        return [
            (self.z - step, self.z - step >= 0, 1),
            (self.z + step, self.z + step < NZ, 0),
        ]

    def more(self, side):
        return self.z + 1 < NZ if side else self.z - 1 >= 0

    def begin(self, m):
        for side in (1, 0):

            @pl.when(self.more(side))
            def _():
                self.zcopy(m, self.z, side, True).start()

        self.xcopy(m, self.z, True).start()
        self.local(m).start()

    def spread(self, m, zb, xb):
        if self.mats[m][2]:
            self.ycopy(m, zb, xb).start()
        self.ccopy(m, zb, xb, self.y).start()

    def take_z(self, m, step):
        for zb, exists, side in self.blocks(step):

            @pl.when(exists)
            def _():
                self.zcopy(m, zb, side).wait_recv()
                if step < NZ - 1:

                    @pl.when(self.more(side))
                    def _():
                        self.zcopy(m, zb, side).start()

                self.xcopy(m, zb).start()
                self.spread(m, zb, self.x)

    def take_x(self, m, step):
        for zb, exists, _ in self.blocks(step):

            def body():
                self.xcopy(m, zb, False, 1 - self.x).wait_recv()
                self.spread(m, zb, 1 - self.x)

            body() if exists is None else pl.when(exists)(body)

    def others(self, m, step, action):
        for zb, exists, _ in self.blocks(step):
            for xb in (self.x, 1 - self.x) if step else (1 - self.x,):
                body = functools.partial(action, m, zb, xb)
                body() if exists is None else pl.when(exists)(body)

    def take_y(self, m, step):
        if not self.mats[m][2]:
            return

        def action(m, zb, xb):
            self.ycopy(m, zb, xb, 1 - self.y).wait_recv()
            self.ccopy(m, zb, xb, 1 - self.y).start()

        self.others(m, step, action)

    def finish(self, m):
        def action(m, zb, xb):
            for yh in (self.y, 1 - self.y) if self.mats[m][2] else (self.y,):
                self.ccopy(m, zb, xb, yh, 1 - self.c).wait_recv()
                self.ccopy(m, zb, xb, yh).wait_send()
            if self.mats[m][2]:
                self.ycopy(m, zb, xb).wait_send()

        for step in range(NZ):
            self.others(m, step, action)
        for side in (1, 0):

            @pl.when(self.more(side))
            def _():
                self.zcopy(m, self.z, side, True).wait_send()

        for step in range(1, NZ):
            for zb, exists, side in self.blocks(step):

                @pl.when(exists)
                def _():
                    self.xcopy(m, zb).wait_send()
                    if step < NZ - 1:

                        @pl.when(self.more(side))
                        def _():
                            self.zcopy(m, zb, side).wait_send()

        self.xcopy(m, self.z, True).wait_send()
        self.local(m).wait()

    def run(self, mats):
        for step in range(NZ):
            for m in mats:
                if step:
                    self.take_z(m, step)
                self.take_x(m, step)
            if step:
                for m in mats:
                    self.take_y(m, step - 1)
        for m in mats:
            self.take_y(m, NZ - 1)
        for m in mats:
            self.finish(m)


def gather_kernel(splits, *refs):
    count = len(splits)
    ada, pack = refs[:2]
    shards = refs[2 : 2 + count]
    rest = refs[2 + count :]
    mod_ref, packs = rest[:2]
    fulls = rest[2 : 2 + count]
    sent, got, s1, r1, s2, r2 = rest[2 + count : 8 + count]
    plan = Gather(shards, fulls, splits, rest[8 + count :])
    dp, ex = lax.axis_index("dp"), lax.axis_index("expert")
    n = NZ * NX
    barrier = pltpu.get_barrier_semaphore()
    for p in range(n):

        @pl.when(p != dp)
        def _():
            greet(barrier, (p, ex))

    greet(barrier, dev(plan.z, plan.x, 1 - plan.y, plan.c))
    greet(barrier, dev(plan.z, plan.x, plan.y, 1 - plan.c))
    pl.semaphore_wait(barrier, n + 1)

    def first(p):
        return remote(pack, packs.at[dp], s1.at[p], r1.at[dp], (p, ex))

    def first_from(p):
        return remote(pack, packs.at[p], s1.at[p], r1.at[p], (p, ex))

    def second(p):
        return remote(sent.at[p], got.at[dp], s2.at[p], r2.at[dp], (p, ex))

    def second_from(p):
        return remote(sent.at[p], got.at[p], s2.at[p], r2.at[p], (p, ex))

    def peers(action):
        for p in range(n):

            @pl.when(p != dp)
            def _():
                action(p)

    peers(lambda p: first(p).start())
    for m in range(count):
        plan.begin(m)
    packs[dp] = pack[...]
    peers(lambda p: first_from(p).wait_recv())
    rows = jnp.concatenate([packs[p, pl.ds(24 + dp, 1), :] for p in range(n)], axis=0)
    width = ada.shape[0]
    partial = dot(rows[:, :width].astype(B16), ada[...])
    for j in range(partial.shape[1] // 128):
        sent[:, j, :] = partial[:, 128 * j : 128 * (j + 1)]
    peers(lambda p: second(p).start())
    got[dp] = sent[dp]

    plan.run(range(count))

    peers(lambda p: second_from(p).wait_recv())
    total = got[0]
    for p in range(1, n):
        total = total + got[p]
    per = mod_ref.shape[1] // 128
    mod_ref[...] = jnp.zeros_like(mod_ref)
    for i in range(6):
        for b in range(per):
            mod_ref[i : i + 1, 128 * b : 128 * (b + 1)] = total[per * i + b : per * i + b + 1, :]
    peers(lambda p: first(p).wait_send())
    peers(lambda p: second(p).wait_send())


def gather_dense(ada, pack, shards, splits):
    n = NZ * NX
    dma = pltpu.SemaphoreType.DMA
    tiles = ada.shape[1] // 128
    tiles = (tiles + 7) // 8 * 8
    fulls = [sds((n * s.shape[0], s.shape[1]), s.dtype) for s in shards]
    out = pl.pallas_call(
        functools.partial(gather_kernel, splits),
        out_shape=[sds((8, ada.shape[1] // 6), F32), sds((n,) + pack.shape, F32)] + fulls,
        in_specs=[VM, VM] + [HB] * len(shards),
        out_specs=[VM, VM] + [HB] * len(shards),
        scratch_shapes=[
            pltpu.VMEM((n, tiles, 128), F32),
            pltpu.VMEM((n, tiles, 128), F32),
            dma((n,)),
            dma((n,)),
            dma((n,)),
            dma((n,)),
        ]
        + Gather.semaphores(len(shards)),
        compiler_params=params(1),
        name="gather_dense",
    )(ada, pack, *shards)
    return out[0], out[1], out[2:]


def choose_rows(place, slots):
    return place == lax.broadcasted_iota(jnp.int32, (place.shape[0], slots), 1)


def front_kernel(
    tok, cot, routes, mod_in, abias, qkv, outw, bias, router,
    normed_o, proj_o, lsum_o, mixed_o, att_o, resid_o, second_o, gates_o, place_o, sbuf_o, gbuf_o, mod_o,
):
    length, width = tok.shape
    mod = mod_in[...] + abias[...]
    mod_o[...] = mod
    source = tok[...].astype(F32)
    n1, _ = norm_parts(source)
    normed = (n1 * (1.0 + mod[1:2]) + mod[0:1]).astype(B16)
    normed_o[...] = normed
    for k in range(3):
        part = dot(normed, qkv[:, k * width : (k + 1) * width])
        if k != 1:
            part = part + bias[k // 2 : k // 2 + 1, :]
        proj_o[:, k * width : (k + 1) * width] = part.astype(B16)
    low_lane = lax.broadcasted_iota(jnp.int32, (length, 128), 1) < HEAD_DIM
    lane = lax.broadcasted_iota(jnp.int32, (length, 128), 1)
    lsum = jnp.zeros((length, 128), F32)
    for p in range(HEADS // 2):
        q2 = proj_o[:, 128 * p : 128 * (p + 1)]
        k2 = proj_o[:, width + 128 * p : width + 128 * (p + 1)]
        v2 = proj_o[:, 2 * width + 128 * p : 2 * width + 128 * (p + 1)]
        outs = []
        for h in range(2):
            mine = low_lane if h == 0 else jnp.logical_not(low_lane)
            s = dot_nt(jnp.where(mine, q2, jnp.zeros_like(q2)), k2) * SCALE
            peak = jnp.max(s, axis=-1, keepdims=True)
            e = jnp.exp(s - peak)
            total = jnp.sum(e, axis=-1, keepdims=True)
            lsum = jnp.where(lane == 2 * p + h, peak + jnp.log(total), lsum)
            outs.append(dot((e / total).astype(B16), v2))
        mixed_o[:, 128 * p : 128 * (p + 1)] = jnp.where(low_lane, outs[0], outs[1]).astype(B16)
    lsum_o[...] = lsum
    att = dot(mixed_o[...], outw[...]) + bias[2:3, :]
    att_o[...] = att
    resid = source + mod[2:3] * att
    resid_o[...] = resid
    n2, _ = norm_parts(resid)
    second = (n2 * (1.0 + mod[4:5]) + mod[3:4]).astype(B16)
    second_o[...] = second
    logits = dot(second, router[...])
    picks = [(routes[:, k : k + 1] == lane) for k in range(2)]
    chosen = [jnp.sum(jnp.where(pick, logits, 0.0), axis=-1, keepdims=True) for pick in picks]
    top = jnp.maximum(chosen[0], chosen[1])
    ex = [jnp.exp(v - top) for v in chosen]
    gates = [v / (ex[0] + ex[1]) for v in ex]
    gates_o[...] = jnp.where(lane == 0, gates[0], jnp.where(lane == 1, gates[1], 0.0))
    both = jnp.where(picks[0], 1.0, 0.0) + jnp.where(picks[1], 1.0, 0.0)
    earlier = (
        lax.broadcasted_iota(jnp.int32, (length, length), 1)
        < lax.broadcasted_iota(jnp.int32, (length, length), 0)
    )
    rank = dot(jnp.where(earlier, 1.0, 0.0).astype(B16), both.astype(B16))
    places = []
    for k in range(2):
        slot = jnp.sum(jnp.where(picks[k], rank, 0.0), axis=-1, keepdims=True).astype(jnp.int32)
        places.append(jnp.where(slot < CAP, routes[:, k : k + 1] * CAP + slot, -1))
    place_o[...] = jnp.where(lane == 0, places[0], jnp.where(lane == 1, places[1], -1))
    maps = [jnp.where(choose_rows(v, E * CAP), 1.0, 0.0) for v in places]
    sbuf_o[...] = dot_tn((maps[0] + maps[1]).astype(B16), second).astype(B16)
    moe_grad = (mod[5:6] * cot[...].astype(F32)).astype(B16).astype(F32)
    pair = [(g * moe_grad).astype(B16) for g in gates]
    gbuf_o[...] = (
        dot_tn(maps[0].astype(B16), pair[0]) + dot_tn(maps[1].astype(B16), pair[1])
    ).astype(B16)


def front(tok, cot, routes, mod_in, abias, qkv, outw, bias, router):
    length, width = tok.shape
    rows = E * CAP
    return pl.pallas_call(
        front_kernel,
        out_shape=[
            sds((length, width), B16),
            sds((length, 3 * width), B16),
            sds((length, 128), F32),
            sds((length, width), B16),
            sds((length, width), F32),
            sds((length, width), F32),
            sds((length, width), B16),
            sds((length, 128), F32),
            sds((length, 128), jnp.int32),
            sds((rows, width), B16),
            sds((rows, width), B16),
            sds((8, width), F32),
        ],
        in_specs=[VM] * 9,
        out_specs=[VM] * 12,
        compiler_params=params(),
        name="attention_front",
    )(tok, cot, routes, mod_in, abias, qkv, outw, bias, router)


def plane_peer(k):
    z, x, y, c = coords()
    xt = 1 - x if k & 1 else x
    ct = 1 - c if k & 2 else c
    yt = 1 - y if k & 4 else y
    return dev(z, xt, yt, ct), 4 * yt + 2 * ct + xt


def plane_rank():
    _, x, y, c = coords()
    return 4 * y + 2 * c + x


def greet_plane():
    barrier = pltpu.get_barrier_semaphore()
    for k in range(1, E):
        greet(barrier, plane_peer(k)[0])
    pl.semaphore_wait(barrier, E - 1)


def slot_rows(ref, rank):
    return ref.at[pl.ds(pl.multiple_of(rank * CAP, 16), CAP), :]


def plane_exchange(sources, targets, send, recv):
    rank = plane_rank()

    def copy(k, i, to=None):
        peer, other = plane_peer(k)
        return remote(
            slot_rows(sources[i], other), slot_rows(targets[i], rank), send.at[i, k], recv.at[i, k], peer
        )

    pairs = [(k, i) for k in (7, 5, 6, 4, 3, 1, 2) for i in range(len(sources))]
    for k, i in pairs:
        copy(k, i).start()
    for source, target in zip(sources, targets):
        start = pl.multiple_of(rank * CAP, 16)
        target[pl.ds(start, CAP), :] = source[pl.ds(start, CAP), :]

    def take(k, i):
        _, other = plane_peer(k)
        return remote(
            slot_rows(sources[i], other), slot_rows(targets[i], other), send.at[i, k], recv.at[i, k],
            plane_peer(k)[0],
        )

    def wait_in():
        for k, i in pairs:
            take(k, i).wait_recv()

    def wait_out():
        for k, i in pairs:
            take(k, i).wait_send()

    return wait_in, wait_out


EXPERT_CHUNK = 512


def expert_kernel(
    sbuf, gbuf, win_h, wout_h, bin_r, bout_r,
    dwin, dwout, res, bgr, ebias,
    rows, grads, win, wout, acc, back, send, recv, wsem,
):
    x = coords()[1]
    loads = [
        pltpu.make_async_copy(win_h.at[x], win, wsem.at[0]),
        pltpu.make_async_copy(wout_h.at[x], wout, wsem.at[1]),
    ]
    for load in loads:
        load.start()
    greet_plane()
    wait_in, wait_out = plane_exchange((sbuf, gbuf), (rows, grads), send, recv)
    for load in loads:
        load.wait()
    first_x = x == 0
    bout = jnp.where(first_x, bout_r[0:1, :], bout_r[1:2, :])
    acc[...] = jnp.zeros_like(acc) + bout
    back[...] = jnp.zeros_like(back)
    ebias[...] = jnp.zeros_like(ebias)
    wait_in()
    width = rows.shape[1]
    hidden = win.shape[1]
    chunk = EXPERT_CHUNK
    tiles = chunk // 128
    column = jnp.sum(grads[...].astype(F32), axis=0, keepdims=True)
    for j in range(width // 128):
        at = hidden // 128 + j
        ebias[at : at + 1, :] = column[:, 128 * j : 128 * (j + 1)]

    def body(f, carry):
        cols = pl.ds(pl.multiple_of(f * chunk, 128), chunk)
        bias = jnp.where(first_x, bin_r[0:1, cols], bin_r[1:2, cols])
        w1 = win[:, cols]
        w2 = wout[cols, :]
        data = rows[...]
        grad = grads[...]
        act, slope = gelu_parts(dot(data, w1) + bias)
        low = act.astype(B16)
        acc[...] += dot(low, w2)
        pre = (dot_nt(grad, w2) * slope).astype(B16)
        dwout[cols, :] = dot_tn(low, grad).astype(B16)
        dwin[:, cols] = dot_tn(data, pre).astype(B16)
        back[...] += dot_nt(pre, w1)
        col = jnp.sum(pre.astype(F32), axis=0, keepdims=True)
        for j in range(tiles):
            ebias[pl.ds(f * tiles + j, 1), :] = col[:, 128 * j : 128 * (j + 1)]
        return carry

    lax.fori_loop(0, hidden // chunk, body, 0)
    res[...] = acc[...].astype(B16)
    bgr[...] = back[...].astype(B16)
    wait_out()


def expert(sbuf, gbuf, win, wout, bin_r, bout_r):
    rows, width = sbuf.shape
    hidden = win.shape[2]
    dma = pltpu.SemaphoreType.DMA
    return pl.pallas_call(
        expert_kernel,
        out_shape=[
            sds((width, hidden), B16),
            sds((hidden, width), B16),
            sds((rows, width), B16),
            sds((rows, width), B16),
            sds((32, 128), F32),
        ],
        in_specs=[VM, VM, HB, HB, VM, VM],
        out_specs=[VM] * 5,
        scratch_shapes=[
            pltpu.VMEM((rows, width), B16),
            pltpu.VMEM((rows, width), B16),
            pltpu.VMEM((width, hidden), B16),
            pltpu.VMEM((hidden, width), B16),
            pltpu.VMEM((rows, width), F32),
            pltpu.VMEM((rows, width), F32),
            dma((2, E)),
            dma((2, E)),
            dma((2,)),
        ],
        compiler_params=params(2),
        name="routed_expert",
    )(sbuf, gbuf, win, wout, bin_r, bout_r)


SHARED_CHUNK = 768


def middle_kernel(
    res, bgr, second_r, resid_r, att_r, cot, routes, mod, sin, sout, sinb, bias, router, gates_r, place_r,
    mixed, outw,
    out_o, rgrad_o, mgrad_o, dsin, dsout, dout, drouter, vecs, mg2,
    ret, retg, shared, sgrad, send, recv,
):
    greet_plane()
    wait_in, wait_out = plane_exchange((res, bgr), (ret, retg), send, recv)
    length, width = second_r.shape
    hidden = sin.shape[1]
    chunk = SHARED_CHUNK
    second = second_r[...]
    grad_out = cot[...].astype(F32)
    moe_low = (mod[5:6] * grad_out).astype(B16)
    moe_grad = moe_low.astype(F32)
    shared[...] = jnp.zeros_like(shared) + bias[3:4, :]
    sgrad[...] = jnp.zeros_like(sgrad)
    vecs[...] = jnp.zeros_like(vecs)

    def body(f, carry):
        cols = pl.ds(pl.multiple_of(f * chunk, 128), chunk)
        w1 = sin[:, cols]
        w2 = sout[cols, :]
        act, slope = gelu_parts(dot(second, w1) + sinb[:, cols])
        low = act.astype(B16)
        shared[...] += dot(low, w2)
        pre = (dot_nt(moe_low, w2) * slope).astype(B16)
        dsout[cols, :] = dot_tn(low, moe_low).astype(B16)
        dsin[:, cols] = dot_tn(second, pre).astype(B16)
        sgrad[...] += dot_nt(pre, w1)
        col = jnp.sum(pre.astype(F32), axis=0, keepdims=True)
        for j in range(chunk // 128):
            vecs[pl.ds(f * (chunk // 128) + j, 1), :] = col[:, 128 * j : 128 * (j + 1)]
        return carry

    lax.fori_loop(0, hidden // chunk, body, 0)
    lane = lax.broadcasted_iota(jnp.int32, (length, 128), 1)
    gates = [gates_r[:, k : k + 1] for k in range(2)]
    maps = [
        jnp.where(choose_rows(place_r[:, k : k + 1], E * CAP), 1.0, 0.0) for k in range(2)
    ]
    wait_in()
    back = ret[...]
    rows = [dot(m.astype(B16), back) for m in maps]
    moe = shared[...] + (gates[0] * rows[0] + gates[1] * rows[1])
    resid = resid_r[...]
    out_o[...] = (resid + mod[5:6] * moe).astype(B16)
    mg2[...] = jnp.zeros_like(mg2)
    mg2[5:6, :] = jnp.sum(grad_out * moe, axis=0, keepdims=True)
    ggrad = [jnp.sum(moe_grad * r, axis=-1, keepdims=True) for r in rows]
    inner = gates[0] * ggrad[0] + gates[1] * ggrad[1]
    lgrad = jnp.zeros((length, 128), F32)
    for k in range(2):
        pick = routes[:, k : k + 1] == lane
        lgrad = lgrad + jnp.where(pick, gates[k] * (ggrad[k] - inner), 0.0)
    lgrad = lgrad.astype(B16)
    drouter[...] = dot_tn(lgrad, second)[0:E, :]
    grad = (
        sgrad[...]
        + dot((maps[0] + maps[1]).astype(B16), retg[...])
        + dot_nt(lgrad, router[...])
    )
    n2, r2 = norm_parts(resid)
    mg2[3:4, :] = jnp.sum(grad, axis=0, keepdims=True)
    mg2[4:5, :] = jnp.sum(grad * n2, axis=0, keepdims=True)
    rgrad = grad_out + norm_back(grad * (1.0 + mod[4:5]), n2, r2)
    rgrad_o[...] = rgrad
    agrad = (mod[2:3] * rgrad).astype(B16)
    mg2[2:3, :] = jnp.sum(rgrad * att_r[...], axis=0, keepdims=True)
    dout[...] = dot_tn(mixed[...], agrad).astype(B16)
    mgrad_o[...] = dot_nt(agrad, outw[...]).astype(B16)
    sums = [
        jnp.sum(moe_grad, axis=0, keepdims=True),
        jnp.sum(agrad.astype(F32), axis=0, keepdims=True),
    ]
    base = hidden // 128
    for i, row in enumerate(sums):
        for j in range(width // 128):
            at = base + i * (width // 128) + j
            vecs[at : at + 1, :] = row[:, 128 * j : 128 * (j + 1)]
    wait_out()


def middle(*args):
    res, second, sin = args[0], args[2], args[8]
    length, width = second.shape
    rows, hidden = res.shape[0], sin.shape[1]
    dma = pltpu.SemaphoreType.DMA
    return pl.pallas_call(
        middle_kernel,
        out_shape=[
            sds((length, width), B16),
            sds((length, width), F32),
            sds((length, width), B16),
            sds((width, hidden), B16),
            sds((hidden, width), B16),
            sds((width, width), B16),
            sds((E, width), F32),
            sds((40, 128), F32),
            sds((8, width), F32),
        ],
        in_specs=[VM] * 17,
        out_specs=[VM] * 9,
        scratch_shapes=[
            pltpu.VMEM((rows, width), B16),
            pltpu.VMEM((rows, width), B16),
            pltpu.VMEM((length, width), F32),
            pltpu.VMEM((length, width), F32),
            dma((2, E)),
            dma((2, E)),
        ],
        compiler_params=params(3),
        name="shared_expert_combine",
    )(*args)


def back_kernel(
    tok, mod, normed, proj, lsum, mgrad, rgrad, qkv, mg2,
    tgrad_o, dqkv, qvec, mgt,
    pgrad,
):
    length, width = tok.shape
    low_lane = lax.broadcasted_iota(jnp.int32, (length, 128), 1) < HEAD_DIM
    for p in range(HEADS // 2):
        q2 = proj[:, 128 * p : 128 * (p + 1)]
        k2 = proj[:, width + 128 * p : width + 128 * (p + 1)]
        v2 = proj[:, 2 * width + 128 * p : 2 * width + 128 * (p + 1)]
        m2 = mgrad[:, 128 * p : 128 * (p + 1)]
        parts = []
        for h in range(2):
            mine = low_lane if h == 0 else jnp.logical_not(low_lane)
            zero = jnp.zeros_like(q2)
            s = dot_nt(jnp.where(mine, q2, zero), k2) * SCALE
            prob = jnp.exp(s - lsum[:, 2 * p + h : 2 * p + h + 1])
            pg = dot_nt(jnp.where(mine, m2, zero), v2)
            inner = jnp.sum(prob * pg, axis=-1, keepdims=True)
            sg = (prob * (pg - inner)).astype(B16)
            parts.append(
                (dot(sg, k2) * SCALE, dot_tn(sg, q2) * SCALE, dot_tn(prob.astype(B16), m2))
            )
        for i in range(3):
            pgrad[:, i * width + 128 * p : i * width + 128 * (p + 1)] = jnp.where(
                low_lane, parts[0][i], parts[1][i]
            ).astype(B16)
    ngrad = dot_nt(pgrad[...], qkv[...])
    for i in range(3):
        dqkv[:, i * width : (i + 1) * width] = dot_tn(
            normed[...], pgrad[:, i * width : (i + 1) * width]
        ).astype(B16)
    per = width // 128
    for i, k in enumerate((0, 2)):
        row = jnp.sum(pgrad[:, k * width : (k + 1) * width].astype(F32), axis=0, keepdims=True)
        for j in range(per):
            qvec[i * per + j : i * per + j + 1, :] = row[:, 128 * j : 128 * (j + 1)]
    for j in range(2 * per, qvec.shape[0]):
        qvec[j : j + 1, :] = jnp.zeros((1, 128), F32)
    n1, r1 = norm_parts(tok[...].astype(F32))
    tgrad_o[...] = rgrad[...] + norm_back(ngrad * (1.0 + mod[1:2]), n1, r1)
    rows = [
        jnp.sum(ngrad, axis=0, keepdims=True),
        jnp.sum(ngrad * n1, axis=0, keepdims=True),
    ] + [mg2[i : i + 1, :] for i in range(2, 6)]
    mgt[...] = jnp.zeros_like(mgt)
    for i, row in enumerate(rows):
        row = row.astype(B16).astype(F32)
        for j in range(per):
            mgt[i * per + j : i * per + j + 1, :] = row[:, 128 * j : 128 * (j + 1)]


def back(*args):
    tok, qkv = args[0], args[7]
    length, width = tok.shape
    return pl.pallas_call(
        back_kernel,
        out_shape=[
            sds((length, width), F32),
            sds(qkv.shape, B16),
            sds((16, 128), F32),
            sds((48, 128), F32),
        ],
        in_specs=[VM] * 9,
        out_specs=[VM] * 4,
        scratch_shapes=[pltpu.VMEM((length, 3 * width), B16)],
        compiler_params=params(),
        name="attention_back",
    )(*args)


PIECES = ((2, 0, 2, True), (3, 0, 1, False), (0, 0, 1, True), (2, 1, 2, False), (1, 0, 1, True))


def add_into(target, source, lead):
    count = 1
    for n in lead:
        count *= n

    def body(i, carry):
        at = []
        rest = i
        for n in reversed(lead):
            at.append(lax.rem(rest, n))
            rest = lax.div(rest, n)
        at = tuple(reversed(at))
        target[at] = (target[at].astype(F32) + source(at).astype(F32)).astype(B16)
        return carry

    lax.fori_loop(0, count, body, 0)


class Reduce:
    def __init__(self, grad, out, col, width, y_first, bufs, sems):
        self.z, self.x, self.y, self.c = coords()
        self.grad, self.out, self.width, self.y_first = grad, out, width, y_first
        self.half = grad.shape[-1] // 2
        self.col = col
        self.cbuf, self.lbuf, self.ebuf, self.fbuf, self.zl, self.zr = bufs
        self.one, self.zsem = sems

    @staticmethod
    def scratch(rows, width):
        vm = lambda *lead: pltpu.VMEM(lead + (rows, width), B16)
        return [
            vm(NZ, NX, 2),
            vm(NZ, NX, 2),
            vm(NZ, 2),
            vm(NZ),
            vm(NZ),
            vm(NZ),
            pltpu.SemaphoreType.DMA((14,)),
            pltpu.SemaphoreType.DMA((4, NZ)),
        ]

    def cols(self, c):
        return pl.ds(pl.multiple_of(c * self.half + self.col, 128), self.width)

    def core_copy(self):
        return remote(
            self.grad.at[:, :, :, :, self.cols(1 - self.c)],
            self.cbuf,
            self.one.at[0],
            self.one.at[1],
            dev(self.z, self.x, self.y, 1 - self.c),
        )

    def load(self):
        return pltpu.make_async_copy(
            self.grad.at[:, :, :, :, self.cols(self.c)], self.lbuf, self.one.at[2]
        )

    def copy1(self):
        if self.y_first:
            source, to = self.cbuf.at[:, :, 1 - self.y], dev(self.z, self.x, 1 - self.y, self.c)
        else:
            source, to = self.cbuf.at[:, 1 - self.x], dev(self.z, 1 - self.x, self.y, self.c)
        return remote(source, self.ebuf, self.one.at[3], self.one.at[4], to)

    def copy2(self):
        if self.y_first:
            source, to = self.ebuf.at[:, 1 - self.x], dev(self.z, 1 - self.x, self.y, self.c)
        else:
            source, to = self.ebuf.at[:, 1 - self.y], dev(self.z, self.x, 1 - self.y, self.c)
        return remote(source, self.fbuf, self.one.at[5], self.one.at[6], to)

    def zcopy(self, zb, side):
        into = self.zl if side else self.zr
        to = lax.rem(self.z + (1 if side else NZ - 1), NZ)
        return remote(
            self.fbuf.at[zb],
            into.at[zb],
            self.zsem.at[side, zb],
            self.zsem.at[2 + side, zb],
            dev(to, self.x, self.y, self.c),
        )

    def own(self):
        return self.fbuf.at[self.z]

    def place(self, y, c):
        return self.out.at[y, :, self.cols(c)]

    def keep(self):
        return pltpu.make_async_copy(self.own(), self.place(self.y, self.c), self.one.at[7])

    def give_y(self):
        return remote(
            self.own(), self.place(self.y, self.c), self.one.at[8], self.one.at[9],
            dev(self.z, self.x, 1 - self.y, self.c),
        )

    def give_c(self):
        return remote(
            self.own(), self.place(self.y, self.c), self.one.at[10], self.one.at[11],
            dev(self.z, self.x, self.y, 1 - self.c),
        )

    def pass_c(self):
        here = self.place(1 - self.y, self.c)
        return remote(
            here, here, self.one.at[12], self.one.at[13], dev(self.z, self.x, self.y, 1 - self.c)
        )

    def absorb(self, zb, side):
        into = self.zl if side else self.zr
        has = self.z > 0 if side else self.z < NZ - 1

        @pl.when(has)
        def _():
            self.zcopy(zb, side).wait_recv()
            self.fbuf[zb] = (self.fbuf[zb].astype(F32) + into[zb].astype(F32)).astype(B16)

    def stage(self, s):
        if s == 0:
            self.core_copy().wait_recv()
            self.load().wait()
            add_into(self.cbuf, lambda i: self.lbuf[i], (NZ, NX, 2))
            self.copy1().start()
        elif s == 1:
            self.copy1().wait_recv()
            if self.y_first:
                add_into(self.ebuf, lambda i: self.cbuf[i[0], i[1], self.y], (NZ, NX))
            else:
                add_into(self.ebuf, lambda i: self.cbuf[i[0], self.x, i[1]], (NZ, 2))
            self.copy2().start()
        elif s == 2:
            self.copy2().wait_recv()
            side = self.x if self.y_first else self.y
            add_into(self.fbuf, lambda i: self.ebuf[i[0], side], (NZ,))
        if 2 <= s < 2 + NZ - 1:
            k = NZ - 1 - (s - 2)
            for side in (1, 0):
                zb = self.z + k if side else self.z - k

                @pl.when(zb < NZ if side else zb >= 0)
                def _():
                    self.absorb(zb, side)
                    self.zcopy(zb, side).start()

        if s == 2 + NZ - 1:
            self.absorb(self.z, 1)
            self.absorb(self.z, 0)
            self.give_y().start()
            self.give_c().start()
            self.keep().start()
        if s == 3 + NZ - 1:
            self.give_y_in().wait_recv()
            self.pass_c().start()
        if s == 4 + NZ - 1:
            self.keep().wait()
            self.give_c_in().wait_recv()
            self.pass_c_in().wait_recv()
            self.core_copy().wait_send()
            self.copy1().wait_send()
            self.copy2().wait_send()
            self.give_y().wait_send()
            self.give_c().wait_send()
            self.pass_c().wait_send()
            for k in range(1, NZ):
                for side in (1, 0):
                    zb = self.z + k if side else self.z - k

                    @pl.when(zb < NZ if side else zb >= 0)
                    def _():
                        self.zcopy(zb, side).wait_send()

    def give_y_in(self):
        return remote(
            self.own(), self.place(1 - self.y, self.c), self.one.at[8], self.one.at[9],
            dev(self.z, self.x, 1 - self.y, self.c),
        )

    def give_c_in(self):
        return remote(
            self.own(), self.place(self.y, 1 - self.c), self.one.at[10], self.one.at[11],
            dev(self.z, self.x, self.y, 1 - self.c),
        )

    def pass_c_in(self):
        here = self.place(1 - self.y, 1 - self.c)
        return remote(
            here, here, self.one.at[12], self.one.at[13], dev(self.z, self.x, self.y, 1 - self.c)
        )

    STAGES = 5 + NZ - 1


def sums_kernel(*refs):
    grads = refs[:4]
    vecs, qvec, drouter, ebias, mgt, condt, ada = refs[4:11]
    outs = refs[11:15]
    small, esum, tiles, cgot = refs[15:19]
    rest = list(refs[19:])
    z, x, y, c = coords()
    dp, ex = lax.axis_index("dp"), lax.axis_index("expert")
    n = NZ * NX

    barrier = pltpu.get_barrier_semaphore()

    def peers(action):
        for p in range(n):

            @pl.when(p != dp)
            def _():
                action(p)

    peers(lambda p: greet(barrier, (p, ex)))
    mates = (dev(z, x, 1 - y, c), dev(z, x, y, 1 - c), dev(z, x, 1 - y, 1 - c))
    for mate in mates:
        greet(barrier, mate)
    pl.semaphore_wait(barrier, n - 1 + 3)

    plans = []
    for matrix, part, share, y_first in PIECES:
        grad = grads[matrix]
        width = grad.shape[-1] // 2 // share
        plans.append(
            Reduce(grad, outs[matrix], part * width, width, y_first, rest[:6], rest[6:8])
        )
        rest = rest[8:]
    ssum, sgot, zgot, esend, egot, mine, csend, sems, dsem, zsem, tsem = rest

    for plan in plans:
        plan.core_copy().start()
        plan.load().start()

    rows = vecs.shape[0]
    ssum[0:rows, :] = vecs[...]
    ssum[rows : rows + 16, :] = qvec[...]
    per = drouter.shape[1] // 128
    for b in range(per):
        ssum[rows + 16 + 8 * b : rows + 24 + 8 * b, :] = drouter[:, 128 * b : 128 * (b + 1)]
    hops = (dev(z, x, y, 1 - c), dev(z, x, 1 - y, c), dev(z, 1 - x, y, c))

    def hop(i):
        return remote(zgot.at[4 + i], sgot.at[i], sems.at[0, i], sems.at[1, i], hops[i])

    def ehop():
        return remote(esend.at[x], egot.at[z, x], sems.at[0, 3], sems.at[1, 3], hops[2])

    def ehop_in():
        return remote(esend.at[x], egot.at[z, 1 - x], sems.at[0, 3], sems.at[1, 3], hops[2])

    mine[0:40, :] = mgt[0:40, :]
    mine[40:48, :] = condt[...]

    def tile(p, at):
        return remote(mine, tiles.at[ex, at], dsem.at[0, p], dsem.at[1, at], (p, ex))

    def spread(i, theirs=False):
        e2 = 2 * (1 - y if i != 1 else y) + (1 - c if i != 0 else c)
        rows = tiles.at[e2 if theirs else ex]
        return remote(rows, rows, tsem.at[0, i], tsem.at[1, i], mates[i])

    def cond_copy(p, at):
        return remote(csend.at[p], cgot.at[at], dsem.at[2, p], dsem.at[3, at], (p, ex))

    def zsum(zb, at):
        return remote(ssum, zgot.at[at], zsem.at[0, zb], zsem.at[1, at], dev(zb, x, y, c))

    def zexp(zb, at):
        return remote(
            egot.at[at], egot.at[at], zsem.at[2, zb], zsem.at[3, at], dev(zb, x, y, c)
        )

    def lines(action):
        for zb in range(NZ):

            @pl.when(zb != z)
            def _():
                action(zb)

    def start_hop(i):
        zgot[4 + i] = ssum[...]
        hop(i).start()

    def end_hop(i):
        hop(i).wait()
        ssum[...] = ssum[...] + sgot[i]

    def small0():
        start_hop(0)
        esend[x] = ebias[...]
        egot[z, x] = ebias[...]
        ehop().start()
        peers(lambda p: tile(p, dp).start())
        tiles[ex, dp] = mine[...]

    def small1():
        end_hop(0)
        start_hop(1)
        peers(lambda p: tile(p, p).wait_recv())
        for i in range(3):
            spread(i).start()
        acc = jnp.zeros((n, ada.shape[0]), F32)
        for j in range(ada.shape[1] // 128):
            acc = acc + dot_nt(tiles[ex, :, j, :].astype(B16), ada[:, 128 * j : 128 * (j + 1)])
        csend[...] = jnp.zeros_like(csend)
        csend[:, 0, 0 : ada.shape[0]] = acc
        peers(lambda p: cond_copy(p, dp).start())
        cgot[dp] = csend[dp]

    def small2():
        end_hop(1)
        start_hop(2)
        ehop().wait_send()
        ehop_in().wait_recv()
        lines(lambda zb: zexp(zb, z).start())

    def small3():
        end_hop(2)
        zgot[z] = ssum[...]
        lines(lambda zb: zsum(zb, z).start())

    def small4():
        lines(lambda zb: zexp(zb, zb).wait_recv())
        lines(lambda zb: zsum(zb, zb).wait_recv())
        total, etotal = zgot[0], egot[0]
        for i in range(1, NZ):
            total = total + zgot[i]
            etotal = etotal + egot[i]
        small[...] = total
        esum[...] = etotal

    def small5():
        peers(lambda p: cond_copy(p, p).wait_recv())
        for i in range(3):
            spread(i, True).wait_recv()
            spread(i).wait_send()
        peers(lambda p: tile(p, p).wait_send())
        peers(lambda p: cond_copy(p, p).wait_send())
        lines(lambda zb: zexp(zb, zb).wait_send())
        lines(lambda zb: zsum(zb, zb).wait_send())

    steps = [small0, small1, small2, small3, small4, small5]
    for t in range(Reduce.STAGES + len(plans) - 1):
        for i, plan in enumerate(plans):
            if 0 <= t - i < Reduce.STAGES:
                plan.stage(t - i)
        if t < len(steps):
            steps[t]()


def device_sums(grads, vecs, qvec, drouter, ebias, mgt, condt, ada):
    n = NZ * NX
    dma = pltpu.SemaphoreType.DMA
    split = [g.reshape(NZ, NX, 2, g.shape[0] // (4 * NZ), g.shape[1]) for g in grads]
    outs = [sds((2, g.shape[3], g.shape[4]), B16) for g in split]
    rows = vecs.shape[0] + 16 + 8 * (drouter.shape[1] // 128)
    scratch = []
    for matrix, _, share, _ in PIECES:
        g = split[matrix]
        scratch += Reduce.scratch(g.shape[3], g.shape[4] // 2 // share)
    vm = pltpu.VMEM
    scratch += [
        vm((rows, 128), F32),
        vm((3, rows, 128), F32),
        vm((NZ + 3, rows, 128), F32),
        vm((2, 32, 128), F32),
        vm((NZ, 2, 32, 128), F32),
        vm((48, 128), F32),
        vm((n, 8, 128), F32),
        dma((2, 4)),
        dma((4, n)),
        dma((4, NZ)),
        dma((2, 3)),
    ]
    out = pl.pallas_call(
        sums_kernel,
        out_shape=outs
        + [
            sds((rows, 128), F32),
            sds((2, 32, 128), F32),
            sds((4, n, 48, 128), F32),
            sds((n, 8, 128), F32),
        ],
        in_specs=[HB] * 4 + [VM] * 7,
        out_specs=[HB] * 4 + [VM] * 4,
        scratch_shapes=scratch,
        compiler_params=params(4),
        name="device_sums",
    )(*split, vecs, qvec, drouter, ebias, mgt, condt, ada)
    return [o.reshape(-1, o.shape[2]).astype(F32) for o in out[:4]], out[4:]


def on_block(
    tokens, conditioning, routes, cotangent, ada_weight, ada_bias, qkv_weight, qv_bias, out_weight, out_bias,
    shared_in, shared_in_bias, shared_out, shared_out_bias, router,
    expert_in, expert_in_bias, expert_out, expert_out_bias,
):
    n = NZ * NX
    dp = lax.axis_index("dp")
    x = lax.rem(dp, NX)
    width = tokens.shape[2]
    hidden = shared_in.shape[1]
    part = width // n
    tok, cot, route = tokens[0], cotangent[0], routes[0]
    cond_act, silu_back = jax.vjp(jax.nn.silu, conditioning.astype(F32))
    cond_low = cond_act.astype(B16).astype(F32)

    def rows_of(v, count):
        v = v.astype(F32).reshape(-1)
        return jnp.pad(v, (0, count * 128 - v.shape[0])).reshape(count, 128)

    def wide(v):
        return jnp.pad(v.astype(F32), ((0, 0), (0, 128 - part)))

    pack = jnp.concatenate(
        [
            wide(qv_bias),
            wide(out_bias[None]),
            wide(shared_out_bias[None]),
            rows_of(shared_in_bias, 4),
            rows_of(ada_bias, 8),
            rows_of(router, 8),
            wide(cond_low.reshape(n, part)),
        ],
        axis=0,
    )
    mod_raw, packs, fulls = gather_dense(
        ada_weight, pack, (qkv_weight, out_weight, shared_in, shared_out), (True, True, True, False)
    )
    qkv_full, out_full, sin_full, sout_full = fulls
    bias = jnp.pad(packs[:, 0:4, :part].transpose(1, 0, 2).reshape(4, width), ((0, 4), (0, 0)))
    sinb = packs[:, 4:7, :].reshape(1, hidden)
    abias = packs[:, 8:16, :].reshape(n, -1)[:, : ada_bias.shape[0]].reshape(6, width)
    abias = jnp.pad(abias, ((0, 2), (0, 0)))
    router_full = packs[:, 16:24, :].reshape(n, -1)[:, : part * E].reshape(width, E)
    router_full = jnp.pad(router_full, ((0, 0), (0, 128 - E))).astype(B16)

    (normed, proj, lsum, mixed, att, resid, second, gates, place, sbuf, gbuf, mod) = front(
        tok, cot, route, mod_raw, abias, qkv_full, out_full, bias, router_full
    )
    dwin, dwout, res, bgr, ebias = expert(
        sbuf, gbuf, expert_in, expert_out, expert_in_bias.astype(F32), expert_out_bias.astype(F32)
    )
    line = [[NX * z + xx for z in range(NZ)] for xx in range(NX)]
    turn = [(i, i // NX * NX + 1 - i % NX) for i in range(n)]

    def over_z(grad):
        mine = lax.psum_scatter(
            grad, "dp", scatter_dimension=0, axis_index_groups=line, tiled=True
        )
        pair = mine.reshape(NX, -1, mine.shape[1])
        keep = lax.dynamic_index_in_dim(pair, x, 0, keepdims=False)
        give = lax.dynamic_index_in_dim(pair, 1 - x, 0, keepdims=False)
        came = lax.ppermute(give, "dp", turn)
        first = x == 0
        return jnp.stack([jnp.where(first, keep, came), jnp.where(first, came, keep)]).astype(F32)

    dwout_sum = over_z(dwout)
    dwin_sum = over_z(dwin)
    (output, rgrad, mgrad, dsin, dsout, dout, drouter, vecs, mg2) = middle(
        res, bgr, second, resid, att, cot, route, mod, sin_full, sout_full, sinb, bias, router_full, gates, place,
        mixed, out_full,
    )
    tgrad, dqkv, qvec, mgt = back(tok, mod, normed, proj, lsum, mgrad, rgrad, qkv_full, mg2)
    condt = jnp.pad(cond_low.reshape(-1, 128), ((0, 2), (0, 0)))
    dense, (small, esum, tiles, cgot) = device_sums(
        (dqkv, dout, dsin, dsout), vecs, qvec, drouter, ebias, mgt, condt, ada_weight
    )

    def share(v, size):
        return lax.dynamic_slice_in_dim(v.reshape(-1), dp * size, size, 0)

    per = width // 128
    base = hidden // 128
    sinb_grad = share(small[:base], hidden // n)
    soutb_grad = share(small[base : base + per], part)
    outb_grad = share(small[base + per : base + 2 * per], part)
    qvb_grad = jnp.stack(
        [share(small[40 : 40 + per], part), share(small[40 + per : 40 + 2 * per], part)]
    )
    router_grad = small[56:].reshape(per, E, 128).transpose(0, 2, 1).reshape(width, E)
    router_grad = lax.dynamic_slice_in_dim(router_grad, dp * part, part, 0)
    ein_b = lax.dynamic_slice_in_dim(
        esum[:, :base].reshape(2, hidden), dp * (hidden // n), hidden // n, 1
    )
    eout_b = lax.dynamic_slice_in_dim(
        esum[:, base : base + per].reshape(2, width), dp * part, part, 1
    )
    images = tiles.shape[0] * n
    mods = tiles[:, :, : 6 * per].reshape(images, 6 * width)
    conds = lax.dynamic_slice_in_dim(
        tiles[:, :, 40 : 40 + per].reshape(images, width), dp * part, part, 1
    )
    ada_grad = lax.dot_general(
        conds.astype(B16), mods.astype(B16), (((0,), (0,)), ((), ())), preferred_element_type=F32
    )
    adab_grad = share(jnp.sum(mods, axis=0), ada_bias.shape[0])
    cond_grad = silu_back(cgot[:, 0, :part].reshape(1, width))[0]
    return (
        output[None],
        tgrad[None],
        cond_grad,
        ada_grad,
        adab_grad,
        dense[0],
        qvb_grad,
        dense[1],
        outb_grad,
        dense[2],
        sinb_grad,
        dense[3],
        soutb_grad,
        router_grad,
        dwin_sum,
        ein_b,
        dwout_sum,
        eout_b,
    )


def layer_norm(rows):
    centred = rows - jnp.mean(rows, axis=-1, keepdims=True)
    return centred * lax.rsqrt(jnp.mean(centred * centred, axis=-1, keepdims=True) + 1e-06)


def modulate(rows, shift, scale):
    return layer_norm(rows) * (1.0 + scale) + shift


def gelu_tanh(values_in):
    return jax.nn.gelu(values_in, approximate=True)


def on_device(
    tokens,
    conditioning,
    routes,
    cotangent,
    ada_weight,
    ada_bias,
    qkv_weight,
    qv_bias,
    out_weight,
    out_bias,
    shared_in,
    shared_in_bias,
    shared_out,
    shared_out_bias,
    router,
    expert_in,
    expert_in_bias,
    expert_out,
    expert_out_bias,
):
    f32 = jnp.float32
    b16 = jnp.bfloat16
    gathered_dense = (
        lax.all_gather(ada_weight, "dp", axis=0, tiled=True),
        lax.all_gather(ada_bias, "dp", axis=0, tiled=True),
        lax.all_gather(qkv_weight, "dp", axis=0, tiled=True),
        lax.all_gather(qv_bias, "dp", axis=1, tiled=True),
        lax.all_gather(out_weight, "dp", axis=0, tiled=True),
        lax.all_gather(out_bias, "dp", axis=0, tiled=True),
        lax.all_gather(shared_in, "dp", axis=0, tiled=True),
        lax.all_gather(shared_in_bias, "dp", axis=0, tiled=True),
        lax.all_gather(shared_out, "dp", axis=0, tiled=True),
        lax.all_gather(shared_out_bias, "dp", axis=0, tiled=True),
        lax.all_gather(router, "dp", axis=0, tiled=True),
    )
    (
        ada_full,
        ada_bias_full,
        qkv_full,
        qv_bias_full,
        out_full,
        out_bias_full,
        shared_in_full,
        shared_in_bias_full,
        shared_out_full,
        shared_out_bias_full,
        router_full,
    ) = gathered_dense
    image_count, length, width = tokens.shape
    row_count = image_count * length
    scaling = HEAD_DIM ** (-0.5)
    head_shape = (image_count, length, HEADS, HEAD_DIM)
    cond_float = conditioning.astype(f32)
    cond_act, silu_back = jax.vjp(jax.nn.silu, cond_float)
    cond_low = cond_act.astype(b16)
    modulation = jnp.dot(cond_low, ada_full, preferred_element_type=f32) + ada_bias_full.astype(f32)
    pieces = [modulation[:, None, index * width : (index + 1) * width] for index in range(6)]
    source = tokens.astype(f32)
    first_norm, first_back = jax.vjp(modulate, source, pieces[0], pieces[1])
    normed = first_norm.astype(b16)
    projected = jnp.einsum("isd,de->ise", normed, qkv_full, preferred_element_type=f32)
    query_heads = (
        (projected[..., :width] + qv_bias_full[0].astype(f32)).astype(b16).reshape(head_shape)
    )
    key_heads = projected[..., width : 2 * width].astype(b16).reshape(head_shape)
    value_heads = (
        (projected[..., 2 * width :] + qv_bias_full[1].astype(f32)).astype(b16).reshape(head_shape)
    )
    scores = (
        jnp.einsum("iqhc,ikhc->ihqk", query_heads, key_heads, preferred_element_type=f32) * scaling
    )
    peak_score = jnp.max(scores, axis=-1, keepdims=True)
    unscaled = jnp.exp(scores - peak_score)
    exp_total = jnp.sum(unscaled, axis=-1, keepdims=True)
    log_total = peak_score + jnp.log(exp_total)
    probs_low = (unscaled / exp_total).astype(b16)
    mixed = (
        jnp.einsum("ihqk,ikhc->iqhc", probs_low, value_heads, preferred_element_type=f32)
        .reshape(image_count, length, width)
        .astype(b16)
    )
    attended = jnp.einsum(
        "isd,de->ise", mixed, out_full, preferred_element_type=f32
    ) + out_bias_full.astype(f32)
    resid = source + pieces[2] * attended
    second_float, second_back = jax.vjp(modulate, resid, pieces[3], pieces[4])
    second = second_float.astype(b16)
    shared_pre = jnp.einsum(
        "isd,df->isf", second, shared_in_full, preferred_element_type=f32
    ) + shared_in_bias_full.astype(f32)
    shared_act, shared_gelu_back = jax.vjp(gelu_tanh, shared_pre)
    shared_low = shared_act.astype(b16)
    shared = jnp.einsum(
        "isf,fd->isd", shared_low, shared_out_full, preferred_element_type=f32
    ) + shared_out_bias_full.astype(f32)
    second_rows = second.reshape(row_count, width)
    logits = jnp.dot(second_rows, router_full, preferred_element_type=f32)
    route_flat = routes.reshape(-1)
    one_hot = (route_flat[:, None] == jnp.arange(E, dtype=jnp.int32)).astype(jnp.int32)
    slot_index = jnp.sum(
        (jnp.cumsum(one_hot, axis=0, dtype=jnp.int32) - one_hot) * one_hot, axis=1, dtype=jnp.int32
    )
    position = jnp.where(slot_index < CAP, route_flat * CAP + slot_index, E * CAP)
    pair_rows = jnp.repeat(second_rows, 2, axis=0)
    buffer = (
        jnp.zeros((E * CAP, width), b16)
        .at[position]
        .set(pair_rows, mode="drop")
        .reshape(E, CAP, width)
    )
    received = lax.all_to_all(buffer, "expert", split_axis=0, concat_axis=1, tiled=True)
    expert_pre = (
        jnp.einsum("erd,edf->erf", received, expert_in, preferred_element_type=f32)
        + expert_in_bias.astype(f32)[:, None, :]
    )
    expert_low = gelu_tanh(expert_pre).astype(b16)
    expert_result = (
        jnp.einsum("erf,efd->erd", expert_low, expert_out, preferred_element_type=f32)
        + expert_out_bias.astype(f32)[:, None, :]
    ).astype(b16)
    returned = lax.all_to_all(
        expert_result, "expert", split_axis=1, concat_axis=0, tiled=True
    ).reshape(E * CAP, width)
    gathered = (
        returned.at[position]
        .get(mode="fill", fill_value=0)
        .reshape(row_count, 2, width)
        .astype(f32)
    )
    pair_mask = one_hot.reshape(row_count, 2, E).astype(f32)
    chosen = jnp.sum(logits[:, None, :] * pair_mask, axis=-1)
    gates = jax.nn.softmax(chosen, axis=-1)
    moe = (shared.reshape(row_count, width) + jnp.sum(gates[..., None] * gathered, axis=1)).reshape(
        image_count, length, width
    )
    output = (resid + pieces[5] * moe).astype(b16)
    ada_back, qkv_back, out_back, shared_in_back, shared_out_back, router_back = (
        ada_full,
        qkv_full,
        out_full,
        shared_in_full,
        shared_out_full,
        router_full,
    )
    grad_out = cotangent.astype(f32)
    gate_two_grad = jnp.sum(grad_out * moe, axis=1, keepdims=True)
    moe_grad = (pieces[5] * grad_out).astype(b16)
    moe_rows_grad = moe_grad.reshape(row_count, width)
    moe_rows_float = moe_rows_grad.astype(f32)
    pair_grad = (
        (gates[..., None] * moe_rows_float[:, None, :]).astype(b16).reshape(2 * row_count, width)
    )
    gate_grad = jnp.sum(moe_rows_float[:, None, :] * gathered, axis=-1)
    chosen_grad = gates * (gate_grad - jnp.sum(gates * gate_grad, axis=-1, keepdims=True))
    logits_grad = jnp.sum(chosen_grad[..., None] * pair_mask, axis=1).astype(b16)
    grad_buffer = (
        jnp.zeros((E * CAP, width), b16)
        .at[position]
        .set(pair_grad, mode="drop")
        .reshape(E, CAP, width)
    )
    result_grad = lax.all_to_all(grad_buffer, "expert", split_axis=0, concat_axis=1, tiled=True)
    pre_again = (
        jnp.einsum("erd,edf->erf", received, expert_in, preferred_element_type=f32)
        + expert_in_bias.astype(f32)[:, None, :]
    )
    act_again, expert_gelu_back = jax.vjp(gelu_tanh, pre_again)
    low_again = act_again.astype(b16)
    expert_out_grad = jnp.einsum("erf,erd->efd", low_again, result_grad, preferred_element_type=f32)
    expert_out_bias_grad = jnp.sum(result_grad.astype(f32), axis=1)
    expert_act_grad = jnp.einsum(
        "erd,efd->erf", result_grad, expert_out, preferred_element_type=f32
    )
    pre_grad = expert_gelu_back(expert_act_grad)[0].astype(b16)
    expert_in_grad = jnp.einsum("erd,erf->edf", received, pre_grad, preferred_element_type=f32)
    expert_in_bias_grad = jnp.sum(pre_grad.astype(f32), axis=1)
    received_grad = jnp.einsum(
        "erf,edf->erd", pre_grad, expert_in, preferred_element_type=f32
    ).astype(b16)
    sent_grad = lax.all_to_all(
        received_grad, "expert", split_axis=1, concat_axis=0, tiled=True
    ).reshape(E * CAP, width)
    dispatch_rows_grad = jnp.sum(
        sent_grad.at[position]
        .get(mode="fill", fill_value=0)
        .reshape(row_count, 2, width)
        .astype(f32),
        axis=1,
    )
    shared_out_grad = jnp.einsum("isf,isd->fd", shared_low, moe_grad, preferred_element_type=f32)
    shared_out_bias_grad = jnp.sum(moe_rows_float, axis=0)
    shared_act_grad = jnp.einsum(
        "isd,fd->isf", moe_grad, shared_out_back, preferred_element_type=f32
    )
    shared_pre_grad = shared_gelu_back(shared_act_grad)[0].astype(b16)
    shared_in_grad = jnp.einsum("isd,isf->df", second, shared_pre_grad, preferred_element_type=f32)
    shared_in_bias_grad = jnp.sum(shared_pre_grad.astype(f32), axis=(0, 1))
    router_grad = jnp.einsum("rd,re->de", second_rows, logits_grad, preferred_element_type=f32)
    second_grad = jnp.einsum(
        "isf,df->isd", shared_pre_grad, shared_in_back, preferred_element_type=f32
    )
    side_grad = dispatch_rows_grad + jnp.einsum(
        "re,de->rd", logits_grad, router_back, preferred_element_type=f32
    )
    second_grad = second_grad + side_grad.reshape(image_count, length, width)
    resid_extra, shift_two_grad, scale_two_grad = second_back(second_grad)
    resid_grad = grad_out + resid_extra
    attended_grad = (pieces[2] * resid_grad).astype(b16)
    gate_one_grad = jnp.sum(resid_grad * attended, axis=1, keepdims=True)
    out_weight_grad = jnp.einsum("isd,ise->de", mixed, attended_grad, preferred_element_type=f32)
    out_bias_grad = jnp.sum(attended_grad.astype(f32), axis=(0, 1))
    mixed_grad = (
        jnp.einsum("ise,de->isd", attended_grad, out_back, preferred_element_type=f32)
        .astype(b16)
        .reshape(head_shape)
    )
    again_scores = (
        jnp.einsum("iqhc,ikhc->ihqk", query_heads, key_heads, preferred_element_type=f32) * scaling
    )
    probs_float = jnp.exp(again_scores - log_total)
    again_low = probs_float.astype(b16)
    probs_grad = jnp.einsum("iqhc,ikhc->ihqk", mixed_grad, value_heads, preferred_element_type=f32)
    values_grad = jnp.einsum(
        "ihqk,iqhc->ikhc", again_low, mixed_grad, preferred_element_type=f32
    ).astype(b16)
    scores_grad = (
        probs_float * (probs_grad - jnp.sum(probs_float * probs_grad, axis=-1, keepdims=True))
    ).astype(b16)
    query_grad = (
        jnp.einsum("ihqk,ikhc->iqhc", scores_grad, key_heads, preferred_element_type=f32) * scaling
    ).astype(b16)
    keys_grad = (
        jnp.einsum("ihqk,iqhc->ikhc", scores_grad, query_heads, preferred_element_type=f32)
        * scaling
    ).astype(b16)
    flat_shape = (image_count, length, width)
    projected_grad = jnp.concatenate(
        [
            query_grad.reshape(flat_shape),
            keys_grad.reshape(flat_shape),
            values_grad.reshape(flat_shape),
        ],
        axis=-1,
    )
    qkv_weight_grad = jnp.einsum("isd,ise->de", normed, projected_grad, preferred_element_type=f32)
    qv_bias_grad = jnp.stack(
        [
            jnp.sum(query_grad.astype(f32), axis=(0, 1)).reshape(width),
            jnp.sum(values_grad.astype(f32), axis=(0, 1)).reshape(width),
        ]
    )
    normed_grad = jnp.einsum("ise,de->isd", projected_grad, qkv_back, preferred_element_type=f32)
    token_extra, shift_one_grad, scale_one_grad = first_back(normed_grad)
    tokens_grad = resid_grad + token_extra
    modulation_grad = jnp.concatenate(
        [
            shift_one_grad,
            scale_one_grad,
            gate_one_grad,
            shift_two_grad,
            scale_two_grad,
            gate_two_grad,
        ],
        axis=-1,
    )[:, 0, :].astype(b16)
    ada_weight_grad = jnp.einsum("id,ie->de", cond_low, modulation_grad, preferred_element_type=f32)
    ada_bias_grad = jnp.sum(modulation_grad.astype(f32), axis=0)
    cond_act_grad = jnp.einsum("ie,de->id", modulation_grad, ada_back, preferred_element_type=f32)
    conditioning_grad = silu_back(cond_act_grad)[0]
    expert_sums = (
        lax.psum_scatter(
            expert_in_grad.astype(jnp.bfloat16), "dp", scatter_dimension=1, tiled=True
        ).astype(jnp.float32),
        lax.psum_scatter(
            expert_in_bias_grad.astype(jnp.bfloat16), "dp", scatter_dimension=1, tiled=True
        ).astype(jnp.float32),
        lax.psum_scatter(
            expert_out_grad.astype(jnp.bfloat16), "dp", scatter_dimension=1, tiled=True
        ).astype(jnp.float32),
        lax.psum_scatter(
            expert_out_bias_grad.astype(jnp.bfloat16), "dp", scatter_dimension=1, tiled=True
        ).astype(jnp.float32),
    )
    dense_parts = (
        lax.psum_scatter(
            ada_weight_grad.astype(jnp.bfloat16), "dp", scatter_dimension=0, tiled=True
        ).astype(jnp.float32),
        lax.psum_scatter(
            ada_bias_grad.astype(jnp.bfloat16), "dp", scatter_dimension=0, tiled=True
        ).astype(jnp.float32),
        lax.psum_scatter(
            qkv_weight_grad.astype(jnp.bfloat16), "dp", scatter_dimension=0, tiled=True
        ).astype(jnp.float32),
        lax.psum_scatter(
            qv_bias_grad.astype(jnp.bfloat16), "dp", scatter_dimension=1, tiled=True
        ).astype(jnp.float32),
        lax.psum_scatter(
            out_weight_grad.astype(jnp.bfloat16), "dp", scatter_dimension=0, tiled=True
        ).astype(jnp.float32),
        lax.psum_scatter(
            out_bias_grad.astype(jnp.bfloat16), "dp", scatter_dimension=0, tiled=True
        ).astype(jnp.float32),
        lax.psum_scatter(
            shared_in_grad.astype(jnp.bfloat16), "dp", scatter_dimension=0, tiled=True
        ).astype(jnp.float32),
        lax.psum_scatter(
            shared_in_bias_grad.astype(jnp.bfloat16), "dp", scatter_dimension=0, tiled=True
        ).astype(jnp.float32),
        lax.psum_scatter(
            shared_out_grad.astype(jnp.bfloat16), "dp", scatter_dimension=0, tiled=True
        ).astype(jnp.float32),
        lax.psum_scatter(
            shared_out_bias_grad.astype(jnp.bfloat16), "dp", scatter_dimension=0, tiled=True
        ).astype(jnp.float32),
        lax.psum_scatter(
            router_grad.astype(jnp.bfloat16), "dp", scatter_dimension=0, tiled=True
        ).astype(jnp.float32),
    )
    dense_sums = lax.psum(
        (
            dense_parts[0],
            dense_parts[1],
            dense_parts[2],
            dense_parts[3],
            dense_parts[4],
            dense_parts[5],
            dense_parts[6],
            dense_parts[7],
            dense_parts[8],
            dense_parts[9],
            dense_parts[10],
        ),
        "expert",
    )
    return (
        output,
        tokens_grad,
        conditioning_grad,
        dense_sums[0],
        dense_sums[1],
        dense_sums[2],
        dense_sums[3],
        dense_sums[4],
        dense_sums[5],
        dense_sums[6],
        dense_sums[7],
        dense_sums[8],
        dense_sums[9],
        dense_sums[10],
        expert_sums[0],
        expert_sums[1],
        expert_sums[2],
        expert_sums[3],
    )


def solution(mesh):
    in_specs = (
        P(("dp", "expert"), None, None),
        P(("dp", "expert"), None),
        P(("dp", "expert"), None, None),
        P(("dp", "expert"), None, None),
        P("dp", None),
        P("dp"),
        P("dp", None),
        P(None, "dp"),
        P("dp", None),
        P("dp"),
        P("dp", None),
        P("dp"),
        P("dp", None),
        P("dp"),
        P("dp", None),
        P("expert", None, None),
        P("expert", None),
        P("expert", None, None),
        P("expert", None),
    )
    out_specs = (
        P(("dp", "expert"), None, None),
        P(("dp", "expert"), None, None),
        P(("dp", "expert"), None),
        P("dp", None),
        P("dp"),
        P("dp", None),
        P(None, "dp"),
        P("dp", None),
        P("dp"),
        P("dp", None),
        P("dp"),
        P("dp", None),
        P("dp"),
        P("dp", None),
        P("expert", "dp", None),
        P("expert", "dp"),
        P("expert", "dp", None),
        P("expert", "dp"),
    )
    body = on_device
    if dict(mesh.shape) == {"dp": NZ * NX, "expert": 4}:
        body = on_block
    return jax.shard_map(
        body, mesh=mesh, in_specs=in_specs, out_specs=out_specs, check_vma=False
    )
```

```python
import functools

import jax
import jax.numpy as jnp
from jax import lax
from jax.experimental import pallas as pl
from jax.experimental.pallas import tpu as pltpu
from jax.sharding import PartitionSpec as P

HEADS = 12
HEAD_DIM = 64
E = 8
CAP = 80
MESH = pl.DeviceIdType.MESH
F32 = jnp.float32
B16 = jnp.bfloat16
VMEM_LIMIT = 60 * 1024 * 1024
SCALE = HEAD_DIM ** (-0.5)
GELU_C = 0.7978845608028654
NZ, NX = 4, 2


def coords():
    dp = lax.axis_index("dp")
    ex = lax.axis_index("expert")
    return lax.div(dp, NX), lax.rem(dp, NX), lax.div(ex, 2), lax.rem(ex, 2)


def dev(z, x, y, c):
    return (NX * z + x, 2 * y + c)


def dot(a, b):
    return jnp.dot(a, b, preferred_element_type=F32)


def dot_nt(a, b):
    return lax.dot_general(a, b, (((1,), (1,)), ((), ())), preferred_element_type=F32)


def dot_tn(a, b):
    return lax.dot_general(a, b, (((0,), (0,)), ((), ())), preferred_element_type=F32)


def gelu_parts(v):
    v2 = v * v
    t = jnp.tanh(GELU_C * v * (1.0 + 0.044715 * v2))
    h = 0.5 * (1.0 + t)
    return v * h, h + 0.5 * v * (1.0 - t * t) * (GELU_C * (1.0 + 0.134145 * v2))


def norm_parts(v):
    centred = v - jnp.mean(v, axis=-1, keepdims=True)
    r = lax.rsqrt(jnp.mean(centred * centred, axis=-1, keepdims=True) + 1e-06)
    return centred * r, r


def norm_back(u, n, r):
    return r * (
        u - jnp.mean(u, axis=-1, keepdims=True) - n * jnp.mean(u * n, axis=-1, keepdims=True)
    )


def remote(src, dst, send, recv, to):
    return pltpu.make_async_remote_copy(
        src_ref=src,
        dst_ref=dst,
        send_sem=send,
        recv_sem=recv,
        device_id=to,
        device_id_type=MESH,
    )


def greet(barrier, to):
    pl.semaphore_signal(barrier, inc=1, device_id=to, device_id_type=MESH)


def params(collective_id=None):
    if collective_id is None:
        return pltpu.CompilerParams(vmem_limit_bytes=VMEM_LIMIT)
    return pltpu.CompilerParams(
        vmem_limit_bytes=VMEM_LIMIT, collective_id=collective_id, has_side_effects=True
    )


VM = pl.BlockSpec(memory_space=pltpu.VMEM)
HB = pl.BlockSpec(memory_space=pl.ANY)


def sds(shape, dtype):
    return jax.ShapeDtypeStruct(shape, dtype)


class Gather:
    def __init__(self, shards, fulls, splits, sems):
        self.z, self.x, self.y, self.c = coords()
        self.mats = list(zip(shards, fulls, splits))
        (self.zs, self.zr, self.xs, self.xr, self.ys, self.yr, self.cs, self.cr, self.loc) = sems

    @staticmethod
    def semaphores(count):
        dma = pltpu.SemaphoreType.DMA
        return [
            dma((count, 2, NZ)),
            dma((count, NZ)),
            dma((count, NZ)),
            dma((count, NZ)),
            dma((count, NZ, NX)),
            dma((count, NZ, NX)),
            dma((count, NZ, NX, 2)),
            dma((count, NZ, NX, 2)),
            dma((count,)),
        ]

    def region(self, m, zb, xb, yh, ch):
        shard, full, split = self.mats[m]
        rows, width = shard.shape[0], shard.shape[1] // 2
        start = (NX * zb + xb) * rows
        if split:
            rows = rows // 2
            start = start + yh * rows
        return full.at[
            pl.ds(pl.multiple_of(start, 16), rows), pl.ds(pl.multiple_of(ch * width, 128), width)
        ]

    def own(self, m):
        shard, full, split = self.mats[m]
        rows, width = shard.shape[0], shard.shape[1] // 2
        start = 0
        if split:
            rows = rows // 2
            start = self.y * rows
        return shard.at[
            pl.ds(pl.multiple_of(start, 16), rows),
            pl.ds(pl.multiple_of(self.c * width, 128), width),
        ]

    def zcopy(self, m, zb, side, mine=False):
        here = self.region(m, zb, self.x, self.y, self.c)
        step = 1 if side else -1
        return remote(
            self.own(m) if mine else here,
            here,
            self.zs.at[m, side, zb],
            self.zr.at[m, zb],
            dev(lax.rem(self.z + step + NZ, NZ), self.x, self.y, self.c),
        )

    def xcopy(self, m, zb, mine=False, xb=None):
        here = self.region(m, zb, self.x if xb is None else xb, self.y, self.c)
        return remote(
            self.own(m) if mine else here,
            here,
            self.xs.at[m, zb],
            self.xr.at[m, zb],
            dev(self.z, 1 - self.x, self.y, self.c),
        )

    def ycopy(self, m, zb, xb, yh=None):
        here = self.region(m, zb, xb, self.y if yh is None else yh, self.c)
        return remote(
            here,
            here,
            self.ys.at[m, zb, xb],
            self.yr.at[m, zb, xb],
            dev(self.z, self.x, 1 - self.y, self.c),
        )

    def ccopy(self, m, zb, xb, yh, ch=None):
        here = self.region(m, zb, xb, yh, self.c if ch is None else ch)
        slot = yh if self.mats[m][2] else 0
        return remote(
            here,
            here,
            self.cs.at[m, zb, xb, slot],
            self.cr.at[m, zb, xb, slot],
            dev(self.z, self.x, self.y, 1 - self.c),
        )

    def local(self, m):
        shard, full, _ = self.mats[m]
        rows = shard.shape[0]
        start = (NX * self.z + self.x) * rows
        return pltpu.make_async_copy(
            shard, full.at[pl.ds(pl.multiple_of(start, 16), rows), :], self.loc.at[m]
        )

    def blocks(self, step):
        if step == 0:
            return [(self.z, None, None)]
        return [
            (self.z - step, self.z - step >= 0, 1),
            (self.z + step, self.z + step < NZ, 0),
        ]

    def more(self, side):
        return self.z + 1 < NZ if side else self.z - 1 >= 0

    def begin(self, m):
        for side in (1, 0):

            @pl.when(self.more(side))
            def _():
                self.zcopy(m, self.z, side, True).start()

        self.xcopy(m, self.z, True).start()
        self.local(m).start()

    def spread(self, m, zb, xb):
        if self.mats[m][2]:
            self.ycopy(m, zb, xb).start()
        self.ccopy(m, zb, xb, self.y).start()

    def take_z(self, m, step):
        for zb, exists, side in self.blocks(step):

            @pl.when(exists)
            def _():
                self.zcopy(m, zb, side).wait_recv()
                if step < NZ - 1:

                    @pl.when(self.more(side))
                    def _():
                        self.zcopy(m, zb, side).start()

                self.xcopy(m, zb).start()
                self.spread(m, zb, self.x)

    def take_x(self, m, step):
        for zb, exists, _ in self.blocks(step):

            def body():
                self.xcopy(m, zb, False, 1 - self.x).wait_recv()
                self.spread(m, zb, 1 - self.x)

            body() if exists is None else pl.when(exists)(body)

    def others(self, m, step, action):
        for zb, exists, _ in self.blocks(step):
            for xb in (self.x, 1 - self.x) if step else (1 - self.x,):
                body = functools.partial(action, m, zb, xb)
                body() if exists is None else pl.when(exists)(body)

    def take_y(self, m, step):
        if not self.mats[m][2]:
            return

        def action(m, zb, xb):
            self.ycopy(m, zb, xb, 1 - self.y).wait_recv()
            self.ccopy(m, zb, xb, 1 - self.y).start()

        self.others(m, step, action)

    def finish(self, m):
        def action(m, zb, xb):
            for yh in (self.y, 1 - self.y) if self.mats[m][2] else (self.y,):
                self.ccopy(m, zb, xb, yh, 1 - self.c).wait_recv()
                self.ccopy(m, zb, xb, yh).wait_send()
            if self.mats[m][2]:
                self.ycopy(m, zb, xb).wait_send()

        for step in range(NZ):
            self.others(m, step, action)
        for side in (1, 0):

            @pl.when(self.more(side))
            def _():
                self.zcopy(m, self.z, side, True).wait_send()

        for step in range(1, NZ):
            for zb, exists, side in self.blocks(step):

                @pl.when(exists)
                def _():
                    self.xcopy(m, zb).wait_send()
                    if step < NZ - 1:

                        @pl.when(self.more(side))
                        def _():
                            self.zcopy(m, zb, side).wait_send()

        self.xcopy(m, self.z, True).wait_send()
        self.local(m).wait()


class Column:
    def __init__(self, shard, column, send, recv, local):
        self.z, self.x, self.y, self.c = coords()
        self.shard, self.column, self.send, self.recv, self.local = shard, column, send, recv, local

    def block(self, zb):
        rows = self.shard.shape[0]
        return self.column.at[pl.ds(pl.multiple_of(zb * rows, 16), rows), :]

    def own(self):
        width = self.shard.shape[1] // 2
        return self.shard.at[:, pl.ds(pl.multiple_of(self.c * width, 128), width)]

    def copy(self, zb, side, mine=False):
        here = self.block(zb)
        to = lax.rem(self.z + (1 if side else NZ - 1), NZ)
        return remote(
            self.own() if mine else here,
            here,
            self.send.at[side, zb],
            self.recv.at[zb],
            dev(to, self.x, self.y, self.c),
        )

    def keep(self):
        return pltpu.make_async_copy(self.own(), self.block(self.z), self.local.at[0])

    def more(self, side):
        return self.z + 1 < NZ if side else self.z - 1 >= 0

    def blocks(self, step):
        return [(self.z - step, self.z - step >= 0, 1), (self.z + step, self.z + step < NZ, 0)]

    def begin(self):
        for side in (1, 0):

            @pl.when(self.more(side))
            def _():
                self.copy(self.z, side, True).start()

        self.keep().start()

    def take(self, step):
        for zb, exists, side in self.blocks(step):

            @pl.when(exists)
            def _():
                self.copy(zb, side).wait_recv()
                if step < NZ - 1:

                    @pl.when(self.more(side))
                    def _():
                        self.copy(zb, side).start()

    def finish(self):
        for side in (1, 0):

            @pl.when(self.more(side))
            def _():
                self.copy(self.z, side, True).wait_send()

        for step in range(1, NZ - 1):
            for zb, exists, side in self.blocks(step):

                @pl.when(jnp.logical_and(exists, self.more(side)))
                def _():
                    self.copy(zb, side).wait_send()

        self.keep().wait()


class Spread:
    def __init__(self, column, full, xs, xr, ys, yr, cs, cr, local):
        self.z, self.x, self.y, self.c = coords()
        self.column, self.full, self.local = column, full, local
        self.xs, self.xr, self.ys, self.yr, self.cs, self.cr = xs, xr, ys, yr, cs, cr

    @staticmethod
    def semaphores():
        dma = pltpu.SemaphoreType.DMA
        return [dma((NZ,))] * 4 + [dma((3, NZ))] * 2 + [dma((NZ,))]

    def cols(self, c):
        width = self.full.shape[3] // 2
        return pl.ds(pl.multiple_of(c * width, 128), width)

    def half(self, y):
        rows = self.full.shape[2] // 2
        return pl.ds(pl.multiple_of(y * rows, 16), rows)

    def source(self, zb):
        rows = self.full.shape[2]
        return self.column.at[zb * rows : (zb + 1) * rows, :]

    def source_half(self, zb):
        rows = self.full.shape[2]
        start = zb * rows + self.y * (rows // 2)
        return self.column.at[pl.ds(pl.multiple_of(start, 16), rows // 2), :]

    def xcopy(self, zb, came=False):
        at = self.full.at[zb, 1 - self.x if came else self.x, self.half(self.y), self.cols(self.c)]
        return remote(
            self.source_half(zb), at, self.xs.at[zb], self.xr.at[zb],
            dev(self.z, 1 - self.x, self.y, self.c),
        )

    def ycopy(self, zb, came=False):
        at = self.full.at[zb, 1 - self.x, self.half(1 - self.y if came else self.y), self.cols(self.c)]
        return remote(
            at, at, self.ys.at[zb], self.yr.at[zb], dev(self.z, self.x, 1 - self.y, self.c)
        )

    def ccopy(self, kind, zb, came=False):
        cols = self.cols(1 - self.c if came else self.c)
        if kind == 0:
            at = self.full.at[zb, self.x, :, cols]
        else:
            at = self.full.at[zb, 1 - self.x, self.half(self.y if kind == 1 else 1 - self.y), cols]
        return remote(
            self.source(zb) if kind == 0 else at, at, self.cs.at[kind, zb], self.cr.at[kind, zb],
            dev(self.z, self.x, self.y, 1 - self.c),
        )

    def keep(self, zb):
        return pltpu.make_async_copy(
            self.source(zb), self.full.at[zb, self.x, :, self.cols(self.c)], self.local.at[zb]
        )

    def begin(self):
        for zb in range(NZ):
            self.xcopy(zb).start()

    def near(self):
        for zb in range(NZ):
            self.ccopy(0, zb).start()
            self.keep(zb).start()

    def take_x(self):
        for zb in range(NZ):
            self.xcopy(zb, True).wait_recv()
            self.ycopy(zb).start()
            self.ccopy(1, zb).start()

    def take_y(self):
        for zb in range(NZ):
            self.ycopy(zb, True).wait_recv()
            self.ccopy(2, zb).start()

    def finish(self):
        for zb in range(NZ):
            for kind in range(3):
                self.ccopy(kind, zb, True).wait_recv()
            self.keep(zb).wait()

    def close(self):
        for zb in range(NZ):
            self.xcopy(zb).wait_send()
            self.ycopy(zb).wait_send()
            for kind in range(3):
                self.ccopy(kind, zb).wait_send()


def choose_rows(place, slots):
    return place == lax.broadcasted_iota(jnp.int32, (place.shape[0], slots), 1)


def plane_peer(k):
    z, x, y, c = coords()
    xt = 1 - x if k & 1 else x
    ct = 1 - c if k & 2 else c
    yt = 1 - y if k & 4 else y
    return dev(z, xt, yt, ct), 4 * yt + 2 * ct + xt


def plane_rank():
    _, x, y, c = coords()
    return 4 * y + 2 * c + x


def slot_rows(ref, rank):
    return ref.at[pl.ds(pl.multiple_of(rank * CAP, 16), CAP), :]


class PlaneExchange:
    ORDER = (7, 5, 6, 4, 3, 1, 2)

    def __init__(self, source, target, send, recv):
        self.source, self.target, self.send, self.recv = source, target, send, recv

    def copy(self, k, into=None):
        peer, other = plane_peer(k)
        return remote(
            slot_rows(self.source, other),
            slot_rows(self.target, plane_rank() if into is None else other),
            self.send.at[k],
            self.recv.at[k],
            peer,
        )

    def start(self):
        for k in self.ORDER:
            self.copy(k).start()
        mine = pl.ds(pl.multiple_of(plane_rank() * CAP, 16), CAP)
        self.target[mine, :] = self.source[mine, :]

    def wait_in(self):
        for k in self.ORDER:
            self.copy(k, True).wait_recv()

    def wait_out(self):
        for k in self.ORDER:
            self.copy(k).wait_send()


CHUNK = 512


def lead_kernel(
    tok, cot, routes, cond, ada, adab, qvb, outb, soutb, sinb_s, router_s, bin_r, bout_r,
    qkv_s, out_s, sin_s, sout_s, win_h, wout_h,
    normed_o, proj_o, lsum_o, mixed_o, att_o, resid_o, second_o, gates_o, place_o, mod_o, bias_o, sinb_o, rt_o,
    condt_o, rows, grads, res_o, qkv_o, outw_o, sin_o, sout_o, slopes_o, dwout_o,
    pack, packs, sent, got, qkv, outw, sbuf, gbuf, win, wout, dwout, lows, slopes, acc,
    s1, r1, s2, r2, ds0, dr0, ds1, dr1, wsem, osem, *gsems,
):
    z, x, y, c = coords()
    dp, ex = lax.axis_index("dp"), lax.axis_index("expert")
    n = NZ * NX
    length, width = tok.shape
    hidden = win.shape[1]
    part = width // n
    per = width // 128
    lead = Gather((qkv_s, out_s), (qkv, outw), (True, False), gsems[:-6])
    later = (Column(sin_s, sin_o, *gsems[-6:-3]), Column(sout_s, sout_o, *gsems[-3:]))

    loads = [
        pltpu.make_async_copy(win_h.at[x], win, wsem.at[0]),
        pltpu.make_async_copy(wout_h.at[x], wout, wsem.at[1]),
    ]

    def peers(action):
        for p in range(n):

            @pl.when(p != dp)
            def _():
                action(p)

    barrier = pltpu.get_barrier_semaphore()
    peers(lambda p: greet(barrier, (p, ex)))
    for k in range(2, E):
        greet(barrier, plane_peer(k)[0])

    pack[...] = jnp.zeros_like(pack)
    pack[0:2, 0:part] = qvb[...].astype(F32)
    pack[2:3, 0:part] = outb[...].astype(F32)
    pack[3:4, 0:part] = soutb[...].astype(F32)
    for j in range(hidden // n // 128):
        pack[4 + j : 5 + j, :] = sinb_s[:, 128 * j : 128 * (j + 1)].astype(F32)
    long = adab.shape[1]
    for j in range(-(-long // 128)):
        size = min(128, long - 128 * j)
        pack[8 + j : 9 + j, 0:size] = adab[:, 128 * j : 128 * j + size].astype(F32)
    pack[16:24, 0:part] = router_s[...].astype(F32)
    cv = cond[...].astype(F32)
    cond_low = (cv / (1.0 + jnp.exp(-cv))).astype(B16).astype(F32)
    for p in range(n):
        pack[24 + p : 25 + p, 0:part] = cond_low[:, part * p : part * (p + 1)]
    condt_o[...] = jnp.zeros_like(condt_o)
    for j in range(per):
        condt_o[j : j + 1, :] = cond_low[:, 128 * j : 128 * (j + 1)]

    pl.semaphore_wait(barrier, n - 1 + E - 2)

    def first(p, at):
        return remote(pack, packs.at[at], s1.at[p], r1.at[at], (p, ex))

    def second_hop(p, at):
        return remote(sent.at[p], got.at[at], s2.at[p], r2.at[at], (p, ex))

    peers(lambda p: first(p, dp).start())
    lead.begin(0)
    lead.begin(1)
    for column in later:
        column.begin()
    for load in loads:
        load.start()
    packs[dp] = pack[...]
    peers(lambda p: first(p, p).wait_recv())
    cond_rows = jnp.concatenate([packs[p, pl.ds(24 + dp, 1), :] for p in range(n)], axis=0)
    partial = dot(cond_rows[:, :part].astype(B16), ada[...])
    for j in range(partial.shape[1] // 128):
        sent[:, j, :] = partial[:, 128 * j : 128 * (j + 1)]
    peers(lambda p: second_hop(p, dp).start())
    got[dp] = sent[dp]

    both_mats = (0, 1)

    def step_of(plan, step):
        for m in both_mats:
            if step:
                plan.take_z(m, step)
            plan.take_x(m, step)
        if step:
            for m in both_mats:
                plan.take_y(m, step - 1)

    for step in range(NZ):
        step_of(lead, step)

    bias_o[...] = jnp.zeros_like(bias_o)
    for p in range(n):
        bias_o[0:4, part * p : part * (p + 1)] = packs[p, 0:4, 0:part]
        rt_o[:, part * p : part * (p + 1)] = packs[p, 16:24, 0:part]
        for j in range(hidden // n // 128):
            at = hidden // n * p + 128 * j
            sinb_o[:, at : at + 128] = packs[p, 4 + j : 5 + j, :]
    peers(lambda p: second_hop(p, p).wait_recv())
    total = got[0]
    for p in range(1, n):
        total = total + got[p]
    mod_o[...] = jnp.zeros_like(mod_o)
    for i in range(6):
        for b in range(per):
            mod_o[i : i + 1, 128 * b : 128 * (b + 1)] = total[per * i + b : per * i + b + 1, :]
    unit = 64
    for p in range(n):
        for u in range(long // unit):
            at = long * p + unit * u
            i, b = at // width, at % width
            mod_o[i : i + 1, b : b + unit] += packs[
                p, 8 + unit * u // 128 : 9 + unit * u // 128, unit * u % 128 : unit * u % 128 + unit
            ]

    mod = mod_o[...]
    source = tok[...].astype(F32)
    n1, _ = norm_parts(source)
    normed = (n1 * (1.0 + mod[1:2]) + mod[0:1]).astype(B16)
    normed_o[...] = normed
    for m in both_mats:
        lead.take_y(m, NZ - 1)
    for m in both_mats:
        lead.finish(m)
    for column in later:
        column.take(1)
    keep = [
        pltpu.make_async_copy(qkv, qkv_o, wsem.at[2]),
        pltpu.make_async_copy(outw, outw_o, wsem.at[3]),
    ]
    for copy in keep:
        copy.start()

    for k in range(3):
        part_k = dot(normed, qkv[:, k * width : (k + 1) * width])
        if k != 1:
            part_k = part_k + bias_o[k // 2 : k // 2 + 1, :]
        proj_o[:, k * width : (k + 1) * width] = part_k.astype(B16)
    lane = lax.broadcasted_iota(jnp.int32, (length, 128), 1)
    low_lane = lane < HEAD_DIM
    lsum = jnp.zeros((length, 128), F32)
    for p in range(HEADS // 2):
        q2 = proj_o[:, 128 * p : 128 * (p + 1)]
        k2 = proj_o[:, width + 128 * p : width + 128 * (p + 1)]
        v2 = proj_o[:, 2 * width + 128 * p : 2 * width + 128 * (p + 1)]
        outs = []
        for h in range(2):
            mine = low_lane if h == 0 else jnp.logical_not(low_lane)
            s = dot_nt(jnp.where(mine, q2, jnp.zeros_like(q2)), k2) * SCALE
            peak = jnp.max(s, axis=-1, keepdims=True)
            e = jnp.exp(s - peak)
            tot = jnp.sum(e, axis=-1, keepdims=True)
            lsum = jnp.where(lane == 2 * p + h, peak + jnp.log(tot), lsum)
            outs.append(dot((e / tot).astype(B16), v2))
        mixed_o[:, 128 * p : 128 * (p + 1)] = jnp.where(low_lane, outs[0], outs[1]).astype(B16)
    lsum_o[...] = lsum
    att = dot(mixed_o[...], outw[...]) + bias_o[2:3, :]
    att_o[...] = att
    resid = source + mod[2:3] * att
    resid_o[...] = resid
    n2, _ = norm_parts(resid)
    second = (n2 * (1.0 + mod[4:5]) + mod[3:4]).astype(B16)
    second_o[...] = second

    lane8 = lax.broadcasted_iota(jnp.int32, (length, E), 1)
    two = (
        lax.broadcasted_iota(jnp.int32, (2, 128), 0) == lax.broadcasted_iota(jnp.int32, (2, 128), 1)
    )
    route_cols = dot_tn(
        routes[...].astype(F32).astype(B16), jnp.where(two, 1.0, 0.0).astype(B16)
    ).astype(jnp.int32)
    route = [route_cols[:, k : k + 1] for k in range(2)]
    picks = [(r == lane8) for r in route]
    both = jnp.where(picks[0], 1.0, 0.0) + jnp.where(picks[1], 1.0, 0.0)
    earlier = (
        lax.broadcasted_iota(jnp.int32, (length, length), 1)
        < lax.broadcasted_iota(jnp.int32, (length, length), 0)
    )
    rank = dot(jnp.where(earlier, 1.0, 0.0).astype(B16), both.astype(B16))
    places = []
    for k in range(2):
        slot = jnp.sum(jnp.where(picks[k], rank, 0.0), axis=-1, keepdims=True).astype(jnp.int32)
        places.append(jnp.where(slot < CAP, route[k] * CAP + slot, -1))
    place_o[...] = jnp.where(
        lane == 0,
        places[0],
        jnp.where(lane == 1, places[1], jnp.where(lane == 2, route[0], route[1])),
    )
    maps = [jnp.where(choose_rows(v, E * CAP), 1.0, 0.0) for v in places]
    sbuf[...] = dot_tn((maps[0] + maps[1]).astype(B16), second).astype(B16)
    give_rows = PlaneExchange(sbuf, rows, ds0, dr0)
    give_rows.start()
    logits = dot_nt(second, rt_o[...].astype(B16))
    chosen = [jnp.sum(jnp.where(pick, logits, 0.0), axis=-1, keepdims=True) for pick in picks]
    top = jnp.maximum(chosen[0], chosen[1])
    e2 = [jnp.exp(v - top) for v in chosen]
    gates = [v / (e2[0] + e2[1]) for v in e2]
    gates_o[...] = jnp.where(lane == 0, gates[0], jnp.where(lane == 1, gates[1], 0.0))
    moe_grad = (mod[5:6] * cot[...].astype(F32)).astype(B16).astype(F32)
    pair = [(g * moe_grad).astype(B16) for g in gates]
    gbuf[...] = (
        dot_tn(maps[0].astype(B16), pair[0]) + dot_tn(maps[1].astype(B16), pair[1])
    ).astype(B16)
    give_grads = PlaneExchange(gbuf, grads, ds1, dr1)
    give_grads.start()
    for column in later:
        column.take(2)

    first_x = x == 0
    acc[...] = jnp.zeros_like(acc) + jnp.where(first_x, bout_r[0:1, :], bout_r[1:2, :]).astype(F32)
    for load in loads:
        load.wait()
    give_rows.wait_in()

    def span(f):
        return pl.ds(pl.multiple_of(f * CHUNK, 128), CHUNK)

    def put_slope(f):
        return pltpu.make_async_copy(slopes.at[:, span(f)], slopes_o.at[:, span(f)], osem.at[1, f])

    def put_out(f):
        return pltpu.make_async_copy(dwout.at[span(f), :], dwout_o.at[span(f), :], osem.at[0, f])

    def forward(f, carry):
        cols = span(f)
        bias = jnp.where(first_x, bin_r[0:1, cols], bin_r[1:2, cols]).astype(F32)
        act, slope = gelu_parts(dot(rows[...], win[:, cols]) + bias)
        low = act.astype(B16)
        lows[:, cols] = low
        slopes[:, cols] = slope
        put_slope(f).start()
        acc[...] += dot(low, wout[cols, :])
        return carry

    count = hidden // CHUNK
    lax.fori_loop(0, count, forward, 0)
    res_o[...] = acc[...].astype(B16)
    give_grads.wait_in()
    for column in later:
        column.take(3)

    def outer(f, carry):
        cols = span(f)
        dwout[cols, :] = dot_tn(lows[:, cols], grads[...]).astype(B16)
        put_out(f).start()
        return carry

    lax.fori_loop(0, count, outer, 0)
    for column in later:
        column.finish()
    for exchange in (give_rows, give_grads):
        exchange.wait_out()
    peers(lambda p: first(p, p).wait_send())
    peers(lambda p: second_hop(p, p).wait_send())
    for copy in keep:
        copy.wait()
    for f in range(count):
        put_slope(f).wait()
        put_out(f).wait()


def lead_part(tok, cot, route, cond, ada, adab, qvb, outb, soutb, sinb, router, bin_r, bout_r, shards, win, wout):
    n = NZ * NX
    length, width = tok.shape
    hidden = win.shape[2]
    slots = E * CAP
    dma = pltpu.SemaphoreType.DMA
    vm = pltpu.VMEM
    tiles = (ada.shape[1] // 128 + 7) // 8 * 8
    wide = [sds((n * s.shape[0], s.shape[1]), B16) for s in shards[:2]]
    wide += [sds((NZ * s.shape[0], s.shape[1] // 2), B16) for s in shards[2:]]
    outs = [
        sds((length, width), B16),
        sds((length, 3 * width), B16),
        sds((length, 128), F32),
        sds((length, width), B16),
        sds((length, width), F32),
        sds((length, width), F32),
        sds((length, width), B16),
        sds((length, 128), F32),
        sds((length, 128), jnp.int32),
        sds((8, width), F32),
        sds((8, width), F32),
        sds((1, hidden), F32),
        sds((E, width), F32),
        sds((8, 128), F32),
        sds((slots, width), B16),
        sds((slots, width), B16),
        sds((slots, width), B16),
    ]
    far = wide + [sds((slots, hidden), F32), sds((hidden, width), B16)]
    return pl.pallas_call(
        lead_kernel,
        out_shape=outs + far,
        in_specs=[VM] * 13 + [HB] * 6,
        out_specs=[VM] * len(outs) + [HB] * len(far),
        scratch_shapes=[
            vm((32, 128), F32),
            vm((n, 32, 128), F32),
            vm((n, tiles, 128), F32),
            vm((n, tiles, 128), F32),
            vm(wide[0].shape, B16),
            vm(wide[1].shape, B16),
            vm((slots, width), B16),
            vm((slots, width), B16),
            vm((width, hidden), B16),
            vm((hidden, width), B16),
            vm((hidden, width), B16),
            vm((slots, hidden), B16),
            vm((slots, hidden), F32),
            vm((slots, width), F32),
            dma((n,)),
            dma((n,)),
            dma((n,)),
            dma((n,)),
        ]
        + [dma((E,))] * 4
        + [dma((4,)), dma((2, hidden // CHUNK))]
        + Gather.semaphores(2)
        + [dma((2, NZ)), dma((NZ,)), dma((1,))] * 2,
        compiler_params=params(1),
        name="front_and_expert",
    )(tok, cot, route, cond, ada, adab, qvb, outb, soutb, sinb, router, bin_r, bout_r, *shards, win, wout)


def expert_back_kernel(which, rows, grads, slopes, win, wout, dwin, bgr, ebias, back):
    f = pl.program_id(0)
    last = pl.num_programs(0) - 1
    width, chunk = rows.shape[1], slopes.shape[1]
    tiles = chunk // 128

    @pl.when(f == 0)
    def _():
        back[...] = jnp.zeros_like(back)
        ebias[...] = jnp.zeros_like(ebias)
        column = jnp.sum(grads[...].astype(F32), axis=0, keepdims=True)
        for j in range(width // 128):
            ebias[pl.ds((last + 1) * tiles + j, 1), :] = column[:, 128 * j : 128 * (j + 1)]

    pre = (dot_nt(grads[...], wout[0]) * slopes[...]).astype(B16)
    dwin[...] = dot_tn(rows[...], pre).astype(B16)
    back[...] += dot_nt(pre, win[0])
    col = jnp.sum(pre.astype(F32), axis=0, keepdims=True)
    for j in range(tiles):
        ebias[pl.ds(f * tiles + j, 1), :] = col[:, 128 * j : 128 * (j + 1)]

    @pl.when(f == last)
    def _():
        bgr[...] = back[...].astype(B16)


def expert_back(which, rows, grads, slopes, win, wout):
    slots, width = rows.shape
    hidden = slopes.shape[1]
    whole = lambda f, w: (0, 0)
    return pl.pallas_call(
        expert_back_kernel,
        out_shape=[sds((width, hidden), B16), sds((slots, width), B16), sds((32, 128), F32)],
        grid_spec=pltpu.PrefetchScalarGridSpec(
            num_scalar_prefetch=1,
            grid=(hidden // CHUNK,),
            in_specs=[
                pl.BlockSpec((slots, width), whole),
                pl.BlockSpec((slots, width), whole),
                pl.BlockSpec((slots, CHUNK), lambda f, w: (0, f)),
                pl.BlockSpec((1, width, CHUNK), lambda f, w: (w[0], 0, f)),
                pl.BlockSpec((1, CHUNK, width), lambda f, w: (w[0], f, 0)),
            ],
            out_specs=[
                pl.BlockSpec((width, CHUNK), lambda f, w: (0, f)),
                pl.BlockSpec((slots, width), whole),
                pl.BlockSpec((32, 128), whole),
            ],
            scratch_shapes=[pltpu.VMEM((slots, width), F32)],
        ),
        compiler_params=params(),
        name="expert_back",
    )(which, rows, grads, slopes, win, wout)


def middle_kernel(
    res, bgr, second_r, resid_r, att_r, cot, mod, sin_c, sout_c, sinb, bias, router, gates_r, place_r,
    mixed, outw,
    out_o, rgrad_o, mgrad_o, dsin, dsout, dout, drouter, vecs, mg2,
    ret, retg, shared, sgrad, sin, sout, send, recv, send2, recv2, *ssems,
):
    barrier = pltpu.get_barrier_semaphore()
    for k in range(1, E):
        greet(barrier, plane_peer(k)[0])
    pl.semaphore_wait(barrier, E - 1)
    count = len(ssems) // 2
    spreads = (Spread(sin_c, sin, *ssems[:count]), Spread(sout_c, sout, *ssems[count:]))
    for spread in spreads:
        spread.begin()
    gives = (PlaneExchange(res, ret, send, recv), PlaneExchange(bgr, retg, send2, recv2))
    for give in gives:
        give.start()
    for spread in spreads:
        spread.near()
    length, width = second_r.shape
    hidden = sin.shape[3]
    chunk = hidden // NZ
    second = second_r[...]
    grad_out = cot[...].astype(F32)
    moe_low = (mod[5:6] * grad_out).astype(B16)
    moe_grad = moe_low.astype(F32)
    shared[...] = jnp.zeros_like(shared) + bias[3:4, :]
    sgrad[...] = jnp.zeros_like(sgrad)
    vecs[...] = jnp.zeros_like(vecs)
    for spread in spreads:
        spread.take_x()
    for spread in spreads:
        spread.take_y()
    for spread in spreads:
        spread.finish()

    def body(f, carry):
        cols = pl.ds(pl.multiple_of(f * chunk, 128), chunk)
        w1 = sin[:, :, :, cols].reshape(width, chunk)
        w2 = sout[f].reshape(chunk, width)
        act, slope = gelu_parts(dot(second, w1) + sinb[:, cols])
        low = act.astype(B16)
        shared[...] += dot(low, w2)
        pre = (dot_nt(moe_low, w2) * slope).astype(B16)
        dsout[cols, :] = dot_tn(low, moe_low).astype(B16)
        dsin[:, cols] = dot_tn(second, pre).astype(B16)
        sgrad[...] += dot_nt(pre, w1)
        col = jnp.sum(pre.astype(F32), axis=0, keepdims=True)
        for j in range(chunk // 128):
            vecs[pl.ds(f * (chunk // 128) + j, 1), :] = col[:, 128 * j : 128 * (j + 1)]
        return carry

    lax.fori_loop(0, hidden // chunk, body, 0)
    lane = lax.broadcasted_iota(jnp.int32, (length, E), 1)
    gates = [gates_r[:, k : k + 1] for k in range(2)]
    maps = [
        jnp.where(choose_rows(place_r[:, k : k + 1], E * CAP), 1.0, 0.0) for k in range(2)
    ]
    for give in gives:
        give.wait_in()
    back = ret[...]
    rows = [dot(m.astype(B16), back) for m in maps]
    moe = shared[...] + (gates[0] * rows[0] + gates[1] * rows[1])
    resid = resid_r[...]
    out_o[...] = (resid + mod[5:6] * moe).astype(B16)
    mg2[...] = jnp.zeros_like(mg2)
    mg2[5:6, :] = jnp.sum(grad_out * moe, axis=0, keepdims=True)
    ggrad = [jnp.sum(moe_grad * r, axis=-1, keepdims=True) for r in rows]
    inner = gates[0] * ggrad[0] + gates[1] * ggrad[1]
    lgrad = jnp.zeros((length, E), F32)
    for k in range(2):
        pick = place_r[:, 2 + k : 3 + k] == lane
        lgrad = lgrad + jnp.where(pick, gates[k] * (ggrad[k] - inner), 0.0)
    lgrad = lgrad.astype(B16)
    drouter[...] = dot_tn(lgrad, second)
    grad = (
        sgrad[...]
        + dot((maps[0] + maps[1]).astype(B16), retg[...])
        + dot(lgrad, router[...].astype(B16))
    )
    n2, r2 = norm_parts(resid)
    mg2[3:4, :] = jnp.sum(grad, axis=0, keepdims=True)
    mg2[4:5, :] = jnp.sum(grad * n2, axis=0, keepdims=True)
    rgrad = grad_out + norm_back(grad * (1.0 + mod[4:5]), n2, r2)
    rgrad_o[...] = rgrad
    agrad = (mod[2:3] * rgrad).astype(B16)
    mg2[2:3, :] = jnp.sum(rgrad * att_r[...], axis=0, keepdims=True)
    dout[...] = dot_tn(mixed[...], agrad).astype(B16)
    mgrad_o[...] = dot_nt(agrad, outw[...]).astype(B16)
    sums = [
        jnp.sum(moe_grad, axis=0, keepdims=True),
        jnp.sum(agrad.astype(F32), axis=0, keepdims=True),
    ]
    base = hidden // 128
    for i, row in enumerate(sums):
        for j in range(width // 128):
            at = base + i * (width // 128) + j
            vecs[at : at + 1, :] = row[:, 128 * j : 128 * (j + 1)]
    for give in gives:
        give.wait_out()
    for spread in spreads:
        spread.close()


def middle(*args):
    res, second, sin = args[0], args[2], args[7]
    length, width = second.shape
    rows, hidden = res.shape[0], 2 * sin.shape[1]
    dma = pltpu.SemaphoreType.DMA
    return pl.pallas_call(
        middle_kernel,
        out_shape=[
            sds((length, width), B16),
            sds((length, width), F32),
            sds((length, width), B16),
            sds((width, hidden), B16),
            sds((hidden, width), B16),
            sds((width, width), B16),
            sds((E, width), F32),
            sds((40, 128), F32),
            sds((8, width), F32),
        ],
        in_specs=[VM] * 7 + [HB] * 2 + [VM] * 7,
        out_specs=[VM] * 9,
        scratch_shapes=[
            pltpu.VMEM((rows, width), B16),
            pltpu.VMEM((rows, width), B16),
            pltpu.VMEM((length, width), F32),
            pltpu.VMEM((length, width), F32),
            pltpu.VMEM((NZ, NX, width // NZ // NX, hidden), B16),
            pltpu.VMEM((NZ, NX, hidden // NZ // NX, width), B16),
            dma((E,)),
            dma((E,)),
            dma((E,)),
            dma((E,)),
        ]
        + Spread.semaphores()
        + Spread.semaphores(),
        compiler_params=params(3),
        name="shared_expert_combine",
    )(*args)


def back_kernel(
    tok, mod, normed, proj, lsum, mgrad, rgrad, qkv, mg2,
    tgrad_o, dqkv, qvec, mgt,
    pgrad,
):
    length, width = tok.shape
    low_lane = lax.broadcasted_iota(jnp.int32, (length, 128), 1) < HEAD_DIM
    for p in range(HEADS // 2):
        q2 = proj[:, 128 * p : 128 * (p + 1)]
        k2 = proj[:, width + 128 * p : width + 128 * (p + 1)]
        v2 = proj[:, 2 * width + 128 * p : 2 * width + 128 * (p + 1)]
        m2 = mgrad[:, 128 * p : 128 * (p + 1)]
        parts = []
        for h in range(2):
            mine = low_lane if h == 0 else jnp.logical_not(low_lane)
            zero = jnp.zeros_like(q2)
            s = dot_nt(jnp.where(mine, q2, zero), k2) * SCALE
            prob = jnp.exp(s - lsum[:, 2 * p + h : 2 * p + h + 1])
            pg = dot_nt(jnp.where(mine, m2, zero), v2)
            inner = jnp.sum(prob * pg, axis=-1, keepdims=True)
            sg = (prob * (pg - inner)).astype(B16)
            parts.append(
                (dot(sg, k2) * SCALE, dot_tn(sg, q2) * SCALE, dot_tn(prob.astype(B16), m2))
            )
        for i in range(3):
            pgrad[:, i * width + 128 * p : i * width + 128 * (p + 1)] = jnp.where(
                low_lane, parts[0][i], parts[1][i]
            ).astype(B16)
    ngrad = dot_nt(pgrad[...], qkv[...])
    for i in range(3):
        dqkv[:, i * width : (i + 1) * width] = dot_tn(
            normed[...], pgrad[:, i * width : (i + 1) * width]
        ).astype(B16)
    per = width // 128
    for i, k in enumerate((0, 2)):
        row = jnp.sum(pgrad[:, k * width : (k + 1) * width].astype(F32), axis=0, keepdims=True)
        for j in range(per):
            qvec[i * per + j : i * per + j + 1, :] = row[:, 128 * j : 128 * (j + 1)]
    for j in range(2 * per, qvec.shape[0]):
        qvec[j : j + 1, :] = jnp.zeros((1, 128), F32)
    n1, r1 = norm_parts(tok[...].astype(F32))
    tgrad_o[...] = rgrad[...] + norm_back(ngrad * (1.0 + mod[1:2]), n1, r1)
    rows = [
        jnp.sum(ngrad, axis=0, keepdims=True),
        jnp.sum(ngrad * n1, axis=0, keepdims=True),
    ] + [mg2[i : i + 1, :] for i in range(2, 6)]
    mgt[...] = jnp.zeros_like(mgt)
    for i, row in enumerate(rows):
        row = row.astype(B16).astype(F32)
        for j in range(per):
            mgt[i * per + j : i * per + j + 1, :] = row[:, 128 * j : 128 * (j + 1)]


def back(*args):
    tok, qkv = args[0], args[7]
    length, width = tok.shape
    return pl.pallas_call(
        back_kernel,
        out_shape=[
            sds((length, width), F32),
            sds(qkv.shape, B16),
            sds((16, 128), F32),
            sds((48, 128), F32),
        ],
        in_specs=[VM] * 9,
        out_specs=[VM] * 4,
        scratch_shapes=[pltpu.VMEM((length, 3 * width), B16)],
        compiler_params=params(),
        name="attention_back",
    )(*args)


PIECES = ((2, 0, 2, True), (3, 0, 1, False), (0, 0, 1, True), (2, 1, 2, False), (1, 0, 1, True))


def add_into(target, source, lead):
    count = 1
    for n in lead:
        count *= n

    def body(i, carry):
        at = []
        rest = i
        for n in reversed(lead):
            at.append(lax.rem(rest, n))
            rest = lax.div(rest, n)
        at = tuple(reversed(at))
        target[at] = (target[at].astype(F32) + source(at).astype(F32)).astype(B16)
        return carry

    lax.fori_loop(0, count, body, 0)


class Reduce:
    def __init__(self, grad, out, col, width, y_first, bufs, sems):
        self.z, self.x, self.y, self.c = coords()
        self.grad, self.out, self.width, self.y_first = grad, out, width, y_first
        self.half = grad.shape[-1] // 2
        self.col = col
        self.cbuf, self.lbuf, self.ebuf, self.fbuf, self.zin = bufs
        self.one, self.zsem = sems

    @staticmethod
    def scratch(rows, width):
        vm = lambda *lead: pltpu.VMEM(lead + (rows, width), B16)
        return [
            vm(NZ, NX, 2),
            vm(NZ, NX, 2),
            vm(NZ, 2),
            vm(NZ),
            vm(NZ),
            pltpu.SemaphoreType.DMA((14,)),
            pltpu.SemaphoreType.DMA((2, NZ)),
        ]

    def cols(self, c):
        return pl.ds(pl.multiple_of(c * self.half + self.col, 128), self.width)

    def core_copy(self):
        return remote(
            self.grad.at[:, :, :, :, self.cols(1 - self.c)],
            self.cbuf,
            self.one.at[0],
            self.one.at[1],
            dev(self.z, self.x, self.y, 1 - self.c),
        )

    def load(self):
        return pltpu.make_async_copy(
            self.grad.at[:, :, :, :, self.cols(self.c)], self.lbuf, self.one.at[2]
        )

    def copy1(self):
        if self.y_first:
            source, to = self.cbuf.at[:, :, 1 - self.y], dev(self.z, self.x, 1 - self.y, self.c)
        else:
            source, to = self.cbuf.at[:, 1 - self.x], dev(self.z, 1 - self.x, self.y, self.c)
        return remote(source, self.ebuf, self.one.at[3], self.one.at[4], to)

    def copy2(self):
        if self.y_first:
            source, to = self.ebuf.at[:, 1 - self.x], dev(self.z, 1 - self.x, self.y, self.c)
        else:
            source, to = self.ebuf.at[:, 1 - self.y], dev(self.z, self.x, 1 - self.y, self.c)
        return remote(source, self.fbuf, self.one.at[5], self.one.at[6], to)

    def zcopy(self, zb, at):
        return remote(
            self.fbuf.at[zb],
            self.zin.at[at],
            self.zsem.at[0, zb],
            self.zsem.at[1, at],
            dev(zb, self.x, self.y, self.c),
        )

    def others(self, action):
        for zb in range(NZ):

            @pl.when(zb != self.z)
            def _():
                action(zb)

    def own(self):
        return self.fbuf.at[self.z]

    def place(self, y, c):
        return self.out.at[y, :, self.cols(c)]

    def keep(self):
        return pltpu.make_async_copy(self.own(), self.place(self.y, self.c), self.one.at[7])

    def give_y(self):
        return remote(
            self.own(), self.place(self.y, self.c), self.one.at[8], self.one.at[9],
            dev(self.z, self.x, 1 - self.y, self.c),
        )

    def give_c(self):
        return remote(
            self.own(), self.place(self.y, self.c), self.one.at[10], self.one.at[11],
            dev(self.z, self.x, self.y, 1 - self.c),
        )

    def pass_c(self):
        here = self.place(1 - self.y, self.c)
        return remote(
            here, here, self.one.at[12], self.one.at[13], dev(self.z, self.x, self.y, 1 - self.c)
        )

    def stage(self, s):
        if s == 0:
            self.core_copy().wait_recv()
            self.load().wait()
            add_into(self.cbuf, lambda i: self.lbuf[i], (NZ, NX, 2))
            self.copy1().start()
        elif s == 1:
            self.copy1().wait_recv()
            if self.y_first:
                add_into(self.ebuf, lambda i: self.cbuf[i[0], i[1], self.y], (NZ, NX))
            else:
                add_into(self.ebuf, lambda i: self.cbuf[i[0], self.x, i[1]], (NZ, 2))
            self.copy2().start()
        elif s == 2:
            self.copy2().wait_recv()
            side = self.x if self.y_first else self.y
            add_into(self.fbuf, lambda i: self.ebuf[i[0], side], (NZ,))
            self.others(lambda zb: self.zcopy(zb, self.z).start())
        elif s == 3:
            self.zin[self.z] = self.fbuf[self.z]
            self.others(lambda zb: self.zcopy(zb, zb).wait_recv())
            total = self.zin[0].astype(F32)
            for zb in range(1, NZ):
                total = total + self.zin[zb].astype(F32)
            self.fbuf[self.z] = total.astype(B16)
            self.give_y().start()
            self.give_c().start()
            self.keep().start()
        elif s == 4:
            self.give_y_in().wait_recv()
            self.pass_c().start()
        elif s == 5:
            self.keep().wait()
            self.give_c_in().wait_recv()
            self.pass_c_in().wait_recv()
            self.core_copy().wait_send()
            self.copy1().wait_send()
            self.copy2().wait_send()
            self.give_y().wait_send()
            self.give_c().wait_send()
            self.pass_c().wait_send()
            self.others(lambda zb: self.zcopy(zb, zb).wait_send())

    def give_y_in(self):
        return remote(
            self.own(), self.place(1 - self.y, self.c), self.one.at[8], self.one.at[9],
            dev(self.z, self.x, 1 - self.y, self.c),
        )

    def give_c_in(self):
        return remote(
            self.own(), self.place(self.y, 1 - self.c), self.one.at[10], self.one.at[11],
            dev(self.z, self.x, self.y, 1 - self.c),
        )

    def pass_c_in(self):
        here = self.place(1 - self.y, 1 - self.c)
        return remote(
            here, here, self.one.at[12], self.one.at[13], dev(self.z, self.x, self.y, 1 - self.c)
        )

    STAGES = 6


def sums_kernel(*refs):
    grads = refs[:4]
    mine_out = refs[4]
    vecs, qvec, drouter, ebias, mgt, condt, ada = refs[5:12]
    outs = refs[12:16]
    pair_out = refs[16]
    small, esum, tiles, cgot = refs[17:21]
    rest = list(refs[21:])
    z, x, y, c = coords()
    dp, ex = lax.axis_index("dp"), lax.axis_index("expert")
    n = NZ * NX

    barrier = pltpu.get_barrier_semaphore()

    def peers(action):
        for p in range(n):

            @pl.when(p != dp)
            def _():
                action(p)

    peers(lambda p: greet(barrier, (p, ex)))
    mates = (dev(z, x, 1 - y, c), dev(z, x, y, 1 - c), dev(z, x, 1 - y, 1 - c))
    for mate in mates:
        greet(barrier, mate)
    pl.semaphore_wait(barrier, n - 1 + 3)

    plans = []
    for matrix, part, share, y_first in PIECES:
        grad = grads[matrix]
        width = grad.shape[-1] // 2 // share
        plans.append(
            Reduce(grad, outs[matrix], part * width, width, y_first, rest[:5], rest[5:7])
        )
        rest = rest[7:]
    ssum, sgot, zgot, esend, egot, mine, csend, sems, dsem, zsem, tsem, wsem = rest

    for plan in plans:
        plan.core_copy().start()
        plan.load().start()

    def swap():
        return remote(
            mine_out.at[1 - x], pair_out.at[x], wsem.at[0], wsem.at[1], dev(z, 1 - x, y, c)
        )

    def swap_in():
        return remote(
            mine_out.at[1 - x], pair_out.at[1 - x], wsem.at[0], wsem.at[1], dev(z, 1 - x, y, c)
        )

    swap().start()
    swap_keep = pltpu.make_async_copy(mine_out.at[x], pair_out.at[x], wsem.at[2])
    swap_keep.start()

    rows = vecs.shape[0]
    ssum[0:rows, :] = vecs[...]
    ssum[rows : rows + 16, :] = qvec[...]
    per = drouter.shape[1] // 128
    for b in range(per):
        ssum[rows + 16 + 8 * b : rows + 24 + 8 * b, :] = drouter[:, 128 * b : 128 * (b + 1)]
    hops = (dev(z, x, y, 1 - c), dev(z, x, 1 - y, c), dev(z, 1 - x, y, c))

    def hop(i):
        return remote(zgot.at[4 + i], sgot.at[i], sems.at[0, i], sems.at[1, i], hops[i])

    def ehop():
        return remote(esend.at[x], egot.at[z, x], sems.at[0, 3], sems.at[1, 3], hops[2])

    def ehop_in():
        return remote(esend.at[x], egot.at[z, 1 - x], sems.at[0, 3], sems.at[1, 3], hops[2])

    mine[0:40, :] = mgt[0:40, :]
    mine[40:48, :] = condt[...]

    def tile(p, at):
        return remote(mine, tiles.at[ex, at], dsem.at[0, p], dsem.at[1, at], (p, ex))

    def spread(i, theirs=False):
        e2 = 2 * (1 - y if i != 1 else y) + (1 - c if i != 0 else c)
        rows = tiles.at[e2 if theirs else ex]
        return remote(rows, rows, tsem.at[0, i], tsem.at[1, i], mates[i])

    def cond_copy(p, at):
        return remote(csend.at[p], cgot.at[at], dsem.at[2, p], dsem.at[3, at], (p, ex))

    def zsum(zb, at):
        return remote(ssum, zgot.at[at], zsem.at[0, zb], zsem.at[1, at], dev(zb, x, y, c))

    def zexp(zb, at):
        return remote(
            egot.at[at], egot.at[at], zsem.at[2, zb], zsem.at[3, at], dev(zb, x, y, c)
        )

    def lines(action):
        for zb in range(NZ):

            @pl.when(zb != z)
            def _():
                action(zb)

    def start_hop(i):
        zgot[4 + i] = ssum[...]
        hop(i).start()

    def end_hop(i):
        hop(i).wait()
        ssum[...] = ssum[...] + sgot[i]

    def small0():
        start_hop(0)
        esend[x] = ebias[...]
        egot[z, x] = ebias[...]
        ehop().start()
        peers(lambda p: tile(p, dp).start())
        tiles[ex, dp] = mine[...]

    def small1():
        end_hop(0)
        start_hop(1)
        peers(lambda p: tile(p, p).wait_recv())
        for i in range(3):
            spread(i).start()
        acc = jnp.zeros((n, ada.shape[0]), F32)
        for j in range(ada.shape[1] // 128):
            acc = acc + dot_nt(tiles[ex, :, j, :].astype(B16), ada[:, 128 * j : 128 * (j + 1)])
        csend[...] = jnp.zeros_like(csend)
        csend[:, 0, 0 : ada.shape[0]] = acc
        peers(lambda p: cond_copy(p, dp).start())
        cgot[dp] = csend[dp]

    def small2():
        end_hop(1)
        start_hop(2)
        ehop().wait_send()
        ehop_in().wait_recv()
        lines(lambda zb: zexp(zb, z).start())

    def small3():
        end_hop(2)
        zgot[z] = ssum[...]
        lines(lambda zb: zsum(zb, z).start())

    def small4():
        lines(lambda zb: zexp(zb, zb).wait_recv())
        lines(lambda zb: zsum(zb, zb).wait_recv())
        total, etotal = zgot[0], egot[0]
        for i in range(1, NZ):
            total = total + zgot[i]
            etotal = etotal + egot[i]
        small[...] = total
        esum[...] = etotal

    def small5():
        peers(lambda p: cond_copy(p, p).wait_recv())
        for i in range(3):
            spread(i, True).wait_recv()
            spread(i).wait_send()
        peers(lambda p: tile(p, p).wait_send())
        peers(lambda p: cond_copy(p, p).wait_send())
        lines(lambda zb: zexp(zb, zb).wait_send())
        lines(lambda zb: zsum(zb, zb).wait_send())

    steps = [small0, small1, small2, small3, small4, small5]
    for t in range(Reduce.STAGES):
        steps[t]()
        for plan in plans:
            plan.stage(t)
    swap_in().wait_recv()
    swap().wait_send()
    swap_keep.wait()


def device_sums(grads, mine_out, vecs, qvec, drouter, ebias, mgt, condt, ada):
    n = NZ * NX
    dma = pltpu.SemaphoreType.DMA
    split = [g.reshape(NZ, NX, 2, g.shape[0] // (4 * NZ), g.shape[1]) for g in grads]
    outs = [sds((2, g.shape[3], g.shape[4]), B16) for g in split]
    rows = vecs.shape[0] + 16 + 8 * (drouter.shape[1] // 128)
    scratch = []
    for matrix, _, share, _ in PIECES:
        g = split[matrix]
        scratch += Reduce.scratch(g.shape[3], g.shape[4] // 2 // share)
    vm = pltpu.VMEM
    scratch += [
        vm((rows, 128), F32),
        vm((3, rows, 128), F32),
        vm((NZ + 3, rows, 128), F32),
        vm((2, 32, 128), F32),
        vm((NZ, 2, 32, 128), F32),
        vm((48, 128), F32),
        vm((n, 8, 128), F32),
        dma((2, 4)),
        dma((4, n)),
        dma((4, NZ)),
        dma((2, 3)),
        dma((3,)),
    ]
    out = pl.pallas_call(
        sums_kernel,
        out_shape=outs
        + [
            sds(mine_out.shape, B16),
            sds((rows, 128), F32),
            sds((2, 32, 128), F32),
            sds((4, n, 48, 128), F32),
            sds((n, 8, 128), F32),
        ],
        in_specs=[HB] * 5 + [VM] * 7,
        out_specs=[HB] * 5 + [VM] * 4,
        scratch_shapes=scratch,
        compiler_params=params(4),
        name="device_sums",
    )(*split, mine_out, vecs, qvec, drouter, ebias, mgt, condt, ada)
    return [o.reshape(-1, o.shape[2]).astype(F32) for o in out[:4]], out[4], out[5:]


def on_block(
    tokens, conditioning, routes, cotangent, ada_weight, ada_bias, qkv_weight, qv_bias, out_weight, out_bias,
    shared_in, shared_in_bias, shared_out, shared_out_bias, router,
    expert_in, expert_in_bias, expert_out, expert_out_bias,
):
    n = NZ * NX
    dp = lax.axis_index("dp")
    x = lax.rem(dp, NX)
    width = tokens.shape[2]
    hidden = shared_in.shape[1]
    part = width // n
    tok, cot, route = tokens[0], cotangent[0], routes[0]
    _, silu_back = jax.vjp(jax.nn.silu, conditioning.astype(F32))
    (
        normed, proj, lsum, mixed, att, resid, second, gates, place, mod, bias, sinb, router_t,
        condt, rows, grads, res, qkv_full, out_full, sin_full, sout_full, slopes, dwout,
    ) = lead_part(
        tok, cot, route.T, conditioning, ada_weight, ada_bias[None], qv_bias, out_bias[None], shared_out_bias[None],
        shared_in_bias[None], router.T, expert_in_bias, expert_out_bias,
        (qkv_weight, out_weight, shared_in, shared_out), expert_in, expert_out,
    )
    line = [[NX * z + xx for z in range(NZ)] for xx in range(NX)]
    turn = [(i, i // NX * NX + 1 - i % NX) for i in range(n)]

    first = x == 0

    def over_z(grad):
        return lax.psum_scatter(grad, "dp", scatter_dimension=0, axis_index_groups=line, tiled=True)

    def swap(pair, axis):
        keep = lax.dynamic_index_in_dim(pair, x, axis, keepdims=False)
        give = lax.dynamic_index_in_dim(pair, 1 - x, axis, keepdims=False)
        came = lax.ppermute(give, "dp", turn)
        return jnp.stack(
            [jnp.where(first, keep, came), jnp.where(first, came, keep)], axis=axis
        )

    dwout_mine = over_z(dwout)
    dwin, bgr, ebias = expert_back(
        jnp.reshape(x, (1,)), rows, grads, slopes, expert_in, expert_out
    )
    dwin_mine = over_z(dwin)
    (output, rgrad, mgrad, dsin, dsout, dout, drouter, vecs, mg2) = middle(
        res, bgr, second, resid, att, cot, mod, sin_full, sout_full, sinb, bias, router_t, gates, place,
        mixed, out_full,
    )
    tgrad, dqkv, qvec, mgt = back(tok, mod, normed, proj, lsum, mgrad, rgrad, qkv_full, mg2)
    dense, dwout_pair, (small, esum, tiles, cgot) = device_sums(
        (dqkv, dout, dsin, dsout), dwout_mine.reshape(NX, hidden // n, width), vecs, qvec, drouter, ebias, mgt, condt, ada_weight
    )

    dwout_sum = dwout_pair.astype(F32)
    dwin_sum = swap(dwin_mine.reshape(NX, part, hidden), 0).astype(F32)

    def share(v, size):
        return lax.dynamic_slice_in_dim(v.reshape(-1), dp * size, size, 0)

    per = width // 128
    base = hidden // 128
    sinb_grad = share(small[:base], hidden // n)
    soutb_grad = share(small[base : base + per], part)
    outb_grad = share(small[base + per : base + 2 * per], part)
    qvb_grad = jnp.stack(
        [share(small[40 : 40 + per], part), share(small[40 + per : 40 + 2 * per], part)]
    )
    router_grad = small[56:].reshape(per, E, 128).transpose(0, 2, 1).reshape(width, E)
    router_grad = lax.dynamic_slice_in_dim(router_grad, dp * part, part, 0)
    ein_b = lax.dynamic_slice_in_dim(
        esum[:, :base].reshape(2, hidden), dp * (hidden // n), hidden // n, 1
    )
    eout_b = lax.dynamic_slice_in_dim(
        esum[:, base : base + per].reshape(2, width), dp * part, part, 1
    )
    images = tiles.shape[0] * n
    mods = tiles[:, :, : 6 * per].reshape(images, 6 * width)
    conds = lax.dynamic_slice_in_dim(
        tiles[:, :, 40 : 40 + per].reshape(images, width), dp * part, part, 1
    )
    ada_grad = lax.dot_general(
        conds.astype(B16), mods.astype(B16), (((0,), (0,)), ((), ())), preferred_element_type=F32
    )
    adab_grad = share(jnp.sum(mods, axis=0), ada_bias.shape[0])
    cond_grad = silu_back(cgot[:, 0, :part].reshape(1, width))[0]
    return (
        output[None],
        tgrad[None],
        cond_grad,
        ada_grad,
        adab_grad,
        dense[0],
        qvb_grad,
        dense[1],
        outb_grad,
        dense[2],
        sinb_grad,
        dense[3],
        soutb_grad,
        router_grad,
        dwin_sum,
        ein_b,
        dwout_sum,
        eout_b,
    )


def layer_norm(rows):
    centred = rows - jnp.mean(rows, axis=-1, keepdims=True)
    return centred * lax.rsqrt(jnp.mean(centred * centred, axis=-1, keepdims=True) + 1e-06)


def modulate(rows, shift, scale):
    return layer_norm(rows) * (1.0 + scale) + shift


def gelu_tanh(values_in):
    return jax.nn.gelu(values_in, approximate=True)


def on_device(
    tokens,
    conditioning,
    routes,
    cotangent,
    ada_weight,
    ada_bias,
    qkv_weight,
    qv_bias,
    out_weight,
    out_bias,
    shared_in,
    shared_in_bias,
    shared_out,
    shared_out_bias,
    router,
    expert_in,
    expert_in_bias,
    expert_out,
    expert_out_bias,
):
    f32 = jnp.float32
    b16 = jnp.bfloat16
    gathered_dense = (
        lax.all_gather(ada_weight, "dp", axis=0, tiled=True),
        lax.all_gather(ada_bias, "dp", axis=0, tiled=True),
        lax.all_gather(qkv_weight, "dp", axis=0, tiled=True),
        lax.all_gather(qv_bias, "dp", axis=1, tiled=True),
        lax.all_gather(out_weight, "dp", axis=0, tiled=True),
        lax.all_gather(out_bias, "dp", axis=0, tiled=True),
        lax.all_gather(shared_in, "dp", axis=0, tiled=True),
        lax.all_gather(shared_in_bias, "dp", axis=0, tiled=True),
        lax.all_gather(shared_out, "dp", axis=0, tiled=True),
        lax.all_gather(shared_out_bias, "dp", axis=0, tiled=True),
        lax.all_gather(router, "dp", axis=0, tiled=True),
    )
    (
        ada_full,
        ada_bias_full,
        qkv_full,
        qv_bias_full,
        out_full,
        out_bias_full,
        shared_in_full,
        shared_in_bias_full,
        shared_out_full,
        shared_out_bias_full,
        router_full,
    ) = gathered_dense
    image_count, length, width = tokens.shape
    row_count = image_count * length
    scaling = HEAD_DIM ** (-0.5)
    head_shape = (image_count, length, HEADS, HEAD_DIM)
    cond_float = conditioning.astype(f32)
    cond_act, silu_back = jax.vjp(jax.nn.silu, cond_float)
    cond_low = cond_act.astype(b16)
    modulation = jnp.dot(cond_low, ada_full, preferred_element_type=f32) + ada_bias_full.astype(f32)
    pieces = [modulation[:, None, index * width : (index + 1) * width] for index in range(6)]
    source = tokens.astype(f32)
    first_norm, first_back = jax.vjp(modulate, source, pieces[0], pieces[1])
    normed = first_norm.astype(b16)
    projected = jnp.einsum("isd,de->ise", normed, qkv_full, preferred_element_type=f32)
    query_heads = (
        (projected[..., :width] + qv_bias_full[0].astype(f32)).astype(b16).reshape(head_shape)
    )
    key_heads = projected[..., width : 2 * width].astype(b16).reshape(head_shape)
    value_heads = (
        (projected[..., 2 * width :] + qv_bias_full[1].astype(f32)).astype(b16).reshape(head_shape)
    )
    scores = (
        jnp.einsum("iqhc,ikhc->ihqk", query_heads, key_heads, preferred_element_type=f32) * scaling
    )
    peak_score = jnp.max(scores, axis=-1, keepdims=True)
    unscaled = jnp.exp(scores - peak_score)
    exp_total = jnp.sum(unscaled, axis=-1, keepdims=True)
    log_total = peak_score + jnp.log(exp_total)
    probs_low = (unscaled / exp_total).astype(b16)
    mixed = (
        jnp.einsum("ihqk,ikhc->iqhc", probs_low, value_heads, preferred_element_type=f32)
        .reshape(image_count, length, width)
        .astype(b16)
    )
    attended = jnp.einsum(
        "isd,de->ise", mixed, out_full, preferred_element_type=f32
    ) + out_bias_full.astype(f32)
    resid = source + pieces[2] * attended
    second_float, second_back = jax.vjp(modulate, resid, pieces[3], pieces[4])
    second = second_float.astype(b16)
    shared_pre = jnp.einsum(
        "isd,df->isf", second, shared_in_full, preferred_element_type=f32
    ) + shared_in_bias_full.astype(f32)
    shared_act, shared_gelu_back = jax.vjp(gelu_tanh, shared_pre)
    shared_low = shared_act.astype(b16)
    shared = jnp.einsum(
        "isf,fd->isd", shared_low, shared_out_full, preferred_element_type=f32
    ) + shared_out_bias_full.astype(f32)
    second_rows = second.reshape(row_count, width)
    logits = jnp.dot(second_rows, router_full, preferred_element_type=f32)
    route_flat = routes.reshape(-1)
    one_hot = (route_flat[:, None] == jnp.arange(E, dtype=jnp.int32)).astype(jnp.int32)
    slot_index = jnp.sum(
        (jnp.cumsum(one_hot, axis=0, dtype=jnp.int32) - one_hot) * one_hot, axis=1, dtype=jnp.int32
    )
    position = jnp.where(slot_index < CAP, route_flat * CAP + slot_index, E * CAP)
    pair_rows = jnp.repeat(second_rows, 2, axis=0)
    buffer = (
        jnp.zeros((E * CAP, width), b16)
        .at[position]
        .set(pair_rows, mode="drop")
        .reshape(E, CAP, width)
    )
    received = lax.all_to_all(buffer, "expert", split_axis=0, concat_axis=1, tiled=True)
    expert_pre = (
        jnp.einsum("erd,edf->erf", received, expert_in, preferred_element_type=f32)
        + expert_in_bias.astype(f32)[:, None, :]
    )
    expert_low = gelu_tanh(expert_pre).astype(b16)
    expert_result = (
        jnp.einsum("erf,efd->erd", expert_low, expert_out, preferred_element_type=f32)
        + expert_out_bias.astype(f32)[:, None, :]
    ).astype(b16)
    returned = lax.all_to_all(
        expert_result, "expert", split_axis=1, concat_axis=0, tiled=True
    ).reshape(E * CAP, width)
    gathered = (
        returned.at[position]
        .get(mode="fill", fill_value=0)
        .reshape(row_count, 2, width)
        .astype(f32)
    )
    pair_mask = one_hot.reshape(row_count, 2, E).astype(f32)
    chosen = jnp.sum(logits[:, None, :] * pair_mask, axis=-1)
    gates = jax.nn.softmax(chosen, axis=-1)
    moe = (shared.reshape(row_count, width) + jnp.sum(gates[..., None] * gathered, axis=1)).reshape(
        image_count, length, width
    )
    output = (resid + pieces[5] * moe).astype(b16)
    ada_back, qkv_back, out_back, shared_in_back, shared_out_back, router_back = (
        ada_full,
        qkv_full,
        out_full,
        shared_in_full,
        shared_out_full,
        router_full,
    )
    grad_out = cotangent.astype(f32)
    gate_two_grad = jnp.sum(grad_out * moe, axis=1, keepdims=True)
    moe_grad = (pieces[5] * grad_out).astype(b16)
    moe_rows_grad = moe_grad.reshape(row_count, width)
    moe_rows_float = moe_rows_grad.astype(f32)
    pair_grad = (
        (gates[..., None] * moe_rows_float[:, None, :]).astype(b16).reshape(2 * row_count, width)
    )
    gate_grad = jnp.sum(moe_rows_float[:, None, :] * gathered, axis=-1)
    chosen_grad = gates * (gate_grad - jnp.sum(gates * gate_grad, axis=-1, keepdims=True))
    logits_grad = jnp.sum(chosen_grad[..., None] * pair_mask, axis=1).astype(b16)
    grad_buffer = (
        jnp.zeros((E * CAP, width), b16)
        .at[position]
        .set(pair_grad, mode="drop")
        .reshape(E, CAP, width)
    )
    result_grad = lax.all_to_all(grad_buffer, "expert", split_axis=0, concat_axis=1, tiled=True)
    pre_again = (
        jnp.einsum("erd,edf->erf", received, expert_in, preferred_element_type=f32)
        + expert_in_bias.astype(f32)[:, None, :]
    )
    act_again, expert_gelu_back = jax.vjp(gelu_tanh, pre_again)
    low_again = act_again.astype(b16)
    expert_out_grad = jnp.einsum("erf,erd->efd", low_again, result_grad, preferred_element_type=f32)
    expert_out_bias_grad = jnp.sum(result_grad.astype(f32), axis=1)
    expert_act_grad = jnp.einsum(
        "erd,efd->erf", result_grad, expert_out, preferred_element_type=f32
    )
    pre_grad = expert_gelu_back(expert_act_grad)[0].astype(b16)
    expert_in_grad = jnp.einsum("erd,erf->edf", received, pre_grad, preferred_element_type=f32)
    expert_in_bias_grad = jnp.sum(pre_grad.astype(f32), axis=1)
    received_grad = jnp.einsum(
        "erf,edf->erd", pre_grad, expert_in, preferred_element_type=f32
    ).astype(b16)
    sent_grad = lax.all_to_all(
        received_grad, "expert", split_axis=1, concat_axis=0, tiled=True
    ).reshape(E * CAP, width)
    dispatch_rows_grad = jnp.sum(
        sent_grad.at[position]
        .get(mode="fill", fill_value=0)
        .reshape(row_count, 2, width)
        .astype(f32),
        axis=1,
    )
    shared_out_grad = jnp.einsum("isf,isd->fd", shared_low, moe_grad, preferred_element_type=f32)
    shared_out_bias_grad = jnp.sum(moe_rows_float, axis=0)
    shared_act_grad = jnp.einsum(
        "isd,fd->isf", moe_grad, shared_out_back, preferred_element_type=f32
    )
    shared_pre_grad = shared_gelu_back(shared_act_grad)[0].astype(b16)
    shared_in_grad = jnp.einsum("isd,isf->df", second, shared_pre_grad, preferred_element_type=f32)
    shared_in_bias_grad = jnp.sum(shared_pre_grad.astype(f32), axis=(0, 1))
    router_grad = jnp.einsum("rd,re->de", second_rows, logits_grad, preferred_element_type=f32)
    second_grad = jnp.einsum(
        "isf,df->isd", shared_pre_grad, shared_in_back, preferred_element_type=f32
    )
    side_grad = dispatch_rows_grad + jnp.einsum(
        "re,de->rd", logits_grad, router_back, preferred_element_type=f32
    )
    second_grad = second_grad + side_grad.reshape(image_count, length, width)
    resid_extra, shift_two_grad, scale_two_grad = second_back(second_grad)
    resid_grad = grad_out + resid_extra
    attended_grad = (pieces[2] * resid_grad).astype(b16)
    gate_one_grad = jnp.sum(resid_grad * attended, axis=1, keepdims=True)
    out_weight_grad = jnp.einsum("isd,ise->de", mixed, attended_grad, preferred_element_type=f32)
    out_bias_grad = jnp.sum(attended_grad.astype(f32), axis=(0, 1))
    mixed_grad = (
        jnp.einsum("ise,de->isd", attended_grad, out_back, preferred_element_type=f32)
        .astype(b16)
        .reshape(head_shape)
    )
    again_scores = (
        jnp.einsum("iqhc,ikhc->ihqk", query_heads, key_heads, preferred_element_type=f32) * scaling
    )
    probs_float = jnp.exp(again_scores - log_total)
    again_low = probs_float.astype(b16)
    probs_grad = jnp.einsum("iqhc,ikhc->ihqk", mixed_grad, value_heads, preferred_element_type=f32)
    values_grad = jnp.einsum(
        "ihqk,iqhc->ikhc", again_low, mixed_grad, preferred_element_type=f32
    ).astype(b16)
    scores_grad = (
        probs_float * (probs_grad - jnp.sum(probs_float * probs_grad, axis=-1, keepdims=True))
    ).astype(b16)
    query_grad = (
        jnp.einsum("ihqk,ikhc->iqhc", scores_grad, key_heads, preferred_element_type=f32) * scaling
    ).astype(b16)
    keys_grad = (
        jnp.einsum("ihqk,iqhc->ikhc", scores_grad, query_heads, preferred_element_type=f32)
        * scaling
    ).astype(b16)
    flat_shape = (image_count, length, width)
    projected_grad = jnp.concatenate(
        [
            query_grad.reshape(flat_shape),
            keys_grad.reshape(flat_shape),
            values_grad.reshape(flat_shape),
        ],
        axis=-1,
    )
    qkv_weight_grad = jnp.einsum("isd,ise->de", normed, projected_grad, preferred_element_type=f32)
    qv_bias_grad = jnp.stack(
        [
            jnp.sum(query_grad.astype(f32), axis=(0, 1)).reshape(width),
            jnp.sum(values_grad.astype(f32), axis=(0, 1)).reshape(width),
        ]
    )
    normed_grad = jnp.einsum("ise,de->isd", projected_grad, qkv_back, preferred_element_type=f32)
    token_extra, shift_one_grad, scale_one_grad = first_back(normed_grad)
    tokens_grad = resid_grad + token_extra
    modulation_grad = jnp.concatenate(
        [
            shift_one_grad,
            scale_one_grad,
            gate_one_grad,
            shift_two_grad,
            scale_two_grad,
            gate_two_grad,
        ],
        axis=-1,
    )[:, 0, :].astype(b16)
    ada_weight_grad = jnp.einsum("id,ie->de", cond_low, modulation_grad, preferred_element_type=f32)
    ada_bias_grad = jnp.sum(modulation_grad.astype(f32), axis=0)
    cond_act_grad = jnp.einsum("ie,de->id", modulation_grad, ada_back, preferred_element_type=f32)
    conditioning_grad = silu_back(cond_act_grad)[0]
    expert_sums = (
        lax.psum_scatter(
            expert_in_grad.astype(jnp.bfloat16), "dp", scatter_dimension=1, tiled=True
        ).astype(jnp.float32),
        lax.psum_scatter(
            expert_in_bias_grad.astype(jnp.bfloat16), "dp", scatter_dimension=1, tiled=True
        ).astype(jnp.float32),
        lax.psum_scatter(
            expert_out_grad.astype(jnp.bfloat16), "dp", scatter_dimension=1, tiled=True
        ).astype(jnp.float32),
        lax.psum_scatter(
            expert_out_bias_grad.astype(jnp.bfloat16), "dp", scatter_dimension=1, tiled=True
        ).astype(jnp.float32),
    )
    dense_parts = (
        lax.psum_scatter(
            ada_weight_grad.astype(jnp.bfloat16), "dp", scatter_dimension=0, tiled=True
        ).astype(jnp.float32),
        lax.psum_scatter(
            ada_bias_grad.astype(jnp.bfloat16), "dp", scatter_dimension=0, tiled=True
        ).astype(jnp.float32),
        lax.psum_scatter(
            qkv_weight_grad.astype(jnp.bfloat16), "dp", scatter_dimension=0, tiled=True
        ).astype(jnp.float32),
        lax.psum_scatter(
            qv_bias_grad.astype(jnp.bfloat16), "dp", scatter_dimension=1, tiled=True
        ).astype(jnp.float32),
        lax.psum_scatter(
            out_weight_grad.astype(jnp.bfloat16), "dp", scatter_dimension=0, tiled=True
        ).astype(jnp.float32),
        lax.psum_scatter(
            out_bias_grad.astype(jnp.bfloat16), "dp", scatter_dimension=0, tiled=True
        ).astype(jnp.float32),
        lax.psum_scatter(
            shared_in_grad.astype(jnp.bfloat16), "dp", scatter_dimension=0, tiled=True
        ).astype(jnp.float32),
        lax.psum_scatter(
            shared_in_bias_grad.astype(jnp.bfloat16), "dp", scatter_dimension=0, tiled=True
        ).astype(jnp.float32),
        lax.psum_scatter(
            shared_out_grad.astype(jnp.bfloat16), "dp", scatter_dimension=0, tiled=True
        ).astype(jnp.float32),
        lax.psum_scatter(
            shared_out_bias_grad.astype(jnp.bfloat16), "dp", scatter_dimension=0, tiled=True
        ).astype(jnp.float32),
        lax.psum_scatter(
            router_grad.astype(jnp.bfloat16), "dp", scatter_dimension=0, tiled=True
        ).astype(jnp.float32),
    )
    dense_sums = lax.psum(
        (
            dense_parts[0],
            dense_parts[1],
            dense_parts[2],
            dense_parts[3],
            dense_parts[4],
            dense_parts[5],
            dense_parts[6],
            dense_parts[7],
            dense_parts[8],
            dense_parts[9],
            dense_parts[10],
        ),
        "expert",
    )
    return (
        output,
        tokens_grad,
        conditioning_grad,
        dense_sums[0],
        dense_sums[1],
        dense_sums[2],
        dense_sums[3],
        dense_sums[4],
        dense_sums[5],
        dense_sums[6],
        dense_sums[7],
        dense_sums[8],
        dense_sums[9],
        dense_sums[10],
        expert_sums[0],
        expert_sums[1],
        expert_sums[2],
        expert_sums[3],
    )


def solution(mesh):
    in_specs = (
        P(("dp", "expert"), None, None),
        P(("dp", "expert"), None),
        P(("dp", "expert"), None, None),
        P(("dp", "expert"), None, None),
        P("dp", None),
        P("dp"),
        P("dp", None),
        P(None, "dp"),
        P("dp", None),
        P("dp"),
        P("dp", None),
        P("dp"),
        P("dp", None),
        P("dp"),
        P("dp", None),
        P("expert", None, None),
        P("expert", None),
        P("expert", None, None),
        P("expert", None),
    )
    out_specs = (
        P(("dp", "expert"), None, None),
        P(("dp", "expert"), None, None),
        P(("dp", "expert"), None),
        P("dp", None),
        P("dp"),
        P("dp", None),
        P(None, "dp"),
        P("dp", None),
        P("dp"),
        P("dp", None),
        P("dp"),
        P("dp", None),
        P("dp"),
        P("dp", None),
        P("expert", "dp", None),
        P("expert", "dp"),
        P("expert", "dp", None),
        P("expert", "dp"),
    )
    body = on_device
    if dict(mesh.shape) == {"dp": NZ * NX, "expert": 4}:
        body = on_block
    return jax.shard_map(
        body, mesh=mesh, in_specs=in_specs, out_specs=out_specs, check_vma=False
    )
```

```python
import functools

import jax
import jax.numpy as jnp
from jax import lax
from jax.experimental import pallas as pl
from jax.experimental.pallas import tpu as pltpu
from jax.sharding import PartitionSpec as P

HEADS = 12
HEAD_DIM = 64
E = 8
CAP = 80
MESH = pl.DeviceIdType.MESH
F32 = jnp.float32
B16 = jnp.bfloat16
VMEM_LIMIT = 60 * 1024 * 1024
SCALE = HEAD_DIM ** (-0.5)
GELU_C = 0.7978845608028654
NZ, NX = 4, 2


def coords():
    dp = lax.axis_index("dp")
    ex = lax.axis_index("expert")
    return lax.div(dp, NX), lax.rem(dp, NX), lax.div(ex, 2), lax.rem(ex, 2)


def dev(z, x, y, c):
    return (NX * z + x, 2 * y + c)


def dot(a, b):
    return jnp.dot(a, b, preferred_element_type=F32)


def dot_nt(a, b):
    return lax.dot_general(a, b, (((1,), (1,)), ((), ())), preferred_element_type=F32)


def dot_tn(a, b):
    return lax.dot_general(a, b, (((0,), (0,)), ((), ())), preferred_element_type=F32)


def gelu(v):
    return v * (0.5 + 0.5 * jnp.tanh(v * (GELU_C + GELU_C * 0.044715 * (v * v))))


def gelu_parts(v):
    v2 = v * v
    t = jnp.tanh(GELU_C * v * (1.0 + 0.044715 * v2))
    h = 0.5 * (1.0 + t)
    return v * h, h + 0.5 * v * (1.0 - t * t) * (GELU_C * (1.0 + 0.134145 * v2))


def norm_parts(v):
    centred = v - jnp.mean(v, axis=-1, keepdims=True)
    r = lax.rsqrt(jnp.mean(centred * centred, axis=-1, keepdims=True) + 1e-06)
    return centred * r, r


def norm_back(u, n, r):
    return r * (
        u - jnp.mean(u, axis=-1, keepdims=True) - n * jnp.mean(u * n, axis=-1, keepdims=True)
    )


def remote(src, dst, send, recv, to):
    return pltpu.make_async_remote_copy(
        src_ref=src,
        dst_ref=dst,
        send_sem=send,
        recv_sem=recv,
        device_id=to,
        device_id_type=MESH,
    )


def greet(barrier, to):
    pl.semaphore_signal(barrier, inc=1, device_id=to, device_id_type=MESH)


def params(collective_id=None):
    if collective_id is None:
        return pltpu.CompilerParams(vmem_limit_bytes=VMEM_LIMIT)
    return pltpu.CompilerParams(
        vmem_limit_bytes=VMEM_LIMIT, collective_id=collective_id, has_side_effects=True
    )


VM = pl.BlockSpec(memory_space=pltpu.VMEM)
HB = pl.BlockSpec(memory_space=pl.ANY)


def sds(shape, dtype):
    return jax.ShapeDtypeStruct(shape, dtype)


class Gather:
    def __init__(self, shards, fulls, splits, sems):
        self.z, self.x, self.y, self.c = coords()
        self.mats = list(zip(shards, fulls, splits))
        (self.zs, self.zr, self.xs, self.xr, self.ys, self.yr, self.cs, self.cr, self.loc) = sems

    @staticmethod
    def semaphores(count):
        dma = pltpu.SemaphoreType.DMA
        return [
            dma((count, 2, NZ)),
            dma((count, NZ)),
            dma((count, NZ)),
            dma((count, NZ)),
            dma((count, NZ, NX)),
            dma((count, NZ, NX)),
            dma((count, NZ, NX, 2)),
            dma((count, NZ, NX, 2)),
            dma((count,)),
        ]

    def region(self, m, zb, xb, yh, ch):
        shard, full, split = self.mats[m]
        rows, width = shard.shape[0], shard.shape[1] // 2
        start = (NX * zb + xb) * rows
        if split:
            rows = rows // 2
            start = start + yh * rows
        return full.at[
            pl.ds(pl.multiple_of(start, 16), rows), pl.ds(pl.multiple_of(ch * width, 128), width)
        ]

    def own(self, m):
        shard, full, split = self.mats[m]
        rows, width = shard.shape[0], shard.shape[1] // 2
        start = 0
        if split:
            rows = rows // 2
            start = self.y * rows
        return shard.at[
            pl.ds(pl.multiple_of(start, 16), rows),
            pl.ds(pl.multiple_of(self.c * width, 128), width),
        ]

    def zcopy(self, m, zb, side, mine=False):
        here = self.region(m, zb, self.x, self.y, self.c)
        step = 1 if side else -1
        return remote(
            self.own(m) if mine else here,
            here,
            self.zs.at[m, side, zb],
            self.zr.at[m, zb],
            dev(lax.rem(self.z + step + NZ, NZ), self.x, self.y, self.c),
        )

    def xcopy(self, m, zb, mine=False, xb=None):
        here = self.region(m, zb, self.x if xb is None else xb, self.y, self.c)
        return remote(
            self.own(m) if mine else here,
            here,
            self.xs.at[m, zb],
            self.xr.at[m, zb],
            dev(self.z, 1 - self.x, self.y, self.c),
        )

    def ycopy(self, m, zb, xb, yh=None):
        here = self.region(m, zb, xb, self.y if yh is None else yh, self.c)
        return remote(
            here,
            here,
            self.ys.at[m, zb, xb],
            self.yr.at[m, zb, xb],
            dev(self.z, self.x, 1 - self.y, self.c),
        )

    def ccopy(self, m, zb, xb, yh, ch=None):
        here = self.region(m, zb, xb, yh, self.c if ch is None else ch)
        slot = yh if self.mats[m][2] else 0
        return remote(
            here,
            here,
            self.cs.at[m, zb, xb, slot],
            self.cr.at[m, zb, xb, slot],
            dev(self.z, self.x, self.y, 1 - self.c),
        )

    def local(self, m):
        shard, full, _ = self.mats[m]
        rows = shard.shape[0]
        start = (NX * self.z + self.x) * rows
        return pltpu.make_async_copy(
            shard, full.at[pl.ds(pl.multiple_of(start, 16), rows), :], self.loc.at[m]
        )

    def blocks(self, step):
        if step == 0:
            return [(self.z, None, None)]
        return [
            (self.z - step, self.z - step >= 0, 1),
            (self.z + step, self.z + step < NZ, 0),
        ]

    def more(self, side):
        return self.z + 1 < NZ if side else self.z - 1 >= 0

    def begin(self, m):
        for side in (1, 0):

            @pl.when(self.more(side))
            def _():
                self.zcopy(m, self.z, side, True).start()

        self.xcopy(m, self.z, True).start()
        self.local(m).start()

    def spread(self, m, zb, xb):
        if self.mats[m][2]:
            self.ycopy(m, zb, xb).start()
        self.ccopy(m, zb, xb, self.y).start()

    def take_z(self, m, step):
        for zb, exists, side in self.blocks(step):

            @pl.when(exists)
            def _():
                self.zcopy(m, zb, side).wait_recv()
                if step < NZ - 1:

                    @pl.when(self.more(side))
                    def _():
                        self.zcopy(m, zb, side).start()

                self.xcopy(m, zb).start()
                self.spread(m, zb, self.x)

    def take_x(self, m, step):
        for zb, exists, _ in self.blocks(step):

            def body():
                self.xcopy(m, zb, False, 1 - self.x).wait_recv()
                self.spread(m, zb, 1 - self.x)

            body() if exists is None else pl.when(exists)(body)

    def others(self, m, step, action):
        for zb, exists, _ in self.blocks(step):
            for xb in (self.x, 1 - self.x) if step else (1 - self.x,):
                body = functools.partial(action, m, zb, xb)
                body() if exists is None else pl.when(exists)(body)

    def take_y(self, m, step):
        if not self.mats[m][2]:
            return

        def action(m, zb, xb):
            self.ycopy(m, zb, xb, 1 - self.y).wait_recv()
            self.ccopy(m, zb, xb, 1 - self.y).start()

        self.others(m, step, action)

    def finish(self, m):
        def action(m, zb, xb):
            for yh in (self.y, 1 - self.y) if self.mats[m][2] else (self.y,):
                self.ccopy(m, zb, xb, yh, 1 - self.c).wait_recv()
                self.ccopy(m, zb, xb, yh).wait_send()
            if self.mats[m][2]:
                self.ycopy(m, zb, xb).wait_send()

        for step in range(NZ):
            self.others(m, step, action)
        for side in (1, 0):

            @pl.when(self.more(side))
            def _():
                self.zcopy(m, self.z, side, True).wait_send()

        for step in range(1, NZ):
            for zb, exists, side in self.blocks(step):

                @pl.when(exists)
                def _():
                    self.xcopy(m, zb).wait_send()
                    if step < NZ - 1:

                        @pl.when(self.more(side))
                        def _():
                            self.zcopy(m, zb, side).wait_send()

        self.xcopy(m, self.z, True).wait_send()
        self.local(m).wait()


class Column:
    def __init__(self, shard, column, other, send, recv, local, xsend, xrecv):
        self.z, self.x, self.y, self.c = coords()
        self.shard, self.column, self.other = shard, column, other
        self.send, self.recv, self.local, self.xsend, self.xrecv = send, recv, local, xsend, xrecv

    @staticmethod
    def semaphores():
        dma = pltpu.SemaphoreType.DMA
        return [dma((2, NZ)), dma((NZ,)), dma((1,)), dma((NZ,)), dma((NZ,))]

    def block(self, zb):
        rows = self.shard.shape[0]
        return self.column.at[pl.ds(pl.multiple_of(zb * rows, 16), rows), :]

    def own(self):
        width = self.shard.shape[1] // 2
        return self.shard.at[:, pl.ds(pl.multiple_of(self.c * width, 128), width)]

    def copy(self, zb, side, mine=False):
        here = self.block(zb)
        to = lax.rem(self.z + (1 if side else NZ - 1), NZ)
        return remote(
            self.own() if mine else here,
            here,
            self.send.at[side, zb],
            self.recv.at[zb],
            dev(to, self.x, self.y, self.c),
        )

    def xcopy(self, zb, mine=False):
        rows, width = self.shard.shape[0], self.shard.shape[1] // 2
        part = rows // 2
        start = pl.multiple_of(self.y * part, 16)
        if mine:
            source = self.shard.at[
                pl.ds(start, part), pl.ds(pl.multiple_of(self.c * width, 128), width)
            ]
        else:
            source = self.column.at[pl.ds(pl.multiple_of(zb * rows + start, 16), part), :]
        return remote(
            source,
            self.other.at[pl.ds(pl.multiple_of(zb * part, 16), part), :],
            self.xsend.at[zb],
            self.xrecv.at[zb],
            dev(self.z, 1 - self.x, self.y, self.c),
        )

    def keep(self):
        return pltpu.make_async_copy(self.own(), self.block(self.z), self.local.at[0])

    def more(self, side):
        return self.z + 1 < NZ if side else self.z - 1 >= 0

    def blocks(self, step):
        return [(self.z - step, self.z - step >= 0, 1), (self.z + step, self.z + step < NZ, 0)]

    def begin(self):
        for side in (1, 0):

            @pl.when(self.more(side))
            def _():
                self.copy(self.z, side, True).start()

        self.keep().start()
        self.xcopy(self.z, True).start()

    def take(self, step):
        for zb, exists, side in self.blocks(step):

            @pl.when(exists)
            def _():
                self.copy(zb, side).wait_recv()
                if step < NZ - 1:

                    @pl.when(self.more(side))
                    def _():
                        self.copy(zb, side).start()

    def push(self, step):
        for zb, exists, _ in self.blocks(step):

            @pl.when(exists)
            def _():
                self.xcopy(zb).start()

    def finish(self):
        for side in (1, 0):

            @pl.when(self.more(side))
            def _():
                self.copy(self.z, side, True).wait_send()

        for step in range(1, NZ - 1):
            for zb, exists, side in self.blocks(step):

                @pl.when(jnp.logical_and(exists, self.more(side)))
                def _():
                    self.copy(zb, side).wait_send()

        self.keep().wait()
        for zb in range(NZ):
            self.xcopy(zb).wait_recv()
            self.xcopy(zb).wait_send()


class Spread:
    def __init__(self, column, other, full, ys, yr, cs, cr, local):
        self.z, self.x, self.y, self.c = coords()
        self.column, self.other, self.full, self.local = column, other, full, local
        self.ys, self.yr, self.cs, self.cr = ys, yr, cs, cr

    @staticmethod
    def semaphores():
        dma = pltpu.SemaphoreType.DMA
        return [dma((NZ,))] * 2 + [dma((3, NZ))] * 2 + [dma((2, NZ))]

    def cols(self, c):
        width = self.full.shape[3] // 2
        return pl.ds(pl.multiple_of(c * width, 128), width)

    def half(self, y):
        rows = self.full.shape[2] // 2
        return pl.ds(pl.multiple_of(y * rows, 16), rows)

    def source(self, kind, zb):
        if kind == 0:
            rows = self.full.shape[2]
            return self.column.at[zb * rows : (zb + 1) * rows, :]
        rows = self.full.shape[2] // 2
        return self.other.at[zb * rows : (zb + 1) * rows, :]

    def place(self, kind, zb, c):
        if kind == 0:
            return self.full.at[zb, self.x, :, self.cols(c)]
        return self.full.at[zb, 1 - self.x, self.half(self.y if kind == 1 else 1 - self.y), self.cols(c)]

    def ycopy(self, zb, came=False):
        return remote(
            self.source(1, zb), self.place(2 if came else 1, zb, self.c), self.ys.at[zb], self.yr.at[zb],
            dev(self.z, self.x, 1 - self.y, self.c),
        )

    def ccopy(self, kind, zb, came=False):
        at = self.place(kind, zb, 1 - self.c if came else self.c)
        return remote(
            at if kind == 2 else self.source(kind, zb), at, self.cs.at[kind, zb], self.cr.at[kind, zb],
            dev(self.z, self.x, self.y, 1 - self.c),
        )

    def keep(self, kind, zb):
        return pltpu.make_async_copy(
            self.source(kind, zb), self.place(kind, zb, self.c), self.local.at[kind, zb]
        )

    def begin(self):
        for zb in range(NZ):
            self.ycopy(zb).start()

    def near(self):
        for zb in range(NZ):
            for kind in range(2):
                self.ccopy(kind, zb).start()
                self.keep(kind, zb).start()

    def take_y(self):
        for zb in range(NZ):
            self.ycopy(zb, True).wait_recv()
            self.ccopy(2, zb).start()

    def finish(self):
        for zb in range(NZ):
            for kind in range(3):
                self.ccopy(kind, zb, True).wait_recv()
            for kind in range(2):
                self.keep(kind, zb).wait()

    def close(self):
        for zb in range(NZ):
            self.ycopy(zb).wait_send()
            for kind in range(3):
                self.ccopy(kind, zb).wait_send()


def choose_rows(place, slots):
    return place == lax.broadcasted_iota(jnp.int32, (place.shape[0], slots), 1)


def plane_peer(k):
    z, x, y, c = coords()
    xt = 1 - x if k & 1 else x
    ct = 1 - c if k & 2 else c
    yt = 1 - y if k & 4 else y
    return dev(z, xt, yt, ct), 4 * yt + 2 * ct + xt


def plane_rank():
    _, x, y, c = coords()
    return 4 * y + 2 * c + x


def slot_rows(ref, rank):
    return ref.at[pl.ds(pl.multiple_of(rank * CAP, 16), CAP), :]


class PlaneExchange:
    ORDER = (7, 5, 6, 4, 3, 1, 2)

    def __init__(self, source, target, send, recv):
        self.source, self.target, self.send, self.recv = source, target, send, recv

    def copy(self, k, into=None):
        peer, other = plane_peer(k)
        return remote(
            slot_rows(self.source, other),
            slot_rows(self.target, plane_rank() if into is None else other),
            self.send.at[k],
            self.recv.at[k],
            peer,
        )

    def start(self):
        for k in self.ORDER:
            self.copy(k).start()
        mine = pl.ds(pl.multiple_of(plane_rank() * CAP, 16), CAP)
        self.target[mine, :] = self.source[mine, :]

    def wait_in(self):
        for k in self.ORDER:
            self.copy(k, True).wait_recv()

    def wait_out(self):
        for k in self.ORDER:
            self.copy(k).wait_send()


CHUNK = 512


def lead_kernel(
    tok, cot, routes, cond, ada, adab, qvb, outb, soutb, sinb_s, router_s, bin_r, bout_r,
    qkv_s, out_s, sin_s, sout_s, win_h, wout_h,
    normed_o, proj_o, lsum_o, mixed_o, att_o, resid_o, second_o, gates_o, place_o, mod_o, bias_o, sinb_o, rt_o,
    condt_o, res_o, bgr_o, ebias, qkv_o, outw_o, sin_o, sout_o, sin_x, sout_x, dwin_o, dwout_o,
    pack, packs, sent, got, qkv, outw, sbuf, gbuf, rows, grads, far_rows, far_grads, win, wout, dwin, dwout,
    lows, pres, acc, back,
    s1, r1, s2, r2, ds0, dr0, ds1, dr1, wsem, osem, fsem, *gsems,
):
    z, x, y, c = coords()
    dp, ex = lax.axis_index("dp"), lax.axis_index("expert")
    n = NZ * NX
    length, width = tok.shape
    hidden = win.shape[1]
    part = width // n
    per = width // 128
    lead = Gather((qkv_s, out_s), (qkv, outw), (True, False), gsems[:-10])
    later = (
        Column(sin_s, sin_o, sin_x, *gsems[-10:-5]),
        Column(sout_s, sout_o, sout_x, *gsems[-5:]),
    )

    loads = [
        pltpu.make_async_copy(win_h.at[x], win, wsem.at[0]),
        pltpu.make_async_copy(wout_h.at[x], wout, wsem.at[1]),
    ]

    def peers(action):
        for p in range(n):

            @pl.when(p != dp)
            def _():
                action(p)

    barrier = pltpu.get_barrier_semaphore()
    peers(lambda p: greet(barrier, (p, ex)))
    for k in range(2, E):
        greet(barrier, plane_peer(k)[0])

    pack[...] = jnp.zeros_like(pack)
    pack[0:2, 0:part] = qvb[...].astype(F32)
    pack[2:3, 0:part] = outb[...].astype(F32)
    pack[3:4, 0:part] = soutb[...].astype(F32)
    for j in range(hidden // n // 128):
        pack[4 + j : 5 + j, :] = sinb_s[:, 128 * j : 128 * (j + 1)].astype(F32)
    long = adab.shape[1]
    for j in range(-(-long // 128)):
        size = min(128, long - 128 * j)
        pack[8 + j : 9 + j, 0:size] = adab[:, 128 * j : 128 * j + size].astype(F32)
    pack[16:24, 0:part] = router_s[...].astype(F32)
    cv = cond[...].astype(F32)
    cond_low = (cv / (1.0 + jnp.exp(-cv))).astype(B16).astype(F32)
    for p in range(n):
        pack[24 + p : 25 + p, 0:part] = cond_low[:, part * p : part * (p + 1)]
    condt_o[...] = jnp.zeros_like(condt_o)
    for j in range(per):
        condt_o[j : j + 1, :] = cond_low[:, 128 * j : 128 * (j + 1)]

    pl.semaphore_wait(barrier, n - 1 + E - 2)

    def first(p, at):
        return remote(pack, packs.at[at], s1.at[p], r1.at[at], (p, ex))

    def second_hop(p, at):
        return remote(sent.at[p], got.at[at], s2.at[p], r2.at[at], (p, ex))

    peers(lambda p: first(p, dp).start())
    lead.begin(0)
    lead.begin(1)
    for load in loads:
        load.start()
    packs[dp] = pack[...]
    peers(lambda p: first(p, p).wait_recv())
    cond_rows = jnp.concatenate([packs[p, pl.ds(24 + dp, 1), :] for p in range(n)], axis=0)
    partial = dot(cond_rows[:, :part].astype(B16), ada[...])
    for j in range(partial.shape[1] // 128):
        sent[:, j, :] = partial[:, 128 * j : 128 * (j + 1)]
    peers(lambda p: second_hop(p, dp).start())
    got[dp] = sent[dp]

    both_mats = (0, 1)

    def step_of(plan, step):
        for m in both_mats:
            if step:
                plan.take_z(m, step)
            plan.take_x(m, step)
        if step:
            for m in both_mats:
                plan.take_y(m, step - 1)

    for step in range(NZ):
        step_of(lead, step)

    for column in later:
        column.begin()

    bias_o[...] = jnp.zeros_like(bias_o)
    for p in range(n):
        bias_o[0:4, part * p : part * (p + 1)] = packs[p, 0:4, 0:part]
        rt_o[:, part * p : part * (p + 1)] = packs[p, 16:24, 0:part]
        for j in range(hidden // n // 128):
            at = hidden // n * p + 128 * j
            sinb_o[:, at : at + 128] = packs[p, 4 + j : 5 + j, :]
    peers(lambda p: second_hop(p, p).wait_recv())
    total = got[0]
    for p in range(1, n):
        total = total + got[p]
    mod_o[...] = jnp.zeros_like(mod_o)
    for i in range(6):
        for b in range(per):
            mod_o[i : i + 1, 128 * b : 128 * (b + 1)] = total[per * i + b : per * i + b + 1, :]
    unit = 64
    for p in range(n):
        for u in range(long // unit):
            at = long * p + unit * u
            i, b = at // width, at % width
            mod_o[i : i + 1, b : b + unit] += packs[
                p, 8 + unit * u // 128 : 9 + unit * u // 128, unit * u % 128 : unit * u % 128 + unit
            ]

    mod = mod_o[...]
    source = tok[...].astype(F32)
    n1, _ = norm_parts(source)
    normed = (n1 * (1.0 + mod[1:2]) + mod[0:1]).astype(B16)
    normed_o[...] = normed
    for m in both_mats:
        lead.take_y(m, NZ - 1)
    for m in both_mats:
        lead.finish(m)
    keep = [
        pltpu.make_async_copy(qkv, qkv_o, wsem.at[2]),
        pltpu.make_async_copy(outw, outw_o, wsem.at[3]),
    ]
    for copy in keep:
        copy.start()

    for k in range(3):
        part_k = dot(normed, qkv[:, k * width : (k + 1) * width])
        if k != 1:
            part_k = part_k + bias_o[k // 2 : k // 2 + 1, :]
        proj_o[:, k * width : (k + 1) * width] = part_k.astype(B16)
    lane = lax.broadcasted_iota(jnp.int32, (length, 128), 1)
    low_lane = lane < HEAD_DIM
    lsum = jnp.zeros((length, 128), F32)
    for p in range(HEADS // 2):
        q2 = proj_o[:, 128 * p : 128 * (p + 1)]
        k2 = proj_o[:, width + 128 * p : width + 128 * (p + 1)]
        v2 = proj_o[:, 2 * width + 128 * p : 2 * width + 128 * (p + 1)]
        outs = []
        for h in range(2):
            mine = low_lane if h == 0 else jnp.logical_not(low_lane)
            s = dot_nt(jnp.where(mine, q2, jnp.zeros_like(q2)), k2) * SCALE
            peak = jnp.max(s, axis=-1, keepdims=True)
            e = jnp.exp(s - peak)
            tot = jnp.sum(e, axis=-1, keepdims=True)
            lsum = jnp.where(lane == 2 * p + h, peak + jnp.log(tot), lsum)
            outs.append(dot((e / tot).astype(B16), v2))
        mixed_o[:, 128 * p : 128 * (p + 1)] = jnp.where(low_lane, outs[0], outs[1]).astype(B16)
    lsum_o[...] = lsum
    att = dot(mixed_o[...], outw[...]) + bias_o[2:3, :]
    att_o[...] = att
    resid = source + mod[2:3] * att
    resid_o[...] = resid
    n2, _ = norm_parts(resid)
    second = (n2 * (1.0 + mod[4:5]) + mod[3:4]).astype(B16)
    second_o[...] = second

    lane8 = lax.broadcasted_iota(jnp.int32, (length, E), 1)
    two = (
        lax.broadcasted_iota(jnp.int32, (2, 128), 0) == lax.broadcasted_iota(jnp.int32, (2, 128), 1)
    )
    route_cols = dot_tn(
        routes[...].astype(F32).astype(B16), jnp.where(two, 1.0, 0.0).astype(B16)
    ).astype(jnp.int32)
    route = [route_cols[:, k : k + 1] for k in range(2)]
    picks = [(r == lane8) for r in route]
    both = jnp.where(picks[0], 1.0, 0.0) + jnp.where(picks[1], 1.0, 0.0)
    earlier = (
        lax.broadcasted_iota(jnp.int32, (length, length), 1)
        < lax.broadcasted_iota(jnp.int32, (length, length), 0)
    )
    rank = dot(jnp.where(earlier, 1.0, 0.0).astype(B16), both.astype(B16))
    places = []
    for k in range(2):
        slot = jnp.sum(jnp.where(picks[k], rank, 0.0), axis=-1, keepdims=True).astype(jnp.int32)
        places.append(jnp.where(slot < CAP, route[k] * CAP + slot, -1))
    place_o[...] = jnp.where(
        lane == 0,
        places[0],
        jnp.where(lane == 1, places[1], jnp.where(lane == 2, route[0], route[1])),
    )
    maps = [jnp.where(choose_rows(v, E * CAP), 1.0, 0.0) for v in places]
    sbuf[...] = dot_tn((maps[0] + maps[1]).astype(B16), second).astype(B16)
    give_rows = PlaneExchange(sbuf, rows, ds0, dr0)
    give_rows.start()
    logits = dot_nt(second, rt_o[...].astype(B16))
    chosen = [jnp.sum(jnp.where(pick, logits, 0.0), axis=-1, keepdims=True) for pick in picks]
    top = jnp.maximum(chosen[0], chosen[1])
    e2 = [jnp.exp(v - top) for v in chosen]
    gates = [v / (e2[0] + e2[1]) for v in e2]
    gates_o[...] = jnp.where(lane == 0, gates[0], jnp.where(lane == 1, gates[1], 0.0))
    moe_grad = (mod[5:6] * cot[...].astype(F32)).astype(B16).astype(F32)
    pair = [(g * moe_grad).astype(B16) for g in gates]
    gbuf[...] = (
        dot_tn(maps[0].astype(B16), pair[0]) + dot_tn(maps[1].astype(B16), pair[1])
    ).astype(B16)
    give_grads = PlaneExchange(gbuf, grads, ds1, dr1)
    give_grads.start()
    for column in later:
        column.take(1)

    first_x = x == 0
    acc[...] = jnp.zeros_like(acc) + jnp.where(first_x, bout_r[0:1, :], bout_r[1:2, :]).astype(F32)
    for load in loads:
        load.wait()
    for column in later:
        column.take(2)
    give_rows.wait_in()

    end = jnp.logical_or(z == 0, z == NZ - 1)
    inner = jnp.logical_not(end)
    partner = dev(z + 1 - 2 * lax.rem(z, 2), x, y, c)

    def far_copy(i):
        source, target = ((rows, far_rows), (grads, far_grads))[i]
        return remote(source, target, fsem.at[0, i], fsem.at[1, i], partner)

    pl.when(end)(lambda: far_copy(0).start())
    for column in later:
        column.push(1)

    def span(f):
        return pl.ds(pl.multiple_of(f * CHUNK, 128), CHUNK)

    def put_in(f):
        return pltpu.make_async_copy(dwin.at[:, span(f)], dwin_o.at[:, span(f)], osem.at[1, f])

    def put_out(f):
        return pltpu.make_async_copy(dwout.at[span(f), :], dwout_o.at[span(f), :], osem.at[0, f])

    def bias_of(cols):
        return jnp.where(first_x, bin_r[0:1, cols], bin_r[1:2, cols]).astype(F32)

    def forward(f, carry):
        cols = span(f)
        pre = dot(rows[...], win[:, cols]) + bias_of(cols)
        pres[:, cols] = pre
        low = gelu(pre).astype(B16)
        lows[:, cols] = low
        acc[...] += dot(low, wout[cols, :])
        return carry

    count = hidden // CHUNK
    lax.fori_loop(0, count, forward, 0)
    res_o[...] = acc[...].astype(B16)
    for column in later:
        column.push(2)
        column.take(3)
        column.push(3)
    give_grads.wait_in()
    pl.when(end)(lambda: far_copy(1).start())
    back[...] = jnp.zeros_like(back)
    ebias[...] = jnp.zeros_like(ebias)
    column_sum = jnp.sum(grads[...].astype(F32), axis=0, keepdims=True)
    for j in range(per):
        at = hidden // 128 + j
        ebias[at : at + 1, :] = column_sum[:, 128 * j : 128 * (j + 1)]

    def backward(f, carry):
        cols = span(f)
        pre = (dot_nt(grads[...], wout[cols, :]) * gelu_parts(pres[:, cols])[1]).astype(B16)
        back[...] += dot_nt(pre, win[:, cols])
        col = jnp.sum(pre.astype(F32), axis=0, keepdims=True)
        for j in range(CHUNK // 128):
            ebias[pl.ds(f * (CHUNK // 128) + j, 1), :] = col[:, 128 * j : 128 * (j + 1)]

        @pl.when(inner)
        def _():
            dwout[cols, :] = dot_tn(lows[:, cols], grads[...]).astype(B16)
            dwin[:, cols] = dot_tn(rows[...], pre).astype(B16)

        return carry

    lax.fori_loop(0, count, backward, 0)
    bgr_o[...] = back[...].astype(B16)

    def far(f, carry):
        cols = span(f)
        data, grad = far_rows[...], far_grads[...]
        act, slope = gelu_parts(dot(data, win[:, cols]) + bias_of(cols))
        pre = (dot_nt(grad, wout[cols, :]) * slope).astype(B16)
        dwout[cols, :] = (dwout[cols, :].astype(F32) + dot_tn(act.astype(B16), grad)).astype(B16)
        put_out(f).start()
        dwin[:, cols] = (dwin[:, cols].astype(F32) + dot_tn(data, pre)).astype(B16)
        put_in(f).start()
        return carry

    @pl.when(inner)
    def _():
        far_copy(0).wait_recv()
        far_copy(1).wait_recv()
        lax.fori_loop(0, count, far, 0)

    for column in later:
        column.finish()
    for exchange in (give_rows, give_grads):
        exchange.wait_out()
    peers(lambda p: first(p, p).wait_send())
    peers(lambda p: second_hop(p, p).wait_send())
    for copy in keep:
        copy.wait()

    @pl.when(end)
    def _():
        far_copy(0).wait_send()
        far_copy(1).wait_send()

    @pl.when(inner)
    def _():
        for f in range(count):
            put_out(f).wait()
            put_in(f).wait()


def lead_part(tok, cot, route, cond, ada, adab, qvb, outb, soutb, sinb, router, bin_r, bout_r, shards, win, wout):
    n = NZ * NX
    length, width = tok.shape
    hidden = win.shape[2]
    slots = E * CAP
    dma = pltpu.SemaphoreType.DMA
    vm = pltpu.VMEM
    tiles = (ada.shape[1] // 128 + 7) // 8 * 8
    wide = [sds((n * s.shape[0], s.shape[1]), B16) for s in shards[:2]]
    wide += [sds((NZ * s.shape[0], s.shape[1] // 2), B16) for s in shards[2:]]
    wide += [sds((NZ * s.shape[0] // 2, s.shape[1] // 2), B16) for s in shards[2:]]
    outs = [
        sds((length, width), B16),
        sds((length, 3 * width), B16),
        sds((length, 128), F32),
        sds((length, width), B16),
        sds((length, width), F32),
        sds((length, width), F32),
        sds((length, width), B16),
        sds((length, 128), F32),
        sds((length, 128), jnp.int32),
        sds((8, width), F32),
        sds((8, width), F32),
        sds((1, hidden), F32),
        sds((E, width), F32),
        sds((8, 128), F32),
        sds((slots, width), B16),
        sds((slots, width), B16),
        sds((32, 128), F32),
    ]
    far = wide + [sds((width, hidden), B16), sds((hidden, width), B16)]
    return pl.pallas_call(
        lead_kernel,
        out_shape=outs + far,
        in_specs=[VM] * 13 + [HB] * 6,
        out_specs=[VM] * len(outs) + [HB] * len(far),
        scratch_shapes=[
            vm((32, 128), F32),
            vm((n, 32, 128), F32),
            vm((n, tiles, 128), F32),
            vm((n, tiles, 128), F32),
            vm(wide[0].shape, B16),
            vm(wide[1].shape, B16),
            vm((slots, width), B16),
            vm((slots, width), B16),
            vm((slots, width), B16),
            vm((slots, width), B16),
            vm((slots, width), B16),
            vm((slots, width), B16),
            vm((width, hidden), B16),
            vm((hidden, width), B16),
            vm((width, hidden), B16),
            vm((hidden, width), B16),
            vm((slots, hidden), B16),
            vm((slots, hidden), F32),
            vm((slots, width), F32),
            vm((slots, width), F32),
            dma((n,)),
            dma((n,)),
            dma((n,)),
            dma((n,)),
        ]
        + [dma((E,))] * 4
        + [dma((4,)), dma((2, hidden // CHUNK)), dma((2, 2))]
        + Gather.semaphores(2)
        + Column.semaphores()
        + Column.semaphores(),
        compiler_params=params(1),
        name="front_and_expert",
    )(tok, cot, route, cond, ada, adab, qvb, outb, soutb, sinb, router, bin_r, bout_r, *shards, win, wout)


def middle_kernel(
    res, bgr, dwout, second_r, resid_r, att_r, cot, mod, sin_c, sout_c, sin_x, sout_x, sinb, bias, router, gates_r, place_r,
    mixed, outw,
    came_o, out_o, rgrad_o, mgrad_o, sin_half, sout_half, dout, drouter, vecs, mg2,
    dsin, dsout, hsem, msem, lows, slopes, ret, retg, shared, sgrad, sin, sout, send, recv, send2, recv2, *ssems,
):
    barrier = pltpu.get_barrier_semaphore()
    for k in range(1, E):
        greet(barrier, plane_peer(k)[0])
    z, x, y, c = coords()
    mate = NZ - 1 - z
    greet(barrier, dev(mate, x, y, c))
    pl.semaphore_wait(barrier, E)
    central = jnp.logical_and(z > 0, z < NZ - 1)

    def across(i):
        block = mate + 1 - 2 * lax.rem(mate, 2) if i == 0 else mate
        return remote(
            dwout.at[block], came_o.at[i], msem.at[0, i], msem.at[1, i], dev(mate, x, y, c)
        )

    @pl.when(central)
    def _():
        across(0).start()
        across(1).start()

    count = len(ssems) // 2
    spreads = (
        Spread(sin_c, sin_x, sin, *ssems[:count]),
        Spread(sout_c, sout_x, sout, *ssems[count:]),
    )
    for spread in spreads:
        spread.begin()
    gives = (PlaneExchange(res, ret, send, recv), PlaneExchange(bgr, retg, send2, recv2))
    for spread in spreads:
        spread.near()
    length, width = second_r.shape
    hidden = sin.shape[3]
    chunk = hidden // NZ
    second = second_r[...]
    grad_out = cot[...].astype(F32)
    moe_low = (mod[5:6] * grad_out).astype(B16)
    moe_grad = moe_low.astype(F32)
    shared[...] = jnp.zeros_like(shared) + bias[3:4, :]
    sgrad[...] = jnp.zeros_like(sgrad)
    vecs[...] = jnp.zeros_like(vecs)
    spreads[0].take_y()
    for give in gives:
        give.start()
    spreads[0].finish()

    def span(f):
        return pl.ds(pl.multiple_of(f * chunk, 128), chunk)

    def forward(f, carry):
        cols = span(f)
        w1 = sin[:, :, :, cols].reshape(width, chunk)
        act, slope = gelu_parts(dot(second, w1) + sinb[:, cols])
        lows[:, cols] = act.astype(B16)
        slopes[:, cols] = slope
        return carry

    lax.fori_loop(0, hidden // chunk, forward, 0)
    spreads[1].take_y()
    spreads[1].finish()

    def body(f, carry):
        cols = span(f)
        w1 = sin[:, :, :, cols].reshape(width, chunk)
        w2 = sout[f].reshape(chunk, width)
        low = lows[:, cols]
        shared[...] += dot(low, w2)
        pre = (dot_nt(moe_low, w2) * slopes[:, cols]).astype(B16)
        dsout[cols, :] = dot_tn(low, moe_low).astype(B16)
        dsin[:, cols] = dot_tn(second, pre).astype(B16)
        sgrad[...] += dot_nt(pre, w1)
        col = jnp.sum(pre.astype(F32), axis=0, keepdims=True)
        for j in range(chunk // 128):
            vecs[pl.ds(f * (chunk // 128) + j, 1), :] = col[:, 128 * j : 128 * (j + 1)]
        return carry

    lax.fori_loop(0, hidden // chunk, body, 0)
    halves = ((dsin, sin_half), (dsout, sout_half))

    def half_cols(i, core):
        size = halves[i][1].shape[1]
        return pl.ds(pl.multiple_of(core * size, 128), size)

    def half_copy(i):
        return remote(
            halves[i][0].at[:, half_cols(i, 1 - c)], halves[i][1], hsem.at[0, i], hsem.at[1, i],
            dev(z, x, y, 1 - c),
        )

    for i in range(2):
        half_copy(i).start()
    lane = lax.broadcasted_iota(jnp.int32, (length, E), 1)
    gates = [gates_r[:, k : k + 1] for k in range(2)]
    maps = [
        jnp.where(choose_rows(place_r[:, k : k + 1], E * CAP), 1.0, 0.0) for k in range(2)
    ]
    for give in gives:
        give.wait_in()
    back = ret[...]
    rows = [dot(m.astype(B16), back) for m in maps]
    moe = shared[...] + (gates[0] * rows[0] + gates[1] * rows[1])
    resid = resid_r[...]
    out_o[...] = (resid + mod[5:6] * moe).astype(B16)
    mg2[...] = jnp.zeros_like(mg2)
    mg2[5:6, :] = jnp.sum(grad_out * moe, axis=0, keepdims=True)
    ggrad = [jnp.sum(moe_grad * r, axis=-1, keepdims=True) for r in rows]
    inner = gates[0] * ggrad[0] + gates[1] * ggrad[1]
    lgrad = jnp.zeros((length, E), F32)
    for k in range(2):
        pick = place_r[:, 2 + k : 3 + k] == lane
        lgrad = lgrad + jnp.where(pick, gates[k] * (ggrad[k] - inner), 0.0)
    lgrad = lgrad.astype(B16)
    drouter[...] = dot_tn(lgrad, second)
    grad = (
        sgrad[...]
        + dot((maps[0] + maps[1]).astype(B16), retg[...])
        + dot(lgrad, router[...].astype(B16))
    )
    n2, r2 = norm_parts(resid)
    mg2[3:4, :] = jnp.sum(grad, axis=0, keepdims=True)
    mg2[4:5, :] = jnp.sum(grad * n2, axis=0, keepdims=True)
    rgrad = grad_out + norm_back(grad * (1.0 + mod[4:5]), n2, r2)
    rgrad_o[...] = rgrad
    agrad = (mod[2:3] * rgrad).astype(B16)
    mg2[2:3, :] = jnp.sum(rgrad * att_r[...], axis=0, keepdims=True)
    dout[...] = dot_tn(mixed[...], agrad).astype(B16)
    mgrad_o[...] = dot_nt(agrad, outw[...]).astype(B16)
    sums = [
        jnp.sum(moe_grad, axis=0, keepdims=True),
        jnp.sum(agrad.astype(F32), axis=0, keepdims=True),
    ]
    base = hidden // 128
    for i, row in enumerate(sums):
        for j in range(width // 128):
            at = base + i * (width // 128) + j
            vecs[at : at + 1, :] = row[:, 128 * j : 128 * (j + 1)]
    for i in range(2):
        half_copy(i).wait_recv()
        whole, part = halves[i]
        step = part.shape[0] // 16

        def add(j, carry):
            at = pl.ds(pl.multiple_of(j * step, 16), step)
            own = whole[at, half_cols(i, c)].astype(F32)
            part[at, :] = (part[at, :].astype(F32) + own).astype(B16)
            return carry

        lax.fori_loop(0, 16, add, 0)
        half_copy(i).wait_send()
    @pl.when(central)
    def _():
        across(0).wait()
        across(1).wait()

    for give in gives:
        give.wait_out()
    for spread in spreads:
        spread.close()


def middle(*args):
    res, dwout, second, sin = args[0], args[2], args[3], args[8]
    length, width = second.shape
    rows, hidden = res.shape[0], 2 * sin.shape[1]
    dma = pltpu.SemaphoreType.DMA
    return pl.pallas_call(
        middle_kernel,
        out_shape=[
            sds((2,) + dwout.shape[1:], B16),
            sds((length, width), B16),
            sds((length, width), F32),
            sds((length, width), B16),
            sds((width, hidden // 2), B16),
            sds((hidden, width // 2), B16),
            sds((width, width), B16),
            sds((E, width), F32),
            sds((40, 128), F32),
            sds((8, width), F32),
        ],
        in_specs=[VM] * 2 + [HB] + [VM] * 5 + [HB] * 4 + [VM] * 7,
        out_specs=[HB] + [VM] * 9,
        scratch_shapes=[
            pltpu.VMEM((width, hidden), B16),
            pltpu.VMEM((hidden, width), B16),
            dma((2, 2)),
            dma((2, 2)),
            pltpu.VMEM((length, hidden), B16),
            pltpu.VMEM((length, hidden), F32),
            pltpu.VMEM((rows, width), B16),
            pltpu.VMEM((rows, width), B16),
            pltpu.VMEM((length, width), F32),
            pltpu.VMEM((length, width), F32),
            pltpu.VMEM((NZ, NX, width // NZ // NX, hidden), B16),
            pltpu.VMEM((NZ, NX, hidden // NZ // NX, width), B16),
            dma((E,)),
            dma((E,)),
            dma((E,)),
            dma((E,)),
        ]
        + Spread.semaphores()
        + Spread.semaphores(),
        compiler_params=params(3),
        name="shared_expert_combine",
    )(*args)


def add_into(target, source, lead):
    count = 1
    for n in lead:
        count *= n

    def body(i, carry):
        at = []
        rest = i
        for n in reversed(lead):
            at.append(lax.rem(rest, n))
            rest = lax.div(rest, n)
        at = tuple(reversed(at))
        target[at] = (target[at].astype(F32) + source(at).astype(F32)).astype(B16)
        return carry

    lax.fori_loop(0, count, body, 0)


class Piece:
    def __init__(self, spec, grad, out, bufs):
        self.z, self.x, self.y, self.c = coords()
        self.half, self.row, self.rows, self.col, self.width, self.y_first = spec
        self.grad, self.out = grad, out
        self.size = out.shape[-1] // 2
        if not self.half:
            self.cbuf, bufs = bufs[0], bufs[1:]
        self.ebuf, self.fbuf, self.zin, self.one, self.zsem = bufs

    @staticmethod
    def scratch(spec):
        half, _, rows, _, width, _ = spec
        vm = lambda *lead: pltpu.VMEM(lead + (rows, width), B16)
        dma = pltpu.SemaphoreType.DMA
        return ([] if half else [vm(NZ, NX, 2)]) + [
            vm(NZ, 2),
            vm(NZ),
            vm(NZ),
            dma((13,)),
            dma((2, NZ)),
        ]

    def cols(self, c):
        return pl.ds(pl.multiple_of(c * self.size + self.col, 128), self.width)

    def core_view(self, *lead):
        if not self.half:
            return self.cbuf.at[lead]
        inner = (slice(self.row, self.row + self.rows), slice(self.col, self.col + self.width))
        return self.grad.at[lead + inner]

    def core_value(self, *lead):
        if not self.half:
            return self.cbuf[lead]
        inner = (slice(self.row, self.row + self.rows), slice(self.col, self.col + self.width))
        return self.grad[lead + inner]

    def core_copy(self):
        return remote(
            self.grad.at[:, :, :, :, self.cols(1 - self.c)],
            self.cbuf,
            self.one.at[0],
            self.one.at[1],
            dev(self.z, self.x, self.y, 1 - self.c),
        )

    def to_x(self):
        return dev(self.z, 1 - self.x, self.y, self.c)

    def to_y(self):
        return dev(self.z, self.x, 1 - self.y, self.c)

    def copy1(self):
        every = slice(None)
        if self.y_first:
            source, to = self.core_view(every, every, 1 - self.y), self.to_y()
        else:
            source, to = self.core_view(every, 1 - self.x, every), self.to_x()
        return remote(source, self.ebuf, self.one.at[3], self.one.at[4], to)

    def copy2(self):
        if self.y_first:
            source, to = self.ebuf.at[:, 1 - self.x], self.to_x()
        else:
            source, to = self.ebuf.at[:, 1 - self.y], self.to_y()
        return remote(source, self.fbuf, self.one.at[5], self.one.at[6], to)

    def zcopy(self, zb, at):
        return remote(
            self.fbuf.at[zb],
            self.zin.at[at],
            self.zsem.at[0, zb],
            self.zsem.at[1, at],
            dev(zb, self.x, self.y, self.c),
        )

    def others(self, action):
        for zb in range(NZ):

            @pl.when(zb != self.z)
            def _():
                action(zb)

    def own(self):
        return self.fbuf.at[self.z]

    def place(self, y, c):
        return self.out.at[y, self.row : self.row + self.rows, self.cols(c)]

    def keep(self):
        return pltpu.make_async_copy(self.own(), self.place(self.y, self.c), self.one.at[7])

    def give_y(self, came=False):
        at = self.place(1 - self.y if came else self.y, self.c)
        return remote(self.own(), at, self.one.at[8], self.one.at[9], self.to_y())

    def give_c(self, came=False):
        at = self.place(self.y, 1 - self.c if came else self.c)
        to = dev(self.z, self.x, self.y, 1 - self.c)
        return remote(self.own(), at, self.one.at[10], self.one.at[11], to)

    def pass_c(self, came=False):
        at = self.place(1 - self.y, 1 - self.c if came else self.c)
        to = dev(self.z, self.x, self.y, 1 - self.c)
        return remote(at, at, self.one.at[12], self.one.at[2], to)

    def stage(self, s):
        if s == 0:
            if not self.half:
                self.core_copy().wait_recv()
                mine = self.cols(self.c)
                add_into(self.cbuf, lambda i: self.grad[i[0], i[1], i[2], :, mine], (NZ, NX, 2))
            self.copy1().start()
        elif s == 1:
            self.copy1().wait_recv()
            if self.y_first:
                add_into(self.ebuf, lambda i: self.core_value(i[0], i[1], self.y), (NZ, NX))
            else:
                add_into(self.ebuf, lambda i: self.core_value(i[0], self.x, i[1]), (NZ, 2))
            self.copy2().start()
        elif s == 2:
            self.copy2().wait_recv()
            side = self.x if self.y_first else self.y
            add_into(self.fbuf, lambda i: self.ebuf[i[0], side], (NZ,))
            self.others(lambda zb: self.zcopy(zb, self.z).start())
        elif s == 3:
            self.zin[self.z] = self.fbuf[self.z]
            self.others(lambda zb: self.zcopy(zb, zb).wait_recv())
            total = self.zin[0].astype(F32)
            for zb in range(1, NZ):
                total = total + self.zin[zb].astype(F32)
            self.fbuf[self.z] = total.astype(B16)
            self.give_y().start()
            self.give_c().start()
            self.keep().start()
        elif s == 4:
            self.give_y(True).wait_recv()
            self.pass_c().start()
        elif s == 5:
            self.keep().wait()
            self.give_c(True).wait_recv()
            self.pass_c(True).wait_recv()
            if not self.half:
                self.core_copy().wait_send()
            self.copy1().wait_send()
            self.copy2().wait_send()
            self.give_y().wait_send()
            self.give_c().wait_send()
            self.pass_c().wait_send()
            self.others(lambda zb: self.zcopy(zb, zb).wait_send())


class MidSum:
    COUNT = 6

    def __init__(self, grad, into, out, total, outer, sems):
        self.z, self.x, self.y, self.c = coords()
        self.grad, self.into, self.out, self.total, self.outer = grad, into, out, total, outer
        self.sems = sems
        self.size = grad.shape[2] // self.COUNT
        self.inner = jnp.logical_and(self.z > 0, self.z < NZ - 1)
        self.end = jnp.logical_not(self.inner)
        self.mate = NZ - 1 - self.z

    @staticmethod
    def scratch(shape):
        vm = pltpu.VMEM
        return [vm(shape[1:], B16), vm(shape[1:], B16), pltpu.SemaphoreType.DMA((9, MidSum.COUNT))]

    def cols(self, p):
        return slice(p * self.size, (p + 1) * self.size)

    @staticmethod
    def beside(z):
        return z + 1 - 2 * lax.rem(z, 2)

    def across(self, i, p):
        block = self.beside(self.mate) if i == 0 else self.mate
        return remote(
            self.grad.at[block, :, self.cols(p)],
            self.into.at[i, :, self.cols(p)],
            self.sems.at[i, p],
            self.sems.at[2 + i, p],
            dev(self.mate, self.x, self.y, self.c),
        )

    def outward(self, p):
        return remote(
            self.outer.at[:, self.cols(p)],
            self.total.at[:, self.cols(p)],
            self.sems.at[4, p],
            self.sems.at[5, p],
            dev(self.beside(self.z), self.x, self.y, self.c),
        )

    def begin(self, i, p):
        pl.when(self.inner)(lambda: self.across(i, p).start())

    def give(self, p, sent=True):
        @pl.when(self.inner)
        def _():
            if sent:
                self.across(0, p).wait_recv()
            cols = self.cols(p)
            self.outer[:, cols] = (
                self.grad[self.beside(self.z), :, cols].astype(F32) + self.into[0, :, cols].astype(F32)
            ).astype(B16)
            self.outward(p).start()

    def swap(self, p, came=False):
        part = self.total.shape[0] // NX
        start = pl.multiple_of((1 - self.x) * part, 16)
        return remote(
            self.total.at[pl.ds(start, part), self.cols(p)],
            self.out.at[1 - self.x if came else self.x, :, self.cols(p)],
            self.sems.at[6, p],
            self.sems.at[7, p],
            dev(self.z, 1 - self.x, self.y, self.c),
        )

    def keep(self, p):
        part = self.total.shape[0] // NX
        start = pl.multiple_of(self.x * part, 16)
        return pltpu.make_async_copy(
            self.total.at[pl.ds(start, part), self.cols(p)],
            self.out.at[self.x, :, self.cols(p)],
            self.sems.at[8, p],
        )

    def final(self, p, sent=True):
        @pl.when(self.inner)
        def _():
            if sent:
                self.across(1, p).wait_recv()
            cols = self.cols(p)
            self.total[:, cols] = (
                self.grad[self.z, :, cols].astype(F32) + self.into[1, :, cols].astype(F32)
            ).astype(B16)

        pl.when(self.end)(lambda: self.outward(p).wait_recv())
        self.swap(p).start()
        self.keep(p).start()

    def close(self, sent=True):
        for p in range(self.COUNT):

            @pl.when(self.inner)
            def _():
                self.outward(p).wait_send()
                if sent:
                    self.across(0, p).wait_send()
                    self.across(1, p).wait_send()

            self.swap(p, True).wait_recv()
            self.swap(p).wait_send()
            self.keep(p).wait()


def piece_specs(width, hidden):
    rows, tall = width // NZ // 4, hidden // NZ // 4
    qkv = 3 * width // 2
    left = (qkv // 128 + 1) // 2 * 128
    early = (
        (2, (True, 0, rows, 0, hidden // 4, True)),
        (3, (True, 0, tall // 2, 0, width // 2, False)),
        (2, (True, 0, rows, hidden // 4, hidden // 4, False)),
        (3, (True, tall // 2, tall // 2, 0, width // 2, True)),
    )
    late = (
        (0, (False, 0, rows, 0, left, True)),
        (0, (False, 0, rows, left, qkv - left, False)),
        (1, (False, 0, rows, 0, width // 2, False)),
    )
    return early, late


def tail_kernel(*refs):
    sin_half, sout_half, dout, dwin, dwout, dwout_came = refs[:6]
    tok, mod, normed, proj, lsum, mgrad, rgrad, qkv, mg2, vecs, drouter, ebias, condt, ada = refs[6:20]
    outs = refs[20:24]
    pair_in, pair_out, tgrad_o, small, esum, tiles, cgot = refs[24:31]
    rest = list(refs[31:])
    z, x, y, c = coords()
    dp, ex = lax.axis_index("dp"), lax.axis_index("expert")
    n = NZ * NX
    length, width = tok.shape
    per = width // 128
    early_specs, late_specs = piece_specs(width, 2 * sin_half.shape[4])
    dqkv, pgrad = rest[:2]
    rest = rest[2:]
    sources = (dqkv, dout, sin_half, sout_half)

    def make(specs, rest):
        made = []
        for matrix, spec in specs:
            count = len(Piece.scratch(spec))
            made.append(Piece(spec, sources[matrix], outs[matrix], rest[:count]))
            rest = rest[count:]
        return made, rest

    early, rest = make(early_specs, rest)
    late, rest = make(late_specs, rest)
    wide = MidSum(dwin, rest[0], pair_in, *rest[1:4])
    tall = MidSum(dwout, dwout_came, pair_out, *rest[4:7])
    rest = rest[7:]
    ssum, sgot, zgot, esend, egot, mine, csend, sems, dsem, zsem, tsem = rest

    barrier = pltpu.get_barrier_semaphore()

    def peers(action):
        for p in range(n):

            @pl.when(p != dp)
            def _():
                action(p)

    peers(lambda p: greet(barrier, (p, ex)))
    mates = (dev(z, x, 1 - y, c), dev(z, x, y, 1 - c), dev(z, x, 1 - y, 1 - c))
    for mate in mates:
        greet(barrier, mate)
    pl.semaphore_wait(barrier, n - 1 + 3)

    every = range(MidSum.COUNT)
    for i in range(2):
        for p in every:
            wide.begin(i, p)
    for piece in early:
        piece.stage(0)
    late[2].core_copy().start()
    for p in every:
        tall.give(p, False)

    low_lane = lax.broadcasted_iota(jnp.int32, (length, 128), 1) < HEAD_DIM
    for p in range(HEADS // 2):
        q2 = proj[:, 128 * p : 128 * (p + 1)]
        k2 = proj[:, width + 128 * p : width + 128 * (p + 1)]
        v2 = proj[:, 2 * width + 128 * p : 2 * width + 128 * (p + 1)]
        m2 = mgrad[:, 128 * p : 128 * (p + 1)]
        parts = []
        for h in range(2):
            head = low_lane if h == 0 else jnp.logical_not(low_lane)
            zero = jnp.zeros_like(q2)
            s = dot_nt(jnp.where(head, q2, zero), k2) * SCALE
            prob = jnp.exp(s - lsum[:, 2 * p + h : 2 * p + h + 1])
            pg = dot_nt(jnp.where(head, m2, zero), v2)
            inner = jnp.sum(prob * pg, axis=-1, keepdims=True)
            sg = (prob * (pg - inner)).astype(B16)
            parts.append(
                (dot(sg, k2) * SCALE, dot_tn(sg, q2) * SCALE, dot_tn(prob.astype(B16), m2))
            )
        for i in range(3):
            pgrad[:, i * width + 128 * p : i * width + 128 * (p + 1)] = jnp.where(
                low_lane, parts[0][i], parts[1][i]
            ).astype(B16)
    lead = dqkv.shape[:4]
    for i in range(3):
        cols = slice(i * width, (i + 1) * width)
        dqkv[:, :, :, :, cols] = dot_tn(normed[...], pgrad[:, cols]).astype(B16).reshape(lead + (width,))
    for piece in late[:2]:
        piece.core_copy().start()

    rows = vecs.shape[0]
    ssum[0:rows, :] = vecs[...]
    for i, k in enumerate((0, 2)):
        row = jnp.sum(pgrad[:, k * width : (k + 1) * width].astype(F32), axis=0, keepdims=True)
        for j in range(per):
            at = rows + i * per + j
            ssum[at : at + 1, :] = row[:, 128 * j : 128 * (j + 1)]
    for at in range(rows + 2 * per, rows + 16):
        ssum[at : at + 1, :] = jnp.zeros((1, 128), F32)
    for b in range(per):
        ssum[rows + 16 + 8 * b : rows + 24 + 8 * b, :] = drouter[:, 128 * b : 128 * (b + 1)]
    hops = (dev(z, x, y, 1 - c), dev(z, x, 1 - y, c), dev(z, 1 - x, y, c))

    def hop(i):
        return remote(zgot.at[4 + i], sgot.at[i], sems.at[0, i], sems.at[1, i], hops[i])

    def ehop(came=False):
        return remote(
            esend.at[x], egot.at[z, 1 - x if came else x], sems.at[0, 3], sems.at[1, 3], hops[2]
        )

    def tile(p, at):
        return remote(mine, tiles.at[ex, at], dsem.at[0, p], dsem.at[1, at], (p, ex))

    def spread(i, theirs=False):
        e2 = 2 * (1 - y if i != 1 else y) + (1 - c if i != 0 else c)
        block = tiles.at[e2 if theirs else ex]
        return remote(block, block, tsem.at[0, i], tsem.at[1, i], mates[i])

    def cond_copy(p, at):
        return remote(csend.at[p], cgot.at[at], dsem.at[2, p], dsem.at[3, at], (p, ex))

    def zsum(zb, at):
        return remote(ssum, zgot.at[at], zsem.at[0, zb], zsem.at[1, at], dev(zb, x, y, c))

    def zexp(zb, at):
        return remote(
            egot.at[at], egot.at[at], zsem.at[2, zb], zsem.at[3, at], dev(zb, x, y, c)
        )

    def lines(action):
        for zb in range(NZ):

            @pl.when(zb != z)
            def _():
                action(zb)

    def start_hop(i):
        zgot[4 + i] = ssum[...]
        hop(i).start()

    def end_hop(i):
        hop(i).wait()
        ssum[...] = ssum[...] + sgot[i]

    start_hop(0)
    esend[x] = ebias[...]
    egot[z, x] = ebias[...]
    ehop().start()

    ngrad = dot_nt(pgrad[...], qkv[...])
    n1, r1 = norm_parts(tok[...].astype(F32))
    tgrad_o[...] = rgrad[...] + norm_back(ngrad * (1.0 + mod[1:2]), n1, r1)
    mod_rows = [
        jnp.sum(ngrad, axis=0, keepdims=True),
        jnp.sum(ngrad * n1, axis=0, keepdims=True),
    ] + [mg2[i : i + 1, :] for i in range(2, 6)]
    mine[...] = jnp.zeros_like(mine)
    for i, row in enumerate(mod_rows):
        row = row.astype(B16).astype(F32)
        for j in range(per):
            mine[i * per + j : i * per + j + 1, :] = row[:, 128 * j : 128 * (j + 1)]
    mine[40:48, :] = condt[...]
    peers(lambda p: tile(p, dp).start())
    tiles[ex, dp] = mine[...]

    def small1():
        end_hop(0)
        start_hop(1)
        peers(lambda p: tile(p, p).wait_recv())
        for i in range(3):
            spread(i).start()
        acc = jnp.zeros((n, ada.shape[0]), F32)
        for j in range(ada.shape[1] // 128):
            acc = acc + dot_nt(tiles[ex, :, j, :].astype(B16), ada[:, 128 * j : 128 * (j + 1)])
        csend[...] = jnp.zeros_like(csend)
        csend[:, 0, 0 : ada.shape[0]] = acc
        peers(lambda p: cond_copy(p, dp).start())
        cgot[dp] = csend[dp]

    def small2():
        end_hop(1)
        start_hop(2)
        ehop().wait_send()
        ehop(True).wait_recv()
        lines(lambda zb: zexp(zb, z).start())

    def small3():
        end_hop(2)
        zgot[z] = ssum[...]
        lines(lambda zb: zsum(zb, z).start())

    def small4():
        lines(lambda zb: zexp(zb, zb).wait_recv())
        lines(lambda zb: zsum(zb, zb).wait_recv())
        total, etotal = zgot[0], egot[0]
        for i in range(1, NZ):
            total = total + zgot[i]
            etotal = etotal + egot[i]
        small[...] = total
        esum[...] = etotal

    def small5():
        peers(lambda p: cond_copy(p, p).wait_recv())
        for i in range(3):
            spread(i, True).wait_recv()
            spread(i).wait_send()
        peers(lambda p: tile(p, p).wait_send())
        peers(lambda p: cond_copy(p, p).wait_send())
        lines(lambda zb: zexp(zb, zb).wait_send())
        lines(lambda zb: zsum(zb, zb).wait_send())

    def run(pieces, s):
        for piece in pieces:
            piece.stage(s)

    run(early[:2], 1)
    run(late, 0)
    for p in every:
        tall.final(p, False)
    run(early[2:], 1)
    for p in every[:3]:
        wide.give(p)
    run(early, 2)
    small1()
    for p in every[3:]:
        wide.give(p)
    run(late, 1)
    small2()
    for p in every[:3]:
        wide.final(p)
    run(early, 3)
    small3()
    run(late, 2)
    for p in every[3:]:
        wide.final(p)
    run(early, 4)
    small4()
    run(late, 3)
    run(early, 5)
    small5()
    run(late, 4)
    run(late, 5)
    tall.close(False)
    wide.close()


def tail_part(sin_half, sout_half, dout, dwin, dwout, dwout_came, *others):
    n = NZ * NX
    dma = pltpu.SemaphoreType.DMA
    vm = pltpu.VMEM
    tok, qkv, vecs = others[0], others[7], others[9]
    width, hidden = qkv.shape[0], 2 * sin_half.shape[1]
    split = lambda g: g.reshape(NZ, NX, 2, g.shape[0] // (4 * NZ), g.shape[1])
    rows, tall = width // NZ // 4, hidden // NZ // 4
    outs = [
        sds((2, rows, 3 * width), B16),
        sds((2, rows, width), B16),
        sds((2, rows, hidden), B16),
        sds((2, tall, width), B16),
    ]
    short = vecs.shape[0] + 16 + 8 * (width // 128)
    scratch = [vm((NZ, NX, 2, rows, 3 * width), B16), vm((tok.shape[0], 3 * width), B16)]
    for specs in piece_specs(width, hidden):
        for _, spec in specs:
            scratch += Piece.scratch(spec)
    scratch += [vm((2,) + dwin.shape[1:], B16)] + MidSum.scratch(dwin.shape) + MidSum.scratch(dwout.shape)
    scratch += [
        vm((short, 128), F32),
        vm((3, short, 128), F32),
        vm((NZ + 3, short, 128), F32),
        vm((2, 32, 128), F32),
        vm((NZ, 2, 32, 128), F32),
        vm((48, 128), F32),
        vm((n, 8, 128), F32),
        dma((2, 4)),
        dma((4, n)),
        dma((4, NZ)),
        dma((2, 3)),
    ]
    out = pl.pallas_call(
        tail_kernel,
        out_shape=outs
        + [
            sds((NX, dwin.shape[1] // NX, dwin.shape[2]), B16),
            sds((NX, dwout.shape[1] // NX, dwout.shape[2]), B16),
            sds(tok.shape, F32),
            sds((short, 128), F32),
            sds((2, 32, 128), F32),
            sds((4, n, 48, 128), F32),
            sds((n, 8, 128), F32),
        ],
        in_specs=[VM] * 20,
        out_specs=[HB] * 6 + [VM] * 5,
        scratch_shapes=scratch,
        compiler_params=params(4),
        name="attention_back_sums",
    )(split(sin_half), split(sout_half), split(dout), dwin, dwout, dwout_came, *others)
    return [o.reshape(-1, o.shape[2]).astype(F32) for o in out[:4]], out[4], out[5], out[6], out[7:]


def on_block(
    tokens, conditioning, routes, cotangent, ada_weight, ada_bias, qkv_weight, qv_bias, out_weight, out_bias,
    shared_in, shared_in_bias, shared_out, shared_out_bias, router,
    expert_in, expert_in_bias, expert_out, expert_out_bias,
):
    n = NZ * NX
    dp = lax.axis_index("dp")
    width = tokens.shape[2]
    hidden = shared_in.shape[1]
    part = width // n
    tok, cot, route = tokens[0], cotangent[0], routes[0]
    _, silu_back = jax.vjp(jax.nn.silu, conditioning.astype(F32))
    (
        normed, proj, lsum, mixed, att, resid, second, gates, place, mod, bias, sinb, router_t,
        condt, res, bgr, ebias, qkv_full, out_full, sin_c, sout_c, sin_x, sout_x, dwin, dwout,
    ) = lead_part(
        tok, cot, route.T, conditioning, ada_weight, ada_bias[None], qv_bias, out_bias[None], shared_out_bias[None],
        shared_in_bias[None], router.T, expert_in_bias, expert_out_bias,
        (qkv_weight, out_weight, shared_in, shared_out), expert_in, expert_out,
    )
    dwout = dwout.reshape(NZ, hidden // NZ, width)
    (dwout_came, output, rgrad, mgrad, sin_half, sout_half, dout, drouter, vecs, mg2) = middle(
        res, bgr, dwout, second, resid, att, cot, mod, sin_c, sout_c, sin_x, sout_x, sinb, bias, router_t, gates, place,
        mixed, out_full,
    )
    dense, dwin_pair, dwout_pair, tgrad, (small, esum, tiles, cgot) = tail_part(
        sin_half, sout_half, dout, dwin.reshape(NZ, NX * part, hidden),
        dwout, dwout_came, tok, mod, normed, proj, lsum, mgrad, rgrad, qkv_full, mg2, vecs, drouter, ebias, condt, ada_weight,
    )
    dwout_sum = dwout_pair.astype(F32)
    dwin_sum = dwin_pair.astype(F32)

    def share(v, size):
        return lax.dynamic_slice_in_dim(v.reshape(-1), dp * size, size, 0)

    per = width // 128
    base = hidden // 128
    sinb_grad = share(small[:base], hidden // n)
    soutb_grad = share(small[base : base + per], part)
    outb_grad = share(small[base + per : base + 2 * per], part)
    qvb_grad = jnp.stack(
        [share(small[40 : 40 + per], part), share(small[40 + per : 40 + 2 * per], part)]
    )
    router_grad = small[56:].reshape(per, E, 128).transpose(0, 2, 1).reshape(width, E)
    router_grad = lax.dynamic_slice_in_dim(router_grad, dp * part, part, 0)
    ein_b = lax.dynamic_slice_in_dim(
        esum[:, :base].reshape(2, hidden), dp * (hidden // n), hidden // n, 1
    )
    eout_b = lax.dynamic_slice_in_dim(
        esum[:, base : base + per].reshape(2, width), dp * part, part, 1
    )
    images = tiles.shape[0] * n
    mods = tiles[:, :, : 6 * per].reshape(images, 6 * width)
    conds = lax.dynamic_slice_in_dim(
        tiles[:, :, 40 : 40 + per].reshape(images, width), dp * part, part, 1
    )
    ada_grad = lax.dot_general(
        conds.astype(B16), mods.astype(B16), (((0,), (0,)), ((), ())), preferred_element_type=F32
    )
    adab_grad = share(jnp.sum(mods, axis=0), ada_bias.shape[0])
    cond_grad = silu_back(cgot[:, 0, :part].reshape(1, width))[0]
    return (
        output[None],
        tgrad[None],
        cond_grad,
        ada_grad,
        adab_grad,
        dense[0],
        qvb_grad,
        dense[1],
        outb_grad,
        dense[2],
        sinb_grad,
        dense[3],
        soutb_grad,
        router_grad,
        dwin_sum,
        ein_b,
        dwout_sum,
        eout_b,
    )


def layer_norm(rows):
    centred = rows - jnp.mean(rows, axis=-1, keepdims=True)
    return centred * lax.rsqrt(jnp.mean(centred * centred, axis=-1, keepdims=True) + 1e-06)


def modulate(rows, shift, scale):
    return layer_norm(rows) * (1.0 + scale) + shift


def gelu_tanh(values_in):
    return jax.nn.gelu(values_in, approximate=True)


def on_device(
    tokens,
    conditioning,
    routes,
    cotangent,
    ada_weight,
    ada_bias,
    qkv_weight,
    qv_bias,
    out_weight,
    out_bias,
    shared_in,
    shared_in_bias,
    shared_out,
    shared_out_bias,
    router,
    expert_in,
    expert_in_bias,
    expert_out,
    expert_out_bias,
):
    f32 = jnp.float32
    b16 = jnp.bfloat16
    gathered_dense = (
        lax.all_gather(ada_weight, "dp", axis=0, tiled=True),
        lax.all_gather(ada_bias, "dp", axis=0, tiled=True),
        lax.all_gather(qkv_weight, "dp", axis=0, tiled=True),
        lax.all_gather(qv_bias, "dp", axis=1, tiled=True),
        lax.all_gather(out_weight, "dp", axis=0, tiled=True),
        lax.all_gather(out_bias, "dp", axis=0, tiled=True),
        lax.all_gather(shared_in, "dp", axis=0, tiled=True),
        lax.all_gather(shared_in_bias, "dp", axis=0, tiled=True),
        lax.all_gather(shared_out, "dp", axis=0, tiled=True),
        lax.all_gather(shared_out_bias, "dp", axis=0, tiled=True),
        lax.all_gather(router, "dp", axis=0, tiled=True),
    )
    (
        ada_full,
        ada_bias_full,
        qkv_full,
        qv_bias_full,
        out_full,
        out_bias_full,
        shared_in_full,
        shared_in_bias_full,
        shared_out_full,
        shared_out_bias_full,
        router_full,
    ) = gathered_dense
    image_count, length, width = tokens.shape
    row_count = image_count * length
    scaling = HEAD_DIM ** (-0.5)
    head_shape = (image_count, length, HEADS, HEAD_DIM)
    cond_float = conditioning.astype(f32)
    cond_act, silu_back = jax.vjp(jax.nn.silu, cond_float)
    cond_low = cond_act.astype(b16)
    modulation = jnp.dot(cond_low, ada_full, preferred_element_type=f32) + ada_bias_full.astype(f32)
    pieces = [modulation[:, None, index * width : (index + 1) * width] for index in range(6)]
    source = tokens.astype(f32)
    first_norm, first_back = jax.vjp(modulate, source, pieces[0], pieces[1])
    normed = first_norm.astype(b16)
    projected = jnp.einsum("isd,de->ise", normed, qkv_full, preferred_element_type=f32)
    query_heads = (
        (projected[..., :width] + qv_bias_full[0].astype(f32)).astype(b16).reshape(head_shape)
    )
    key_heads = projected[..., width : 2 * width].astype(b16).reshape(head_shape)
    value_heads = (
        (projected[..., 2 * width :] + qv_bias_full[1].astype(f32)).astype(b16).reshape(head_shape)
    )
    scores = (
        jnp.einsum("iqhc,ikhc->ihqk", query_heads, key_heads, preferred_element_type=f32) * scaling
    )
    peak_score = jnp.max(scores, axis=-1, keepdims=True)
    unscaled = jnp.exp(scores - peak_score)
    exp_total = jnp.sum(unscaled, axis=-1, keepdims=True)
    log_total = peak_score + jnp.log(exp_total)
    probs_low = (unscaled / exp_total).astype(b16)
    mixed = (
        jnp.einsum("ihqk,ikhc->iqhc", probs_low, value_heads, preferred_element_type=f32)
        .reshape(image_count, length, width)
        .astype(b16)
    )
    attended = jnp.einsum(
        "isd,de->ise", mixed, out_full, preferred_element_type=f32
    ) + out_bias_full.astype(f32)
    resid = source + pieces[2] * attended
    second_float, second_back = jax.vjp(modulate, resid, pieces[3], pieces[4])
    second = second_float.astype(b16)
    shared_pre = jnp.einsum(
        "isd,df->isf", second, shared_in_full, preferred_element_type=f32
    ) + shared_in_bias_full.astype(f32)
    shared_act, shared_gelu_back = jax.vjp(gelu_tanh, shared_pre)
    shared_low = shared_act.astype(b16)
    shared = jnp.einsum(
        "isf,fd->isd", shared_low, shared_out_full, preferred_element_type=f32
    ) + shared_out_bias_full.astype(f32)
    second_rows = second.reshape(row_count, width)
    logits = jnp.dot(second_rows, router_full, preferred_element_type=f32)
    route_flat = routes.reshape(-1)
    one_hot = (route_flat[:, None] == jnp.arange(E, dtype=jnp.int32)).astype(jnp.int32)
    slot_index = jnp.sum(
        (jnp.cumsum(one_hot, axis=0, dtype=jnp.int32) - one_hot) * one_hot, axis=1, dtype=jnp.int32
    )
    position = jnp.where(slot_index < CAP, route_flat * CAP + slot_index, E * CAP)
    pair_rows = jnp.repeat(second_rows, 2, axis=0)
    buffer = (
        jnp.zeros((E * CAP, width), b16)
        .at[position]
        .set(pair_rows, mode="drop")
        .reshape(E, CAP, width)
    )
    received = lax.all_to_all(buffer, "expert", split_axis=0, concat_axis=1, tiled=True)
    expert_pre = (
        jnp.einsum("erd,edf->erf", received, expert_in, preferred_element_type=f32)
        + expert_in_bias.astype(f32)[:, None, :]
    )
    expert_low = gelu_tanh(expert_pre).astype(b16)
    expert_result = (
        jnp.einsum("erf,efd->erd", expert_low, expert_out, preferred_element_type=f32)
        + expert_out_bias.astype(f32)[:, None, :]
    ).astype(b16)
    returned = lax.all_to_all(
        expert_result, "expert", split_axis=1, concat_axis=0, tiled=True
    ).reshape(E * CAP, width)
    gathered = (
        returned.at[position]
        .get(mode="fill", fill_value=0)
        .reshape(row_count, 2, width)
        .astype(f32)
    )
    pair_mask = one_hot.reshape(row_count, 2, E).astype(f32)
    chosen = jnp.sum(logits[:, None, :] * pair_mask, axis=-1)
    gates = jax.nn.softmax(chosen, axis=-1)
    moe = (shared.reshape(row_count, width) + jnp.sum(gates[..., None] * gathered, axis=1)).reshape(
        image_count, length, width
    )
    output = (resid + pieces[5] * moe).astype(b16)
    ada_back, qkv_back, out_back, shared_in_back, shared_out_back, router_back = (
        ada_full,
        qkv_full,
        out_full,
        shared_in_full,
        shared_out_full,
        router_full,
    )
    grad_out = cotangent.astype(f32)
    gate_two_grad = jnp.sum(grad_out * moe, axis=1, keepdims=True)
    moe_grad = (pieces[5] * grad_out).astype(b16)
    moe_rows_grad = moe_grad.reshape(row_count, width)
    moe_rows_float = moe_rows_grad.astype(f32)
    pair_grad = (
        (gates[..., None] * moe_rows_float[:, None, :]).astype(b16).reshape(2 * row_count, width)
    )
    gate_grad = jnp.sum(moe_rows_float[:, None, :] * gathered, axis=-1)
    chosen_grad = gates * (gate_grad - jnp.sum(gates * gate_grad, axis=-1, keepdims=True))
    logits_grad = jnp.sum(chosen_grad[..., None] * pair_mask, axis=1).astype(b16)
    grad_buffer = (
        jnp.zeros((E * CAP, width), b16)
        .at[position]
        .set(pair_grad, mode="drop")
        .reshape(E, CAP, width)
    )
    result_grad = lax.all_to_all(grad_buffer, "expert", split_axis=0, concat_axis=1, tiled=True)
    pre_again = (
        jnp.einsum("erd,edf->erf", received, expert_in, preferred_element_type=f32)
        + expert_in_bias.astype(f32)[:, None, :]
    )
    act_again, expert_gelu_back = jax.vjp(gelu_tanh, pre_again)
    low_again = act_again.astype(b16)
    expert_out_grad = jnp.einsum("erf,erd->efd", low_again, result_grad, preferred_element_type=f32)
    expert_out_bias_grad = jnp.sum(result_grad.astype(f32), axis=1)
    expert_act_grad = jnp.einsum(
        "erd,efd->erf", result_grad, expert_out, preferred_element_type=f32
    )
    pre_grad = expert_gelu_back(expert_act_grad)[0].astype(b16)
    expert_in_grad = jnp.einsum("erd,erf->edf", received, pre_grad, preferred_element_type=f32)
    expert_in_bias_grad = jnp.sum(pre_grad.astype(f32), axis=1)
    received_grad = jnp.einsum(
        "erf,edf->erd", pre_grad, expert_in, preferred_element_type=f32
    ).astype(b16)
    sent_grad = lax.all_to_all(
        received_grad, "expert", split_axis=1, concat_axis=0, tiled=True
    ).reshape(E * CAP, width)
    dispatch_rows_grad = jnp.sum(
        sent_grad.at[position]
        .get(mode="fill", fill_value=0)
        .reshape(row_count, 2, width)
        .astype(f32),
        axis=1,
    )
    shared_out_grad = jnp.einsum("isf,isd->fd", shared_low, moe_grad, preferred_element_type=f32)
    shared_out_bias_grad = jnp.sum(moe_rows_float, axis=0)
    shared_act_grad = jnp.einsum(
        "isd,fd->isf", moe_grad, shared_out_back, preferred_element_type=f32
    )
    shared_pre_grad = shared_gelu_back(shared_act_grad)[0].astype(b16)
    shared_in_grad = jnp.einsum("isd,isf->df", second, shared_pre_grad, preferred_element_type=f32)
    shared_in_bias_grad = jnp.sum(shared_pre_grad.astype(f32), axis=(0, 1))
    router_grad = jnp.einsum("rd,re->de", second_rows, logits_grad, preferred_element_type=f32)
    second_grad = jnp.einsum(
        "isf,df->isd", shared_pre_grad, shared_in_back, preferred_element_type=f32
    )
    side_grad = dispatch_rows_grad + jnp.einsum(
        "re,de->rd", logits_grad, router_back, preferred_element_type=f32
    )
    second_grad = second_grad + side_grad.reshape(image_count, length, width)
    resid_extra, shift_two_grad, scale_two_grad = second_back(second_grad)
    resid_grad = grad_out + resid_extra
    attended_grad = (pieces[2] * resid_grad).astype(b16)
    gate_one_grad = jnp.sum(resid_grad * attended, axis=1, keepdims=True)
    out_weight_grad = jnp.einsum("isd,ise->de", mixed, attended_grad, preferred_element_type=f32)
    out_bias_grad = jnp.sum(attended_grad.astype(f32), axis=(0, 1))
    mixed_grad = (
        jnp.einsum("ise,de->isd", attended_grad, out_back, preferred_element_type=f32)
        .astype(b16)
        .reshape(head_shape)
    )
    again_scores = (
        jnp.einsum("iqhc,ikhc->ihqk", query_heads, key_heads, preferred_element_type=f32) * scaling
    )
    probs_float = jnp.exp(again_scores - log_total)
    again_low = probs_float.astype(b16)
    probs_grad = jnp.einsum("iqhc,ikhc->ihqk", mixed_grad, value_heads, preferred_element_type=f32)
    values_grad = jnp.einsum(
        "ihqk,iqhc->ikhc", again_low, mixed_grad, preferred_element_type=f32
    ).astype(b16)
    scores_grad = (
        probs_float * (probs_grad - jnp.sum(probs_float * probs_grad, axis=-1, keepdims=True))
    ).astype(b16)
    query_grad = (
        jnp.einsum("ihqk,ikhc->iqhc", scores_grad, key_heads, preferred_element_type=f32) * scaling
    ).astype(b16)
    keys_grad = (
        jnp.einsum("ihqk,iqhc->ikhc", scores_grad, query_heads, preferred_element_type=f32)
        * scaling
    ).astype(b16)
    flat_shape = (image_count, length, width)
    projected_grad = jnp.concatenate(
        [
            query_grad.reshape(flat_shape),
            keys_grad.reshape(flat_shape),
            values_grad.reshape(flat_shape),
        ],
        axis=-1,
    )
    qkv_weight_grad = jnp.einsum("isd,ise->de", normed, projected_grad, preferred_element_type=f32)
    qv_bias_grad = jnp.stack(
        [
            jnp.sum(query_grad.astype(f32), axis=(0, 1)).reshape(width),
            jnp.sum(values_grad.astype(f32), axis=(0, 1)).reshape(width),
        ]
    )
    normed_grad = jnp.einsum("ise,de->isd", projected_grad, qkv_back, preferred_element_type=f32)
    token_extra, shift_one_grad, scale_one_grad = first_back(normed_grad)
    tokens_grad = resid_grad + token_extra
    modulation_grad = jnp.concatenate(
        [
            shift_one_grad,
            scale_one_grad,
            gate_one_grad,
            shift_two_grad,
            scale_two_grad,
            gate_two_grad,
        ],
        axis=-1,
    )[:, 0, :].astype(b16)
    ada_weight_grad = jnp.einsum("id,ie->de", cond_low, modulation_grad, preferred_element_type=f32)
    ada_bias_grad = jnp.sum(modulation_grad.astype(f32), axis=0)
    cond_act_grad = jnp.einsum("ie,de->id", modulation_grad, ada_back, preferred_element_type=f32)
    conditioning_grad = silu_back(cond_act_grad)[0]
    expert_sums = (
        lax.psum_scatter(
            expert_in_grad.astype(jnp.bfloat16), "dp", scatter_dimension=1, tiled=True
        ).astype(jnp.float32),
        lax.psum_scatter(
            expert_in_bias_grad.astype(jnp.bfloat16), "dp", scatter_dimension=1, tiled=True
        ).astype(jnp.float32),
        lax.psum_scatter(
            expert_out_grad.astype(jnp.bfloat16), "dp", scatter_dimension=1, tiled=True
        ).astype(jnp.float32),
        lax.psum_scatter(
            expert_out_bias_grad.astype(jnp.bfloat16), "dp", scatter_dimension=1, tiled=True
        ).astype(jnp.float32),
    )
    dense_parts = (
        lax.psum_scatter(
            ada_weight_grad.astype(jnp.bfloat16), "dp", scatter_dimension=0, tiled=True
        ).astype(jnp.float32),
        lax.psum_scatter(
            ada_bias_grad.astype(jnp.bfloat16), "dp", scatter_dimension=0, tiled=True
        ).astype(jnp.float32),
        lax.psum_scatter(
            qkv_weight_grad.astype(jnp.bfloat16), "dp", scatter_dimension=0, tiled=True
        ).astype(jnp.float32),
        lax.psum_scatter(
            qv_bias_grad.astype(jnp.bfloat16), "dp", scatter_dimension=1, tiled=True
        ).astype(jnp.float32),
        lax.psum_scatter(
            out_weight_grad.astype(jnp.bfloat16), "dp", scatter_dimension=0, tiled=True
        ).astype(jnp.float32),
        lax.psum_scatter(
            out_bias_grad.astype(jnp.bfloat16), "dp", scatter_dimension=0, tiled=True
        ).astype(jnp.float32),
        lax.psum_scatter(
            shared_in_grad.astype(jnp.bfloat16), "dp", scatter_dimension=0, tiled=True
        ).astype(jnp.float32),
        lax.psum_scatter(
            shared_in_bias_grad.astype(jnp.bfloat16), "dp", scatter_dimension=0, tiled=True
        ).astype(jnp.float32),
        lax.psum_scatter(
            shared_out_grad.astype(jnp.bfloat16), "dp", scatter_dimension=0, tiled=True
        ).astype(jnp.float32),
        lax.psum_scatter(
            shared_out_bias_grad.astype(jnp.bfloat16), "dp", scatter_dimension=0, tiled=True
        ).astype(jnp.float32),
        lax.psum_scatter(
            router_grad.astype(jnp.bfloat16), "dp", scatter_dimension=0, tiled=True
        ).astype(jnp.float32),
    )
    dense_sums = lax.psum(
        (
            dense_parts[0],
            dense_parts[1],
            dense_parts[2],
            dense_parts[3],
            dense_parts[4],
            dense_parts[5],
            dense_parts[6],
            dense_parts[7],
            dense_parts[8],
            dense_parts[9],
            dense_parts[10],
        ),
        "expert",
    )
    return (
        output,
        tokens_grad,
        conditioning_grad,
        dense_sums[0],
        dense_sums[1],
        dense_sums[2],
        dense_sums[3],
        dense_sums[4],
        dense_sums[5],
        dense_sums[6],
        dense_sums[7],
        dense_sums[8],
        dense_sums[9],
        dense_sums[10],
        expert_sums[0],
        expert_sums[1],
        expert_sums[2],
        expert_sums[3],
    )


def solution(mesh):
    in_specs = (
        P(("dp", "expert"), None, None),
        P(("dp", "expert"), None),
        P(("dp", "expert"), None, None),
        P(("dp", "expert"), None, None),
        P("dp", None),
        P("dp"),
        P("dp", None),
        P(None, "dp"),
        P("dp", None),
        P("dp"),
        P("dp", None),
        P("dp"),
        P("dp", None),
        P("dp"),
        P("dp", None),
        P("expert", None, None),
        P("expert", None),
        P("expert", None, None),
        P("expert", None),
    )
    out_specs = (
        P(("dp", "expert"), None, None),
        P(("dp", "expert"), None, None),
        P(("dp", "expert"), None),
        P("dp", None),
        P("dp"),
        P("dp", None),
        P(None, "dp"),
        P("dp", None),
        P("dp"),
        P("dp", None),
        P("dp"),
        P("dp", None),
        P("dp"),
        P("dp", None),
        P("expert", "dp", None),
        P("expert", "dp"),
        P("expert", "dp", None),
        P("expert", "dp"),
    )
    body = on_device
    if dict(mesh.shape) == {"dp": NZ * NX, "expert": 4}:
        body = on_block
    return jax.shard_map(
        body, mesh=mesh, in_specs=in_specs, out_specs=out_specs, check_vma=False
    )
```

```python
import functools

import jax
import jax.numpy as jnp
from jax import lax
from jax.experimental import pallas as pl
from jax.experimental.pallas import tpu as pltpu
from jax.sharding import PartitionSpec as P

HEADS = 12
HEAD_DIM = 64
E = 8
CAP = 80
MESH = pl.DeviceIdType.MESH
F32 = jnp.float32
B16 = jnp.bfloat16
VMEM_LIMIT = 60 * 1024 * 1024
SCALE = HEAD_DIM ** (-0.5)
GELU_C = 0.7978845608028654
NZ, NX = 4, 2


def coords():
    dp = lax.axis_index("dp")
    ex = lax.axis_index("expert")
    return lax.div(dp, NX), lax.rem(dp, NX), lax.div(ex, 2), lax.rem(ex, 2)


def dev(z, x, y, c):
    return (NX * z + x, 2 * y + c)


def dot(a, b):
    return jnp.dot(a, b, preferred_element_type=F32)


def dot_nt(a, b):
    return lax.dot_general(a, b, (((1,), (1,)), ((), ())), preferred_element_type=F32)


def dot_tn(a, b):
    return lax.dot_general(a, b, (((0,), (0,)), ((), ())), preferred_element_type=F32)


def gelu(v):
    return v * (0.5 + 0.5 * jnp.tanh(v * (GELU_C + GELU_C * 0.044715 * (v * v))))


def gelu_parts(v):
    v2 = v * v
    t = jnp.tanh(GELU_C * v * (1.0 + 0.044715 * v2))
    h = 0.5 * (1.0 + t)
    return v * h, h + 0.5 * v * (1.0 - t * t) * (GELU_C * (1.0 + 0.134145 * v2))


def norm_parts(v):
    centred = v - jnp.mean(v, axis=-1, keepdims=True)
    r = lax.rsqrt(jnp.mean(centred * centred, axis=-1, keepdims=True) + 1e-06)
    return centred * r, r


def norm_back(u, n, r):
    return r * (
        u - jnp.mean(u, axis=-1, keepdims=True) - n * jnp.mean(u * n, axis=-1, keepdims=True)
    )


def remote(src, dst, send, recv, to):
    return pltpu.make_async_remote_copy(
        src_ref=src,
        dst_ref=dst,
        send_sem=send,
        recv_sem=recv,
        device_id=to,
        device_id_type=MESH,
    )


def greet(barrier, to):
    pl.semaphore_signal(barrier, inc=1, device_id=to, device_id_type=MESH)


def params(collective_id=None):
    if collective_id is None:
        return pltpu.CompilerParams(vmem_limit_bytes=VMEM_LIMIT)
    return pltpu.CompilerParams(
        vmem_limit_bytes=VMEM_LIMIT, collective_id=collective_id, has_side_effects=True
    )


VM = pl.BlockSpec(memory_space=pltpu.VMEM)
HB = pl.BlockSpec(memory_space=pl.ANY)


def sds(shape, dtype):
    return jax.ShapeDtypeStruct(shape, dtype)


class Gather:
    def __init__(self, shards, fulls, splits, sems):
        self.z, self.x, self.y, self.c = coords()
        self.mats = list(zip(shards, fulls, splits))
        (self.zs, self.zr, self.xs, self.xr, self.ys, self.yr, self.cs, self.cr, self.loc) = sems

    @staticmethod
    def semaphores(count):
        dma = pltpu.SemaphoreType.DMA
        return [
            dma((count, 2, NZ)),
            dma((count, NZ)),
            dma((count, NZ)),
            dma((count, NZ)),
            dma((count, NZ, NX)),
            dma((count, NZ, NX)),
            dma((count, NZ, NX, 2)),
            dma((count, NZ, NX, 2)),
            dma((count,)),
        ]

    def region(self, m, zb, xb, yh, ch):
        shard, full, split = self.mats[m]
        rows, width = shard.shape[0], shard.shape[1] // 2
        start = (NX * zb + xb) * rows
        if split:
            rows = rows // 2
            start = start + yh * rows
        return full.at[
            pl.ds(pl.multiple_of(start, 16), rows), pl.ds(pl.multiple_of(ch * width, 128), width)
        ]

    def own(self, m):
        shard, full, split = self.mats[m]
        rows, width = shard.shape[0], shard.shape[1] // 2
        start = 0
        if split:
            rows = rows // 2
            start = self.y * rows
        return shard.at[
            pl.ds(pl.multiple_of(start, 16), rows),
            pl.ds(pl.multiple_of(self.c * width, 128), width),
        ]

    def zcopy(self, m, zb, side, mine=False):
        here = self.region(m, zb, self.x, self.y, self.c)
        step = 1 if side else -1
        return remote(
            self.own(m) if mine else here,
            here,
            self.zs.at[m, side, zb],
            self.zr.at[m, zb],
            dev(lax.rem(self.z + step + NZ, NZ), self.x, self.y, self.c),
        )

    def xcopy(self, m, zb, mine=False, xb=None):
        here = self.region(m, zb, self.x if xb is None else xb, self.y, self.c)
        return remote(
            self.own(m) if mine else here,
            here,
            self.xs.at[m, zb],
            self.xr.at[m, zb],
            dev(self.z, 1 - self.x, self.y, self.c),
        )

    def ycopy(self, m, zb, xb, yh=None):
        here = self.region(m, zb, xb, self.y if yh is None else yh, self.c)
        return remote(
            here,
            here,
            self.ys.at[m, zb, xb],
            self.yr.at[m, zb, xb],
            dev(self.z, self.x, 1 - self.y, self.c),
        )

    def ccopy(self, m, zb, xb, yh, ch=None):
        here = self.region(m, zb, xb, yh, self.c if ch is None else ch)
        slot = yh if self.mats[m][2] else 0
        return remote(
            here,
            here,
            self.cs.at[m, zb, xb, slot],
            self.cr.at[m, zb, xb, slot],
            dev(self.z, self.x, self.y, 1 - self.c),
        )

    def local(self, m):
        shard, full, _ = self.mats[m]
        rows = shard.shape[0]
        start = (NX * self.z + self.x) * rows
        return pltpu.make_async_copy(
            shard, full.at[pl.ds(pl.multiple_of(start, 16), rows), :], self.loc.at[m]
        )

    def blocks(self, step):
        if step == 0:
            return [(self.z, None, None)]
        return [
            (self.z - step, self.z - step >= 0, 1),
            (self.z + step, self.z + step < NZ, 0),
        ]

    def more(self, side):
        return self.z + 1 < NZ if side else self.z - 1 >= 0

    def begin(self, m):
        for side in (1, 0):

            @pl.when(self.more(side))
            def _():
                self.zcopy(m, self.z, side, True).start()

        self.xcopy(m, self.z, True).start()
        self.local(m).start()

    def spread(self, m, zb, xb):
        if self.mats[m][2]:
            self.ycopy(m, zb, xb).start()
        self.ccopy(m, zb, xb, self.y).start()

    def take_z(self, m, step):
        for zb, exists, side in self.blocks(step):

            @pl.when(exists)
            def _():
                self.zcopy(m, zb, side).wait_recv()
                if step < NZ - 1:

                    @pl.when(self.more(side))
                    def _():
                        self.zcopy(m, zb, side).start()

                self.xcopy(m, zb).start()
                self.spread(m, zb, self.x)

    def take_x(self, m, step):
        for zb, exists, _ in self.blocks(step):

            def body():
                self.xcopy(m, zb, False, 1 - self.x).wait_recv()
                self.spread(m, zb, 1 - self.x)

            body() if exists is None else pl.when(exists)(body)

    def others(self, m, step, action):
        for zb, exists, _ in self.blocks(step):
            for xb in (self.x, 1 - self.x) if step else (1 - self.x,):
                body = functools.partial(action, m, zb, xb)
                body() if exists is None else pl.when(exists)(body)

    def take_y(self, m, step):
        if not self.mats[m][2]:
            return

        def action(m, zb, xb):
            self.ycopy(m, zb, xb, 1 - self.y).wait_recv()
            self.ccopy(m, zb, xb, 1 - self.y).start()

        self.others(m, step, action)

    def finish(self, m):
        def action(m, zb, xb):
            for yh in (self.y, 1 - self.y) if self.mats[m][2] else (self.y,):
                self.ccopy(m, zb, xb, yh, 1 - self.c).wait_recv()
                self.ccopy(m, zb, xb, yh).wait_send()
            if self.mats[m][2]:
                self.ycopy(m, zb, xb).wait_send()

        for step in range(NZ):
            self.others(m, step, action)
        for side in (1, 0):

            @pl.when(self.more(side))
            def _():
                self.zcopy(m, self.z, side, True).wait_send()

        for step in range(1, NZ):
            for zb, exists, side in self.blocks(step):

                @pl.when(exists)
                def _():
                    self.xcopy(m, zb).wait_send()
                    if step < NZ - 1:

                        @pl.when(self.more(side))
                        def _():
                            self.zcopy(m, zb, side).wait_send()

        self.xcopy(m, self.z, True).wait_send()
        self.local(m).wait()


class Column:
    def __init__(self, shard, column, other, send, recv, local, xsend, xrecv):
        self.z, self.x, self.y, self.c = coords()
        self.shard, self.column, self.other = shard, column, other
        self.send, self.recv, self.local, self.xsend, self.xrecv = send, recv, local, xsend, xrecv

    @staticmethod
    def semaphores():
        dma = pltpu.SemaphoreType.DMA
        return [dma((2, NZ)), dma((NZ,)), dma((1,)), dma((NZ,)), dma((NZ,))]

    def block(self, zb):
        rows = self.shard.shape[0]
        return self.column.at[pl.ds(pl.multiple_of(zb * rows, 16), rows), :]

    def own(self):
        width = self.shard.shape[1] // 2
        return self.shard.at[:, pl.ds(pl.multiple_of(self.c * width, 128), width)]

    def copy(self, zb, side, mine=False):
        here = self.block(zb)
        to = lax.rem(self.z + (1 if side else NZ - 1), NZ)
        return remote(
            self.own() if mine else here,
            here,
            self.send.at[side, zb],
            self.recv.at[zb],
            dev(to, self.x, self.y, self.c),
        )

    def xcopy(self, zb, mine=False):
        rows, width = self.shard.shape[0], self.shard.shape[1] // 2
        part = rows // 2
        start = pl.multiple_of(self.y * part, 16)
        if mine:
            source = self.shard.at[
                pl.ds(start, part), pl.ds(pl.multiple_of(self.c * width, 128), width)
            ]
        else:
            source = self.column.at[pl.ds(pl.multiple_of(zb * rows + start, 16), part), :]
        return remote(
            source,
            self.other.at[pl.ds(pl.multiple_of(zb * part, 16), part), :],
            self.xsend.at[zb],
            self.xrecv.at[zb],
            dev(self.z, 1 - self.x, self.y, self.c),
        )

    def keep(self):
        return pltpu.make_async_copy(self.own(), self.block(self.z), self.local.at[0])

    def more(self, side):
        return self.z + 1 < NZ if side else self.z - 1 >= 0

    def blocks(self, step):
        return [(self.z - step, self.z - step >= 0, 1), (self.z + step, self.z + step < NZ, 0)]

    def begin(self):
        for side in (1, 0):

            @pl.when(self.more(side))
            def _():
                self.copy(self.z, side, True).start()

        self.keep().start()
        self.xcopy(self.z, True).start()

    def take(self, step):
        for zb, exists, side in self.blocks(step):

            @pl.when(exists)
            def _():
                self.copy(zb, side).wait_recv()
                if step < NZ - 1:

                    @pl.when(self.more(side))
                    def _():
                        self.copy(zb, side).start()

    def push(self, step):
        for zb, exists, _ in self.blocks(step):

            @pl.when(exists)
            def _():
                self.xcopy(zb).start()

    def finish(self):
        for side in (1, 0):

            @pl.when(self.more(side))
            def _():
                self.copy(self.z, side, True).wait_send()

        for step in range(1, NZ - 1):
            for zb, exists, side in self.blocks(step):

                @pl.when(jnp.logical_and(exists, self.more(side)))
                def _():
                    self.copy(zb, side).wait_send()

        for zb in range(NZ):
            self.xcopy(zb).wait_send()


class Spread:
    def __init__(self, column, other, full, ys, yr, cs, cr, local):
        self.z, self.x, self.y, self.c = coords()
        self.column, self.other, self.full, self.local = column, other, full, local
        self.ys, self.yr, self.cs, self.cr = ys, yr, cs, cr

    @staticmethod
    def semaphores():
        dma = pltpu.SemaphoreType.DMA
        return [dma((NZ,))] * 2 + [dma((3, NZ))] * 2 + [dma((2, NZ))]

    def cols(self, c):
        width = self.full.shape[3] // 2
        return pl.ds(pl.multiple_of(c * width, 128), width)

    def half(self, y):
        rows = self.full.shape[2] // 2
        return pl.ds(pl.multiple_of(y * rows, 16), rows)

    def source(self, kind, zb):
        rows = self.full.shape[2] // (1 if kind == 0 else 2)
        ref = self.column if kind == 0 else self.other
        return ref.at[pl.ds(pl.multiple_of(zb * rows, 16), rows), :]

    def place(self, kind, zb, c):
        if kind == 0:
            return self.full.at[zb, self.x, :, self.cols(c)]
        return self.full.at[zb, 1 - self.x, self.half(self.y if kind == 1 else 1 - self.y), self.cols(c)]

    def ycopy(self, zb, came=False):
        return remote(
            self.source(1, zb), self.place(2 if came else 1, zb, self.c), self.ys.at[zb], self.yr.at[zb],
            dev(self.z, self.x, 1 - self.y, self.c),
        )

    def ccopy(self, kind, zb, came=False):
        at = self.place(kind, zb, 1 - self.c if came else self.c)
        return remote(
            at if kind == 2 else self.source(kind, zb), at, self.cs.at[kind, zb], self.cr.at[kind, zb],
            dev(self.z, self.x, self.y, 1 - self.c),
        )

    def keep(self, kind, zb):
        return pltpu.make_async_copy(
            self.source(kind, zb), self.place(kind, zb, self.c), self.local.at[kind, zb]
        )

    def near(self):
        for zb in range(NZ):
            self.ccopy(0, zb).start()
            self.keep(0, zb).start()

    def pass_x(self, zb):
        self.ycopy(zb).start()
        self.ccopy(1, zb).start()
        self.keep(1, zb).start()

    def pass_y(self, zb):
        self.ycopy(zb, True).wait_recv()
        self.ccopy(2, zb).start()

    def finish(self):
        for zb in range(NZ):
            for kind in range(3):
                self.ccopy(kind, zb, True).wait_recv()
                self.ccopy(kind, zb).wait_send()
            for kind in range(2):
                self.keep(kind, zb).wait()
            self.ycopy(zb).wait_send()


def choose_rows(place, slots):
    return place == lax.broadcasted_iota(jnp.int32, (place.shape[0], slots), 1)


def plane_peer(k):
    z, x, y, c = coords()
    xt = 1 - x if k & 1 else x
    ct = 1 - c if k & 2 else c
    yt = 1 - y if k & 4 else y
    return dev(z, xt, yt, ct), 4 * yt + 2 * ct + xt


def plane_rank():
    _, x, y, c = coords()
    return 4 * y + 2 * c + x


def slot_rows(ref, rank):
    return ref.at[pl.ds(pl.multiple_of(rank * CAP, 16), CAP), :]


class PlaneExchange:
    ORDER = (7, 5, 6, 4, 3, 1, 2)

    def __init__(self, source, target, send, recv):
        self.source, self.target, self.send, self.recv = source, target, send, recv

    def copy(self, k, into=None):
        peer, other = plane_peer(k)
        return remote(
            slot_rows(self.source, other),
            slot_rows(self.target, plane_rank() if into is None else other),
            self.send.at[k],
            self.recv.at[k],
            peer,
        )

    def mine(self):
        rank = plane_rank()
        return pltpu.make_async_copy(
            slot_rows(self.source, rank), slot_rows(self.target, rank), self.send.at[0]
        )

    def start(self):
        for k in self.ORDER:
            self.copy(k).start()
        self.mine().start()

    def wait_in(self):
        self.mine().wait()
        for k in self.ORDER:
            self.copy(k, True).wait_recv()

    def wait_out(self):
        for k in self.ORDER:
            self.copy(k).wait_send()


CHUNK = 512


def lead_kernel(
    tok, cot, routes, cond, ada, adab, qvb, outb, soutb, sinb_s, router_s, bin_r, bout_r,
    qkv_s, out_s, sin_s, sout_s, win_h, wout_h,
    normed_o, proj_o, lsum_o, mixed_o, att_o, resid_o, second_o, gates_o, place_o, mod_o, bias_o, sinb_o, rt_o,
    condt_o, ebias, ret_o, retg_o, qkv_o, outw_o, sin_o, sout_o, dwin_o, dwout_o, came_o,
    pack, packs, sent, got, qkv, outw, sbuf, gbuf, res, bgr, rows, grads, far_rows, far_grads, win, wout, dwin, dwout,
    pres, acc, sin_c, sout_c, sin_x, sout_x,
    s1, r1, s2, r2, ds0, dr0, ds1, dr1, ds2, dr2, ds3, dr3, wsem, osem, fsem, msem, *gsems,
):
    z, x, y, c = coords()
    dp, ex = lax.axis_index("dp"), lax.axis_index("expert")
    n = NZ * NX
    length, width = tok.shape
    hidden = win.shape[1]
    part = width // n
    per = width // 128
    count = len(Column.semaphores())
    lead = Gather((qkv_s, out_s), (qkv, outw), (True, False), gsems[: len(Gather.semaphores(2))])
    gsems = gsems[len(Gather.semaphores(2)) :]
    later = (
        Column(sin_s, sin_c, sin_x, *gsems[:count]),
        Column(sout_s, sout_c, sout_x, *gsems[count : 2 * count]),
    )
    gsems = gsems[2 * count :]
    count = len(Spread.semaphores())
    spreads = (
        Spread(sin_c, sin_x, sin_o, *gsems[:count]),
        Spread(sout_c, sout_x, sout_o, *gsems[count:]),
    )

    def per_block(step, action):
        for zb, exists in [(z, None)] if step == 0 else [v[:2] for v in later[0].blocks(step)]:
            body = functools.partial(action, zb)
            body() if exists is None else pl.when(exists)(body)

    def pass_x(step):
        def action(zb):
            for column, spread in zip(later, spreads):
                column.xcopy(zb).wait_recv()
                spread.pass_x(zb)

        per_block(step, action)

    def pass_y(step):
        def action(zb):
            for spread in spreads:
                spread.pass_y(zb)

        per_block(step, action)

    loads = [
        pltpu.make_async_copy(win_h.at[x], win, wsem.at[0]),
        pltpu.make_async_copy(wout_h.at[x], wout, wsem.at[1]),
    ]

    def peers(action):
        for p in range(n):

            @pl.when(p != dp)
            def _():
                action(p)

    barrier = pltpu.get_barrier_semaphore()
    peers(lambda p: greet(barrier, (p, ex)))
    for k in range(2, E):
        greet(barrier, plane_peer(k)[0])

    pack[...] = jnp.zeros_like(pack)
    pack[0:2, 0:part] = qvb[...].astype(F32)
    pack[2:3, 0:part] = outb[...].astype(F32)
    pack[3:4, 0:part] = soutb[...].astype(F32)
    for j in range(hidden // n // 128):
        pack[4 + j : 5 + j, :] = sinb_s[:, 128 * j : 128 * (j + 1)].astype(F32)
    long = adab.shape[1]
    for j in range(-(-long // 128)):
        size = min(128, long - 128 * j)
        pack[8 + j : 9 + j, 0:size] = adab[:, 128 * j : 128 * j + size].astype(F32)
    pack[16:24, 0:part] = router_s[...].astype(F32)
    cv = cond[...].astype(F32)
    cond_low = (cv / (1.0 + jnp.exp(-cv))).astype(B16).astype(F32)
    for p in range(n):
        pack[24 + p : 25 + p, 0:part] = cond_low[:, part * p : part * (p + 1)]
    condt_o[...] = jnp.zeros_like(condt_o)
    for j in range(per):
        condt_o[j : j + 1, :] = cond_low[:, 128 * j : 128 * (j + 1)]

    pl.semaphore_wait(barrier, n - 1 + E - 2)

    def first(p, at):
        return remote(pack, packs.at[at], s1.at[p], r1.at[at], (p, ex))

    def second_hop(p, at):
        return remote(sent.at[p], got.at[at], s2.at[p], r2.at[at], (p, ex))

    peers(lambda p: first(p, dp).start())
    lead.begin(0)
    lead.begin(1)
    for load in loads:
        load.start()
    packs[dp] = pack[...]
    peers(lambda p: first(p, p).wait_recv())
    cond_rows = jnp.concatenate([packs[p, pl.ds(24 + dp, 1), :] for p in range(n)], axis=0)
    partial = dot(cond_rows[:, :part].astype(B16), ada[...])
    for j in range(partial.shape[1] // 128):
        sent[:, j, :] = partial[:, 128 * j : 128 * (j + 1)]
    peers(lambda p: second_hop(p, dp).start())
    got[dp] = sent[dp]

    both_mats = (0, 1)

    def step_of(plan, step):
        for m in both_mats:
            if step:
                plan.take_z(m, step)
            plan.take_x(m, step)
        if step:
            for m in both_mats:
                plan.take_y(m, step - 1)

    for step in range(NZ):
        step_of(lead, step)

    for column in later:
        column.begin()

    bias_o[...] = jnp.zeros_like(bias_o)
    for p in range(n):
        bias_o[0:4, part * p : part * (p + 1)] = packs[p, 0:4, 0:part]
        rt_o[:, part * p : part * (p + 1)] = packs[p, 16:24, 0:part]
        for j in range(hidden // n // 128):
            at = hidden // n * p + 128 * j
            sinb_o[:, at : at + 128] = packs[p, 4 + j : 5 + j, :]
    peers(lambda p: second_hop(p, p).wait_recv())
    total = got[0]
    for p in range(1, n):
        total = total + got[p]
    mod_o[...] = jnp.zeros_like(mod_o)
    for i in range(6):
        for b in range(per):
            mod_o[i : i + 1, 128 * b : 128 * (b + 1)] = total[per * i + b : per * i + b + 1, :]
    unit = 64
    for p in range(n):
        for u in range(long // unit):
            at = long * p + unit * u
            i, b = at // width, at % width
            mod_o[i : i + 1, b : b + unit] += packs[
                p, 8 + unit * u // 128 : 9 + unit * u // 128, unit * u % 128 : unit * u % 128 + unit
            ]

    mod = mod_o[...]
    source = tok[...].astype(F32)
    n1, _ = norm_parts(source)
    normed = (n1 * (1.0 + mod[1:2]) + mod[0:1]).astype(B16)
    normed_o[...] = normed
    for m in both_mats:
        lead.take_y(m, NZ - 1)
    for m in both_mats:
        lead.finish(m)
    keep = [
        pltpu.make_async_copy(qkv, qkv_o, wsem.at[2]),
        pltpu.make_async_copy(outw, outw_o, wsem.at[3]),
    ]
    for copy in keep:
        copy.start()

    for k in range(3):
        part_k = dot(normed, qkv[:, k * width : (k + 1) * width])
        if k != 1:
            part_k = part_k + bias_o[k // 2 : k // 2 + 1, :]
        proj_o[:, k * width : (k + 1) * width] = part_k.astype(B16)
    lane = lax.broadcasted_iota(jnp.int32, (length, 128), 1)
    low_lane = lane < HEAD_DIM
    lsum = jnp.zeros((length, 128), F32)
    for p in range(HEADS // 2):
        q2 = proj_o[:, 128 * p : 128 * (p + 1)]
        k2 = proj_o[:, width + 128 * p : width + 128 * (p + 1)]
        v2 = proj_o[:, 2 * width + 128 * p : 2 * width + 128 * (p + 1)]
        outs = []
        for h in range(2):
            mine = low_lane if h == 0 else jnp.logical_not(low_lane)
            s = dot_nt(jnp.where(mine, q2, jnp.zeros_like(q2)), k2) * SCALE
            peak = jnp.max(s, axis=-1, keepdims=True)
            e = jnp.exp(s - peak)
            tot = jnp.sum(e, axis=-1, keepdims=True)
            lsum = jnp.where(lane == 2 * p + h, peak + jnp.log(tot), lsum)
            outs.append(dot((e / tot).astype(B16), v2))
        mixed_o[:, 128 * p : 128 * (p + 1)] = jnp.where(low_lane, outs[0], outs[1]).astype(B16)
    lsum_o[...] = lsum
    att = dot(mixed_o[...], outw[...]) + bias_o[2:3, :]
    att_o[...] = att
    resid = source + mod[2:3] * att
    resid_o[...] = resid
    n2, _ = norm_parts(resid)
    second = (n2 * (1.0 + mod[4:5]) + mod[3:4]).astype(B16)
    second_o[...] = second

    lane8 = lax.broadcasted_iota(jnp.int32, (length, E), 1)
    two = (
        lax.broadcasted_iota(jnp.int32, (2, 128), 0) == lax.broadcasted_iota(jnp.int32, (2, 128), 1)
    )
    route_cols = dot_tn(
        routes[...].astype(F32).astype(B16), jnp.where(two, 1.0, 0.0).astype(B16)
    ).astype(jnp.int32)
    route = [route_cols[:, k : k + 1] for k in range(2)]
    picks = [(r == lane8) for r in route]
    both = jnp.where(picks[0], 1.0, 0.0) + jnp.where(picks[1], 1.0, 0.0)
    earlier = (
        lax.broadcasted_iota(jnp.int32, (length, length), 1)
        < lax.broadcasted_iota(jnp.int32, (length, length), 0)
    )
    rank = dot(jnp.where(earlier, 1.0, 0.0).astype(B16), both.astype(B16))
    places = []
    for k in range(2):
        slot = jnp.sum(jnp.where(picks[k], rank, 0.0), axis=-1, keepdims=True).astype(jnp.int32)
        places.append(jnp.where(slot < CAP, route[k] * CAP + slot, -1))
    place_o[...] = jnp.where(
        lane == 0,
        places[0],
        jnp.where(lane == 1, places[1], jnp.where(lane == 2, route[0], route[1])),
    )
    maps = [jnp.where(choose_rows(v, E * CAP), 1.0, 0.0) for v in places]
    sbuf[...] = dot_tn((maps[0] + maps[1]).astype(B16), second).astype(B16)
    give_rows = PlaneExchange(sbuf, rows, ds0, dr0)
    give_rows.start()
    logits = dot_nt(second, rt_o[...].astype(B16))
    chosen = [jnp.sum(jnp.where(pick, logits, 0.0), axis=-1, keepdims=True) for pick in picks]
    top = jnp.maximum(chosen[0], chosen[1])
    e2 = [jnp.exp(v - top) for v in chosen]
    gates = [v / (e2[0] + e2[1]) for v in e2]
    gates_o[...] = jnp.where(lane == 0, gates[0], jnp.where(lane == 1, gates[1], 0.0))
    moe_grad = (mod[5:6] * cot[...].astype(F32)).astype(B16).astype(F32)
    pair = [(g * moe_grad).astype(B16) for g in gates]
    gbuf[...] = (
        dot_tn(maps[0].astype(B16), pair[0]) + dot_tn(maps[1].astype(B16), pair[1])
    ).astype(B16)
    give_grads = PlaneExchange(gbuf, grads, ds1, dr1)
    give_grads.start()
    for column in later:
        column.take(1)

    first_x = x == 0
    acc[...] = jnp.zeros_like(acc) + jnp.where(first_x, bout_r[0:1, :], bout_r[1:2, :]).astype(F32)
    for load in loads:
        load.wait()
    for column in later:
        column.take(2)
    give_rows.wait_in()

    end = jnp.logical_or(z == 0, z == NZ - 1)
    inner = jnp.logical_not(end)
    partner = dev(z + 1 - 2 * lax.rem(z, 2), x, y, c)

    def far_copy(i):
        source, target = ((rows, far_rows), (grads, far_grads))[i]
        return remote(source, target, fsem.at[0, i], fsem.at[1, i], partner)

    pl.when(end)(lambda: far_copy(0).start())
    for column in later:
        column.push(1)

    def span(f):
        return pl.ds(pl.multiple_of(f * CHUNK, 128), CHUNK)

    def put_in(f):
        return pltpu.make_async_copy(dwin.at[:, span(f)], dwin_o.at[:, span(f)], osem.at[1, f])

    def put_out(f):
        return pltpu.make_async_copy(dwout.at[span(f), :], dwout_o.at[span(f), :], osem.at[0, f])

    def bias_of(cols):
        return jnp.where(first_x, bin_r[0:1, cols], bin_r[1:2, cols]).astype(F32)

    def forward(f, carry):
        cols = span(f)
        pre = dot(rows[...], win[:, cols]) + bias_of(cols)
        pres[:, cols] = pre
        low = gelu(pre).astype(B16)
        acc[...] += dot(low, wout[cols, :])
        return carry

    count = hidden // CHUNK
    lax.fori_loop(0, count, forward, 0)
    res[...] = acc[...].astype(B16)
    give_res = PlaneExchange(res, ret_o, ds2, dr2)
    give_res.start()
    for column in later:
        column.push(2)
        column.take(3)
        column.push(3)
    for column, spread in zip(later, spreads):
        column.keep().wait()
        spread.near()
    pass_x(0)
    pass_x(1)
    give_grads.wait_in()
    pl.when(end)(lambda: far_copy(1).start())
    acc[...] = jnp.zeros_like(acc)
    ebias[...] = jnp.zeros_like(ebias)
    column_sum = jnp.sum(grads[...].astype(F32), axis=0, keepdims=True)
    for j in range(per):
        at = hidden // 128 + j
        ebias[at : at + 1, :] = column_sum[:, 128 * j : 128 * (j + 1)]

    def backward(f, carry):
        cols = span(f)
        act, slope = gelu_parts(pres[:, cols])
        pre = (dot_nt(grads[...], wout[cols, :]) * slope).astype(B16)
        acc[...] += dot_nt(pre, win[:, cols])
        col = jnp.sum(pre.astype(F32), axis=0, keepdims=True)
        for j in range(CHUNK // 128):
            ebias[pl.ds(f * (CHUNK // 128) + j, 1), :] = col[:, 128 * j : 128 * (j + 1)]

        @pl.when(inner)
        def _():
            dwout[cols, :] = dot_tn(act.astype(B16), grads[...]).astype(B16)
            dwin[:, cols] = dot_tn(rows[...], pre).astype(B16)

        return carry

    lax.fori_loop(0, count, backward, 0)
    bgr[...] = acc[...].astype(B16)
    give_bgr = PlaneExchange(bgr, retg_o, ds3, dr3)
    give_bgr.start()

    mate = NZ - 1 - z

    def across():
        start = lax.div(mate, 2) * (hidden // 2)
        return remote(
            dwout.at[pl.ds(pl.multiple_of(start, 16), CHUNK), :], came_o, msem.at[0], msem.at[1], dev(mate, x, y, c)
        )

    def far(i, carry):
        f = lax.rem(i + lax.div(mate, 2) * (count // 2), count)
        cols = span(f)
        data, grad = far_rows[...], far_grads[...]
        act, slope = gelu_parts(dot(data, win[:, cols]) + bias_of(cols))
        pre = (dot_nt(grad, wout[cols, :]) * slope).astype(B16)
        dwout[cols, :] = (dwout[cols, :].astype(F32) + dot_tn(act.astype(B16), grad)).astype(B16)
        put_out(f).start()
        dwin[:, cols] = (dwin[:, cols].astype(F32) + dot_tn(data, pre)).astype(B16)
        put_in(f).start()
        pl.when(i == 0)(lambda: across().start())
        return carry

    pass_x(2)
    pass_x(3)
    pass_y(0)
    pass_y(1)

    @pl.when(inner)
    def _():
        far_copy(0).wait_recv()
        far_copy(1).wait_recv()
        lax.fori_loop(0, count, far, 0)

    pass_y(2)
    pass_y(3)
    for spread in spreads:
        spread.finish()

    @pl.when(inner)
    def _():
        across().wait()

    for column in later:
        column.finish()
    for exchange in (give_res, give_bgr):
        exchange.wait_in()
    for exchange in (give_rows, give_grads, give_res, give_bgr):
        exchange.wait_out()
    peers(lambda p: first(p, p).wait_send())
    peers(lambda p: second_hop(p, p).wait_send())
    for copy in keep:
        copy.wait()

    @pl.when(end)
    def _():
        far_copy(0).wait_send()
        far_copy(1).wait_send()

    @pl.when(inner)
    def _():
        for f in range(count):
            put_out(f).wait()
            put_in(f).wait()


def lead_part(tok, cot, route, cond, ada, adab, qvb, outb, soutb, sinb, router, bin_r, bout_r, shards, win, wout):
    n = NZ * NX
    length, width = tok.shape
    hidden = win.shape[2]
    slots = E * CAP
    dma = pltpu.SemaphoreType.DMA
    vm = pltpu.VMEM
    tiles = (ada.shape[1] // 128 + 7) // 8 * 8
    wide = [sds((n * s.shape[0], s.shape[1]), B16) for s in shards[:2]]
    outs = [
        sds((length, width), B16),
        sds((length, 3 * width), B16),
        sds((length, 128), F32),
        sds((length, width), B16),
        sds((length, width), F32),
        sds((length, width), F32),
        sds((length, width), B16),
        sds((length, 128), F32),
        sds((length, 128), jnp.int32),
        sds((8, width), F32),
        sds((8, width), F32),
        sds((1, hidden), F32),
        sds((E, width), F32),
        sds((8, 128), F32),
        sds((32, 128), F32),
    ]
    back = [sds((slots, width), B16)] * 2
    wide += [sds((NZ, NX) + s.shape, B16) for s in shards[2:]]
    far = back + wide + [
        sds((width, hidden), B16),
        sds((hidden, width), B16),
        sds((CHUNK, width), B16),
    ]
    return pl.pallas_call(
        lead_kernel,
        out_shape=outs + far,
        in_specs=[VM] * 13 + [HB] * 6,
        out_specs=[VM] * len(outs) + [HB] * len(far),
        scratch_shapes=[
            vm((32, 128), F32),
            vm((n, 32, 128), F32),
            vm((n, tiles, 128), F32),
            vm((n, tiles, 128), F32),
            vm(wide[0].shape, B16),
            vm(wide[1].shape, B16),
            vm((slots, width), B16),
            vm((slots, width), B16),
            vm((slots, width), B16),
            vm((slots, width), B16),
            vm((slots, width), B16),
            vm((slots, width), B16),
            vm((slots, width), B16),
            vm((slots, width), B16),
            vm((width, hidden), B16),
            vm((hidden, width), B16),
            vm((width, hidden), B16),
            vm((hidden, width), B16),
            vm((slots, hidden), F32),
            vm((slots, width), F32),
        ]
        + [vm((NZ * s.shape[0], s.shape[1] // 2), B16) for s in shards[2:]]
        + [vm((NZ * s.shape[0] // 2, s.shape[1] // 2), B16) for s in shards[2:]]
        + [
            dma((n,)),
            dma((n,)),
            dma((n,)),
            dma((n,)),
        ]
        + [dma((E,))] * 8
        + [dma((4,)), dma((2, hidden // CHUNK)), dma((2, 2)), dma((2,))]
        + Gather.semaphores(2)
        + Column.semaphores()
        + Column.semaphores()
        + Spread.semaphores()
        + Spread.semaphores(),
        compiler_params=params(1),
        name="front_and_expert",
    )(tok, cot, route, cond, ada, adab, qvb, outb, soutb, sinb, router, bin_r, bout_r, *shards, win, wout)


def middle_kernel(
    ret, retg, dwout, second_r, resid_r, att_r, cot, mod, sin_h, sout_h, sinb, bias, router, gates_r, place_r,
    mixed, outw,
    came_o, out_o, rgrad_o, mgrad_o, sin_half, sout_half, dout, drouter, vecs, mg2,
    sin, sout, dsin, dsout, hsem, msem, lsem, shared, sgrad,
):
    chunks = range(NZ)
    size = sin.shape[3] // NZ
    loads = []
    for f in chunks:
        cols = slice(f * size, (f + 1) * size)
        loads.append(
            (
                pltpu.make_async_copy(sin_h.at[:, :, :, cols], sin.at[:, :, :, cols], lsem.at[0, f]),
                pltpu.make_async_copy(sout_h.at[f], sout.at[f], lsem.at[1, f]),
            )
        )
        for load in loads[-1]:
            load.start()
    barrier = pltpu.get_barrier_semaphore()
    z, x, y, c = coords()
    mate = NZ - 1 - z
    greet(barrier, dev(mate, x, y, c))
    greet(barrier, dev(z, x, y, 1 - c))
    pl.semaphore_wait(barrier, 2)
    central = jnp.logical_and(z > 0, z < NZ - 1)

    def across():
        rows = dwout.shape[0] // 2
        start = pl.multiple_of(lax.div(mate, 2) * rows + CHUNK, 16)
        return remote(
            dwout.at[pl.ds(start, rows - CHUNK), :], came_o, msem.at[0], msem.at[1], dev(mate, x, y, c)
        )

    pl.when(central)(lambda: across().start())
    length, width = second_r.shape
    hidden = sin.shape[3]
    chunk = hidden // NZ
    second = second_r[...]
    grad_out = cot[...].astype(F32)
    moe_low = (mod[5:6] * grad_out).astype(B16)
    moe_grad = moe_low.astype(F32)
    shared[...] = jnp.zeros_like(shared) + bias[3:4, :]
    sgrad[...] = jnp.zeros_like(sgrad)
    vecs[...] = jnp.zeros_like(vecs)

    def body(f):
        for load in loads[f]:
            load.wait()
        cols = slice(f * chunk, (f + 1) * chunk)
        w1 = sin[:, :, :, cols].reshape(width, chunk)
        w2 = sout[f].reshape(chunk, width)
        act, slope = gelu_parts(dot(second, w1) + sinb[:, cols])
        low = act.astype(B16)
        shared[...] += dot(low, w2)
        pre = (dot_nt(moe_low, w2) * slope).astype(B16)
        dsout[cols, :] = dot_tn(low, moe_low).astype(B16)
        dsin[:, cols] = dot_tn(second, pre).astype(B16)
        sgrad[...] += dot_nt(pre, w1)
        col = jnp.sum(pre.astype(F32), axis=0, keepdims=True)
        for j in range(chunk // 128):
            at = f * (chunk // 128) + j
            vecs[at : at + 1, :] = col[:, 128 * j : 128 * (j + 1)]

    for f in chunks:
        body(f)
    halves = ((dsin, sin_half), (dsout, sout_half))

    def half_cols(i, core):
        size = halves[i][1].shape[1]
        return pl.ds(pl.multiple_of(core * size, 128), size)

    def half_copy(i):
        return remote(
            halves[i][0].at[:, half_cols(i, 1 - c)], halves[i][1], hsem.at[0, i], hsem.at[1, i],
            dev(z, x, y, 1 - c),
        )

    for i in range(2):
        half_copy(i).start()
    lane = lax.broadcasted_iota(jnp.int32, (length, E), 1)
    gates = [gates_r[:, k : k + 1] for k in range(2)]
    maps = [
        jnp.where(choose_rows(place_r[:, k : k + 1], E * CAP), 1.0, 0.0) for k in range(2)
    ]
    back = ret[...]
    rows = [dot(m.astype(B16), back) for m in maps]
    moe = shared[...] + (gates[0] * rows[0] + gates[1] * rows[1])
    resid = resid_r[...]
    out_o[...] = (resid + mod[5:6] * moe).astype(B16)
    mg2[...] = jnp.zeros_like(mg2)
    mg2[5:6, :] = jnp.sum(grad_out * moe, axis=0, keepdims=True)
    ggrad = [jnp.sum(moe_grad * r, axis=-1, keepdims=True) for r in rows]
    inner = gates[0] * ggrad[0] + gates[1] * ggrad[1]
    lgrad = jnp.zeros((length, E), F32)
    for k in range(2):
        pick = place_r[:, 2 + k : 3 + k] == lane
        lgrad = lgrad + jnp.where(pick, gates[k] * (ggrad[k] - inner), 0.0)
    lgrad = lgrad.astype(B16)
    drouter[...] = dot_tn(lgrad, second)
    grad = (
        sgrad[...]
        + dot((maps[0] + maps[1]).astype(B16), retg[...])
        + dot(lgrad, router[...].astype(B16))
    )
    n2, r2 = norm_parts(resid)
    mg2[3:4, :] = jnp.sum(grad, axis=0, keepdims=True)
    mg2[4:5, :] = jnp.sum(grad * n2, axis=0, keepdims=True)
    rgrad = grad_out + norm_back(grad * (1.0 + mod[4:5]), n2, r2)
    rgrad_o[...] = rgrad
    agrad = (mod[2:3] * rgrad).astype(B16)
    mg2[2:3, :] = jnp.sum(rgrad * att_r[...], axis=0, keepdims=True)
    dout[...] = dot_tn(mixed[...], agrad).astype(B16)
    mgrad_o[...] = dot_nt(agrad, outw[...]).astype(B16)
    sums = [
        jnp.sum(moe_grad, axis=0, keepdims=True),
        jnp.sum(agrad.astype(F32), axis=0, keepdims=True),
    ]
    base = hidden // 128
    for i, row in enumerate(sums):
        for j in range(width // 128):
            at = base + i * (width // 128) + j
            vecs[at : at + 1, :] = row[:, 128 * j : 128 * (j + 1)]
    for i in range(2):
        half_copy(i).wait_recv()
        whole, part = halves[i]
        step = part.shape[0] // 16

        def add(j, carry):
            at = pl.ds(pl.multiple_of(j * step, 16), step)
            own = whole[at, half_cols(i, c)].astype(F32)
            part[at, :] = (part[at, :].astype(F32) + own).astype(B16)
            return carry

        lax.fori_loop(0, 16, add, 0)
        half_copy(i).wait_send()
    pl.when(central)(lambda: across().wait())


def middle(*args):
    res, dwout, second, sin = args[0], args[2], args[3], args[8]
    length, width = second.shape
    rows, hidden = res.shape[0], sin.shape[3]
    dma = pltpu.SemaphoreType.DMA
    return pl.pallas_call(
        middle_kernel,
        out_shape=[
            sds((hidden // 2 - CHUNK, width), B16),
            sds((length, width), B16),
            sds((length, width), F32),
            sds((length, width), B16),
            sds((width, hidden // 2), B16),
            sds((hidden, width // 2), B16),
            sds((width, width), B16),
            sds((E, width), F32),
            sds((40, 128), F32),
            sds((8, width), F32),
        ],
        in_specs=[VM] * 2 + [HB] + [VM] * 5 + [HB] * 2 + [VM] * 7,
        out_specs=[HB] + [VM] * 9,
        scratch_shapes=[
            pltpu.VMEM(sin.shape, B16),
            pltpu.VMEM((NZ, NX, hidden // NZ // NX, width), B16),
            pltpu.VMEM((width, hidden), B16),
            pltpu.VMEM((hidden, width), B16),
            dma((2, 2)),
            dma((2,)),
            dma((2, NZ)),
            pltpu.VMEM((length, width), F32),
            pltpu.VMEM((length, width), F32),
        ],
        compiler_params=params(3),
        name="shared_expert_combine",
    )(*args)


def add_into(target, source, lead):
    count = 1
    for n in lead:
        count *= n

    def body(i, carry):
        at = []
        rest = i
        for n in reversed(lead):
            at.append(lax.rem(rest, n))
            rest = lax.div(rest, n)
        at = tuple(reversed(at))
        target[at] = (target[at].astype(F32) + source(at).astype(F32)).astype(B16)
        return carry

    lax.fori_loop(0, count, body, 0)


class Piece:
    def __init__(self, spec, grad, out, bufs, start=None):
        self.z, self.x, self.y, self.c = coords()
        self.half, self.row, self.rows, self.col, self.width, self.y_first = spec
        self.grad, self.out = grad, out
        self.origin = grad if start is None else start
        self.size = out.shape[-1] // 2
        if not self.half:
            self.cbuf, bufs = bufs[0], bufs[1:]
        self.ebuf, self.fbuf, self.zin, self.one, self.zsem = bufs

    @staticmethod
    def scratch(spec):
        half, _, rows, _, width, _ = spec
        vm = lambda *lead: pltpu.VMEM(lead + (rows, width), B16)
        dma = pltpu.SemaphoreType.DMA
        return ([] if half else [vm(NZ, NX, 2)]) + [
            vm(NZ, 2),
            vm(NZ),
            vm(NZ),
            dma((13,)),
            dma((2, NZ)),
        ]

    def cols(self, c):
        return pl.ds(pl.multiple_of(c * self.size + self.col, 128), self.width)

    def core_view(self, *lead):
        if not self.half:
            return self.cbuf.at[lead]
        inner = (slice(self.row, self.row + self.rows), slice(self.col, self.col + self.width))
        return self.origin.at[lead + inner]

    def core_value(self, *lead):
        if not self.half:
            return self.cbuf[lead]
        inner = (slice(self.row, self.row + self.rows), slice(self.col, self.col + self.width))
        return self.grad[lead + inner]

    def core_copy(self):
        return remote(
            self.grad.at[:, :, :, :, self.cols(1 - self.c)],
            self.cbuf,
            self.one.at[0],
            self.one.at[1],
            dev(self.z, self.x, self.y, 1 - self.c),
        )

    def to_x(self):
        return dev(self.z, 1 - self.x, self.y, self.c)

    def to_y(self):
        return dev(self.z, self.x, 1 - self.y, self.c)

    def copy1(self):
        every = slice(None)
        if self.y_first:
            source, to = self.core_view(every, every, 1 - self.y), self.to_y()
        else:
            source, to = self.core_view(every, 1 - self.x, every), self.to_x()
        return remote(source, self.ebuf, self.one.at[3], self.one.at[4], to)

    def copy2(self):
        if self.y_first:
            source, to = self.ebuf.at[:, 1 - self.x], self.to_x()
        else:
            source, to = self.ebuf.at[:, 1 - self.y], self.to_y()
        return remote(source, self.fbuf, self.one.at[5], self.one.at[6], to)

    def zcopy(self, zb, at):
        return remote(
            self.fbuf.at[zb],
            self.zin.at[at],
            self.zsem.at[0, zb],
            self.zsem.at[1, at],
            dev(zb, self.x, self.y, self.c),
        )

    def others(self, action):
        for zb in range(NZ):

            @pl.when(zb != self.z)
            def _():
                action(zb)

    def own(self):
        return self.fbuf.at[self.z]

    def place(self, y, c):
        return self.out.at[y, self.row : self.row + self.rows, self.cols(c)]

    def keep(self):
        return pltpu.make_async_copy(self.own(), self.place(self.y, self.c), self.one.at[7])

    def give_y(self, came=False):
        at = self.place(1 - self.y if came else self.y, self.c)
        return remote(self.own(), at, self.one.at[8], self.one.at[9], self.to_y())

    def give_c(self, came=False):
        at = self.place(self.y, 1 - self.c if came else self.c)
        to = dev(self.z, self.x, self.y, 1 - self.c)
        return remote(self.own(), at, self.one.at[10], self.one.at[11], to)

    def pass_c(self, came=False):
        at = self.place(1 - self.y, 1 - self.c if came else self.c)
        to = dev(self.z, self.x, self.y, 1 - self.c)
        return remote(at, at, self.one.at[12], self.one.at[2], to)

    def stage(self, s):
        if s == 0:
            if not self.half:
                self.core_copy().wait_recv()
                mine = self.cols(self.c)
                add_into(self.cbuf, lambda i: self.grad[i[0], i[1], i[2], :, mine], (NZ, NX, 2))
            self.copy1().start()
        elif s == 1:
            self.copy1().wait_recv()
            if self.y_first:
                add_into(self.ebuf, lambda i: self.core_value(i[0], i[1], self.y), (NZ, NX))
            else:
                add_into(self.ebuf, lambda i: self.core_value(i[0], self.x, i[1]), (NZ, 2))
            self.copy2().start()
        elif s == 2:
            self.copy2().wait_recv()
            side = self.x if self.y_first else self.y
            add_into(self.fbuf, lambda i: self.ebuf[i[0], side], (NZ,))
            self.others(lambda zb: self.zcopy(zb, self.z).start())
        elif s == 3:
            self.zin[self.z] = self.fbuf[self.z]
            self.others(lambda zb: self.zcopy(zb, zb).wait_recv())
            total = self.zin[0].astype(F32)
            for zb in range(1, NZ):
                total = total + self.zin[zb].astype(F32)
            self.fbuf[self.z] = total.astype(B16)
            self.give_y().start()
            self.give_c().start()
            self.keep().start()
        elif s == 4:
            self.give_y(True).wait_recv()
            self.pass_c().start()
        elif s == 5:
            self.keep().wait()
            self.give_c(True).wait_recv()
            self.pass_c(True).wait_recv()
            if not self.half:
                self.core_copy().wait_send()
            self.copy1().wait_send()
            self.copy2().wait_send()
            self.give_y().wait_send()
            self.give_c().wait_send()
            self.pass_c().wait_send()
            self.others(lambda zb: self.zcopy(zb, zb).wait_send())


class MidSum:
    COUNT = 6

    def __init__(self, origin, grad, into, out, total, outer, sems):
        self.z, self.x, self.y, self.c = coords()
        self.origin = origin
        self.grad, self.into, self.out, self.total, self.outer = grad, into, out, total, outer
        self.sems = sems
        self.size = grad.shape[2] // self.COUNT
        self.inner = jnp.logical_and(self.z > 0, self.z < NZ - 1)
        self.end = jnp.logical_not(self.inner)
        self.mate = NZ - 1 - self.z

    @staticmethod
    def scratch(shape):
        vm = pltpu.VMEM
        return [vm(shape[1:], B16), vm(shape[1:], B16), pltpu.SemaphoreType.DMA((9, MidSum.COUNT))]

    def cols(self, p):
        return slice(p * self.size, (p + 1) * self.size)

    @staticmethod
    def beside(z):
        return z + 1 - 2 * lax.rem(z, 2)

    def landing(self, z, block):
        rows = self.grad.shape[1]
        return pl.ds(pl.multiple_of((block - 2 * lax.div(z, 2)) * rows, 16), rows)

    def across(self, i, p, came=False):
        z = self.z if came else self.mate
        block = self.beside(z) if i == 0 else z
        return remote(
            self.origin.at[block, :, self.cols(p)],
            self.into.at[self.landing(z, block), self.cols(p)],
            self.sems.at[i, p],
            self.sems.at[2 + i, p],
            dev(self.mate, self.x, self.y, self.c),
        )

    def came(self, block, p):
        return self.into[self.landing(self.z, block), self.cols(p)].astype(F32)

    def outward(self, p):
        return remote(
            self.outer.at[:, self.cols(p)],
            self.total.at[:, self.cols(p)],
            self.sems.at[4, p],
            self.sems.at[5, p],
            dev(self.beside(self.z), self.x, self.y, self.c),
        )

    def begin(self, i, p):
        pl.when(self.inner)(lambda: self.across(i, p).start())

    def give(self, p, sent=True):
        @pl.when(self.inner)
        def _():
            if sent:
                self.across(0, p, True).wait_recv()
            cols = self.cols(p)
            self.outer[:, cols] = (
                self.grad[self.beside(self.z), :, cols].astype(F32) + self.came(self.beside(self.z), p)
            ).astype(B16)
            self.outward(p).start()

    def swap(self, p, came=False):
        part = self.total.shape[0] // NX
        start = pl.multiple_of((1 - self.x) * part, 16)
        return remote(
            self.total.at[pl.ds(start, part), self.cols(p)],
            self.out.at[1 - self.x if came else self.x, :, self.cols(p)],
            self.sems.at[6, p],
            self.sems.at[7, p],
            dev(self.z, 1 - self.x, self.y, self.c),
        )

    def keep(self, p):
        part = self.total.shape[0] // NX
        start = pl.multiple_of(self.x * part, 16)
        return pltpu.make_async_copy(
            self.total.at[pl.ds(start, part), self.cols(p)],
            self.out.at[self.x, :, self.cols(p)],
            self.sems.at[8, p],
        )

    def final(self, p, sent=True):
        @pl.when(self.inner)
        def _():
            if sent:
                self.across(1, p, True).wait_recv()
            cols = self.cols(p)
            self.total[:, cols] = (
                self.grad[self.z, :, cols].astype(F32) + self.came(self.z, p)
            ).astype(B16)

        pl.when(self.end)(lambda: self.outward(p).wait_recv())
        self.swap(p).start()
        self.keep(p).start()

    def close(self, sent=True):
        for p in range(self.COUNT):

            @pl.when(self.inner)
            def _():
                self.outward(p).wait_send()
                if sent:
                    self.across(0, p).wait_send()
                    self.across(1, p).wait_send()

            self.swap(p, True).wait_recv()
            self.swap(p).wait_send()
            self.keep(p).wait()


def piece_specs(width, hidden):
    rows, tall = width // NZ // 4, hidden // NZ // 4
    qkv = 3 * width // 2
    left = (qkv // 128 + 1) // 2 * 128
    early = (
        (2, (True, 0, rows, 0, hidden // 4, True)),
        (3, (True, 0, tall // 2, 0, width // 2, False)),
        (2, (True, 0, rows, hidden // 4, hidden // 4, False)),
        (3, (True, tall // 2, tall // 2, 0, width // 2, True)),
    )
    late = (
        (0, (False, 0, rows, 0, left, True)),
        (0, (False, 0, rows, left, qkv - left, True)),
        (1, (False, 0, rows, 0, width // 2, True)),
    )
    return early, late


def tail_kernel(*refs):
    sin_half_h, sout_half_h, dout, dwin_h, dwout_h, came_a, came_b = refs[:7]
    tok, mod, normed, proj, lsum, mgrad, rgrad, qkv_h, mg2, vecs, drouter, ebias, condt, ada = refs[7:21]
    outs = refs[21:25]
    pair_in, pair_out, tgrad_o, small, esum, tiles, cgot = refs[25:32]
    rest = list(refs[32:])
    z, x, y, c = coords()
    dp, ex = lax.axis_index("dp"), lax.axis_index("expert")
    n = NZ * NX
    length, width = tok.shape
    per = width // 128
    early_specs, late_specs = piece_specs(width, 2 * sin_half_h.shape[4])
    dqkv, pgrad, sin_half, sout_half, dwin, dwout, qkv, lsem = rest[:8]
    rest = rest[8:]
    sources = (dqkv, dout, sin_half, sout_half)
    starts = (None, None, sin_half_h, sout_half_h)

    def make(specs, rest):
        made = []
        for matrix, spec in specs:
            count = len(Piece.scratch(spec))
            made.append(
                Piece(spec, sources[matrix], outs[matrix], rest[:count], starts[matrix])
            )
            rest = rest[count:]
        return made, rest

    early, rest = make(early_specs, rest)
    late, rest = make(late_specs, rest)
    wide = MidSum(dwin_h, dwin, rest[0], pair_in, *rest[1:4])
    tall = MidSum(dwout_h, dwout, rest[4], pair_out, *rest[5:8])
    rest = rest[8:]
    first_rows = came_a.shape[0]
    loads = [
        pltpu.make_async_copy(came_a, tall.into.at[0:first_rows, :], lsem.at[0]),
        pltpu.make_async_copy(came_b, tall.into.at[first_rows:, :], lsem.at[1]),
        pltpu.make_async_copy(dwout_h, dwout, lsem.at[2]),
        pltpu.make_async_copy(sin_half_h, sin_half, lsem.at[3]),
        pltpu.make_async_copy(sout_half_h, sout_half, lsem.at[4]),
        pltpu.make_async_copy(qkv_h, qkv, lsem.at[5]),
        pltpu.make_async_copy(dwin_h, dwin, lsem.at[6]),
    ]
    ssum, sgot, zgot, esend, egot, mine, csend, sems, dsem, zsem, tsem = rest

    barrier = pltpu.get_barrier_semaphore()

    def peers(action):
        for p in range(n):

            @pl.when(p != dp)
            def _():
                action(p)

    peers(lambda p: greet(barrier, (p, ex)))
    mates = (dev(z, x, 1 - y, c), dev(z, x, y, 1 - c), dev(z, x, 1 - y, 1 - c))
    for mate in mates:
        greet(barrier, mate)
    pl.semaphore_wait(barrier, n - 1 + 3)

    every = range(MidSum.COUNT)
    for i in range(2):
        for p in every:
            wide.begin(i, p)
    for piece in early:
        piece.stage(0)
    late[2].core_copy().start()
    for load in loads:
        load.start()
    for load in loads[:3]:
        load.wait()
    for p in every:
        tall.give(p, False)

    low_lane = lax.broadcasted_iota(jnp.int32, (length, 128), 1) < HEAD_DIM
    for p in range(HEADS // 2):
        q2 = proj[:, 128 * p : 128 * (p + 1)]
        k2 = proj[:, width + 128 * p : width + 128 * (p + 1)]
        v2 = proj[:, 2 * width + 128 * p : 2 * width + 128 * (p + 1)]
        m2 = mgrad[:, 128 * p : 128 * (p + 1)]
        parts = []
        for h in range(2):
            head = low_lane if h == 0 else jnp.logical_not(low_lane)
            zero = jnp.zeros_like(q2)
            s = dot_nt(jnp.where(head, q2, zero), k2) * SCALE
            prob = jnp.exp(s - lsum[:, 2 * p + h : 2 * p + h + 1])
            pg = dot_nt(jnp.where(head, m2, zero), v2)
            inner = jnp.sum(prob * pg, axis=-1, keepdims=True)
            sg = (prob * (pg - inner)).astype(B16)
            parts.append(
                (dot(sg, k2) * SCALE, dot_tn(sg, q2) * SCALE, dot_tn(prob.astype(B16), m2))
            )
        for i in range(3):
            pgrad[:, i * width + 128 * p : i * width + 128 * (p + 1)] = jnp.where(
                low_lane, parts[0][i], parts[1][i]
            ).astype(B16)
    lead = dqkv.shape[:4]
    for i in range(3):
        cols = slice(i * width, (i + 1) * width)
        dqkv[:, :, :, :, cols] = dot_tn(normed[...], pgrad[:, cols]).astype(B16).reshape(lead + (width,))
    for piece in late[:2]:
        piece.core_copy().start()

    rows = vecs.shape[0]
    ssum[0:rows, :] = vecs[...]
    for i, k in enumerate((0, 2)):
        row = jnp.sum(pgrad[:, k * width : (k + 1) * width].astype(F32), axis=0, keepdims=True)
        for j in range(per):
            at = rows + i * per + j
            ssum[at : at + 1, :] = row[:, 128 * j : 128 * (j + 1)]
    for at in range(rows + 2 * per, rows + 16):
        ssum[at : at + 1, :] = jnp.zeros((1, 128), F32)
    for b in range(per):
        ssum[rows + 16 + 8 * b : rows + 24 + 8 * b, :] = drouter[:, 128 * b : 128 * (b + 1)]
    hops = (dev(z, x, y, 1 - c), dev(z, x, 1 - y, c), dev(z, 1 - x, y, c))

    def hop(i):
        return remote(zgot.at[4 + i], sgot.at[i], sems.at[0, i], sems.at[1, i], hops[i])

    def ehop(came=False):
        return remote(
            esend.at[x], egot.at[z, 1 - x if came else x], sems.at[0, 3], sems.at[1, 3], hops[2]
        )

    def tile(p, at):
        return remote(mine, tiles.at[ex, at], dsem.at[0, p], dsem.at[1, at], (p, ex))

    def spread(i, theirs=False):
        e2 = 2 * (1 - y if i != 1 else y) + (1 - c if i != 0 else c)
        block = tiles.at[e2 if theirs else ex]
        return remote(block, block, tsem.at[0, i], tsem.at[1, i], mates[i])

    def cond_copy(p, at):
        return remote(csend.at[p], cgot.at[at], dsem.at[2, p], dsem.at[3, at], (p, ex))

    def zsum(zb, at):
        return remote(ssum, zgot.at[at], zsem.at[0, zb], zsem.at[1, at], dev(zb, x, y, c))

    def zexp(zb, at):
        return remote(
            egot.at[at], egot.at[at], zsem.at[2, zb], zsem.at[3, at], dev(zb, x, y, c)
        )

    def lines(action):
        for zb in range(NZ):

            @pl.when(zb != z)
            def _():
                action(zb)

    def start_hop(i):
        zgot[4 + i] = ssum[...]
        hop(i).start()

    def end_hop(i):
        hop(i).wait()
        ssum[...] = ssum[...] + sgot[i]

    start_hop(0)
    esend[x] = ebias[...]
    egot[z, x] = ebias[...]
    ehop().start()

    for load in loads[3:]:
        load.wait()
    ngrad = dot_nt(pgrad[...], qkv[...])
    n1, r1 = norm_parts(tok[...].astype(F32))
    tgrad_o[...] = rgrad[...] + norm_back(ngrad * (1.0 + mod[1:2]), n1, r1)
    mod_rows = [
        jnp.sum(ngrad, axis=0, keepdims=True),
        jnp.sum(ngrad * n1, axis=0, keepdims=True),
    ] + [mg2[i : i + 1, :] for i in range(2, 6)]
    mine[...] = jnp.zeros_like(mine)
    for i, row in enumerate(mod_rows):
        row = row.astype(B16).astype(F32)
        for j in range(per):
            mine[i * per + j : i * per + j + 1, :] = row[:, 128 * j : 128 * (j + 1)]
    mine[40:48, :] = condt[...]
    peers(lambda p: tile(p, dp).start())
    tiles[ex, dp] = mine[...]

    def small1():
        end_hop(0)
        start_hop(1)
        peers(lambda p: tile(p, p).wait_recv())
        for i in range(3):
            spread(i).start()
        acc = jnp.zeros((n, ada.shape[0]), F32)
        for j in range(ada.shape[1] // 128):
            acc = acc + dot_nt(tiles[ex, :, j, :].astype(B16), ada[:, 128 * j : 128 * (j + 1)])
        csend[...] = jnp.zeros_like(csend)
        csend[:, 0, 0 : ada.shape[0]] = acc
        peers(lambda p: cond_copy(p, dp).start())
        cgot[dp] = csend[dp]

    def small2():
        end_hop(1)
        start_hop(2)
        ehop().wait_send()
        ehop(True).wait_recv()
        lines(lambda zb: zexp(zb, z).start())

    def small3():
        end_hop(2)
        zgot[z] = ssum[...]
        lines(lambda zb: zsum(zb, z).start())

    def small4():
        lines(lambda zb: zexp(zb, zb).wait_recv())
        lines(lambda zb: zsum(zb, zb).wait_recv())
        total, etotal = zgot[0], egot[0]
        for i in range(1, NZ):
            total = total + zgot[i]
            etotal = etotal + egot[i]
        small[...] = total
        esum[...] = etotal

    def small5():
        peers(lambda p: cond_copy(p, p).wait_recv())
        for i in range(3):
            spread(i, True).wait_recv()
            spread(i).wait_send()
        peers(lambda p: tile(p, p).wait_send())
        peers(lambda p: cond_copy(p, p).wait_send())
        lines(lambda zb: zexp(zb, zb).wait_send())
        lines(lambda zb: zsum(zb, zb).wait_send())

    def run(pieces, s):
        for piece in pieces:
            piece.stage(s)

    run(early[:2], 1)
    run(late, 0)
    for p in every:
        tall.final(p, False)
    run(early[2:], 1)
    for p in every[:3]:
        wide.give(p)
    run(early, 2)
    small1()
    for p in every[3:]:
        wide.give(p)
    run(late, 1)
    small2()
    for p in every[:3]:
        wide.final(p)
    run(early, 3)
    small3()
    run(late, 2)
    for p in every[3:]:
        wide.final(p)
    run(early, 4)
    small4()
    run(late, 3)
    run(early, 5)
    small5()
    run(late, 4)
    run(late, 5)
    tall.close(False)
    wide.close()


def tail_part(sin_half, sout_half, dout, dwin, dwout, came_a, came_b, *others):
    n = NZ * NX
    dma = pltpu.SemaphoreType.DMA
    vm = pltpu.VMEM
    tok, qkv, vecs = others[0], others[7], others[9]
    width, hidden = qkv.shape[0], 2 * sin_half.shape[1]
    split = lambda g: g.reshape(NZ, NX, 2, g.shape[0] // (4 * NZ), g.shape[1])
    rows, tall = width // NZ // 4, hidden // NZ // 4
    outs = [
        sds((2, rows, 3 * width), B16),
        sds((2, rows, width), B16),
        sds((2, rows, hidden), B16),
        sds((2, tall, width), B16),
    ]
    short = vecs.shape[0] + 16 + 8 * (width // 128)
    halves = [split(sin_half), split(sout_half)]
    scratch = [vm((NZ, NX, 2, rows, 3 * width), B16), vm((tok.shape[0], 3 * width), B16)]
    scratch += [vm(v.shape, B16) for v in (*halves, dwin, dwout, qkv)] + [dma((7,))]
    for specs in piece_specs(width, hidden):
        for _, spec in specs:
            scratch += Piece.scratch(spec)
    for shape in (dwin.shape, dwout.shape):
        scratch += [vm((2 * shape[1], shape[2]), B16)] + MidSum.scratch(shape)
    scratch += [
        vm((short, 128), F32),
        vm((3, short, 128), F32),
        vm((NZ + 3, short, 128), F32),
        vm((2, 32, 128), F32),
        vm((NZ, 2, 32, 128), F32),
        vm((48, 128), F32),
        vm((n, 8, 128), F32),
        dma((2, 4)),
        dma((4, n)),
        dma((4, NZ)),
        dma((2, 3)),
    ]
    out = pl.pallas_call(
        tail_kernel,
        out_shape=outs
        + [
            sds((NX, dwin.shape[1] // NX, dwin.shape[2]), B16),
            sds((NX, dwout.shape[1] // NX, dwout.shape[2]), B16),
            sds(tok.shape, F32),
            sds((short, 128), F32),
            sds((2, 32, 128), F32),
            sds((4, n, 48, 128), F32),
            sds((n, 8, 128), F32),
        ],
        in_specs=[HB] * 2 + [VM] + [HB] * 4 + [VM] * 7 + [HB] + [VM] * 6,
        out_specs=[HB] * 6 + [VM] * 5,
        scratch_shapes=scratch,
        compiler_params=params(4),
        name="attention_back_sums",
    )(*halves, split(dout), dwin, dwout, came_a, came_b, *others)
    return [o.reshape(-1, o.shape[2]) for o in out[:4]], out[4], out[5], out[6], out[7:]


def pick_part(flat, part, dp):
    chosen = jnp.zeros((flat.shape[0], part), flat.dtype)
    for p in range(NZ * NX):
        chosen = jnp.where(dp == p, flat[:, p * part : (p + 1) * part], chosen)
    return chosen


def finish_kernel(*refs):
    dense, pairs = refs[:4], refs[4:6]
    small, esum, tiles, cgot, cond = refs[6:11]
    outs = refs[11:17]
    ada_o, adab_o, qvb_o, outb_o, sinb_o, soutb_o, router_o, einb_o, eoutb_o, cond_o = refs[17:27]
    bufs, sems = refs[27:33], refs[33]
    dp = lax.axis_index("dp")
    n = NZ * NX
    copies = []
    for i in (4, 5, 2, 3, 0, 1):
        bufs[i][...] = (dense + pairs)[i][...].astype(F32)
        copies.append(pltpu.make_async_copy(bufs[i], outs[i], sems.at[i]))
        copies[-1].start()
    width = cond.shape[1]
    per, part = width // 128, width // n
    hidden = sinb_o.shape[1] * n
    base = hidden // 128
    images = tiles.shape[0] * tiles.shape[1]

    def flat(row, count=per):
        return jnp.concatenate([small[row + j : row + j + 1, :] for j in range(count)], axis=1)

    soutb_o[...] = pick_part(flat(base), part, dp)
    outb_o[...] = pick_part(flat(base + per), part, dp)
    qvb_o[0:1, :] = pick_part(flat(40), part, dp)
    qvb_o[1:2, :] = pick_part(flat(40 + per), part, dp)
    own = base // n
    for j in range(own):
        sinb_o[:, 128 * j : 128 * (j + 1)] = small[pl.ds(own * dp + j, 1), :]
        for i in range(NX):
            einb_o[i : i + 1, 128 * j : 128 * (j + 1)] = esum[i, pl.ds(own * dp + j, 1), :]
    for i in range(NX):
        row = jnp.concatenate([esum[i, base + j : base + j + 1, :] for j in range(per)], axis=1)
        eoutb_o[i : i + 1, :] = pick_part(row, part, dp)
    router = jnp.concatenate([small[56 + E * b : 56 + E * (b + 1), :] for b in range(per)], axis=1)
    router_o[...] = pick_part(router, part, dp)

    conds = jnp.concatenate(
        [tiles[:, :, 40 + j, :].reshape(images, 128) for j in range(per)], axis=1
    )
    conds = pick_part(conds, part, dp).astype(B16)
    sums = []
    for j in range(6 * per):
        mods = tiles[:, :, j, :].reshape(images, 128)
        ada_o[:, 128 * j : 128 * (j + 1)] = dot_tn(conds, mods.astype(B16))
        sums.append(jnp.sum(mods, axis=0, keepdims=True))
    adab_o[...] = pick_part(jnp.concatenate(sums, axis=1), adab_o.shape[1], dp)
    v = cond[...].astype(F32)
    sig = 1.0 / (1.0 + jnp.exp(-v))
    grad = jnp.concatenate([cgot[p, 0:1, 0:part] for p in range(n)], axis=1)
    cond_o[...] = grad * (sig * (1.0 + v * (1.0 - sig)))
    for copy in copies:
        copy.wait()


def finish(dense, pairs, small, esum, tiles, cgot, cond, hidden):
    n = NZ * NX
    width = cond.shape[1]
    part = width // n
    big = [sds(v.shape, F32) for v in (*dense, *pairs)]
    short = [
        sds((part, 6 * width), F32),
        sds((1, 6 * part), F32),
        sds((2, part), F32),
        sds((1, part), F32),
        sds((1, hidden // n), F32),
        sds((1, part), F32),
        sds((E, part), F32),
        sds((NX, hidden // n), F32),
        sds((NX, part), F32),
        sds((1, width), F32),
    ]
    return pl.pallas_call(
        finish_kernel,
        out_shape=big + short,
        in_specs=[VM] * 11,
        out_specs=[HB] * 6 + [VM] * 10,
        scratch_shapes=[pltpu.VMEM(v.shape, F32) for v in big] + [pltpu.SemaphoreType.DMA((6,))],
        compiler_params=params(),
        name="final_form",
    )(*dense, *pairs, small, esum, tiles, cgot, cond)


def on_block(
    tokens, conditioning, routes, cotangent, ada_weight, ada_bias, qkv_weight, qv_bias, out_weight, out_bias,
    shared_in, shared_in_bias, shared_out, shared_out_bias, router,
    expert_in, expert_in_bias, expert_out, expert_out_bias,
):
    n = NZ * NX
    width = tokens.shape[2]
    hidden = shared_in.shape[1]
    part = width // n
    tok, cot, route = tokens[0], cotangent[0], routes[0]
    (
        normed, proj, lsum, mixed, att, resid, second, gates, place, mod, bias, sinb, router_t,
        condt, ebias, ret, retg, qkv_full, out_full, sin_full, sout_full, dwin, dwout, came_a,
    ) = lead_part(
        tok, cot, route.T, conditioning, ada_weight, ada_bias[None], qv_bias, out_bias[None], shared_out_bias[None],
        shared_in_bias[None], router.T, expert_in_bias, expert_out_bias,
        (qkv_weight, out_weight, shared_in, shared_out), expert_in, expert_out,
    )
    (came_b, output, rgrad, mgrad, sin_half, sout_half, dout, drouter, vecs, mg2) = middle(
        ret, retg, dwout, second, resid, att, cot, mod, sin_full, sout_full, sinb, bias, router_t, gates, place,
        mixed, out_full,
    )
    dense, dwin_pair, dwout_pair, tgrad, (small, esum, tiles, cgot) = tail_part(
        sin_half, sout_half, dout, dwin.reshape(NZ, NX * part, hidden),
        dwout.reshape(NZ, hidden // NZ, width), came_a, came_b, tok, mod, normed, proj, lsum, mgrad, rgrad, qkv_full, mg2, vecs, drouter, ebias, condt, ada_weight,
    )
    (
        qkv_grad, out_grad, sin_grad, sout_grad, dwin_sum, dwout_sum, ada_grad, adab_grad, qvb_grad, outb_grad,
        sinb_grad, soutb_grad, router_grad, ein_b, eout_b, cond_grad,
    ) = finish(dense, (dwin_pair, dwout_pair), small, esum, tiles, cgot, conditioning, hidden)
    return (
        output[None],
        tgrad[None],
        cond_grad,
        ada_grad,
        adab_grad[0],
        qkv_grad,
        qvb_grad,
        out_grad,
        outb_grad[0],
        sin_grad,
        sinb_grad[0],
        sout_grad,
        soutb_grad[0],
        router_grad.T,
        dwin_sum,
        ein_b,
        dwout_sum,
        eout_b,
    )


def layer_norm(rows):
    centred = rows - jnp.mean(rows, axis=-1, keepdims=True)
    return centred * lax.rsqrt(jnp.mean(centred * centred, axis=-1, keepdims=True) + 1e-06)


def modulate(rows, shift, scale):
    return layer_norm(rows) * (1.0 + scale) + shift


def gelu_tanh(values_in):
    return jax.nn.gelu(values_in, approximate=True)


def on_device(
    tokens,
    conditioning,
    routes,
    cotangent,
    ada_weight,
    ada_bias,
    qkv_weight,
    qv_bias,
    out_weight,
    out_bias,
    shared_in,
    shared_in_bias,
    shared_out,
    shared_out_bias,
    router,
    expert_in,
    expert_in_bias,
    expert_out,
    expert_out_bias,
):
    f32 = jnp.float32
    b16 = jnp.bfloat16
    gathered_dense = (
        lax.all_gather(ada_weight, "dp", axis=0, tiled=True),
        lax.all_gather(ada_bias, "dp", axis=0, tiled=True),
        lax.all_gather(qkv_weight, "dp", axis=0, tiled=True),
        lax.all_gather(qv_bias, "dp", axis=1, tiled=True),
        lax.all_gather(out_weight, "dp", axis=0, tiled=True),
        lax.all_gather(out_bias, "dp", axis=0, tiled=True),
        lax.all_gather(shared_in, "dp", axis=0, tiled=True),
        lax.all_gather(shared_in_bias, "dp", axis=0, tiled=True),
        lax.all_gather(shared_out, "dp", axis=0, tiled=True),
        lax.all_gather(shared_out_bias, "dp", axis=0, tiled=True),
        lax.all_gather(router, "dp", axis=0, tiled=True),
    )
    (
        ada_full,
        ada_bias_full,
        qkv_full,
        qv_bias_full,
        out_full,
        out_bias_full,
        shared_in_full,
        shared_in_bias_full,
        shared_out_full,
        shared_out_bias_full,
        router_full,
    ) = gathered_dense
    image_count, length, width = tokens.shape
    row_count = image_count * length
    scaling = HEAD_DIM ** (-0.5)
    head_shape = (image_count, length, HEADS, HEAD_DIM)
    cond_float = conditioning.astype(f32)
    cond_act, silu_back = jax.vjp(jax.nn.silu, cond_float)
    cond_low = cond_act.astype(b16)
    modulation = jnp.dot(cond_low, ada_full, preferred_element_type=f32) + ada_bias_full.astype(f32)
    pieces = [modulation[:, None, index * width : (index + 1) * width] for index in range(6)]
    source = tokens.astype(f32)
    first_norm, first_back = jax.vjp(modulate, source, pieces[0], pieces[1])
    normed = first_norm.astype(b16)
    projected = jnp.einsum("isd,de->ise", normed, qkv_full, preferred_element_type=f32)
    query_heads = (
        (projected[..., :width] + qv_bias_full[0].astype(f32)).astype(b16).reshape(head_shape)
    )
    key_heads = projected[..., width : 2 * width].astype(b16).reshape(head_shape)
    value_heads = (
        (projected[..., 2 * width :] + qv_bias_full[1].astype(f32)).astype(b16).reshape(head_shape)
    )
    scores = (
        jnp.einsum("iqhc,ikhc->ihqk", query_heads, key_heads, preferred_element_type=f32) * scaling
    )
    peak_score = jnp.max(scores, axis=-1, keepdims=True)
    unscaled = jnp.exp(scores - peak_score)
    exp_total = jnp.sum(unscaled, axis=-1, keepdims=True)
    log_total = peak_score + jnp.log(exp_total)
    probs_low = (unscaled / exp_total).astype(b16)
    mixed = (
        jnp.einsum("ihqk,ikhc->iqhc", probs_low, value_heads, preferred_element_type=f32)
        .reshape(image_count, length, width)
        .astype(b16)
    )
    attended = jnp.einsum(
        "isd,de->ise", mixed, out_full, preferred_element_type=f32
    ) + out_bias_full.astype(f32)
    resid = source + pieces[2] * attended
    second_float, second_back = jax.vjp(modulate, resid, pieces[3], pieces[4])
    second = second_float.astype(b16)
    shared_pre = jnp.einsum(
        "isd,df->isf", second, shared_in_full, preferred_element_type=f32
    ) + shared_in_bias_full.astype(f32)
    shared_act, shared_gelu_back = jax.vjp(gelu_tanh, shared_pre)
    shared_low = shared_act.astype(b16)
    shared = jnp.einsum(
        "isf,fd->isd", shared_low, shared_out_full, preferred_element_type=f32
    ) + shared_out_bias_full.astype(f32)
    second_rows = second.reshape(row_count, width)
    logits = jnp.dot(second_rows, router_full, preferred_element_type=f32)
    route_flat = routes.reshape(-1)
    one_hot = (route_flat[:, None] == jnp.arange(E, dtype=jnp.int32)).astype(jnp.int32)
    slot_index = jnp.sum(
        (jnp.cumsum(one_hot, axis=0, dtype=jnp.int32) - one_hot) * one_hot, axis=1, dtype=jnp.int32
    )
    position = jnp.where(slot_index < CAP, route_flat * CAP + slot_index, E * CAP)
    pair_rows = jnp.repeat(second_rows, 2, axis=0)
    buffer = (
        jnp.zeros((E * CAP, width), b16)
        .at[position]
        .set(pair_rows, mode="drop")
        .reshape(E, CAP, width)
    )
    received = lax.all_to_all(buffer, "expert", split_axis=0, concat_axis=1, tiled=True)
    expert_pre = (
        jnp.einsum("erd,edf->erf", received, expert_in, preferred_element_type=f32)
        + expert_in_bias.astype(f32)[:, None, :]
    )
    expert_low = gelu_tanh(expert_pre).astype(b16)
    expert_result = (
        jnp.einsum("erf,efd->erd", expert_low, expert_out, preferred_element_type=f32)
        + expert_out_bias.astype(f32)[:, None, :]
    ).astype(b16)
    returned = lax.all_to_all(
        expert_result, "expert", split_axis=1, concat_axis=0, tiled=True
    ).reshape(E * CAP, width)
    gathered = (
        returned.at[position]
        .get(mode="fill", fill_value=0)
        .reshape(row_count, 2, width)
        .astype(f32)
    )
    pair_mask = one_hot.reshape(row_count, 2, E).astype(f32)
    chosen = jnp.sum(logits[:, None, :] * pair_mask, axis=-1)
    gates = jax.nn.softmax(chosen, axis=-1)
    moe = (shared.reshape(row_count, width) + jnp.sum(gates[..., None] * gathered, axis=1)).reshape(
        image_count, length, width
    )
    output = (resid + pieces[5] * moe).astype(b16)
    ada_back, qkv_back, out_back, shared_in_back, shared_out_back, router_back = (
        ada_full,
        qkv_full,
        out_full,
        shared_in_full,
        shared_out_full,
        router_full,
    )
    grad_out = cotangent.astype(f32)
    gate_two_grad = jnp.sum(grad_out * moe, axis=1, keepdims=True)
    moe_grad = (pieces[5] * grad_out).astype(b16)
    moe_rows_grad = moe_grad.reshape(row_count, width)
    moe_rows_float = moe_rows_grad.astype(f32)
    pair_grad = (
        (gates[..., None] * moe_rows_float[:, None, :]).astype(b16).reshape(2 * row_count, width)
    )
    gate_grad = jnp.sum(moe_rows_float[:, None, :] * gathered, axis=-1)
    chosen_grad = gates * (gate_grad - jnp.sum(gates * gate_grad, axis=-1, keepdims=True))
    logits_grad = jnp.sum(chosen_grad[..., None] * pair_mask, axis=1).astype(b16)
    grad_buffer = (
        jnp.zeros((E * CAP, width), b16)
        .at[position]
        .set(pair_grad, mode="drop")
        .reshape(E, CAP, width)
    )
    result_grad = lax.all_to_all(grad_buffer, "expert", split_axis=0, concat_axis=1, tiled=True)
    pre_again = (
        jnp.einsum("erd,edf->erf", received, expert_in, preferred_element_type=f32)
        + expert_in_bias.astype(f32)[:, None, :]
    )
    act_again, expert_gelu_back = jax.vjp(gelu_tanh, pre_again)
    low_again = act_again.astype(b16)
    expert_out_grad = jnp.einsum("erf,erd->efd", low_again, result_grad, preferred_element_type=f32)
    expert_out_bias_grad = jnp.sum(result_grad.astype(f32), axis=1)
    expert_act_grad = jnp.einsum(
        "erd,efd->erf", result_grad, expert_out, preferred_element_type=f32
    )
    pre_grad = expert_gelu_back(expert_act_grad)[0].astype(b16)
    expert_in_grad = jnp.einsum("erd,erf->edf", received, pre_grad, preferred_element_type=f32)
    expert_in_bias_grad = jnp.sum(pre_grad.astype(f32), axis=1)
    received_grad = jnp.einsum(
        "erf,edf->erd", pre_grad, expert_in, preferred_element_type=f32
    ).astype(b16)
    sent_grad = lax.all_to_all(
        received_grad, "expert", split_axis=1, concat_axis=0, tiled=True
    ).reshape(E * CAP, width)
    dispatch_rows_grad = jnp.sum(
        sent_grad.at[position]
        .get(mode="fill", fill_value=0)
        .reshape(row_count, 2, width)
        .astype(f32),
        axis=1,
    )
    shared_out_grad = jnp.einsum("isf,isd->fd", shared_low, moe_grad, preferred_element_type=f32)
    shared_out_bias_grad = jnp.sum(moe_rows_float, axis=0)
    shared_act_grad = jnp.einsum(
        "isd,fd->isf", moe_grad, shared_out_back, preferred_element_type=f32
    )
    shared_pre_grad = shared_gelu_back(shared_act_grad)[0].astype(b16)
    shared_in_grad = jnp.einsum("isd,isf->df", second, shared_pre_grad, preferred_element_type=f32)
    shared_in_bias_grad = jnp.sum(shared_pre_grad.astype(f32), axis=(0, 1))
    router_grad = jnp.einsum("rd,re->de", second_rows, logits_grad, preferred_element_type=f32)
    second_grad = jnp.einsum(
        "isf,df->isd", shared_pre_grad, shared_in_back, preferred_element_type=f32
    )
    side_grad = dispatch_rows_grad + jnp.einsum(
        "re,de->rd", logits_grad, router_back, preferred_element_type=f32
    )
    second_grad = second_grad + side_grad.reshape(image_count, length, width)
    resid_extra, shift_two_grad, scale_two_grad = second_back(second_grad)
    resid_grad = grad_out + resid_extra
    attended_grad = (pieces[2] * resid_grad).astype(b16)
    gate_one_grad = jnp.sum(resid_grad * attended, axis=1, keepdims=True)
    out_weight_grad = jnp.einsum("isd,ise->de", mixed, attended_grad, preferred_element_type=f32)
    out_bias_grad = jnp.sum(attended_grad.astype(f32), axis=(0, 1))
    mixed_grad = (
        jnp.einsum("ise,de->isd", attended_grad, out_back, preferred_element_type=f32)
        .astype(b16)
        .reshape(head_shape)
    )
    again_scores = (
        jnp.einsum("iqhc,ikhc->ihqk", query_heads, key_heads, preferred_element_type=f32) * scaling
    )
    probs_float = jnp.exp(again_scores - log_total)
    again_low = probs_float.astype(b16)
    probs_grad = jnp.einsum("iqhc,ikhc->ihqk", mixed_grad, value_heads, preferred_element_type=f32)
    values_grad = jnp.einsum(
        "ihqk,iqhc->ikhc", again_low, mixed_grad, preferred_element_type=f32
    ).astype(b16)
    scores_grad = (
        probs_float * (probs_grad - jnp.sum(probs_float * probs_grad, axis=-1, keepdims=True))
    ).astype(b16)
    query_grad = (
        jnp.einsum("ihqk,ikhc->iqhc", scores_grad, key_heads, preferred_element_type=f32) * scaling
    ).astype(b16)
    keys_grad = (
        jnp.einsum("ihqk,iqhc->ikhc", scores_grad, query_heads, preferred_element_type=f32)
        * scaling
    ).astype(b16)
    flat_shape = (image_count, length, width)
    projected_grad = jnp.concatenate(
        [
            query_grad.reshape(flat_shape),
            keys_grad.reshape(flat_shape),
            values_grad.reshape(flat_shape),
        ],
        axis=-1,
    )
    qkv_weight_grad = jnp.einsum("isd,ise->de", normed, projected_grad, preferred_element_type=f32)
    qv_bias_grad = jnp.stack(
        [
            jnp.sum(query_grad.astype(f32), axis=(0, 1)).reshape(width),
            jnp.sum(values_grad.astype(f32), axis=(0, 1)).reshape(width),
        ]
    )
    normed_grad = jnp.einsum("ise,de->isd", projected_grad, qkv_back, preferred_element_type=f32)
    token_extra, shift_one_grad, scale_one_grad = first_back(normed_grad)
    tokens_grad = resid_grad + token_extra
    modulation_grad = jnp.concatenate(
        [
            shift_one_grad,
            scale_one_grad,
            gate_one_grad,
            shift_two_grad,
            scale_two_grad,
            gate_two_grad,
        ],
        axis=-1,
    )[:, 0, :].astype(b16)
    ada_weight_grad = jnp.einsum("id,ie->de", cond_low, modulation_grad, preferred_element_type=f32)
    ada_bias_grad = jnp.sum(modulation_grad.astype(f32), axis=0)
    cond_act_grad = jnp.einsum("ie,de->id", modulation_grad, ada_back, preferred_element_type=f32)
    conditioning_grad = silu_back(cond_act_grad)[0]
    expert_sums = (
        lax.psum_scatter(
            expert_in_grad.astype(jnp.bfloat16), "dp", scatter_dimension=1, tiled=True
        ).astype(jnp.float32),
        lax.psum_scatter(
            expert_in_bias_grad.astype(jnp.bfloat16), "dp", scatter_dimension=1, tiled=True
        ).astype(jnp.float32),
        lax.psum_scatter(
            expert_out_grad.astype(jnp.bfloat16), "dp", scatter_dimension=1, tiled=True
        ).astype(jnp.float32),
        lax.psum_scatter(
            expert_out_bias_grad.astype(jnp.bfloat16), "dp", scatter_dimension=1, tiled=True
        ).astype(jnp.float32),
    )
    dense_parts = (
        lax.psum_scatter(
            ada_weight_grad.astype(jnp.bfloat16), "dp", scatter_dimension=0, tiled=True
        ).astype(jnp.float32),
        lax.psum_scatter(
            ada_bias_grad.astype(jnp.bfloat16), "dp", scatter_dimension=0, tiled=True
        ).astype(jnp.float32),
        lax.psum_scatter(
            qkv_weight_grad.astype(jnp.bfloat16), "dp", scatter_dimension=0, tiled=True
        ).astype(jnp.float32),
        lax.psum_scatter(
            qv_bias_grad.astype(jnp.bfloat16), "dp", scatter_dimension=1, tiled=True
        ).astype(jnp.float32),
        lax.psum_scatter(
            out_weight_grad.astype(jnp.bfloat16), "dp", scatter_dimension=0, tiled=True
        ).astype(jnp.float32),
        lax.psum_scatter(
            out_bias_grad.astype(jnp.bfloat16), "dp", scatter_dimension=0, tiled=True
        ).astype(jnp.float32),
        lax.psum_scatter(
            shared_in_grad.astype(jnp.bfloat16), "dp", scatter_dimension=0, tiled=True
        ).astype(jnp.float32),
        lax.psum_scatter(
            shared_in_bias_grad.astype(jnp.bfloat16), "dp", scatter_dimension=0, tiled=True
        ).astype(jnp.float32),
        lax.psum_scatter(
            shared_out_grad.astype(jnp.bfloat16), "dp", scatter_dimension=0, tiled=True
        ).astype(jnp.float32),
        lax.psum_scatter(
            shared_out_bias_grad.astype(jnp.bfloat16), "dp", scatter_dimension=0, tiled=True
        ).astype(jnp.float32),
        lax.psum_scatter(
            router_grad.astype(jnp.bfloat16), "dp", scatter_dimension=0, tiled=True
        ).astype(jnp.float32),
    )
    dense_sums = lax.psum(
        (
            dense_parts[0],
            dense_parts[1],
            dense_parts[2],
            dense_parts[3],
            dense_parts[4],
            dense_parts[5],
            dense_parts[6],
            dense_parts[7],
            dense_parts[8],
            dense_parts[9],
            dense_parts[10],
        ),
        "expert",
    )
    return (
        output,
        tokens_grad,
        conditioning_grad,
        dense_sums[0],
        dense_sums[1],
        dense_sums[2],
        dense_sums[3],
        dense_sums[4],
        dense_sums[5],
        dense_sums[6],
        dense_sums[7],
        dense_sums[8],
        dense_sums[9],
        dense_sums[10],
        expert_sums[0],
        expert_sums[1],
        expert_sums[2],
        expert_sums[3],
    )


def solution(mesh):
    in_specs = (
        P(("dp", "expert"), None, None),
        P(("dp", "expert"), None),
        P(("dp", "expert"), None, None),
        P(("dp", "expert"), None, None),
        P("dp", None),
        P("dp"),
        P("dp", None),
        P(None, "dp"),
        P("dp", None),
        P("dp"),
        P("dp", None),
        P("dp"),
        P("dp", None),
        P("dp"),
        P("dp", None),
        P("expert", None, None),
        P("expert", None),
        P("expert", None, None),
        P("expert", None),
    )
    out_specs = (
        P(("dp", "expert"), None, None),
        P(("dp", "expert"), None, None),
        P(("dp", "expert"), None),
        P("dp", None),
        P("dp"),
        P("dp", None),
        P(None, "dp"),
        P("dp", None),
        P("dp"),
        P("dp", None),
        P("dp"),
        P("dp", None),
        P("dp"),
        P("dp", None),
        P("expert", "dp", None),
        P("expert", "dp"),
        P("expert", "dp", None),
        P("expert", "dp"),
    )
    body = on_device
    if dict(mesh.shape) == {"dp": NZ * NX, "expert": 4}:
        body = on_block
    return jax.shard_map(
        body, mesh=mesh, in_specs=in_specs, out_specs=out_specs, check_vma=False
    )
```

```python
import functools

import jax
import jax.numpy as jnp
from jax import lax
from jax.experimental import pallas as pl
from jax.experimental.pallas import tpu as pltpu
from jax.sharding import PartitionSpec as P

HEADS = 12
HEAD_DIM = 64
E = 8
CAP = 80
MESH = pl.DeviceIdType.MESH
F32 = jnp.float32
B16 = jnp.bfloat16
VMEM_LIMIT = 60 * 1024 * 1024
SCALE = HEAD_DIM ** (-0.5)
GELU_C = 0.7978845608028654
NZ, NX = 4, 2


def coords():
    dp = lax.axis_index("dp")
    ex = lax.axis_index("expert")
    return lax.div(dp, NX), lax.rem(dp, NX), lax.div(ex, 2), lax.rem(ex, 2)


def dev(z, x, y, c):
    return (NX * z + x, 2 * y + c)


def dot(a, b):
    return jnp.dot(a, b, preferred_element_type=F32)


def dot_nt(a, b):
    return lax.dot_general(a, b, (((1,), (1,)), ((), ())), preferred_element_type=F32)


def dot_tn(a, b):
    return lax.dot_general(a, b, (((0,), (0,)), ((), ())), preferred_element_type=F32)


def gelu(v):
    return v * (0.5 + 0.5 * jnp.tanh(v * (GELU_C + GELU_C * 0.044715 * (v * v))))


def gelu_parts(v):
    v2 = v * v
    t = jnp.tanh(GELU_C * v * (1.0 + 0.044715 * v2))
    h = 0.5 * (1.0 + t)
    return v * h, h + 0.5 * v * (1.0 - t * t) * (GELU_C * (1.0 + 0.134145 * v2))


def norm_parts(v):
    centred = v - jnp.mean(v, axis=-1, keepdims=True)
    r = lax.rsqrt(jnp.mean(centred * centred, axis=-1, keepdims=True) + 1e-06)
    return centred * r, r


def norm_back(u, n, r):
    return r * (
        u - jnp.mean(u, axis=-1, keepdims=True) - n * jnp.mean(u * n, axis=-1, keepdims=True)
    )


def remote(src, dst, send, recv, to):
    return pltpu.make_async_remote_copy(
        src_ref=src,
        dst_ref=dst,
        send_sem=send,
        recv_sem=recv,
        device_id=to,
        device_id_type=MESH,
    )


def greet(barrier, to):
    pl.semaphore_signal(barrier, inc=1, device_id=to, device_id_type=MESH)


def params(collective_id=None):
    if collective_id is None:
        return pltpu.CompilerParams(vmem_limit_bytes=VMEM_LIMIT)
    return pltpu.CompilerParams(
        vmem_limit_bytes=VMEM_LIMIT, collective_id=collective_id, has_side_effects=True
    )


VM = pl.BlockSpec(memory_space=pltpu.VMEM)
HB = pl.BlockSpec(memory_space=pl.ANY)


def sds(shape, dtype):
    return jax.ShapeDtypeStruct(shape, dtype)


class Gather:
    def __init__(self, shards, fulls, splits, sems):
        self.z, self.x, self.y, self.c = coords()
        self.mats = list(zip(shards, fulls, splits))
        (self.zs, self.zr, self.xs, self.xr, self.ys, self.yr, self.cs, self.cr, self.loc) = sems

    @staticmethod
    def semaphores(count):
        dma = pltpu.SemaphoreType.DMA
        return [
            dma((count, 2, NZ)),
            dma((count, NZ)),
            dma((count, NZ)),
            dma((count, NZ)),
            dma((count, NZ, NX)),
            dma((count, NZ, NX)),
            dma((count, NZ, NX, 2)),
            dma((count, NZ, NX, 2)),
            dma((count,)),
        ]

    def region(self, m, zb, xb, yh, ch):
        shard, full, split = self.mats[m]
        rows, width = shard.shape[0], shard.shape[1] // 2
        start = (NX * zb + xb) * rows
        if split:
            rows = rows // 2
            start = start + yh * rows
        return full.at[
            pl.ds(pl.multiple_of(start, 16), rows), pl.ds(pl.multiple_of(ch * width, 128), width)
        ]

    def own(self, m):
        shard, full, split = self.mats[m]
        rows, width = shard.shape[0], shard.shape[1] // 2
        start = 0
        if split:
            rows = rows // 2
            start = self.y * rows
        return shard.at[
            pl.ds(pl.multiple_of(start, 16), rows),
            pl.ds(pl.multiple_of(self.c * width, 128), width),
        ]

    def zcopy(self, m, zb, side, mine=False):
        here = self.region(m, zb, self.x, self.y, self.c)
        step = 1 if side else -1
        return remote(
            self.own(m) if mine else here,
            here,
            self.zs.at[m, side, zb],
            self.zr.at[m, zb],
            dev(lax.rem(self.z + step + NZ, NZ), self.x, self.y, self.c),
        )

    def xcopy(self, m, zb, mine=False, xb=None):
        here = self.region(m, zb, self.x if xb is None else xb, self.y, self.c)
        return remote(
            self.own(m) if mine else here,
            here,
            self.xs.at[m, zb],
            self.xr.at[m, zb],
            dev(self.z, 1 - self.x, self.y, self.c),
        )

    def ycopy(self, m, zb, xb, yh=None):
        here = self.region(m, zb, xb, self.y if yh is None else yh, self.c)
        return remote(
            here,
            here,
            self.ys.at[m, zb, xb],
            self.yr.at[m, zb, xb],
            dev(self.z, self.x, 1 - self.y, self.c),
        )

    def ccopy(self, m, zb, xb, yh, ch=None):
        here = self.region(m, zb, xb, yh, self.c if ch is None else ch)
        slot = yh if self.mats[m][2] else 0
        return remote(
            here,
            here,
            self.cs.at[m, zb, xb, slot],
            self.cr.at[m, zb, xb, slot],
            dev(self.z, self.x, self.y, 1 - self.c),
        )

    def local(self, m):
        shard, full, _ = self.mats[m]
        rows = shard.shape[0]
        start = (NX * self.z + self.x) * rows
        return pltpu.make_async_copy(
            shard, full.at[pl.ds(pl.multiple_of(start, 16), rows), :], self.loc.at[m]
        )

    def blocks(self, step):
        if step == 0:
            return [(self.z, None, None)]
        return [
            (self.z - step, self.z - step >= 0, 1),
            (self.z + step, self.z + step < NZ, 0),
        ]

    def more(self, side):
        return self.z + 1 < NZ if side else self.z - 1 >= 0

    def begin(self, m):
        for side in (1, 0):

            @pl.when(self.more(side))
            def _():
                self.zcopy(m, self.z, side, True).start()

        self.xcopy(m, self.z, True).start()
        self.local(m).start()

    def spread(self, m, zb, xb):
        if self.mats[m][2]:
            self.ycopy(m, zb, xb).start()
        self.ccopy(m, zb, xb, self.y).start()

    def take_z(self, m, step):
        for zb, exists, side in self.blocks(step):

            @pl.when(exists)
            def _():
                self.zcopy(m, zb, side).wait_recv()
                if step < NZ - 1:

                    @pl.when(self.more(side))
                    def _():
                        self.zcopy(m, zb, side).start()

                self.xcopy(m, zb).start()
                self.spread(m, zb, self.x)

    def take_x(self, m, step):
        for zb, exists, _ in self.blocks(step):

            def body():
                self.xcopy(m, zb, False, 1 - self.x).wait_recv()
                self.spread(m, zb, 1 - self.x)

            body() if exists is None else pl.when(exists)(body)

    def others(self, m, step, action):
        for zb, exists, _ in self.blocks(step):
            for xb in (self.x, 1 - self.x) if step else (1 - self.x,):
                body = functools.partial(action, m, zb, xb)
                body() if exists is None else pl.when(exists)(body)

    def take_y(self, m, step):
        if not self.mats[m][2]:
            return

        def action(m, zb, xb):
            self.ycopy(m, zb, xb, 1 - self.y).wait_recv()
            self.ccopy(m, zb, xb, 1 - self.y).start()

        self.others(m, step, action)

    def finish(self, m):
        def action(m, zb, xb):
            for yh in (self.y, 1 - self.y) if self.mats[m][2] else (self.y,):
                self.ccopy(m, zb, xb, yh, 1 - self.c).wait_recv()
                self.ccopy(m, zb, xb, yh).wait_send()
            if self.mats[m][2]:
                self.ycopy(m, zb, xb).wait_send()

        for step in range(NZ):
            self.others(m, step, action)
        for side in (1, 0):

            @pl.when(self.more(side))
            def _():
                self.zcopy(m, self.z, side, True).wait_send()

        for step in range(1, NZ):
            for zb, exists, side in self.blocks(step):

                @pl.when(exists)
                def _():
                    self.xcopy(m, zb).wait_send()
                    if step < NZ - 1:

                        @pl.when(self.more(side))
                        def _():
                            self.zcopy(m, zb, side).wait_send()

        self.xcopy(m, self.z, True).wait_send()
        self.local(m).wait()


class Column:
    def __init__(self, shard, column, other, send, recv, local, xsend, xrecv):
        self.z, self.x, self.y, self.c = coords()
        self.shard, self.column, self.other = shard, column, other
        self.send, self.recv, self.local, self.xsend, self.xrecv = send, recv, local, xsend, xrecv

    @staticmethod
    def semaphores():
        dma = pltpu.SemaphoreType.DMA
        return [dma((2, NZ)), dma((NZ,)), dma((1,)), dma((NZ,)), dma((NZ,))]

    def block(self, zb):
        rows = self.shard.shape[0]
        return self.column.at[pl.ds(pl.multiple_of(zb * rows, 16), rows), :]

    def own(self):
        width = self.shard.shape[1] // 2
        return self.shard.at[:, pl.ds(pl.multiple_of(self.c * width, 128), width)]

    def copy(self, zb, side, mine=False):
        here = self.block(zb)
        to = lax.rem(self.z + (1 if side else NZ - 1), NZ)
        return remote(
            self.own() if mine else here,
            here,
            self.send.at[side, zb],
            self.recv.at[zb],
            dev(to, self.x, self.y, self.c),
        )

    def xcopy(self, zb, mine=False):
        rows, width = self.shard.shape[0], self.shard.shape[1] // 2
        part = rows // 2
        start = pl.multiple_of(self.y * part, 16)
        if mine:
            source = self.shard.at[
                pl.ds(start, part), pl.ds(pl.multiple_of(self.c * width, 128), width)
            ]
        else:
            source = self.column.at[pl.ds(pl.multiple_of(zb * rows + start, 16), part), :]
        return remote(
            source,
            self.other.at[pl.ds(pl.multiple_of(zb * part, 16), part), :],
            self.xsend.at[zb],
            self.xrecv.at[zb],
            dev(self.z, 1 - self.x, self.y, self.c),
        )

    def keep(self):
        return pltpu.make_async_copy(self.own(), self.block(self.z), self.local.at[0])

    def more(self, side):
        return self.z + 1 < NZ if side else self.z - 1 >= 0

    def blocks(self, step):
        return [(self.z - step, self.z - step >= 0, 1), (self.z + step, self.z + step < NZ, 0)]

    def begin(self):
        for side in (1, 0):

            @pl.when(self.more(side))
            def _():
                self.copy(self.z, side, True).start()

        self.keep().start()
        self.xcopy(self.z, True).start()

    def take(self, step):
        for zb, exists, side in self.blocks(step):

            @pl.when(exists)
            def _():
                self.copy(zb, side).wait_recv()
                if step < NZ - 1:

                    @pl.when(self.more(side))
                    def _():
                        self.copy(zb, side).start()

    def push(self, step):
        for zb, exists, _ in self.blocks(step):

            @pl.when(exists)
            def _():
                self.xcopy(zb).start()

    def finish(self):
        for side in (1, 0):

            @pl.when(self.more(side))
            def _():
                self.copy(self.z, side, True).wait_send()

        for step in range(1, NZ - 1):
            for zb, exists, side in self.blocks(step):

                @pl.when(jnp.logical_and(exists, self.more(side)))
                def _():
                    self.copy(zb, side).wait_send()

        for zb in range(NZ):
            self.xcopy(zb).wait_send()


class Spread:
    def __init__(self, column, other, full, ys, yr, cs, cr, local):
        self.z, self.x, self.y, self.c = coords()
        self.column, self.other, self.full, self.local = column, other, full, local
        self.ys, self.yr, self.cs, self.cr = ys, yr, cs, cr

    @staticmethod
    def semaphores():
        dma = pltpu.SemaphoreType.DMA
        return [dma((NZ,))] * 2 + [dma((3, NZ))] * 2 + [dma((2, NZ))]

    def cols(self, c):
        width = self.full.shape[3] // 2
        return pl.ds(pl.multiple_of(c * width, 128), width)

    def half(self, y):
        rows = self.full.shape[2] // 2
        return pl.ds(pl.multiple_of(y * rows, 16), rows)

    def source(self, kind, zb):
        rows = self.full.shape[2] // (1 if kind == 0 else 2)
        ref = self.column if kind == 0 else self.other
        return ref.at[pl.ds(pl.multiple_of(zb * rows, 16), rows), :]

    def place(self, kind, zb, c):
        if kind == 0:
            return self.full.at[zb, self.x, :, self.cols(c)]
        return self.full.at[zb, 1 - self.x, self.half(self.y if kind == 1 else 1 - self.y), self.cols(c)]

    def ycopy(self, zb, came=False):
        return remote(
            self.source(1, zb), self.place(2 if came else 1, zb, self.c), self.ys.at[zb], self.yr.at[zb],
            dev(self.z, self.x, 1 - self.y, self.c),
        )

    def ccopy(self, kind, zb, came=False):
        at = self.place(kind, zb, 1 - self.c if came else self.c)
        return remote(
            at if kind == 2 else self.source(kind, zb), at, self.cs.at[kind, zb], self.cr.at[kind, zb],
            dev(self.z, self.x, self.y, 1 - self.c),
        )

    def keep(self, kind, zb):
        return pltpu.make_async_copy(
            self.source(kind, zb), self.place(kind, zb, self.c), self.local.at[kind, zb]
        )

    def near(self):
        for zb in range(NZ):
            self.ccopy(0, zb).start()
            self.keep(0, zb).start()

    def pass_x(self, zb):
        self.ycopy(zb).start()
        self.ccopy(1, zb).start()
        self.keep(1, zb).start()

    def pass_y(self, zb):
        self.ycopy(zb, True).wait_recv()
        self.ccopy(2, zb).start()

    def finish(self):
        for zb in range(NZ):
            for kind in range(3):
                self.ccopy(kind, zb, True).wait_recv()
                self.ccopy(kind, zb).wait_send()
            for kind in range(2):
                self.keep(kind, zb).wait()
            self.ycopy(zb).wait_send()


def choose_rows(place, slots):
    return place == lax.broadcasted_iota(jnp.int32, (place.shape[0], slots), 1)


def plane_peer(k):
    z, x, y, c = coords()
    xt = 1 - x if k & 1 else x
    ct = 1 - c if k & 2 else c
    yt = 1 - y if k & 4 else y
    return dev(z, xt, yt, ct), 4 * yt + 2 * ct + xt


def plane_rank():
    _, x, y, c = coords()
    return 4 * y + 2 * c + x


def slot_rows(ref, rank):
    return ref.at[pl.ds(pl.multiple_of(rank * CAP, 16), CAP), :]


class PlaneExchange:
    ORDER = (7, 5, 6, 4, 3, 1, 2)

    def __init__(self, source, target, send, recv):
        self.source, self.target, self.send, self.recv = source, target, send, recv

    def copy(self, k, into=None):
        peer, other = plane_peer(k)
        return remote(
            slot_rows(self.source, other),
            slot_rows(self.target, plane_rank() if into is None else other),
            self.send.at[k],
            self.recv.at[k],
            peer,
        )

    def mine(self):
        rank = plane_rank()
        return pltpu.make_async_copy(
            slot_rows(self.source, rank), slot_rows(self.target, rank), self.send.at[0]
        )

    def start(self):
        for k in self.ORDER:
            self.copy(k).start()
        self.mine().start()

    def wait_in(self):
        self.mine().wait()
        for k in self.ORDER:
            self.copy(k, True).wait_recv()

    def wait_out(self):
        for k in self.ORDER:
            self.copy(k).wait_send()


CHUNK = 512


def lead_kernel(
    tok, cot, routes, cond, ada, adab, qvb, outb, soutb, sinb_s, router_s, bin_r, bout_r,
    qkv_s, out_s, sin_s, sout_s, win_h, wout_h,
    normed_o, proj_o, lsum_o, mixed_o, att_o, resid_o, second_o, gates_o, place_o, mod_o, bias_o, sinb_o, rt_o,
    condt_o, ebias, ret_o, retg_o, qkv_o, outw_o, sin_o, sout_o, dwin_o, dwout_o, came_o,
    pack, packs, sent, got, qkv, outw, sbuf, gbuf, res, bgr, rows, grads, far_rows, far_grads, win, wout, dwin, dwout,
    pres, acc, sin_c, sout_c, sin_x, sout_x,
    s1, r1, s2, r2, ds0, dr0, ds1, dr1, ds2, dr2, ds3, dr3, wsem, osem, fsem, msem, *gsems,
):
    z, x, y, c = coords()
    dp, ex = lax.axis_index("dp"), lax.axis_index("expert")
    n = NZ * NX
    length, width = tok.shape
    hidden = win.shape[1]
    part = width // n
    per = width // 128
    count = len(Column.semaphores())
    lead = Gather((qkv_s, out_s), (qkv, outw), (True, False), gsems[: len(Gather.semaphores(2))])
    gsems = gsems[len(Gather.semaphores(2)) :]
    later = (
        Column(sin_s, sin_c, sin_x, *gsems[:count]),
        Column(sout_s, sout_c, sout_x, *gsems[count : 2 * count]),
    )
    gsems = gsems[2 * count :]
    count = len(Spread.semaphores())
    spreads = (
        Spread(sin_c, sin_x, sin_o, *gsems[:count]),
        Spread(sout_c, sout_x, sout_o, *gsems[count:]),
    )

    def per_block(step, action):
        for zb, exists in [(z, None)] if step == 0 else [v[:2] for v in later[0].blocks(step)]:
            body = functools.partial(action, zb)
            body() if exists is None else pl.when(exists)(body)

    def pass_x(step):
        def action(zb):
            for column, spread in zip(later, spreads):
                column.xcopy(zb).wait_recv()
                spread.pass_x(zb)

        per_block(step, action)

    def pass_y(step):
        def action(zb):
            for spread in spreads:
                spread.pass_y(zb)

        per_block(step, action)

    loads = [
        pltpu.make_async_copy(win_h.at[x], win, wsem.at[0]),
        pltpu.make_async_copy(wout_h.at[x], wout, wsem.at[1]),
    ]

    def peers(action):
        for p in range(n):

            @pl.when(p != dp)
            def _():
                action(p)

    barrier = pltpu.get_barrier_semaphore()
    peers(lambda p: greet(barrier, (p, ex)))
    for k in range(2, E):
        greet(barrier, plane_peer(k)[0])

    pack[...] = jnp.zeros_like(pack)
    pack[0:2, 0:part] = qvb[...].astype(F32)
    pack[2:3, 0:part] = outb[...].astype(F32)
    pack[3:4, 0:part] = soutb[...].astype(F32)
    for j in range(hidden // n // 128):
        pack[4 + j : 5 + j, :] = sinb_s[:, 128 * j : 128 * (j + 1)].astype(F32)
    long = adab.shape[1]
    for j in range(-(-long // 128)):
        size = min(128, long - 128 * j)
        pack[8 + j : 9 + j, 0:size] = adab[:, 128 * j : 128 * j + size].astype(F32)
    pack[16:24, 0:part] = router_s[...].astype(F32)
    cv = cond[...].astype(F32)
    cond_low = (cv / (1.0 + jnp.exp(-cv))).astype(B16).astype(F32)
    for p in range(n):
        pack[24 + p : 25 + p, 0:part] = cond_low[:, part * p : part * (p + 1)]
    condt_o[...] = jnp.zeros_like(condt_o)
    for j in range(per):
        condt_o[j : j + 1, :] = cond_low[:, 128 * j : 128 * (j + 1)]

    pl.semaphore_wait(barrier, n - 1 + E - 2)

    def first(p, at):
        return remote(pack, packs.at[at], s1.at[p], r1.at[at], (p, ex))

    def second_hop(p, at):
        return remote(sent.at[p], got.at[at], s2.at[p], r2.at[at], (p, ex))

    peers(lambda p: first(p, dp).start())
    lead.begin(0)
    lead.begin(1)
    for load in loads:
        load.start()
    packs[dp] = pack[...]
    peers(lambda p: first(p, p).wait_recv())
    cond_rows = jnp.concatenate([packs[p, pl.ds(24 + dp, 1), :] for p in range(n)], axis=0)
    partial = dot(cond_rows[:, :part].astype(B16), ada[...])
    for j in range(partial.shape[1] // 128):
        sent[:, j, :] = partial[:, 128 * j : 128 * (j + 1)]
    peers(lambda p: second_hop(p, dp).start())
    got[dp] = sent[dp]

    both_mats = (0, 1)

    def step_of(plan, step):
        for m in both_mats:
            if step:
                plan.take_z(m, step)
            plan.take_x(m, step)
        if step:
            for m in both_mats:
                plan.take_y(m, step - 1)

    for step in range(NZ):
        step_of(lead, step)

    for column in later:
        column.begin()

    bias_o[...] = jnp.zeros_like(bias_o)
    for p in range(n):
        bias_o[0:4, part * p : part * (p + 1)] = packs[p, 0:4, 0:part]
        rt_o[:, part * p : part * (p + 1)] = packs[p, 16:24, 0:part]
        for j in range(hidden // n // 128):
            at = hidden // n * p + 128 * j
            sinb_o[:, at : at + 128] = packs[p, 4 + j : 5 + j, :]
    peers(lambda p: second_hop(p, p).wait_recv())
    total = got[0]
    for p in range(1, n):
        total = total + got[p]
    mod_o[...] = jnp.zeros_like(mod_o)
    for i in range(6):
        for b in range(per):
            mod_o[i : i + 1, 128 * b : 128 * (b + 1)] = total[per * i + b : per * i + b + 1, :]
    unit = 64
    for p in range(n):
        for u in range(long // unit):
            at = long * p + unit * u
            i, b = at // width, at % width
            mod_o[i : i + 1, b : b + unit] += packs[
                p, 8 + unit * u // 128 : 9 + unit * u // 128, unit * u % 128 : unit * u % 128 + unit
            ]

    mod = mod_o[...]
    source = tok[...].astype(F32)
    n1, _ = norm_parts(source)
    normed = (n1 * (1.0 + mod[1:2]) + mod[0:1]).astype(B16)
    normed_o[...] = normed
    for m in both_mats:
        lead.take_y(m, NZ - 1)
    for m in both_mats:
        lead.finish(m)
    keep = [
        pltpu.make_async_copy(qkv, qkv_o, wsem.at[2]),
        pltpu.make_async_copy(outw, outw_o, wsem.at[3]),
    ]
    for copy in keep:
        copy.start()

    for k in range(3):
        part_k = dot(normed, qkv[:, k * width : (k + 1) * width])
        if k != 1:
            part_k = part_k + bias_o[k // 2 : k // 2 + 1, :]
        proj_o[:, k * width : (k + 1) * width] = part_k.astype(B16)
    lane = lax.broadcasted_iota(jnp.int32, (length, 128), 1)
    low_lane = lane < HEAD_DIM
    lsum = jnp.zeros((length, 128), F32)
    for p in range(HEADS // 2):
        q2 = proj_o[:, 128 * p : 128 * (p + 1)]
        k2 = proj_o[:, width + 128 * p : width + 128 * (p + 1)]
        v2 = proj_o[:, 2 * width + 128 * p : 2 * width + 128 * (p + 1)]
        outs = []
        for h in range(2):
            mine = low_lane if h == 0 else jnp.logical_not(low_lane)
            s = dot_nt(jnp.where(mine, q2, jnp.zeros_like(q2)), k2) * SCALE
            peak = jnp.max(s, axis=-1, keepdims=True)
            e = jnp.exp(s - peak)
            tot = jnp.sum(e, axis=-1, keepdims=True)
            lsum = jnp.where(lane == 2 * p + h, peak + jnp.log(tot), lsum)
            outs.append(dot((e / tot).astype(B16), v2))
        mixed_o[:, 128 * p : 128 * (p + 1)] = jnp.where(low_lane, outs[0], outs[1]).astype(B16)
    lsum_o[...] = lsum
    att = dot(mixed_o[...], outw[...]) + bias_o[2:3, :]
    att_o[...] = att
    resid = source + mod[2:3] * att
    resid_o[...] = resid
    n2, _ = norm_parts(resid)
    second = (n2 * (1.0 + mod[4:5]) + mod[3:4]).astype(B16)
    second_o[...] = second

    lane8 = lax.broadcasted_iota(jnp.int32, (length, E), 1)
    two = (
        lax.broadcasted_iota(jnp.int32, (2, 128), 0) == lax.broadcasted_iota(jnp.int32, (2, 128), 1)
    )
    route_cols = dot_tn(
        routes[...].astype(F32).astype(B16), jnp.where(two, 1.0, 0.0).astype(B16)
    ).astype(jnp.int32)
    route = [route_cols[:, k : k + 1] for k in range(2)]
    picks = [(r == lane8) for r in route]
    both = jnp.where(picks[0], 1.0, 0.0) + jnp.where(picks[1], 1.0, 0.0)
    earlier = (
        lax.broadcasted_iota(jnp.int32, (length, length), 1)
        < lax.broadcasted_iota(jnp.int32, (length, length), 0)
    )
    rank = dot(jnp.where(earlier, 1.0, 0.0).astype(B16), both.astype(B16))
    places = []
    for k in range(2):
        slot = jnp.sum(jnp.where(picks[k], rank, 0.0), axis=-1, keepdims=True).astype(jnp.int32)
        places.append(jnp.where(slot < CAP, route[k] * CAP + slot, -1))
    place_o[...] = jnp.where(
        lane == 0,
        places[0],
        jnp.where(lane == 1, places[1], jnp.where(lane == 2, route[0], route[1])),
    )
    maps = [jnp.where(choose_rows(v, E * CAP), 1.0, 0.0) for v in places]
    sbuf[...] = dot_tn((maps[0] + maps[1]).astype(B16), second).astype(B16)
    give_rows = PlaneExchange(sbuf, rows, ds0, dr0)
    give_rows.start()
    logits = dot_nt(second, rt_o[...].astype(B16))
    chosen = [jnp.sum(jnp.where(pick, logits, 0.0), axis=-1, keepdims=True) for pick in picks]
    top = jnp.maximum(chosen[0], chosen[1])
    e2 = [jnp.exp(v - top) for v in chosen]
    gates = [v / (e2[0] + e2[1]) for v in e2]
    gates_o[...] = jnp.where(lane == 0, gates[0], jnp.where(lane == 1, gates[1], 0.0))
    moe_grad = (mod[5:6] * cot[...].astype(F32)).astype(B16).astype(F32)
    pair = [(g * moe_grad).astype(B16) for g in gates]
    gbuf[...] = (
        dot_tn(maps[0].astype(B16), pair[0]) + dot_tn(maps[1].astype(B16), pair[1])
    ).astype(B16)
    give_grads = PlaneExchange(gbuf, grads, ds1, dr1)
    give_grads.start()
    for column in later:
        column.take(1)

    first_x = x == 0
    acc[...] = jnp.zeros_like(acc) + jnp.where(first_x, bout_r[0:1, :], bout_r[1:2, :]).astype(F32)
    for load in loads:
        load.wait()
    for column in later:
        column.take(2)
    give_rows.wait_in()

    end = jnp.logical_or(z == 0, z == NZ - 1)
    inner = jnp.logical_not(end)
    partner = dev(z + 1 - 2 * lax.rem(z, 2), x, y, c)

    def far_copy(i):
        source, target = ((rows, far_rows), (grads, far_grads))[i]
        return remote(source, target, fsem.at[0, i], fsem.at[1, i], partner)

    pl.when(end)(lambda: far_copy(0).start())
    for column in later:
        column.push(1)

    def span(f):
        return pl.ds(pl.multiple_of(f * CHUNK, 128), CHUNK)

    def put_in(f):
        return pltpu.make_async_copy(dwin.at[:, span(f)], dwin_o.at[:, span(f)], osem.at[1, f])

    def put_out(f):
        return pltpu.make_async_copy(dwout.at[span(f), :], dwout_o.at[span(f), :], osem.at[0, f])

    def bias_of(cols):
        return jnp.where(first_x, bin_r[0:1, cols], bin_r[1:2, cols]).astype(F32)

    def forward(f, carry):
        cols = span(f)
        pre = dot(rows[...], win[:, cols]) + bias_of(cols)
        pres[:, cols] = pre
        low = gelu(pre).astype(B16)
        acc[...] += dot(low, wout[cols, :])
        return carry

    count = hidden // CHUNK
    lax.fori_loop(0, count, forward, 0)
    res[...] = acc[...].astype(B16)
    give_res = PlaneExchange(res, ret_o, ds2, dr2)
    give_res.start()
    for column in later:
        column.push(2)
        column.take(3)
        column.push(3)
    for column, spread in zip(later, spreads):
        column.keep().wait()
        spread.near()
    pass_x(0)
    pass_x(1)
    give_grads.wait_in()
    pl.when(end)(lambda: far_copy(1).start())
    acc[...] = jnp.zeros_like(acc)
    ebias[...] = jnp.zeros_like(ebias)
    column_sum = jnp.sum(grads[...].astype(F32), axis=0, keepdims=True)
    for p in range(n):
        at = hidden // 128 + p
        ebias[at : at + 1, 0:part] = column_sum[:, part * p : part * (p + 1)]

    def backward(f, carry):
        cols = span(f)
        act, slope = gelu_parts(pres[:, cols])
        pre = (dot_nt(grads[...], wout[cols, :]) * slope).astype(B16)
        acc[...] += dot_nt(pre, win[:, cols])
        col = jnp.sum(pre.astype(F32), axis=0, keepdims=True)
        for j in range(CHUNK // 128):
            ebias[pl.ds(f * (CHUNK // 128) + j, 1), :] = col[:, 128 * j : 128 * (j + 1)]

        @pl.when(inner)
        def _():
            dwout[cols, :] = dot_tn(act.astype(B16), grads[...]).astype(B16)
            dwin[:, cols] = dot_tn(rows[...], pre).astype(B16)

        return carry

    lax.fori_loop(0, count, backward, 0)
    bgr[...] = acc[...].astype(B16)
    give_bgr = PlaneExchange(bgr, retg_o, ds3, dr3)
    give_bgr.start()

    mate = NZ - 1 - z

    def across():
        start = lax.div(mate, 2) * (hidden // 2)
        return remote(
            dwout.at[pl.ds(pl.multiple_of(start, 16), CHUNK), :], came_o, msem.at[0], msem.at[1], dev(mate, x, y, c)
        )

    def far(i, carry):
        f = lax.rem(i + lax.div(mate, 2) * (count // 2), count)
        cols = span(f)
        data, grad = far_rows[...], far_grads[...]
        act, slope = gelu_parts(dot(data, win[:, cols]) + bias_of(cols))
        pre = (dot_nt(grad, wout[cols, :]) * slope).astype(B16)
        dwout[cols, :] = (dwout[cols, :].astype(F32) + dot_tn(act.astype(B16), grad)).astype(B16)
        put_out(f).start()
        dwin[:, cols] = (dwin[:, cols].astype(F32) + dot_tn(data, pre)).astype(B16)
        put_in(f).start()
        pl.when(i == 0)(lambda: across().start())
        return carry

    pass_x(2)
    pass_x(3)
    pass_y(0)
    pass_y(1)

    @pl.when(inner)
    def _():
        far_copy(0).wait_recv()
        far_copy(1).wait_recv()
        lax.fori_loop(0, count, far, 0)

    pass_y(2)
    pass_y(3)
    for spread in spreads:
        spread.finish()

    @pl.when(inner)
    def _():
        across().wait()

    for column in later:
        column.finish()
    for exchange in (give_res, give_bgr):
        exchange.wait_in()
    for exchange in (give_rows, give_grads, give_res, give_bgr):
        exchange.wait_out()
    peers(lambda p: first(p, p).wait_send())
    peers(lambda p: second_hop(p, p).wait_send())
    for copy in keep:
        copy.wait()

    @pl.when(end)
    def _():
        far_copy(0).wait_send()
        far_copy(1).wait_send()

    @pl.when(inner)
    def _():
        for f in range(count):
            put_out(f).wait()
            put_in(f).wait()


def lead_part(tok, cot, route, cond, ada, adab, qvb, outb, soutb, sinb, router, bin_r, bout_r, shards, win, wout):
    n = NZ * NX
    length, width = tok.shape
    hidden = win.shape[2]
    slots = E * CAP
    dma = pltpu.SemaphoreType.DMA
    vm = pltpu.VMEM
    tiles = (ada.shape[1] // 128 + 7) // 8 * 8
    wide = [sds((n * s.shape[0], s.shape[1]), B16) for s in shards[:2]]
    outs = [
        sds((length, width), B16),
        sds((length, 3 * width), B16),
        sds((length, 128), F32),
        sds((length, width), B16),
        sds((length, width), F32),
        sds((length, width), F32),
        sds((length, width), B16),
        sds((length, 128), F32),
        sds((length, 128), jnp.int32),
        sds((8, width), F32),
        sds((8, width), F32),
        sds((1, hidden), F32),
        sds((E, width), F32),
        sds((8, 128), F32),
        sds((32, 128), F32),
    ]
    back = [sds((slots, width), B16)] * 2
    wide += [sds((NZ, NX) + s.shape, B16) for s in shards[2:]]
    far = back + wide + [
        sds((width, hidden), B16),
        sds((hidden, width), B16),
        sds((CHUNK, width), B16),
    ]
    return pl.pallas_call(
        lead_kernel,
        out_shape=outs + far,
        in_specs=[VM] * 13 + [HB] * 6,
        out_specs=[VM] * len(outs) + [HB] * len(far),
        scratch_shapes=[
            vm((32, 128), F32),
            vm((n, 32, 128), F32),
            vm((n, tiles, 128), F32),
            vm((n, tiles, 128), F32),
            vm(wide[0].shape, B16),
            vm(wide[1].shape, B16),
            vm((slots, width), B16),
            vm((slots, width), B16),
            vm((slots, width), B16),
            vm((slots, width), B16),
            vm((slots, width), B16),
            vm((slots, width), B16),
            vm((slots, width), B16),
            vm((slots, width), B16),
            vm((width, hidden), B16),
            vm((hidden, width), B16),
            vm((width, hidden), B16),
            vm((hidden, width), B16),
            vm((slots, hidden), F32),
            vm((slots, width), F32),
        ]
        + [vm((NZ * s.shape[0], s.shape[1] // 2), B16) for s in shards[2:]]
        + [vm((NZ * s.shape[0] // 2, s.shape[1] // 2), B16) for s in shards[2:]]
        + [
            dma((n,)),
            dma((n,)),
            dma((n,)),
            dma((n,)),
        ]
        + [dma((E,))] * 8
        + [dma((4,)), dma((2, hidden // CHUNK)), dma((2, 2)), dma((2,))]
        + Gather.semaphores(2)
        + Column.semaphores()
        + Column.semaphores()
        + Spread.semaphores()
        + Spread.semaphores(),
        compiler_params=params(1),
        name="front_and_expert",
    )(tok, cot, route, cond, ada, adab, qvb, outb, soutb, sinb, router, bin_r, bout_r, *shards, win, wout)


def add_into(target, source, lead):
    count = 1
    for n in lead:
        count *= n

    def body(i, carry):
        at = []
        rest = i
        for n in reversed(lead):
            at.append(lax.rem(rest, n))
            rest = lax.div(rest, n)
        at = tuple(reversed(at))
        target[at] = (target[at].astype(F32) + source(at).astype(F32)).astype(B16)
        return carry

    lax.fori_loop(0, count, body, 0)


def piece_specs(width, hidden):
    rows, tall = width // NZ // 4, hidden // NZ // 4
    qkv = 3 * width // 2
    left = (qkv // 128 + 1) // 2 * 128
    early = (
        (2, (True, 0, rows, 0, hidden // 4, True)),
        (3, (True, 0, tall // 2, 0, width // 2, False)),
        (2, (True, 0, rows, hidden // 4, hidden // 4, False)),
        (3, (True, tall // 2, tall // 2, 0, width // 2, True)),
    )
    late = (
        (0, (False, 0, rows, 0, left, True)),
        (0, (False, 0, rows, left, qkv - left, True)),
        (1, (False, 0, rows, 0, width // 2, True)),
    )
    return early, late


class FirstHop:
    def __init__(self, spec, half, ebuf, sems):
        self.z, self.x, self.y, self.c = coords()
        _, self.row, self.rows, self.col, self.width, self.y_first = spec
        self.half, self.ebuf, self.sems = half, ebuf, sems

    def inner(self, *lead):
        return lead + (slice(self.row, self.row + self.rows), slice(self.col, self.col + self.width))

    def copy(self):
        every = slice(None)
        if self.y_first:
            at, to = self.inner(every, every, 1 - self.y), dev(self.z, self.x, 1 - self.y, self.c)
        else:
            at, to = self.inner(every, 1 - self.x, every), dev(self.z, 1 - self.x, self.y, self.c)
        return remote(self.half.at[at], self.ebuf, self.sems.at[0], self.sems.at[1], to)

    def absorb(self):
        self.copy().wait_recv()
        if self.y_first:
            source = lambda i: self.half[self.inner(i[0], i[1], self.y)]
        else:
            source = lambda i: self.half[self.inner(i[0], self.x, i[1])]
        add_into(self.ebuf, source, (NZ, 2))


def middle_kernel(
    ret, retg, second_r, resid_r, att_r, cot, mod, sinb, bias, router, gates_r, place_r, mixed, outw,
    tok, normed, proj, lsum, condt, ebias, sin_h, sout_h, qkv_h, dwout, dwin,
    out_o, dout, shares, dqkv, tgrad_o, mine_o, e0, e1, e2, e3, came_o, came_w,
    sin, sout, dsin, dsout, sin_half, sout_half, qkv, shared, sgrad, mgrad, rgrad_s, mg2, pgrad, tile,
    hsem, msem, lsem, qsem, s0, s1, s2, s3,
):
    chunks = range(NZ)
    size = sin.shape[3] // NZ
    loads = []
    for f in chunks:
        cols = slice(f * size, (f + 1) * size)
        loads.append(
            (
                pltpu.make_async_copy(sin_h.at[:, :, :, cols], sin.at[:, :, :, cols], lsem.at[0, f]),
                pltpu.make_async_copy(sout_h.at[f], sout.at[f], lsem.at[1, f]),
            )
        )
        for load in loads[-1]:
            load.start()
    qkv_load = pltpu.make_async_copy(qkv_h, qkv, qsem.at[0])
    qkv_load.start()
    barrier = pltpu.get_barrier_semaphore()
    z, x, y, c = coords()
    mate = NZ - 1 - z
    for to in (dev(mate, x, y, c), dev(z, x, y, 1 - c), dev(z, x, 1 - y, c), dev(z, 1 - x, y, c)):
        greet(barrier, to)
    pl.semaphore_wait(barrier, 4)
    central = jnp.logical_and(z > 0, z < NZ - 1)

    def across():
        rows = dwout.shape[0] // 2
        start = pl.multiple_of(lax.div(mate, 2) * rows + CHUNK, 16)
        return remote(
            dwout.at[pl.ds(start, rows - CHUNK), :], came_o, msem.at[0], msem.at[1], dev(mate, x, y, c)
        )

    def across_wide():
        rows = dwin.shape[0] // 2
        start = pl.multiple_of(lax.div(mate, 2) * rows, 16)
        return remote(
            dwin.at[pl.ds(start, rows), 0 : came_w.shape[1]], came_w, msem.at[2], msem.at[3], dev(mate, x, y, c)
        )

    @pl.when(central)
    def _():
        across().start()
        across_wide().start()

    length, width = second_r.shape
    hidden = sin.shape[3]
    chunk = hidden // NZ
    second = second_r[...]
    grad_out = cot[...].astype(F32)
    moe_low = (mod[5:6] * grad_out).astype(B16)
    moe_grad = moe_low.astype(F32)
    shared[...] = jnp.zeros_like(shared) + bias[3:4, :]
    sgrad[...] = jnp.zeros_like(sgrad)
    shares[...] = jnp.zeros_like(shares)
    n = NZ * NX
    part = width // n
    own_tiles = hidden // n // 128

    def cut(at, rows):
        for p in range(n):
            shares[p, at : at + rows.shape[0], 0:part] = rows[:, part * p : part * (p + 1)]

    for p in range(n):
        shares[p, 16 : 16 + own_tiles, :] = ebias[own_tiles * p : own_tiles * (p + 1), :]
        at = hidden // 128 + p
        shares[p, 19:20, 0:part] = ebias[at : at + 1, 0:part]

    def body(f):
        for load in loads[f]:
            load.wait()
        cols = slice(f * chunk, (f + 1) * chunk)
        w1 = sin[:, :, :, cols].reshape(width, chunk)
        w2 = sout[f].reshape(chunk, width)
        act, slope = gelu_parts(dot(second, w1) + sinb[:, cols])
        low = act.astype(B16)
        shared[...] += dot(low, w2)
        pre = (dot_nt(moe_low, w2) * slope).astype(B16)
        dsout[f] = dot_tn(low, moe_low).astype(B16).reshape(dsout.shape[1:])
        dsin[:, :, :, :, cols] = dot_tn(second, pre).astype(B16).reshape(dsin.shape[:4] + (chunk,))
        sgrad[...] += dot_nt(pre, w1)
        col = jnp.sum(pre.astype(F32), axis=0, keepdims=True)
        for j in range(chunk // 128):
            at = f * (chunk // 128) + j
            shares[at // own_tiles, 4 + at % own_tiles : 5 + at % own_tiles, :] = col[
                :, 128 * j : 128 * (j + 1)
            ]

    for f in chunks:
        body(f)
    halves = ((dsin, sin_half), (dsout, sout_half))

    def half_cols(i, core):
        size = halves[i][1].shape[4]
        return pl.ds(pl.multiple_of(core * size, 128), size)

    def half_copy(i):
        return remote(
            halves[i][0].at[:, :, :, :, half_cols(i, 1 - c)], halves[i][1], hsem.at[0, i], hsem.at[1, i],
            dev(z, x, y, 1 - c),
        )

    for i in range(2):
        half_copy(i).start()
    lane = lax.broadcasted_iota(jnp.int32, (length, E), 1)
    gates = [gates_r[:, k : k + 1] for k in range(2)]
    maps = [
        jnp.where(choose_rows(place_r[:, k : k + 1], E * CAP), 1.0, 0.0) for k in range(2)
    ]
    back = ret[...]
    rows = [dot(m.astype(B16), back) for m in maps]
    moe = shared[...] + (gates[0] * rows[0] + gates[1] * rows[1])
    resid = resid_r[...]
    out_o[...] = (resid + mod[5:6] * moe).astype(B16)
    mg2[...] = jnp.zeros_like(mg2)
    mg2[5:6, :] = jnp.sum(grad_out * moe, axis=0, keepdims=True)
    ggrad = [jnp.sum(moe_grad * r, axis=-1, keepdims=True) for r in rows]
    inner = gates[0] * ggrad[0] + gates[1] * ggrad[1]
    lgrad = jnp.zeros((length, E), F32)
    for k in range(2):
        pick = place_r[:, 2 + k : 3 + k] == lane
        lgrad = lgrad + jnp.where(pick, gates[k] * (ggrad[k] - inner), 0.0)
    lgrad = lgrad.astype(B16)
    cut(8, dot_tn(lgrad, second))
    grad = (
        sgrad[...]
        + dot((maps[0] + maps[1]).astype(B16), retg[...])
        + dot(lgrad, router[...].astype(B16))
    )
    n2, r2 = norm_parts(resid)
    mg2[3:4, :] = jnp.sum(grad, axis=0, keepdims=True)
    mg2[4:5, :] = jnp.sum(grad * n2, axis=0, keepdims=True)
    rgrad = grad_out + norm_back(grad * (1.0 + mod[4:5]), n2, r2)
    rgrad_s[...] = rgrad
    agrad = (mod[2:3] * rgrad).astype(B16)
    mg2[2:3, :] = jnp.sum(rgrad * att_r[...], axis=0, keepdims=True)
    dout[...] = dot_tn(mixed[...], agrad).astype(B16)
    mgrad[...] = dot_nt(agrad, outw[...]).astype(B16)
    cut(3, jnp.sum(moe_grad, axis=0, keepdims=True))
    cut(2, jnp.sum(agrad.astype(F32), axis=0, keepdims=True))
    for i in range(2):
        half_copy(i).wait_recv()
        whole, kept = halves[i]
        own = half_cols(i, c)
        add_into(kept, lambda at: whole[at[0], at[1], at[2], :, own], (NZ, NX, 2))
        half_copy(i).wait_send()
    hops = [
        FirstHop(spec, sin_half if matrix == 2 else sout_half, ebuf, sem)
        for (matrix, spec), ebuf, sem in zip(
            piece_specs(width, hidden)[0], (e0, e1, e2, e3), (s0, s1, s2, s3)
        )
    ]
    for hop in hops:
        hop.copy().start()

    low_lane = lax.broadcasted_iota(jnp.int32, (length, 128), 1) < HEAD_DIM
    for p in range(HEADS // 2):
        q2 = proj[:, 128 * p : 128 * (p + 1)]
        k2 = proj[:, width + 128 * p : width + 128 * (p + 1)]
        v2 = proj[:, 2 * width + 128 * p : 2 * width + 128 * (p + 1)]
        m2 = mgrad[:, 128 * p : 128 * (p + 1)]
        parts = []
        for h in range(2):
            head = low_lane if h == 0 else jnp.logical_not(low_lane)
            zero = jnp.zeros_like(q2)
            s = dot_nt(jnp.where(head, q2, zero), k2) * SCALE
            prob = jnp.exp(s - lsum[:, 2 * p + h : 2 * p + h + 1])
            pg = dot_nt(jnp.where(head, m2, zero), v2)
            inner = jnp.sum(prob * pg, axis=-1, keepdims=True)
            sg = (prob * (pg - inner)).astype(B16)
            parts.append(
                (dot(sg, k2) * SCALE, dot_tn(sg, q2) * SCALE, dot_tn(prob.astype(B16), m2))
            )
        for i in range(3):
            pgrad[:, i * width + 128 * p : i * width + 128 * (p + 1)] = jnp.where(
                low_lane, parts[0][i], parts[1][i]
            ).astype(B16)
    lead = dqkv.shape[:4]
    for i in range(3):
        cols = slice(i * width, (i + 1) * width)
        dqkv[:, :, :, :, cols] = dot_tn(normed[...], pgrad[:, cols]).astype(B16).reshape(lead + (width,))
    qkv_load.wait()
    ngrad = dot_nt(pgrad[...], qkv[...])
    n1, r1 = norm_parts(tok[...].astype(F32))
    tgrad_o[...] = rgrad_s[...] + norm_back(ngrad * (1.0 + mod[1:2]), n1, r1)
    per = width // 128
    for i, k in enumerate((0, 2)):
        cut(i, jnp.sum(pgrad[:, k * width : (k + 1) * width].astype(F32), axis=0, keepdims=True))
    mod_rows = [
        jnp.sum(ngrad, axis=0, keepdims=True),
        jnp.sum(ngrad * n1, axis=0, keepdims=True),
    ] + [mg2[i : i + 1, :] for i in range(2, 6)]
    tile[...] = jnp.zeros_like(tile)
    for i, row in enumerate(mod_rows):
        row = row.astype(B16).astype(F32)
        for j in range(per):
            tile[i * per + j : i * per + j + 1, :] = row[:, 128 * j : 128 * (j + 1)]
    tile[40:48, :] = condt[...]
    mine_o[...] = tile[...].astype(B16)
    for hop in hops:
        hop.absorb()
    for hop in hops:
        hop.copy().wait_send()

    @pl.when(central)
    def _():
        across().wait()
        across_wide().wait()


def middle(*args):
    second, sin = args[2], args[20]
    length, width = second.shape
    hidden = sin.shape[3]
    rows, tall = width // NZ // 4, hidden // NZ // 4
    dma = pltpu.SemaphoreType.DMA
    vm = pltpu.VMEM
    early = piece_specs(width, hidden)[0]
    return pl.pallas_call(
        middle_kernel,
        out_shape=[
            sds((length, width), B16),
            sds((width, width), B16),
            sds((NZ * NX, 24, 128), F32),
            sds((NZ, NX, 2, rows, 3 * width), B16),
            sds((length, width), F32),
            sds((48, 128), B16),
        ]
        + [sds((NZ, 2, spec[2], spec[4]), B16) for _, spec in early]
        + [
            sds((hidden // 2 - CHUNK, width), B16),
            sds((width // 2, hidden // MidSum.COUNT), B16),
        ],
        in_specs=[VM] * 20 + [HB] * 5,
        out_specs=[VM] * 10 + [HB] * 2,
        scratch_shapes=[
            vm(sin.shape, B16),
            vm((NZ, NX, hidden // NZ // NX, width), B16),
            vm((NZ, NX, 2, rows, hidden), B16),
            vm((NZ, NX, 2, tall, width), B16),
            vm((NZ, NX, 2, rows, hidden // 2), B16),
            vm((NZ, NX, 2, tall, width // 2), B16),
            vm((width, 3 * width), B16),
            vm((length, width), F32),
            vm((length, width), F32),
            vm((length, width), B16),
            vm((length, width), F32),
            vm((8, width), F32),
            vm((length, 3 * width), B16),
            vm((48, 128), F32),
            dma((2, 2)),
            dma((4,)),
            dma((2, NZ)),
            dma((1,)),
        ]
        + [dma((2,))] * 4,
        compiler_params=params(3),
        name="shared_expert_attention_back",
    )(*args)


class Piece:
    def __init__(self, spec, grad, out, bufs):
        self.z, self.x, self.y, self.c = coords()
        self.half, self.row, self.rows, self.col, self.width, self.y_first = spec
        self.grad, self.out = grad, out
        self.size = out.shape[-1] // 2
        if self.half:
            self.ebuf = grad
        else:
            self.cbuf, self.ebuf, bufs = bufs[0], bufs[1], bufs[2:]
        self.fbuf, self.zin, self.one, self.zsem = bufs
        self.inner = jnp.logical_and(self.z > 0, self.z < NZ - 1)
        self.end = jnp.logical_not(self.inner)
        self.mate = NZ - 1 - self.z
        self.beside = self.z + 1 - 2 * lax.rem(self.z, 2)

    @staticmethod
    def scratch(spec):
        half, _, rows, _, width, _ = spec
        vm = lambda *lead: pltpu.VMEM(lead + (rows, width), B16)
        dma = pltpu.SemaphoreType.DMA
        return ([] if half else [vm(NZ, NX, 2), vm(NZ, 2)]) + [
            vm(NZ),
            vm(NZ + 3),
            dma((13,)),
            dma((2, 3)),
        ]

    def cols(self, c):
        return pl.ds(pl.multiple_of(c * self.size + self.col, 128), self.width)

    def core_copy(self):
        return remote(
            self.grad.at[:, :, :, :, self.cols(1 - self.c)],
            self.cbuf,
            self.one.at[0],
            self.one.at[1],
            dev(self.z, self.x, self.y, 1 - self.c),
        )

    def to_x(self):
        return dev(self.z, 1 - self.x, self.y, self.c)

    def to_y(self):
        return dev(self.z, self.x, 1 - self.y, self.c)

    def copy1(self):
        every = slice(None)
        if self.y_first:
            source, to = self.cbuf.at[every, every, 1 - self.y], self.to_y()
        else:
            source, to = self.cbuf.at[every, 1 - self.x], self.to_x()
        return remote(source, self.ebuf, self.one.at[3], self.one.at[4], to)

    def copy2(self):
        if self.y_first:
            source, to = self.ebuf.at[:, 1 - self.x], self.to_x()
        else:
            source, to = self.ebuf.at[:, 1 - self.y], self.to_y()
        return remote(source, self.fbuf, self.one.at[5], self.one.at[6], to)

    def zcopy(self, step):
        if step == 0:
            at = pl.ds(jnp.where(lax.rem(self.z, NZ - 1) == 0, lax.rem(self.z + 1, NZ), 0), NZ - 1)
            source, target, to = self.fbuf.at[at], self.zin.at[at], self.beside
        elif step == 1:
            at = pl.ds(2 * lax.div(self.mate, 2), 2)
            source, target, to = self.fbuf.at[at], self.zin.at[NZ : NZ + 2], self.mate
        else:
            source, target, to = self.fbuf.at[self.beside], self.zin.at[NZ + 2], self.beside
        return remote(
            source, target, self.zsem.at[0, step], self.zsem.at[1, step], dev(to, self.x, self.y, self.c)
        )

    def plus(self, block, came):
        self.fbuf[block] = (self.fbuf[block].astype(F32) + self.zin[came].astype(F32)).astype(B16)

    def own(self):
        return self.fbuf.at[self.z]

    def place(self, y, c):
        return self.out.at[y, self.row : self.row + self.rows, self.cols(c)]

    def keep(self):
        return pltpu.make_async_copy(self.own(), self.place(self.y, self.c), self.one.at[7])

    def give_y(self, came=False):
        at = self.place(1 - self.y if came else self.y, self.c)
        return remote(self.own(), at, self.one.at[8], self.one.at[9], self.to_y())

    def give_c(self, came=False):
        at = self.place(self.y, 1 - self.c if came else self.c)
        to = dev(self.z, self.x, self.y, 1 - self.c)
        return remote(self.own(), at, self.one.at[10], self.one.at[11], to)

    def pass_c(self, came=False):
        at = self.place(1 - self.y, 1 - self.c if came else self.c)
        to = dev(self.z, self.x, self.y, 1 - self.c)
        return remote(at, at, self.one.at[12], self.one.at[2], to)

    def stage(self, s):
        if s == 0 and not self.half:
            self.core_copy().wait_recv()
            mine = self.cols(self.c)
            add_into(self.cbuf, lambda i: self.grad[i[0], i[1], i[2], :, mine], (NZ, NX, 2))
            self.copy1().start()
        elif s == 1:
            if not self.half:
                self.copy1().wait_recv()
                if self.y_first:
                    add_into(self.ebuf, lambda i: self.cbuf[i[0], i[1], self.y], (NZ, NX))
                else:
                    add_into(self.ebuf, lambda i: self.cbuf[i[0], self.x, i[1]], (NZ, 2))
            self.copy2().start()
        elif s == 2:
            self.copy2().wait_recv()
            side = self.x if self.y_first else self.y
            add_into(self.fbuf, lambda i: self.ebuf[i[0], side], (NZ,))
            pl.when(self.end)(lambda: self.zcopy(0).start())
        elif s == 3:

            @pl.when(self.inner)
            def _():
                self.zcopy(0).wait_recv()
                first = lax.rem(self.z, 2)
                for i in range(NZ - 1):
                    self.plus(first + i, first + i)
                self.zcopy(1).start()

        elif s == 4:

            @pl.when(self.inner)
            def _():
                self.zcopy(1).wait_recv()
                for i in range(2):
                    self.plus(2 * lax.div(self.z, 2) + i, NZ + i)
                self.zcopy(2).start()

        elif s == 5:

            @pl.when(self.end)
            def _():
                self.zcopy(2).wait_recv()
                self.plus(self.z, NZ + 2)

            self.give_y().start()
            self.give_c().start()
            self.keep().start()
        elif s == 6:
            self.give_y(True).wait_recv()
            self.pass_c().start()
        elif s == 7:
            self.keep().wait()
            self.give_c(True).wait_recv()
            self.pass_c(True).wait_recv()
            if not self.half:
                self.core_copy().wait_send()
                self.copy1().wait_send()
            self.copy2().wait_send()
            self.give_y().wait_send()
            self.give_c().wait_send()
            self.pass_c().wait_send()
            pl.when(self.end)(lambda: self.zcopy(0).wait_send())

            @pl.when(self.inner)
            def _():
                self.zcopy(1).wait_send()
                self.zcopy(2).wait_send()


class MidSum:
    COUNT = 6

    def __init__(self, origin, grad, into, out, total, outer, sems):
        self.z, self.x, self.y, self.c = coords()
        self.origin = origin
        self.grad, self.into, self.out, self.total, self.outer = grad, into, out, total, outer
        self.sems = sems
        self.size = grad.shape[2] // self.COUNT
        self.inner = jnp.logical_and(self.z > 0, self.z < NZ - 1)
        self.end = jnp.logical_not(self.inner)
        self.mate = NZ - 1 - self.z

    @staticmethod
    def scratch(shape):
        vm = pltpu.VMEM
        return [vm(shape[1:], B16), vm(shape[1:], B16), pltpu.SemaphoreType.DMA((9, MidSum.COUNT))]

    def cols(self, p):
        return slice(p * self.size, (p + 1) * self.size)

    @staticmethod
    def beside(z):
        return z + 1 - 2 * lax.rem(z, 2)

    def landing(self, z, block):
        rows = self.grad.shape[1]
        return pl.ds(pl.multiple_of((block - 2 * lax.div(z, 2)) * rows, 16), rows)

    def across(self, i, p, came=False):
        z = self.z if came else self.mate
        block = self.beside(z) if i == 0 else z
        return remote(
            self.origin.at[block, :, self.cols(p)],
            self.into.at[self.landing(z, block), self.cols(p)],
            self.sems.at[i, p],
            self.sems.at[2 + i, p],
            dev(self.mate, self.x, self.y, self.c),
        )

    def came(self, block, p):
        return self.into[self.landing(self.z, block), self.cols(p)].astype(F32)

    def outward(self, p):
        return remote(
            self.outer.at[:, self.cols(p)],
            self.total.at[:, self.cols(p)],
            self.sems.at[4, p],
            self.sems.at[5, p],
            dev(self.beside(self.z), self.x, self.y, self.c),
        )

    def begin(self, i, p):
        pl.when(self.inner)(lambda: self.across(i, p).start())

    def give(self, p, sent=True):
        @pl.when(self.inner)
        def _():
            if sent:
                self.across(0, p, True).wait_recv()
            cols = self.cols(p)
            self.outer[:, cols] = (
                self.grad[self.beside(self.z), :, cols].astype(F32) + self.came(self.beside(self.z), p)
            ).astype(B16)
            self.outward(p).start()

    def swap(self, p, came=False):
        part = self.total.shape[0] // NX
        start = pl.multiple_of((1 - self.x) * part, 16)
        return remote(
            self.total.at[pl.ds(start, part), self.cols(p)],
            self.out.at[1 - self.x if came else self.x, :, self.cols(p)],
            self.sems.at[6, p],
            self.sems.at[7, p],
            dev(self.z, 1 - self.x, self.y, self.c),
        )

    def keep(self, p):
        part = self.total.shape[0] // NX
        start = pl.multiple_of(self.x * part, 16)
        return pltpu.make_async_copy(
            self.total.at[pl.ds(start, part), self.cols(p)],
            self.out.at[self.x, :, self.cols(p)],
            self.sems.at[8, p],
        )

    def final(self, p, sent=True):
        @pl.when(self.inner)
        def _():
            if sent:
                self.across(1, p, True).wait_recv()
            cols = self.cols(p)
            self.total[:, cols] = (
                self.grad[self.z, :, cols].astype(F32) + self.came(self.z, p)
            ).astype(B16)

        pl.when(self.end)(lambda: self.outward(p).wait_recv())
        self.swap(p).start()
        self.keep(p).start()

    def close(self, sent):
        for p in range(self.COUNT):

            @pl.when(self.inner)
            def _():
                self.outward(p).wait_send()
                if p in sent:
                    self.across(0, p).wait_send()
                    self.across(1, p).wait_send()

            self.swap(p, True).wait_recv()
            self.swap(p).wait_send()
            self.keep(p).wait()


def tail_kernel(*refs):
    ebufs, dqkv, dout = refs[:4], refs[4], refs[5]
    shares, mine, ada = refs[6:9]
    dwin_h, dwout_h, came_a, came_b, came_w = refs[9:14]
    outs = refs[14:18]
    pair_in, pair_out, small, esum, tiles, cgot = refs[18:24]
    rest = list(refs[24:])
    z, x, y, c = coords()
    dp, ex = lax.axis_index("dp"), lax.axis_index("expert")
    n = NZ * NX
    width = dwout_h.shape[2]
    early_specs, late_specs = piece_specs(width, dwin_h.shape[2])
    dwin, dwout, lsem = rest[:3]
    rest = rest[3:]

    def make(specs, rest, sources):
        made = []
        for (matrix, spec), source in zip(specs, sources):
            count = len(Piece.scratch(spec))
            made.append(Piece(spec, source, outs[matrix], rest[:count]))
            rest = rest[count:]
        return made, rest

    early, rest = make(early_specs, rest, ebufs)
    late, rest = make(late_specs, rest, (dqkv, dqkv, dout))
    wide = MidSum(dwin_h, dwin, rest[0], pair_in, *rest[1:4])
    tall = MidSum(dwout_h, dwout, rest[4], pair_out, *rest[5:8])
    rest = rest[8:]
    first_rows = came_a.shape[0]
    loads = [
        pltpu.make_async_copy(came_a, tall.into.at[0:first_rows, :], lsem.at[0]),
        pltpu.make_async_copy(came_b, tall.into.at[first_rows:, :], lsem.at[1]),
        pltpu.make_async_copy(dwout_h, dwout, lsem.at[2]),
        pltpu.make_async_copy(dwin_h, dwin, lsem.at[3]),
        pltpu.make_async_copy(came_w, wide.into.at[:, 0 : came_w.shape[1]], lsem.at[4]),
    ]
    sgot, dall, floats, csend, dsem, tsem = rest

    barrier = pltpu.get_barrier_semaphore()

    def peers(action):
        for p in range(n):

            @pl.when(p != dp)
            def _():
                action(p)

    peers(lambda p: greet(barrier, (p, ex)))
    mates = (dev(z, x, 1 - y, c), dev(z, x, y, 1 - c), dev(z, x, 1 - y, 1 - c))
    for mate in mates:
        greet(barrier, mate)
    pl.semaphore_wait(barrier, n - 1 + 3)

    def share_copy(p, at):
        return remote(shares.at[p], sgot.at[at], dsem.at[4, p], dsem.at[5, at], (p, ex))

    def tile(p, at):
        return remote(mine, tiles.at[ex, at], dsem.at[0, p], dsem.at[1, at], (p, ex))

    def mate_rank(i):
        return 2 * (1 - y if i != 1 else y) + (1 - c if i != 0 else c)

    def spread(i, theirs=False):
        rows = tiles.at[mate_rank(i) if theirs else ex]
        return remote(rows, rows, tsem.at[0, i], tsem.at[1, i], mates[i])

    def total_copy(i, theirs=False):
        rows = dall.at[mate_rank(i) if theirs else ex]
        return remote(rows, rows, tsem.at[2, i], tsem.at[3, i], mates[i])

    def cond_copy(p, at):
        return remote(csend.at[p], cgot.at[at], dsem.at[2, p], dsem.at[3, at], (p, ex))

    peers(lambda p: share_copy(p, dp).start())
    peers(lambda p: tile(p, dp).start())

    every = range(MidSum.COUNT)
    for piece in early:
        piece.stage(1)
    for piece in late:
        piece.core_copy().start()
    for p in every[1:]:
        for i in range(2):
            wide.begin(i, p)
    for load in loads:
        load.start()
    sgot[dp] = shares[dp]
    tiles[ex, dp] = mine[...]

    def small1():
        peers(lambda p: share_copy(p, p).wait_recv())
        peers(lambda p: tile(p, p).wait_recv())
        total = sgot[0, 0:16, :]
        for p in range(1, n):
            total = total + sgot[p, 0:16, :]
        dall[ex] = total
        for i in range(NX):
            own = sgot[i, 16:24, :]
            for zb in range(1, NZ):
                own = own + sgot[NX * zb + i, 16:24, :]
            esum[i] = own
        for i in range(3):
            total_copy(i).start()
            spread(i).start()
        floats[...] = tiles[ex].astype(F32)
        acc = jnp.zeros((n, ada.shape[0]), F32)
        for j in range(ada.shape[1] // 128):
            acc = acc + dot_nt(floats[:, j, :].astype(B16), ada[:, 128 * j : 128 * (j + 1)])
        csend[...] = jnp.zeros_like(csend)
        csend[:, 0, 0 : ada.shape[0]] = acc
        peers(lambda p: cond_copy(p, dp).start())
        cgot[dp] = csend[dp]

    def small2():
        for i in range(3):
            total_copy(i, True).wait_recv()
            spread(i, True).wait_recv()
        total = dall[0]
        for i in range(1, 4):
            total = total + dall[i]
        small[...] = total
        peers(lambda p: cond_copy(p, p).wait_recv())
        for i in range(3):
            total_copy(i).wait_send()
            spread(i).wait_send()
        peers(lambda p: share_copy(p, p).wait_send())
        peers(lambda p: tile(p, p).wait_send())
        peers(lambda p: cond_copy(p, p).wait_send())

    def run(pieces, s):
        for piece in pieces:
            piece.stage(s)

    run(late, 0)
    for load in loads[:3]:
        load.wait()
    for p in every:
        tall.give(p, False)
    for load in loads[3:]:
        load.wait()
    wide.give(0, False)
    small1()
    run(early, 2)
    for p in every[1:3]:
        wide.give(p)
    run(late, 1)
    run(early, 3)
    for p in every:
        tall.final(p, False)
    run(early, 4)
    for p in every[3:]:
        wide.give(p)
    run(late, 2)
    run(early, 5)
    wide.final(0, False)
    run(late, 3)
    for p in every[1:3]:
        wide.final(p)
    run(early, 6)
    run(late, 4)
    for p in every[3:]:
        wide.final(p)
    run(late, 5)
    run(early, 7)
    small2()
    run(late, 6)
    run(late, 7)
    tall.close(())
    wide.close(every[1:])


def tail_part(ebufs, dqkv, dout, shares, mine, ada, dwin, dwout, came_a, came_b, came_w):
    n = NZ * NX
    dma = pltpu.SemaphoreType.DMA
    vm = pltpu.VMEM
    width, hidden = dwout.shape[2], dwin.shape[2]
    rows, tall = width // NZ // 4, hidden // NZ // 4
    outs = [
        sds((2, rows, 3 * width), B16),
        sds((2, rows, width), B16),
        sds((2, rows, hidden), B16),
        sds((2, tall, width), B16),
    ]
    scratch = [vm(dwin.shape, B16), vm(dwout.shape, B16), dma((5,))]
    for specs in piece_specs(width, hidden):
        for _, spec in specs:
            scratch += Piece.scratch(spec)
    for shape in (dwin.shape, dwout.shape):
        scratch += [vm((2 * shape[1], shape[2]), B16)] + MidSum.scratch(shape)
    scratch += [
        vm(shares.shape, F32),
        vm((4, 16, 128), F32),
        vm((n, 48, 128), F32),
        vm((n, 8, 128), F32),
        dma((6, n)),
        dma((4, 3)),
    ]
    out = pl.pallas_call(
        tail_kernel,
        out_shape=outs
        + [
            sds((NX, dwin.shape[1] // NX, hidden), B16),
            sds((NX, dwout.shape[1] // NX, width), B16),
            sds((16, 128), F32),
            sds((NX, 8, 128), F32),
            sds((4, n, 48, 128), B16),
            sds((n, 8, 128), F32),
        ],
        in_specs=[VM] * 9 + [HB] * 5,
        out_specs=[HB] * 6 + [VM] * 4,
        scratch_shapes=scratch,
        compiler_params=params(4),
        name="device_sums",
    )(
        *ebufs,
        dqkv,
        dout.reshape(NZ, NX, 2, rows, width),
        shares,
        mine,
        ada,
        dwin,
        dwout,
        came_a,
        came_b,
        came_w,
    )
    return [o.reshape(-1, o.shape[2]) for o in out[:4]], out[4:6], out[6:]


def pick_part(flat, part, dp):
    chosen = jnp.zeros((flat.shape[0], part), flat.dtype)
    for p in range(NZ * NX):
        chosen = jnp.where(dp == p, flat[:, p * part : (p + 1) * part], chosen)
    return chosen


def finish_kernel(*refs):
    large = refs[:6]
    small, esum, tiles, cgot, cond = refs[6:11]
    outs = refs[11:17]
    ada_o, adab_o, qvb_o, outb_o, sinb_o, soutb_o, router_o, einb_o, eoutb_o, cond_o = refs[17:27]
    bufs, floats, sems = refs[27:33], refs[33], refs[34]
    dp = lax.axis_index("dp")
    n = NZ * NX
    copies = []
    for i in (4, 5, 2, 3, 0, 1):
        bufs[i][...] = large[i][...].astype(F32)
        copies.append(pltpu.make_async_copy(bufs[i], outs[i], sems.at[i]))
        copies[-1].start()
    width = cond.shape[1]
    per, part = width // 128, width // n
    hidden = sinb_o.shape[1] * n
    images = tiles.shape[0] * tiles.shape[1]
    floats[...] = tiles[...].astype(F32)
    qvb_o[...] = small[0:2, 0:part]
    outb_o[...] = small[2:3, 0:part]
    soutb_o[...] = small[3:4, 0:part]
    router_o[...] = small[8:16, 0:part]
    for j in range(hidden // n // 128):
        cols = slice(128 * j, 128 * (j + 1))
        sinb_o[:, cols] = small[4 + j : 5 + j, :]
        for i in range(NX):
            einb_o[i : i + 1, cols] = esum[i, j : j + 1, :]
    for i in range(NX):
        eoutb_o[i : i + 1, :] = esum[i, 3:4, 0:part]

    conds = jnp.concatenate(
        [floats[:, :, 40 + j, :].reshape(images, 128) for j in range(per)], axis=1
    )
    conds = pick_part(conds, part, dp).astype(B16)
    sums = []
    for j in range(6 * per):
        mods = floats[:, :, j, :].reshape(images, 128)
        ada_o[:, 128 * j : 128 * (j + 1)] = dot_tn(conds, mods.astype(B16))
        sums.append(jnp.sum(mods, axis=0, keepdims=True))
    adab_o[...] = pick_part(jnp.concatenate(sums, axis=1), adab_o.shape[1], dp)
    v = cond[...].astype(F32)
    sig = 1.0 / (1.0 + jnp.exp(-v))
    grad = jnp.concatenate([cgot[p, 0:1, 0:part] for p in range(n)], axis=1)
    cond_o[...] = grad * (sig * (1.0 + v * (1.0 - sig)))
    for copy in copies:
        copy.wait()


def finish(dense, pairs, small, esum, tiles, cgot, cond, hidden):
    n = NZ * NX
    width = cond.shape[1]
    part = width // n
    big = [sds(v.shape, F32) for v in (*dense, *pairs)]
    short = [
        sds((part, 6 * width), F32),
        sds((1, 6 * part), F32),
        sds((2, part), F32),
        sds((1, part), F32),
        sds((1, hidden // n), F32),
        sds((1, part), F32),
        sds((E, part), F32),
        sds((NX, hidden // n), F32),
        sds((NX, part), F32),
        sds((1, width), F32),
    ]
    return pl.pallas_call(
        finish_kernel,
        out_shape=big + short,
        in_specs=[VM] * 11,
        out_specs=[HB] * 6 + [VM] * 10,
        scratch_shapes=[pltpu.VMEM(v.shape, F32) for v in big]
        + [pltpu.VMEM(tiles.shape, F32), pltpu.SemaphoreType.DMA((6,))],
        compiler_params=params(),
        name="final_form",
    )(*dense, *pairs, small, esum, tiles, cgot, cond)


def on_block(
    tokens, conditioning, routes, cotangent, ada_weight, ada_bias, qkv_weight, qv_bias, out_weight, out_bias,
    shared_in, shared_in_bias, shared_out, shared_out_bias, router,
    expert_in, expert_in_bias, expert_out, expert_out_bias,
):
    n = NZ * NX
    width = tokens.shape[2]
    hidden = shared_in.shape[1]
    part = width // n
    tok, cot, route = tokens[0], cotangent[0], routes[0]
    (
        normed, proj, lsum, mixed, att, resid, second, gates, place, mod, bias, sinb, router_t,
        condt, ebias, ret, retg, qkv_full, out_full, sin_full, sout_full, dwin, dwout, came_a,
    ) = lead_part(
        tok, cot, route.T, conditioning, ada_weight, ada_bias[None], qv_bias, out_bias[None], shared_out_bias[None],
        shared_in_bias[None], router.T, expert_in_bias, expert_out_bias,
        (qkv_weight, out_weight, shared_in, shared_out), expert_in, expert_out,
    )
    (output, dout, shares, dqkv, tgrad, mine, e0, e1, e2, e3, came_b, came_w) = middle(
        ret, retg, second, resid, att, cot, mod, sinb, bias, router_t, gates, place, mixed, out_full,
        tok, normed, proj, lsum, condt, ebias, sin_full, sout_full, qkv_full, dwout, dwin,
    )
    dense, pairs, (small, esum, tiles, cgot) = tail_part(
        (e0, e1, e2, e3), dqkv, dout, shares, mine, ada_weight,
        dwin.reshape(NZ, NX * part, hidden), dwout.reshape(NZ, hidden // NZ, width), came_a, came_b, came_w,
    )
    (
        qkv_grad, out_grad, sin_grad, sout_grad, dwin_sum, dwout_sum, ada_grad, adab_grad, qvb_grad, outb_grad,
        sinb_grad, soutb_grad, router_grad, ein_b, eout_b, cond_grad,
    ) = finish(dense, pairs, small, esum, tiles, cgot, conditioning, hidden)
    return (
        output[None],
        tgrad[None],
        cond_grad,
        ada_grad,
        adab_grad[0],
        qkv_grad,
        qvb_grad,
        out_grad,
        outb_grad[0],
        sin_grad,
        sinb_grad[0],
        sout_grad,
        soutb_grad[0],
        router_grad.T,
        dwin_sum,
        ein_b,
        dwout_sum,
        eout_b,
    )


def layer_norm(rows):
    centred = rows - jnp.mean(rows, axis=-1, keepdims=True)
    return centred * lax.rsqrt(jnp.mean(centred * centred, axis=-1, keepdims=True) + 1e-06)


def modulate(rows, shift, scale):
    return layer_norm(rows) * (1.0 + scale) + shift


def gelu_tanh(values_in):
    return jax.nn.gelu(values_in, approximate=True)


def on_device(
    tokens,
    conditioning,
    routes,
    cotangent,
    ada_weight,
    ada_bias,
    qkv_weight,
    qv_bias,
    out_weight,
    out_bias,
    shared_in,
    shared_in_bias,
    shared_out,
    shared_out_bias,
    router,
    expert_in,
    expert_in_bias,
    expert_out,
    expert_out_bias,
):
    f32 = jnp.float32
    b16 = jnp.bfloat16
    gathered_dense = (
        lax.all_gather(ada_weight, "dp", axis=0, tiled=True),
        lax.all_gather(ada_bias, "dp", axis=0, tiled=True),
        lax.all_gather(qkv_weight, "dp", axis=0, tiled=True),
        lax.all_gather(qv_bias, "dp", axis=1, tiled=True),
        lax.all_gather(out_weight, "dp", axis=0, tiled=True),
        lax.all_gather(out_bias, "dp", axis=0, tiled=True),
        lax.all_gather(shared_in, "dp", axis=0, tiled=True),
        lax.all_gather(shared_in_bias, "dp", axis=0, tiled=True),
        lax.all_gather(shared_out, "dp", axis=0, tiled=True),
        lax.all_gather(shared_out_bias, "dp", axis=0, tiled=True),
        lax.all_gather(router, "dp", axis=0, tiled=True),
    )
    (
        ada_full,
        ada_bias_full,
        qkv_full,
        qv_bias_full,
        out_full,
        out_bias_full,
        shared_in_full,
        shared_in_bias_full,
        shared_out_full,
        shared_out_bias_full,
        router_full,
    ) = gathered_dense
    image_count, length, width = tokens.shape
    row_count = image_count * length
    scaling = HEAD_DIM ** (-0.5)
    head_shape = (image_count, length, HEADS, HEAD_DIM)
    cond_float = conditioning.astype(f32)
    cond_act, silu_back = jax.vjp(jax.nn.silu, cond_float)
    cond_low = cond_act.astype(b16)
    modulation = jnp.dot(cond_low, ada_full, preferred_element_type=f32) + ada_bias_full.astype(f32)
    pieces = [modulation[:, None, index * width : (index + 1) * width] for index in range(6)]
    source = tokens.astype(f32)
    first_norm, first_back = jax.vjp(modulate, source, pieces[0], pieces[1])
    normed = first_norm.astype(b16)
    projected = jnp.einsum("isd,de->ise", normed, qkv_full, preferred_element_type=f32)
    query_heads = (
        (projected[..., :width] + qv_bias_full[0].astype(f32)).astype(b16).reshape(head_shape)
    )
    key_heads = projected[..., width : 2 * width].astype(b16).reshape(head_shape)
    value_heads = (
        (projected[..., 2 * width :] + qv_bias_full[1].astype(f32)).astype(b16).reshape(head_shape)
    )
    scores = (
        jnp.einsum("iqhc,ikhc->ihqk", query_heads, key_heads, preferred_element_type=f32) * scaling
    )
    peak_score = jnp.max(scores, axis=-1, keepdims=True)
    unscaled = jnp.exp(scores - peak_score)
    exp_total = jnp.sum(unscaled, axis=-1, keepdims=True)
    log_total = peak_score + jnp.log(exp_total)
    probs_low = (unscaled / exp_total).astype(b16)
    mixed = (
        jnp.einsum("ihqk,ikhc->iqhc", probs_low, value_heads, preferred_element_type=f32)
        .reshape(image_count, length, width)
        .astype(b16)
    )
    attended = jnp.einsum(
        "isd,de->ise", mixed, out_full, preferred_element_type=f32
    ) + out_bias_full.astype(f32)
    resid = source + pieces[2] * attended
    second_float, second_back = jax.vjp(modulate, resid, pieces[3], pieces[4])
    second = second_float.astype(b16)
    shared_pre = jnp.einsum(
        "isd,df->isf", second, shared_in_full, preferred_element_type=f32
    ) + shared_in_bias_full.astype(f32)
    shared_act, shared_gelu_back = jax.vjp(gelu_tanh, shared_pre)
    shared_low = shared_act.astype(b16)
    shared = jnp.einsum(
        "isf,fd->isd", shared_low, shared_out_full, preferred_element_type=f32
    ) + shared_out_bias_full.astype(f32)
    second_rows = second.reshape(row_count, width)
    logits = jnp.dot(second_rows, router_full, preferred_element_type=f32)
    route_flat = routes.reshape(-1)
    one_hot = (route_flat[:, None] == jnp.arange(E, dtype=jnp.int32)).astype(jnp.int32)
    slot_index = jnp.sum(
        (jnp.cumsum(one_hot, axis=0, dtype=jnp.int32) - one_hot) * one_hot, axis=1, dtype=jnp.int32
    )
    position = jnp.where(slot_index < CAP, route_flat * CAP + slot_index, E * CAP)
    pair_rows = jnp.repeat(second_rows, 2, axis=0)
    buffer = (
        jnp.zeros((E * CAP, width), b16)
        .at[position]
        .set(pair_rows, mode="drop")
        .reshape(E, CAP, width)
    )
    received = lax.all_to_all(buffer, "expert", split_axis=0, concat_axis=1, tiled=True)
    expert_pre = (
        jnp.einsum("erd,edf->erf", received, expert_in, preferred_element_type=f32)
        + expert_in_bias.astype(f32)[:, None, :]
    )
    expert_low = gelu_tanh(expert_pre).astype(b16)
    expert_result = (
        jnp.einsum("erf,efd->erd", expert_low, expert_out, preferred_element_type=f32)
        + expert_out_bias.astype(f32)[:, None, :]
    ).astype(b16)
    returned = lax.all_to_all(
        expert_result, "expert", split_axis=1, concat_axis=0, tiled=True
    ).reshape(E * CAP, width)
    gathered = (
        returned.at[position]
        .get(mode="fill", fill_value=0)
        .reshape(row_count, 2, width)
        .astype(f32)
    )
    pair_mask = one_hot.reshape(row_count, 2, E).astype(f32)
    chosen = jnp.sum(logits[:, None, :] * pair_mask, axis=-1)
    gates = jax.nn.softmax(chosen, axis=-1)
    moe = (shared.reshape(row_count, width) + jnp.sum(gates[..., None] * gathered, axis=1)).reshape(
        image_count, length, width
    )
    output = (resid + pieces[5] * moe).astype(b16)
    ada_back, qkv_back, out_back, shared_in_back, shared_out_back, router_back = (
        ada_full,
        qkv_full,
        out_full,
        shared_in_full,
        shared_out_full,
        router_full,
    )
    grad_out = cotangent.astype(f32)
    gate_two_grad = jnp.sum(grad_out * moe, axis=1, keepdims=True)
    moe_grad = (pieces[5] * grad_out).astype(b16)
    moe_rows_grad = moe_grad.reshape(row_count, width)
    moe_rows_float = moe_rows_grad.astype(f32)
    pair_grad = (
        (gates[..., None] * moe_rows_float[:, None, :]).astype(b16).reshape(2 * row_count, width)
    )
    gate_grad = jnp.sum(moe_rows_float[:, None, :] * gathered, axis=-1)
    chosen_grad = gates * (gate_grad - jnp.sum(gates * gate_grad, axis=-1, keepdims=True))
    logits_grad = jnp.sum(chosen_grad[..., None] * pair_mask, axis=1).astype(b16)
    grad_buffer = (
        jnp.zeros((E * CAP, width), b16)
        .at[position]
        .set(pair_grad, mode="drop")
        .reshape(E, CAP, width)
    )
    result_grad = lax.all_to_all(grad_buffer, "expert", split_axis=0, concat_axis=1, tiled=True)
    pre_again = (
        jnp.einsum("erd,edf->erf", received, expert_in, preferred_element_type=f32)
        + expert_in_bias.astype(f32)[:, None, :]
    )
    act_again, expert_gelu_back = jax.vjp(gelu_tanh, pre_again)
    low_again = act_again.astype(b16)
    expert_out_grad = jnp.einsum("erf,erd->efd", low_again, result_grad, preferred_element_type=f32)
    expert_out_bias_grad = jnp.sum(result_grad.astype(f32), axis=1)
    expert_act_grad = jnp.einsum(
        "erd,efd->erf", result_grad, expert_out, preferred_element_type=f32
    )
    pre_grad = expert_gelu_back(expert_act_grad)[0].astype(b16)
    expert_in_grad = jnp.einsum("erd,erf->edf", received, pre_grad, preferred_element_type=f32)
    expert_in_bias_grad = jnp.sum(pre_grad.astype(f32), axis=1)
    received_grad = jnp.einsum(
        "erf,edf->erd", pre_grad, expert_in, preferred_element_type=f32
    ).astype(b16)
    sent_grad = lax.all_to_all(
        received_grad, "expert", split_axis=1, concat_axis=0, tiled=True
    ).reshape(E * CAP, width)
    dispatch_rows_grad = jnp.sum(
        sent_grad.at[position]
        .get(mode="fill", fill_value=0)
        .reshape(row_count, 2, width)
        .astype(f32),
        axis=1,
    )
    shared_out_grad = jnp.einsum("isf,isd->fd", shared_low, moe_grad, preferred_element_type=f32)
    shared_out_bias_grad = jnp.sum(moe_rows_float, axis=0)
    shared_act_grad = jnp.einsum(
        "isd,fd->isf", moe_grad, shared_out_back, preferred_element_type=f32
    )
    shared_pre_grad = shared_gelu_back(shared_act_grad)[0].astype(b16)
    shared_in_grad = jnp.einsum("isd,isf->df", second, shared_pre_grad, preferred_element_type=f32)
    shared_in_bias_grad = jnp.sum(shared_pre_grad.astype(f32), axis=(0, 1))
    router_grad = jnp.einsum("rd,re->de", second_rows, logits_grad, preferred_element_type=f32)
    second_grad = jnp.einsum(
        "isf,df->isd", shared_pre_grad, shared_in_back, preferred_element_type=f32
    )
    side_grad = dispatch_rows_grad + jnp.einsum(
        "re,de->rd", logits_grad, router_back, preferred_element_type=f32
    )
    second_grad = second_grad + side_grad.reshape(image_count, length, width)
    resid_extra, shift_two_grad, scale_two_grad = second_back(second_grad)
    resid_grad = grad_out + resid_extra
    attended_grad = (pieces[2] * resid_grad).astype(b16)
    gate_one_grad = jnp.sum(resid_grad * attended, axis=1, keepdims=True)
    out_weight_grad = jnp.einsum("isd,ise->de", mixed, attended_grad, preferred_element_type=f32)
    out_bias_grad = jnp.sum(attended_grad.astype(f32), axis=(0, 1))
    mixed_grad = (
        jnp.einsum("ise,de->isd", attended_grad, out_back, preferred_element_type=f32)
        .astype(b16)
        .reshape(head_shape)
    )
    again_scores = (
        jnp.einsum("iqhc,ikhc->ihqk", query_heads, key_heads, preferred_element_type=f32) * scaling
    )
    probs_float = jnp.exp(again_scores - log_total)
    again_low = probs_float.astype(b16)
    probs_grad = jnp.einsum("iqhc,ikhc->ihqk", mixed_grad, value_heads, preferred_element_type=f32)
    values_grad = jnp.einsum(
        "ihqk,iqhc->ikhc", again_low, mixed_grad, preferred_element_type=f32
    ).astype(b16)
    scores_grad = (
        probs_float * (probs_grad - jnp.sum(probs_float * probs_grad, axis=-1, keepdims=True))
    ).astype(b16)
    query_grad = (
        jnp.einsum("ihqk,ikhc->iqhc", scores_grad, key_heads, preferred_element_type=f32) * scaling
    ).astype(b16)
    keys_grad = (
        jnp.einsum("ihqk,iqhc->ikhc", scores_grad, query_heads, preferred_element_type=f32)
        * scaling
    ).astype(b16)
    flat_shape = (image_count, length, width)
    projected_grad = jnp.concatenate(
        [
            query_grad.reshape(flat_shape),
            keys_grad.reshape(flat_shape),
            values_grad.reshape(flat_shape),
        ],
        axis=-1,
    )
    qkv_weight_grad = jnp.einsum("isd,ise->de", normed, projected_grad, preferred_element_type=f32)
    qv_bias_grad = jnp.stack(
        [
            jnp.sum(query_grad.astype(f32), axis=(0, 1)).reshape(width),
            jnp.sum(values_grad.astype(f32), axis=(0, 1)).reshape(width),
        ]
    )
    normed_grad = jnp.einsum("ise,de->isd", projected_grad, qkv_back, preferred_element_type=f32)
    token_extra, shift_one_grad, scale_one_grad = first_back(normed_grad)
    tokens_grad = resid_grad + token_extra
    modulation_grad = jnp.concatenate(
        [
            shift_one_grad,
            scale_one_grad,
            gate_one_grad,
            shift_two_grad,
            scale_two_grad,
            gate_two_grad,
        ],
        axis=-1,
    )[:, 0, :].astype(b16)
    ada_weight_grad = jnp.einsum("id,ie->de", cond_low, modulation_grad, preferred_element_type=f32)
    ada_bias_grad = jnp.sum(modulation_grad.astype(f32), axis=0)
    cond_act_grad = jnp.einsum("ie,de->id", modulation_grad, ada_back, preferred_element_type=f32)
    conditioning_grad = silu_back(cond_act_grad)[0]
    expert_sums = (
        lax.psum_scatter(
            expert_in_grad.astype(jnp.bfloat16), "dp", scatter_dimension=1, tiled=True
        ).astype(jnp.float32),
        lax.psum_scatter(
            expert_in_bias_grad.astype(jnp.bfloat16), "dp", scatter_dimension=1, tiled=True
        ).astype(jnp.float32),
        lax.psum_scatter(
            expert_out_grad.astype(jnp.bfloat16), "dp", scatter_dimension=1, tiled=True
        ).astype(jnp.float32),
        lax.psum_scatter(
            expert_out_bias_grad.astype(jnp.bfloat16), "dp", scatter_dimension=1, tiled=True
        ).astype(jnp.float32),
    )
    dense_parts = (
        lax.psum_scatter(
            ada_weight_grad.astype(jnp.bfloat16), "dp", scatter_dimension=0, tiled=True
        ).astype(jnp.float32),
        lax.psum_scatter(
            ada_bias_grad.astype(jnp.bfloat16), "dp", scatter_dimension=0, tiled=True
        ).astype(jnp.float32),
        lax.psum_scatter(
            qkv_weight_grad.astype(jnp.bfloat16), "dp", scatter_dimension=0, tiled=True
        ).astype(jnp.float32),
        lax.psum_scatter(
            qv_bias_grad.astype(jnp.bfloat16), "dp", scatter_dimension=1, tiled=True
        ).astype(jnp.float32),
        lax.psum_scatter(
            out_weight_grad.astype(jnp.bfloat16), "dp", scatter_dimension=0, tiled=True
        ).astype(jnp.float32),
        lax.psum_scatter(
            out_bias_grad.astype(jnp.bfloat16), "dp", scatter_dimension=0, tiled=True
        ).astype(jnp.float32),
        lax.psum_scatter(
            shared_in_grad.astype(jnp.bfloat16), "dp", scatter_dimension=0, tiled=True
        ).astype(jnp.float32),
        lax.psum_scatter(
            shared_in_bias_grad.astype(jnp.bfloat16), "dp", scatter_dimension=0, tiled=True
        ).astype(jnp.float32),
        lax.psum_scatter(
            shared_out_grad.astype(jnp.bfloat16), "dp", scatter_dimension=0, tiled=True
        ).astype(jnp.float32),
        lax.psum_scatter(
            shared_out_bias_grad.astype(jnp.bfloat16), "dp", scatter_dimension=0, tiled=True
        ).astype(jnp.float32),
        lax.psum_scatter(
            router_grad.astype(jnp.bfloat16), "dp", scatter_dimension=0, tiled=True
        ).astype(jnp.float32),
    )
    dense_sums = lax.psum(
        (
            dense_parts[0],
            dense_parts[1],
            dense_parts[2],
            dense_parts[3],
            dense_parts[4],
            dense_parts[5],
            dense_parts[6],
            dense_parts[7],
            dense_parts[8],
            dense_parts[9],
            dense_parts[10],
        ),
        "expert",
    )
    return (
        output,
        tokens_grad,
        conditioning_grad,
        dense_sums[0],
        dense_sums[1],
        dense_sums[2],
        dense_sums[3],
        dense_sums[4],
        dense_sums[5],
        dense_sums[6],
        dense_sums[7],
        dense_sums[8],
        dense_sums[9],
        dense_sums[10],
        expert_sums[0],
        expert_sums[1],
        expert_sums[2],
        expert_sums[3],
    )


def solution(mesh):
    in_specs = (
        P(("dp", "expert"), None, None),
        P(("dp", "expert"), None),
        P(("dp", "expert"), None, None),
        P(("dp", "expert"), None, None),
        P("dp", None),
        P("dp"),
        P("dp", None),
        P(None, "dp"),
        P("dp", None),
        P("dp"),
        P("dp", None),
        P("dp"),
        P("dp", None),
        P("dp"),
        P("dp", None),
        P("expert", None, None),
        P("expert", None),
        P("expert", None, None),
        P("expert", None),
    )
    out_specs = (
        P(("dp", "expert"), None, None),
        P(("dp", "expert"), None, None),
        P(("dp", "expert"), None),
        P("dp", None),
        P("dp"),
        P("dp", None),
        P(None, "dp"),
        P("dp", None),
        P("dp"),
        P("dp", None),
        P("dp"),
        P("dp", None),
        P("dp"),
        P("dp", None),
        P("expert", "dp", None),
        P("expert", "dp"),
        P("expert", "dp", None),
        P("expert", "dp"),
    )
    body = on_device
    if dict(mesh.shape) == {"dp": NZ * NX, "expert": 4}:
        body = on_block
    return jax.shard_map(
        body, mesh=mesh, in_specs=in_specs, out_specs=out_specs, check_vma=False
    )
```

```python
import functools

import jax
import jax.numpy as jnp
from jax import lax
from jax.experimental import pallas as pl
from jax.experimental.pallas import tpu as pltpu
from jax.sharding import PartitionSpec as P

HEADS = 12
HEAD_DIM = 64
E = 8
CAP = 80
MESH = pl.DeviceIdType.MESH
F32 = jnp.float32
B16 = jnp.bfloat16
VMEM_LIMIT = 60 * 1024 * 1024
SCALE = HEAD_DIM ** (-0.5)
GELU_C = 0.7978845608028654
NZ, NX = 4, 2


def coords():
    dp = lax.axis_index("dp")
    ex = lax.axis_index("expert")
    return lax.div(dp, NX), lax.rem(dp, NX), lax.div(ex, 2), lax.rem(ex, 2)


def dev(z, x, y, c):
    return (NX * z + x, 2 * y + c)


def dot(a, b):
    return jnp.dot(a, b, preferred_element_type=F32)


def dot_nt(a, b):
    return lax.dot_general(a, b, (((1,), (1,)), ((), ())), preferred_element_type=F32)


def dot_tn(a, b):
    return lax.dot_general(a, b, (((0,), (0,)), ((), ())), preferred_element_type=F32)


def gelu(v):
    return v * (0.5 + 0.5 * jnp.tanh(v * (GELU_C + GELU_C * 0.044715 * (v * v))))


def gelu_parts(v):
    v2 = v * v
    t = jnp.tanh(GELU_C * v * (1.0 + 0.044715 * v2))
    h = 0.5 * (1.0 + t)
    return v * h, h + 0.5 * v * (1.0 - t * t) * (GELU_C * (1.0 + 0.134145 * v2))


def norm_parts(v):
    centred = v - jnp.mean(v, axis=-1, keepdims=True)
    r = lax.rsqrt(jnp.mean(centred * centred, axis=-1, keepdims=True) + 1e-06)
    return centred * r, r


def norm_back(u, n, r):
    return r * (
        u - jnp.mean(u, axis=-1, keepdims=True) - n * jnp.mean(u * n, axis=-1, keepdims=True)
    )


def remote(src, dst, send, recv, to):
    return pltpu.make_async_remote_copy(
        src_ref=src,
        dst_ref=dst,
        send_sem=send,
        recv_sem=recv,
        device_id=to,
        device_id_type=MESH,
    )


def greet(barrier, to):
    pl.semaphore_signal(barrier, inc=1, device_id=to, device_id_type=MESH)


def params(collective_id=None):
    if collective_id is None:
        return pltpu.CompilerParams(vmem_limit_bytes=VMEM_LIMIT)
    return pltpu.CompilerParams(
        vmem_limit_bytes=VMEM_LIMIT, collective_id=collective_id, has_side_effects=True
    )


VM = pl.BlockSpec(memory_space=pltpu.VMEM)
HB = pl.BlockSpec(memory_space=pl.ANY)


def sds(shape, dtype):
    return jax.ShapeDtypeStruct(shape, dtype)


class Gather:
    def __init__(self, shards, fulls, splits, sems):
        self.z, self.x, self.y, self.c = coords()
        self.mats = list(zip(shards, fulls, splits))
        (self.zs, self.zr, self.xs, self.xr, self.ys, self.yr, self.cs, self.cr, self.loc) = sems

    @staticmethod
    def semaphores(count):
        dma = pltpu.SemaphoreType.DMA
        return [
            dma((count, 2, NZ)),
            dma((count, NZ)),
            dma((count, NZ)),
            dma((count, NZ)),
            dma((count, NZ, NX)),
            dma((count, NZ, NX)),
            dma((count, NZ, NX, 2)),
            dma((count, NZ, NX, 2)),
            dma((count,)),
        ]

    def region(self, m, zb, xb, yh, ch):
        shard, full, split = self.mats[m]
        rows, width = shard.shape[0], shard.shape[1] // 2
        start = (NX * zb + xb) * rows
        if split:
            rows = rows // 2
            start = start + yh * rows
        return full.at[
            pl.ds(pl.multiple_of(start, 16), rows), pl.ds(pl.multiple_of(ch * width, 128), width)
        ]

    def own(self, m):
        shard, full, split = self.mats[m]
        rows, width = shard.shape[0], shard.shape[1] // 2
        start = 0
        if split:
            rows = rows // 2
            start = self.y * rows
        return shard.at[
            pl.ds(pl.multiple_of(start, 16), rows),
            pl.ds(pl.multiple_of(self.c * width, 128), width),
        ]

    def zcopy(self, m, zb, side, mine=False):
        here = self.region(m, zb, self.x, self.y, self.c)
        step = 1 if side else -1
        return remote(
            self.own(m) if mine else here,
            here,
            self.zs.at[m, side, zb],
            self.zr.at[m, zb],
            dev(lax.rem(self.z + step + NZ, NZ), self.x, self.y, self.c),
        )

    def xcopy(self, m, zb, mine=False, xb=None):
        here = self.region(m, zb, self.x if xb is None else xb, self.y, self.c)
        return remote(
            self.own(m) if mine else here,
            here,
            self.xs.at[m, zb],
            self.xr.at[m, zb],
            dev(self.z, 1 - self.x, self.y, self.c),
        )

    def ycopy(self, m, zb, xb, yh=None):
        here = self.region(m, zb, xb, self.y if yh is None else yh, self.c)
        return remote(
            here,
            here,
            self.ys.at[m, zb, xb],
            self.yr.at[m, zb, xb],
            dev(self.z, self.x, 1 - self.y, self.c),
        )

    def ccopy(self, m, zb, xb, yh, ch=None):
        here = self.region(m, zb, xb, yh, self.c if ch is None else ch)
        slot = yh if self.mats[m][2] else 0
        return remote(
            here,
            here,
            self.cs.at[m, zb, xb, slot],
            self.cr.at[m, zb, xb, slot],
            dev(self.z, self.x, self.y, 1 - self.c),
        )

    def local(self, m):
        shard, full, _ = self.mats[m]
        rows = shard.shape[0]
        start = (NX * self.z + self.x) * rows
        return pltpu.make_async_copy(
            shard, full.at[pl.ds(pl.multiple_of(start, 16), rows), :], self.loc.at[m]
        )

    def blocks(self, step):
        if step == 0:
            return [(self.z, None, None)]
        return [
            (self.z - step, self.z - step >= 0, 1),
            (self.z + step, self.z + step < NZ, 0),
        ]

    def more(self, side):
        return self.z + 1 < NZ if side else self.z - 1 >= 0

    def begin(self, m):
        for side in (1, 0):

            @pl.when(self.more(side))
            def _():
                self.zcopy(m, self.z, side, True).start()

        self.xcopy(m, self.z, True).start()
        self.local(m).start()

    def spread(self, m, zb, xb):
        if self.mats[m][2]:
            self.ycopy(m, zb, xb).start()
        self.ccopy(m, zb, xb, self.y).start()

    def take_z(self, m, step):
        for zb, exists, side in self.blocks(step):

            @pl.when(exists)
            def _():
                self.zcopy(m, zb, side).wait_recv()
                if step < NZ - 1:

                    @pl.when(self.more(side))
                    def _():
                        self.zcopy(m, zb, side).start()

                self.xcopy(m, zb).start()
                self.spread(m, zb, self.x)

    def take_x(self, m, step):
        for zb, exists, _ in self.blocks(step):

            def body():
                self.xcopy(m, zb, False, 1 - self.x).wait_recv()
                self.spread(m, zb, 1 - self.x)

            body() if exists is None else pl.when(exists)(body)

    def others(self, m, step, action):
        for zb, exists, _ in self.blocks(step):
            for xb in (self.x, 1 - self.x) if step else (1 - self.x,):
                body = functools.partial(action, m, zb, xb)
                body() if exists is None else pl.when(exists)(body)

    def take_y(self, m, step):
        if not self.mats[m][2]:
            return

        def action(m, zb, xb):
            self.ycopy(m, zb, xb, 1 - self.y).wait_recv()
            self.ccopy(m, zb, xb, 1 - self.y).start()

        self.others(m, step, action)

    def finish(self, m):
        def action(m, zb, xb):
            for yh in (self.y, 1 - self.y) if self.mats[m][2] else (self.y,):
                self.ccopy(m, zb, xb, yh, 1 - self.c).wait_recv()
                self.ccopy(m, zb, xb, yh).wait_send()
            if self.mats[m][2]:
                self.ycopy(m, zb, xb).wait_send()

        for step in range(NZ):
            self.others(m, step, action)
        for side in (1, 0):

            @pl.when(self.more(side))
            def _():
                self.zcopy(m, self.z, side, True).wait_send()

        for step in range(1, NZ):
            for zb, exists, side in self.blocks(step):

                @pl.when(exists)
                def _():
                    self.xcopy(m, zb).wait_send()
                    if step < NZ - 1:

                        @pl.when(self.more(side))
                        def _():
                            self.zcopy(m, zb, side).wait_send()

        self.xcopy(m, self.z, True).wait_send()
        self.local(m).wait()


class Column:
    def __init__(self, shard, column, other, send, recv, local, xsend, xrecv):
        self.z, self.x, self.y, self.c = coords()
        self.shard, self.column, self.other = shard, column, other
        self.send, self.recv, self.local, self.xsend, self.xrecv = send, recv, local, xsend, xrecv

    @staticmethod
    def semaphores():
        dma = pltpu.SemaphoreType.DMA
        return [dma((2, NZ)), dma((NZ,)), dma((1,)), dma((NZ,)), dma((NZ,))]

    def block(self, zb):
        rows = self.shard.shape[0]
        return self.column.at[pl.ds(pl.multiple_of(zb * rows, 16), rows), :]

    def own(self):
        width = self.shard.shape[1] // 2
        return self.shard.at[:, pl.ds(pl.multiple_of(self.c * width, 128), width)]

    def copy(self, zb, side, mine=False):
        here = self.block(zb)
        to = lax.rem(self.z + (1 if side else NZ - 1), NZ)
        return remote(
            self.own() if mine else here,
            here,
            self.send.at[side, zb],
            self.recv.at[zb],
            dev(to, self.x, self.y, self.c),
        )

    def xcopy(self, zb, mine=False):
        rows, width = self.shard.shape[0], self.shard.shape[1] // 2
        part = rows // 2
        start = pl.multiple_of(self.y * part, 16)
        if mine:
            source = self.shard.at[
                pl.ds(start, part), pl.ds(pl.multiple_of(self.c * width, 128), width)
            ]
        else:
            source = self.column.at[pl.ds(pl.multiple_of(zb * rows + start, 16), part), :]
        return remote(
            source,
            self.other.at[pl.ds(pl.multiple_of(zb * part, 16), part), :],
            self.xsend.at[zb],
            self.xrecv.at[zb],
            dev(self.z, 1 - self.x, self.y, self.c),
        )

    def keep(self):
        return pltpu.make_async_copy(self.own(), self.block(self.z), self.local.at[0])

    def more(self, side):
        return self.z + 1 < NZ if side else self.z - 1 >= 0

    def blocks(self, step):
        return [(self.z - step, self.z - step >= 0, 1), (self.z + step, self.z + step < NZ, 0)]

    def begin(self):
        for side in (1, 0):

            @pl.when(self.more(side))
            def _():
                self.copy(self.z, side, True).start()

        self.keep().start()
        self.xcopy(self.z, True).start()

    def take(self, step):
        for zb, exists, side in self.blocks(step):

            @pl.when(exists)
            def _():
                self.copy(zb, side).wait_recv()
                if step < NZ - 1:

                    @pl.when(self.more(side))
                    def _():
                        self.copy(zb, side).start()

    def push(self, step):
        for zb, exists, _ in self.blocks(step):

            @pl.when(exists)
            def _():
                self.xcopy(zb).start()

    def finish(self):
        for side in (1, 0):

            @pl.when(self.more(side))
            def _():
                self.copy(self.z, side, True).wait_send()

        for step in range(1, NZ - 1):
            for zb, exists, side in self.blocks(step):

                @pl.when(jnp.logical_and(exists, self.more(side)))
                def _():
                    self.copy(zb, side).wait_send()

        for zb in range(NZ):
            self.xcopy(zb).wait_send()


class Spread:
    def __init__(self, column, other, full, ys, yr, cs, cr, local):
        self.z, self.x, self.y, self.c = coords()
        self.column, self.other, self.full, self.local = column, other, full, local
        self.ys, self.yr, self.cs, self.cr = ys, yr, cs, cr

    @staticmethod
    def semaphores():
        dma = pltpu.SemaphoreType.DMA
        return [dma((NZ,))] * 2 + [dma((3, NZ))] * 2 + [dma((2, NZ))]

    def cols(self, c):
        width = self.full.shape[3] // 2
        return pl.ds(pl.multiple_of(c * width, 128), width)

    def half(self, y):
        rows = self.full.shape[2] // 2
        return pl.ds(pl.multiple_of(y * rows, 16), rows)

    def source(self, kind, zb):
        rows = self.full.shape[2] // (1 if kind == 0 else 2)
        ref = self.column if kind == 0 else self.other
        return ref.at[pl.ds(pl.multiple_of(zb * rows, 16), rows), :]

    def place(self, kind, zb, c):
        if kind == 0:
            return self.full.at[zb, self.x, :, self.cols(c)]
        return self.full.at[zb, 1 - self.x, self.half(self.y if kind == 1 else 1 - self.y), self.cols(c)]

    def ycopy(self, zb, came=False):
        return remote(
            self.source(1, zb), self.place(2 if came else 1, zb, self.c), self.ys.at[zb], self.yr.at[zb],
            dev(self.z, self.x, 1 - self.y, self.c),
        )

    def ccopy(self, kind, zb, came=False):
        at = self.place(kind, zb, 1 - self.c if came else self.c)
        return remote(
            at if kind == 2 else self.source(kind, zb), at, self.cs.at[kind, zb], self.cr.at[kind, zb],
            dev(self.z, self.x, self.y, 1 - self.c),
        )

    def keep(self, kind, zb):
        return pltpu.make_async_copy(
            self.source(kind, zb), self.place(kind, zb, self.c), self.local.at[kind, zb]
        )

    def near(self):
        for zb in range(NZ):
            self.ccopy(0, zb).start()
            self.keep(0, zb).start()

    def pass_x(self, zb):
        self.ycopy(zb).start()
        self.ccopy(1, zb).start()
        self.keep(1, zb).start()

    def pass_y(self, zb):
        self.ycopy(zb, True).wait_recv()
        self.ccopy(2, zb).start()

    def finish(self):
        for zb in range(NZ):
            for kind in range(3):
                self.ccopy(kind, zb, True).wait_recv()
                self.ccopy(kind, zb).wait_send()
            for kind in range(2):
                self.keep(kind, zb).wait()
            self.ycopy(zb).wait_send()


def choose_rows(place, slots):
    return place == lax.broadcasted_iota(jnp.int32, (place.shape[0], slots), 1)


def plane_peer(k):
    z, x, y, c = coords()
    xt = 1 - x if k & 1 else x
    ct = 1 - c if k & 2 else c
    yt = 1 - y if k & 4 else y
    return dev(z, xt, yt, ct), 4 * yt + 2 * ct + xt


def plane_rank():
    _, x, y, c = coords()
    return 4 * y + 2 * c + x


def slot_rows(ref, rank):
    return ref.at[pl.ds(pl.multiple_of(rank * CAP, 16), CAP), :]


class PlaneExchange:
    ORDER = (7, 5, 6, 4, 3, 1, 2)

    def __init__(self, source, target, send, recv):
        self.source, self.target, self.send, self.recv = source, target, send, recv

    def copy(self, k, into=None):
        peer, other = plane_peer(k)
        return remote(
            slot_rows(self.source, other),
            slot_rows(self.target, plane_rank() if into is None else other),
            self.send.at[k],
            self.recv.at[k],
            peer,
        )

    def mine(self):
        rank = plane_rank()
        return pltpu.make_async_copy(
            slot_rows(self.source, rank), slot_rows(self.target, rank), self.send.at[0]
        )

    def start(self):
        for k in self.ORDER:
            self.copy(k).start()
        self.mine().start()

    def wait_in(self):
        self.mine().wait()
        for k in self.ORDER:
            self.copy(k, True).wait_recv()

    def wait_out(self):
        for k in self.ORDER:
            self.copy(k).wait_send()


CHUNK = 512


def lead_kernel(
    tok, cot, routes, cond, ada, adab, qvb, outb, soutb, sinb_s, router_s, bin_r, bout_r,
    qkv_s, out_s, sin_s, sout_s, win_h, wout_h,
    normed_o, proj_o, lsum_o, mixed_o, att_o, resid_o, second_o, gates_o, place_o, mod_o, bias_o, sinb_o, rt_o,
    condt_o, ebias, ret_o, retg_o, qkv_o, outw_o, sin_o, sout_o, dwin_o, dwout_o, came_o,
    pack, packs, sent, got, qkv, outw, sbuf, gbuf, res, bgr, rows, grads, far_rows, far_grads, win, wout, dwin, dwout,
    pres, acc, sin_c, sout_c, sin_x, sout_x,
    s1, r1, s2, r2, ds0, dr0, ds1, dr1, ds2, dr2, ds3, dr3, wsem, osem, fsem, msem, *gsems,
):
    z, x, y, c = coords()
    dp, ex = lax.axis_index("dp"), lax.axis_index("expert")
    n = NZ * NX
    length, width = tok.shape
    hidden = win.shape[1]
    part = width // n
    per = width // 128
    count = len(Column.semaphores())
    lead = Gather((qkv_s, out_s), (qkv, outw), (True, False), gsems[: len(Gather.semaphores(2))])
    gsems = gsems[len(Gather.semaphores(2)) :]
    later = (
        Column(sin_s, sin_c, sin_x, *gsems[:count]),
        Column(sout_s, sout_c, sout_x, *gsems[count : 2 * count]),
    )
    gsems = gsems[2 * count :]
    count = len(Spread.semaphores())
    spreads = (
        Spread(sin_c, sin_x, sin_o, *gsems[:count]),
        Spread(sout_c, sout_x, sout_o, *gsems[count:]),
    )

    def per_block(step, action):
        for zb, exists in [(z, None)] if step == 0 else [v[:2] for v in later[0].blocks(step)]:
            body = functools.partial(action, zb)
            body() if exists is None else pl.when(exists)(body)

    def pass_x(step):
        def action(zb):
            for column, spread in zip(later, spreads):
                column.xcopy(zb).wait_recv()
                spread.pass_x(zb)

        per_block(step, action)

    def pass_y(step):
        def action(zb):
            for spread in spreads:
                spread.pass_y(zb)

        per_block(step, action)

    loads = [
        pltpu.make_async_copy(win_h.at[x], win, wsem.at[0]),
        pltpu.make_async_copy(wout_h.at[x], wout, wsem.at[1]),
    ]

    def peers(action):
        for p in range(n):

            @pl.when(p != dp)
            def _():
                action(p)

    barrier = pltpu.get_barrier_semaphore()
    peers(lambda p: greet(barrier, (p, ex)))
    for k in range(2, E):
        greet(barrier, plane_peer(k)[0])

    pack[...] = jnp.zeros_like(pack)
    pack[0:2, 0:part] = qvb[...].astype(F32)
    pack[2:3, 0:part] = outb[...].astype(F32)
    pack[3:4, 0:part] = soutb[...].astype(F32)
    for j in range(hidden // n // 128):
        pack[4 + j : 5 + j, :] = sinb_s[128 * j : 128 * (j + 1)].astype(F32).reshape(1, 128)
    long = adab.shape[0]
    for j in range(-(-long // 128)):
        size = min(128, long - 128 * j)
        pack[8 + j : 9 + j, 0:size] = adab[128 * j : 128 * j + size].astype(F32).reshape(1, size)
    pack[16:24, 0:part] = router_s[...].astype(F32)
    cv = cond[...].astype(F32)
    cond_low = (cv / (1.0 + jnp.exp(-cv))).astype(B16).astype(F32)
    for p in range(n):
        pack[24 + p : 25 + p, 0:part] = cond_low[:, part * p : part * (p + 1)]
    condt_o[...] = jnp.zeros_like(condt_o)
    for j in range(per):
        condt_o[j : j + 1, :] = cond_low[:, 128 * j : 128 * (j + 1)]

    pl.semaphore_wait(barrier, n - 1 + E - 2)

    def first(p, at):
        return remote(pack, packs.at[at], s1.at[p], r1.at[at], (p, ex))

    def second_hop(p, at):
        return remote(sent.at[p], got.at[at], s2.at[p], r2.at[at], (p, ex))

    peers(lambda p: first(p, dp).start())
    lead.begin(0)
    lead.begin(1)
    for load in loads:
        load.start()
    packs[dp] = pack[...]
    peers(lambda p: first(p, p).wait_recv())
    cond_rows = jnp.concatenate([packs[p, pl.ds(24 + dp, 1), :] for p in range(n)], axis=0)
    partial = dot(cond_rows[:, :part].astype(B16), ada[...])
    for j in range(partial.shape[1] // 128):
        sent[:, j, :] = partial[:, 128 * j : 128 * (j + 1)]
    peers(lambda p: second_hop(p, dp).start())
    got[dp] = sent[dp]

    both_mats = (0, 1)

    def step_of(plan, step):
        for m in both_mats:
            if step:
                plan.take_z(m, step)
            plan.take_x(m, step)
        if step:
            for m in both_mats:
                plan.take_y(m, step - 1)

    for step in range(NZ):
        step_of(lead, step)

    for column in later:
        column.begin()

    bias_o[...] = jnp.zeros_like(bias_o)
    for p in range(n):
        bias_o[0:4, part * p : part * (p + 1)] = packs[p, 0:4, 0:part]
        rt_o[:, part * p : part * (p + 1)] = packs[p, 16:24, 0:part]
        for j in range(hidden // n // 128):
            at = hidden // n * p + 128 * j
            sinb_o[:, at : at + 128] = packs[p, 4 + j : 5 + j, :]
    peers(lambda p: second_hop(p, p).wait_recv())
    total = got[0]
    for p in range(1, n):
        total = total + got[p]
    mod_o[...] = jnp.zeros_like(mod_o)
    for i in range(6):
        for b in range(per):
            mod_o[i : i + 1, 128 * b : 128 * (b + 1)] = total[per * i + b : per * i + b + 1, :]
    unit = 64
    for p in range(n):
        for u in range(long // unit):
            at = long * p + unit * u
            i, b = at // width, at % width
            mod_o[i : i + 1, b : b + unit] += packs[
                p, 8 + unit * u // 128 : 9 + unit * u // 128, unit * u % 128 : unit * u % 128 + unit
            ]

    mod = mod_o[...]
    source = tok[...].astype(F32)
    n1, _ = norm_parts(source)
    normed = (n1 * (1.0 + mod[1:2]) + mod[0:1]).astype(B16)
    normed_o[...] = normed
    for m in both_mats:
        lead.take_y(m, NZ - 1)
    for m in both_mats:
        lead.finish(m)
    keep = [
        pltpu.make_async_copy(qkv, qkv_o, wsem.at[2]),
        pltpu.make_async_copy(outw, outw_o, wsem.at[3]),
    ]
    for copy in keep:
        copy.start()

    for k in range(3):
        part_k = dot(normed, qkv[:, k * width : (k + 1) * width])
        if k != 1:
            part_k = part_k + bias_o[k // 2 : k // 2 + 1, :]
        proj_o[:, k * width : (k + 1) * width] = part_k.astype(B16)
    lane = lax.broadcasted_iota(jnp.int32, (length, 128), 1)
    low_lane = lane < HEAD_DIM
    lsum = jnp.zeros((length, 128), F32)
    for p in range(HEADS // 2):
        q2 = proj_o[:, 128 * p : 128 * (p + 1)]
        k2 = proj_o[:, width + 128 * p : width + 128 * (p + 1)]
        v2 = proj_o[:, 2 * width + 128 * p : 2 * width + 128 * (p + 1)]
        outs = []
        for h in range(2):
            mine = low_lane if h == 0 else jnp.logical_not(low_lane)
            s = dot_nt(jnp.where(mine, q2, jnp.zeros_like(q2)), k2) * SCALE
            peak = jnp.max(s, axis=-1, keepdims=True)
            e = jnp.exp(s - peak)
            tot = jnp.sum(e, axis=-1, keepdims=True)
            lsum = jnp.where(lane == 2 * p + h, peak + jnp.log(tot), lsum)
            outs.append(dot((e / tot).astype(B16), v2))
        mixed_o[:, 128 * p : 128 * (p + 1)] = jnp.where(low_lane, outs[0], outs[1]).astype(B16)
    lsum_o[...] = lsum
    att = dot(mixed_o[...], outw[...]) + bias_o[2:3, :]
    att_o[...] = att
    resid = source + mod[2:3] * att
    resid_o[...] = resid
    n2, _ = norm_parts(resid)
    second = (n2 * (1.0 + mod[4:5]) + mod[3:4]).astype(B16)
    second_o[...] = second

    lane8 = lax.broadcasted_iota(jnp.int32, (length, E), 1)
    two = (
        lax.broadcasted_iota(jnp.int32, (2, 128), 0) == lax.broadcasted_iota(jnp.int32, (2, 128), 1)
    )
    route_cols = dot_tn(
        routes[...].astype(F32).astype(B16), jnp.where(two, 1.0, 0.0).astype(B16)
    ).astype(jnp.int32)
    route = [route_cols[:, k : k + 1] for k in range(2)]
    picks = [(r == lane8) for r in route]
    both = jnp.where(picks[0], 1.0, 0.0) + jnp.where(picks[1], 1.0, 0.0)
    earlier = (
        lax.broadcasted_iota(jnp.int32, (length, length), 1)
        < lax.broadcasted_iota(jnp.int32, (length, length), 0)
    )
    rank = dot(jnp.where(earlier, 1.0, 0.0).astype(B16), both.astype(B16))
    places = []
    for k in range(2):
        slot = jnp.sum(jnp.where(picks[k], rank, 0.0), axis=-1, keepdims=True).astype(jnp.int32)
        places.append(jnp.where(slot < CAP, route[k] * CAP + slot, -1))
    place_o[...] = jnp.where(
        lane == 0,
        places[0],
        jnp.where(lane == 1, places[1], jnp.where(lane == 2, route[0], route[1])),
    )
    maps = [jnp.where(choose_rows(v, E * CAP), 1.0, 0.0) for v in places]
    sbuf[...] = dot_tn((maps[0] + maps[1]).astype(B16), second).astype(B16)
    give_rows = PlaneExchange(sbuf, rows, ds0, dr0)
    give_rows.start()
    logits = dot_nt(second, rt_o[...].astype(B16))
    chosen = [jnp.sum(jnp.where(pick, logits, 0.0), axis=-1, keepdims=True) for pick in picks]
    top = jnp.maximum(chosen[0], chosen[1])
    e2 = [jnp.exp(v - top) for v in chosen]
    gates = [v / (e2[0] + e2[1]) for v in e2]
    gates_o[...] = jnp.where(lane == 0, gates[0], jnp.where(lane == 1, gates[1], 0.0))
    moe_grad = (mod[5:6] * cot[...].astype(F32)).astype(B16).astype(F32)
    pair = [(g * moe_grad).astype(B16) for g in gates]
    gbuf[...] = (
        dot_tn(maps[0].astype(B16), pair[0]) + dot_tn(maps[1].astype(B16), pair[1])
    ).astype(B16)
    give_grads = PlaneExchange(gbuf, grads, ds1, dr1)
    give_grads.start()
    for column in later:
        column.take(1)

    first_x = x == 0
    acc[...] = jnp.zeros_like(acc) + jnp.where(first_x, bout_r[0:1, :], bout_r[1:2, :]).astype(F32)
    for load in loads:
        load.wait()
    for column in later:
        column.take(2)
    give_rows.wait_in()

    end = jnp.logical_or(z == 0, z == NZ - 1)
    inner = jnp.logical_not(end)
    partner = dev(z + 1 - 2 * lax.rem(z, 2), x, y, c)

    def far_copy(i):
        source, target = ((rows, far_rows), (grads, far_grads))[i]
        return remote(source, target, fsem.at[0, i], fsem.at[1, i], partner)

    pl.when(end)(lambda: far_copy(0).start())
    for column in later:
        column.push(1)

    def span(f):
        return pl.ds(pl.multiple_of(f * CHUNK, 128), CHUNK)

    def put_in(f):
        return pltpu.make_async_copy(dwin.at[:, span(f)], dwin_o.at[:, span(f)], osem.at[1, f])

    def put_out(f):
        return pltpu.make_async_copy(dwout.at[span(f), :], dwout_o.at[span(f), :], osem.at[0, f])

    def bias_of(cols):
        return jnp.where(first_x, bin_r[0:1, cols], bin_r[1:2, cols]).astype(F32)

    def forward(f, carry):
        cols = span(f)
        pre = dot(rows[...], win[:, cols]) + bias_of(cols)
        pres[:, cols] = pre
        low = gelu(pre).astype(B16)
        acc[...] += dot(low, wout[cols, :])
        return carry

    count = hidden // CHUNK
    lax.fori_loop(0, count, forward, 0)
    res[...] = acc[...].astype(B16)
    give_res = PlaneExchange(res, ret_o, ds2, dr2)
    give_res.start()
    for column in later:
        column.push(2)
        column.take(3)
        column.push(3)
    for column, spread in zip(later, spreads):
        column.keep().wait()
        spread.near()
    pass_x(0)
    pass_x(1)
    give_grads.wait_in()
    pl.when(end)(lambda: far_copy(1).start())
    acc[...] = jnp.zeros_like(acc)
    ebias[...] = jnp.zeros_like(ebias)
    column_sum = jnp.sum(grads[...].astype(F32), axis=0, keepdims=True)
    for p in range(n):
        at = hidden // 128 + p
        ebias[at : at + 1, 0:part] = column_sum[:, part * p : part * (p + 1)]

    def backward(f, carry):
        cols = span(f)
        act, slope = gelu_parts(pres[:, cols])
        pre = (dot_nt(grads[...], wout[cols, :]) * slope).astype(B16)
        acc[...] += dot_nt(pre, win[:, cols])
        col = jnp.sum(pre.astype(F32), axis=0, keepdims=True)
        for j in range(CHUNK // 128):
            ebias[pl.ds(f * (CHUNK // 128) + j, 1), :] = col[:, 128 * j : 128 * (j + 1)]

        @pl.when(inner)
        def _():
            dwout[cols, :] = dot_tn(act.astype(B16), grads[...]).astype(B16)
            dwin[:, cols] = dot_tn(rows[...], pre).astype(B16)

        return carry

    lax.fori_loop(0, count, backward, 0)
    bgr[...] = acc[...].astype(B16)
    give_bgr = PlaneExchange(bgr, retg_o, ds3, dr3)
    give_bgr.start()

    mate = NZ - 1 - z

    def across():
        start = lax.div(mate, 2) * (hidden // 2)
        return remote(
            dwout.at[pl.ds(pl.multiple_of(start, 16), CHUNK), :], came_o, msem.at[0], msem.at[1], dev(mate, x, y, c)
        )

    def far(i, carry):
        f = lax.rem(i + lax.div(mate, 2) * (count // 2), count)
        cols = span(f)
        data, grad = far_rows[...], far_grads[...]
        act, slope = gelu_parts(dot(data, win[:, cols]) + bias_of(cols))
        pre = (dot_nt(grad, wout[cols, :]) * slope).astype(B16)
        dwout[cols, :] = (dwout[cols, :].astype(F32) + dot_tn(act.astype(B16), grad)).astype(B16)
        put_out(f).start()
        dwin[:, cols] = (dwin[:, cols].astype(F32) + dot_tn(data, pre)).astype(B16)
        put_in(f).start()
        pl.when(i == 0)(lambda: across().start())
        return carry

    pass_x(2)
    pass_x(3)
    pass_y(0)
    pass_y(1)

    @pl.when(inner)
    def _():
        far_copy(0).wait_recv()
        far_copy(1).wait_recv()
        lax.fori_loop(0, count, far, 0)

    pass_y(2)
    pass_y(3)
    for spread in spreads:
        spread.finish()

    @pl.when(inner)
    def _():
        across().wait()

    for column in later:
        column.finish()
    for exchange in (give_res, give_bgr):
        exchange.wait_in()
    for exchange in (give_rows, give_grads, give_res, give_bgr):
        exchange.wait_out()
    peers(lambda p: first(p, p).wait_send())
    peers(lambda p: second_hop(p, p).wait_send())
    for copy in keep:
        copy.wait()

    @pl.when(end)
    def _():
        far_copy(0).wait_send()
        far_copy(1).wait_send()

    @pl.when(inner)
    def _():
        for f in range(count):
            put_out(f).wait()
            put_in(f).wait()


def lead_part(tok, cot, route, cond, ada, adab, qvb, outb, soutb, sinb, router, bin_r, bout_r, shards, win, wout):
    n = NZ * NX
    length, width = tok.shape
    hidden = win.shape[2]
    slots = E * CAP
    dma = pltpu.SemaphoreType.DMA
    vm = pltpu.VMEM
    tiles = (ada.shape[1] // 128 + 7) // 8 * 8
    wide = [sds((n * s.shape[0], s.shape[1]), B16) for s in shards[:2]]
    outs = [
        sds((length, width), B16),
        sds((length, 3 * width), B16),
        sds((length, 128), F32),
        sds((length, width), B16),
        sds((length, width), F32),
        sds((length, width), F32),
        sds((length, width), B16),
        sds((length, 128), F32),
        sds((length, 128), jnp.int32),
        sds((8, width), F32),
        sds((8, width), F32),
        sds((1, hidden), F32),
        sds((E, width), F32),
        sds((8, 128), F32),
        sds((32, 128), F32),
    ]
    back = [sds((slots, width), B16)] * 2
    wide += [sds((NZ, NX) + s.shape, B16) for s in shards[2:]]
    far = back + wide + [
        sds((width, hidden), B16),
        sds((hidden, width), B16),
        sds((CHUNK, width), B16),
    ]
    return pl.pallas_call(
        lead_kernel,
        out_shape=outs + far,
        in_specs=[VM] * 13 + [HB] * 6,
        out_specs=[VM] * len(outs) + [HB] * len(far),
        scratch_shapes=[
            vm((32, 128), F32),
            vm((n, 32, 128), F32),
            vm((n, tiles, 128), F32),
            vm((n, tiles, 128), F32),
            vm(wide[0].shape, B16),
            vm(wide[1].shape, B16),
            vm((slots, width), B16),
            vm((slots, width), B16),
            vm((slots, width), B16),
            vm((slots, width), B16),
            vm((slots, width), B16),
            vm((slots, width), B16),
            vm((slots, width), B16),
            vm((slots, width), B16),
            vm((width, hidden), B16),
            vm((hidden, width), B16),
            vm((width, hidden), B16),
            vm((hidden, width), B16),
            vm((slots, hidden), F32),
            vm((slots, width), F32),
        ]
        + [vm((NZ * s.shape[0], s.shape[1] // 2), B16) for s in shards[2:]]
        + [vm((NZ * s.shape[0] // 2, s.shape[1] // 2), B16) for s in shards[2:]]
        + [
            dma((n,)),
            dma((n,)),
            dma((n,)),
            dma((n,)),
        ]
        + [dma((E,))] * 8
        + [dma((4,)), dma((2, hidden // CHUNK)), dma((2, 2)), dma((2,))]
        + Gather.semaphores(2)
        + Column.semaphores()
        + Column.semaphores()
        + Spread.semaphores()
        + Spread.semaphores(),
        compiler_params=params(1),
        name="front_and_expert",
    )(tok, cot, route, cond, ada, adab, qvb, outb, soutb, sinb, router, bin_r, bout_r, *shards, win, wout)


def add_into(target, source, lead):
    count = 1
    for n in lead:
        count *= n

    def body(i, carry):
        at = []
        rest = i
        for n in reversed(lead):
            at.append(lax.rem(rest, n))
            rest = lax.div(rest, n)
        at = tuple(reversed(at))
        target[at] = (target[at].astype(F32) + source(at).astype(F32)).astype(B16)
        return carry

    lax.fori_loop(0, count, body, 0)


def piece_specs(width, hidden):
    rows, tall = width // NZ // 4, hidden // NZ // 4
    qkv = 3 * width // 2
    left = (qkv // 128 + 1) // 2 * 128
    early = (
        (2, (True, 0, rows, 0, hidden // 4, True)),
        (3, (True, 0, tall // 2, 0, width // 2, False)),
        (2, (True, 0, rows, hidden // 4, hidden // 4, False)),
        (3, (True, tall // 2, tall // 2, 0, width // 2, True)),
    )
    late = (
        (0, (False, 0, rows, 0, left, True)),
        (0, (False, 0, rows, left, qkv - left, True)),
        (1, (False, 0, rows, 0, width // 2, True)),
    )
    return early, late


class FirstHop:
    def __init__(self, spec, half, ebuf, sems):
        self.z, self.x, self.y, self.c = coords()
        _, self.row, self.rows, self.col, self.width, self.y_first = spec
        self.half, self.ebuf, self.sems = half, ebuf, sems

    def inner(self, *lead):
        return lead + (slice(self.row, self.row + self.rows), slice(self.col, self.col + self.width))

    def copy(self):
        every = slice(None)
        if self.y_first:
            at, to = self.inner(every, every, 1 - self.y), dev(self.z, self.x, 1 - self.y, self.c)
        else:
            at, to = self.inner(every, 1 - self.x, every), dev(self.z, 1 - self.x, self.y, self.c)
        return remote(self.half.at[at], self.ebuf, self.sems.at[0], self.sems.at[1], to)

    def absorb(self):
        self.copy().wait_recv()
        if self.y_first:
            source = lambda i: self.half[self.inner(i[0], i[1], self.y)]
        else:
            source = lambda i: self.half[self.inner(i[0], self.x, i[1])]
        add_into(self.ebuf, source, (NZ, 2))


def middle_kernel(
    ret, retg, second_r, resid_r, att_r, cot, mod, sinb, bias, router, gates_r, place_r, mixed, outw,
    tok, normed, proj, lsum, condt, ebias, sin_h, sout_h, qkv_h, dwout, dwin,
    out_o, out_half, shares, qkv_half, tgrad_o, mine_o, e0, e1, e2, e3, came_o, came_w,
    sin, sout, dsin, dsout, sin_half, sout_half, qkv, shared, sgrad, mgrad, rgrad_s, mg2, pgrad, tile, dqkv, dout,
    hsem, gsem, msem, lsem, qsem, s0, s1, s2, s3,
):
    chunks = range(NZ)
    size = sin.shape[3] // NZ
    loads = []
    for f in chunks:
        cols = slice(f * size, (f + 1) * size)
        loads.append(
            (
                pltpu.make_async_copy(sin_h.at[:, :, :, cols], sin.at[:, :, :, cols], lsem.at[0, f]),
                pltpu.make_async_copy(sout_h.at[f], sout.at[f], lsem.at[1, f]),
            )
        )
        for load in loads[-1]:
            load.start()
    qkv_load = pltpu.make_async_copy(qkv_h, qkv, qsem.at[0])
    qkv_load.start()
    barrier = pltpu.get_barrier_semaphore()
    z, x, y, c = coords()
    mate = NZ - 1 - z
    for to in (dev(mate, x, y, c), dev(z, x, y, 1 - c), dev(z, x, 1 - y, c), dev(z, 1 - x, y, c)):
        greet(barrier, to)
    pl.semaphore_wait(barrier, 4)
    central = jnp.logical_and(z > 0, z < NZ - 1)

    def across():
        rows = dwout.shape[0] // 2
        start = pl.multiple_of(lax.div(mate, 2) * rows + CHUNK, 16)
        return remote(
            dwout.at[pl.ds(start, rows - CHUNK), :], came_o, msem.at[0], msem.at[1], dev(mate, x, y, c)
        )

    def across_wide():
        rows = dwin.shape[0] // 2
        start = pl.multiple_of(lax.div(mate, 2) * rows, 16)
        return remote(
            dwin.at[pl.ds(start, rows), 0 : came_w.shape[1]], came_w, msem.at[2], msem.at[3], dev(mate, x, y, c)
        )

    @pl.when(central)
    def _():
        across().start()
        across_wide().start()

    length, width = second_r.shape
    hidden = sin.shape[3]
    chunk = hidden // NZ
    second = second_r[...]
    grad_out = cot[...].astype(F32)
    moe_low = (mod[5:6] * grad_out).astype(B16)
    moe_grad = moe_low.astype(F32)
    shared[...] = jnp.zeros_like(shared) + bias[3:4, :]
    sgrad[...] = jnp.zeros_like(sgrad)
    shares[...] = jnp.zeros_like(shares)
    n = NZ * NX
    part = width // n
    own_tiles = hidden // n // 128

    def cut(at, rows):
        for p in range(n):
            shares[p, at : at + rows.shape[0], 0:part] = rows[:, part * p : part * (p + 1)]

    for p in range(n):
        shares[p, 16 : 16 + own_tiles, :] = ebias[own_tiles * p : own_tiles * (p + 1), :]
        at = hidden // 128 + p
        shares[p, 19:20, 0:part] = ebias[at : at + 1, 0:part]

    other_core = dev(z, x, y, 1 - c)

    def half_cols(size, core):
        return pl.ds(pl.multiple_of(core * size, 128), size)

    def sout_copy(f):
        cols = half_cols(width // 2, 1 - c)
        return remote(
            dsout.at[f, :, :, :, cols], sout_half.at[f], hsem.at[0, 1, f], hsem.at[1, 1, f], other_core
        )

    def sin_copy(f):
        at = f % (NZ // 2)
        return remote(
            dsin.at[:, :, :, :, f * chunk : (f + 1) * chunk],
            sin_half.at[:, :, :, :, at * chunk : (at + 1) * chunk],
            hsem.at[0, 0, at],
            hsem.at[1, 0, at],
            other_core,
        )

    def core_copy(i):
        whole, half = ((dqkv, qkv_half), (dout, out_half))[i]
        cols = half_cols(half.shape[4], 1 - c)
        return remote(whole.at[:, :, :, :, cols], half, gsem.at[0, i], gsem.at[1, i], other_core)

    def core_add(half, whole):
        own = half_cols(half.shape[4], c)
        add_into(half, lambda at: whole[at[0], at[1], at[2], :, own], (NZ, NX, 2))

    def body(f):
        for load in loads[f]:
            load.wait()
        cols = slice(f * chunk, (f + 1) * chunk)
        w1 = sin[:, :, :, cols].reshape(width, chunk)
        w2 = sout[f].reshape(chunk, width)
        act, slope = gelu_parts(dot(second, w1) + sinb[:, cols])
        low = act.astype(B16)
        shared[...] += dot(low, w2)
        pre = (dot_nt(moe_low, w2) * slope).astype(B16)
        dsout[f] = dot_tn(low, moe_low).astype(B16).reshape(dsout.shape[1:])
        dsin[:, :, :, :, cols] = dot_tn(second, pre).astype(B16).reshape(dsin.shape[:4] + (chunk,))
        sout_copy(f).start()
        pl.when(c == 1 - f // (NZ // 2))(lambda: sin_copy(f).start())
        sgrad[...] += dot_nt(pre, w1)
        col = jnp.sum(pre.astype(F32), axis=0, keepdims=True)
        for j in range(chunk // 128):
            at = f * (chunk // 128) + j
            shares[at // own_tiles, 4 + at % own_tiles : 5 + at % own_tiles, :] = col[
                :, 128 * j : 128 * (j + 1)
            ]

    for f in chunks:
        body(f)
    lane = lax.broadcasted_iota(jnp.int32, (length, E), 1)
    gates = [gates_r[:, k : k + 1] for k in range(2)]
    maps = [
        jnp.where(choose_rows(place_r[:, k : k + 1], E * CAP), 1.0, 0.0) for k in range(2)
    ]
    back = ret[...]
    rows = [dot(m.astype(B16), back) for m in maps]
    moe = shared[...] + (gates[0] * rows[0] + gates[1] * rows[1])
    for f in range(NZ // 2):
        sin_copy(f).wait_recv()
    for f in chunks:
        sout_copy(f).wait_recv()
    core_add(sin_half, dsin)
    core_add(sout_half, dsout)
    hops = [
        FirstHop(spec, sin_half if matrix == 2 else sout_half, ebuf, sem)
        for (matrix, spec), ebuf, sem in zip(
            piece_specs(width, hidden)[0], (e0, e1, e2, e3), (s0, s1, s2, s3)
        )
    ]
    for hop in hops:
        hop.copy().start()

    resid = resid_r[...]
    out_o[...] = (resid + mod[5:6] * moe).astype(B16)
    mg2[...] = jnp.zeros_like(mg2)
    mg2[5:6, :] = jnp.sum(grad_out * moe, axis=0, keepdims=True)
    ggrad = [jnp.sum(moe_grad * r, axis=-1, keepdims=True) for r in rows]
    inner = gates[0] * ggrad[0] + gates[1] * ggrad[1]
    lgrad = jnp.zeros((length, E), F32)
    for k in range(2):
        pick = place_r[:, 2 + k : 3 + k] == lane
        lgrad = lgrad + jnp.where(pick, gates[k] * (ggrad[k] - inner), 0.0)
    lgrad = lgrad.astype(B16)
    cut(8, dot_tn(lgrad, second))
    grad = (
        sgrad[...]
        + dot((maps[0] + maps[1]).astype(B16), retg[...])
        + dot(lgrad, router[...].astype(B16))
    )
    n2, r2 = norm_parts(resid)
    mg2[3:4, :] = jnp.sum(grad, axis=0, keepdims=True)
    mg2[4:5, :] = jnp.sum(grad * n2, axis=0, keepdims=True)
    rgrad = grad_out + norm_back(grad * (1.0 + mod[4:5]), n2, r2)
    rgrad_s[...] = rgrad
    agrad = (mod[2:3] * rgrad).astype(B16)
    mg2[2:3, :] = jnp.sum(rgrad * att_r[...], axis=0, keepdims=True)
    dout[...] = dot_tn(mixed[...], agrad).astype(B16).reshape(dout.shape)
    core_copy(1).start()
    mgrad[...] = dot_nt(agrad, outw[...]).astype(B16)
    cut(3, jnp.sum(moe_grad, axis=0, keepdims=True))
    cut(2, jnp.sum(agrad.astype(F32), axis=0, keepdims=True))
    low_lane = lax.broadcasted_iota(jnp.int32, (length, 128), 1) < HEAD_DIM
    for p in range(HEADS // 2):
        q2 = proj[:, 128 * p : 128 * (p + 1)]
        k2 = proj[:, width + 128 * p : width + 128 * (p + 1)]
        v2 = proj[:, 2 * width + 128 * p : 2 * width + 128 * (p + 1)]
        m2 = mgrad[:, 128 * p : 128 * (p + 1)]
        parts = []
        for h in range(2):
            head = low_lane if h == 0 else jnp.logical_not(low_lane)
            zero = jnp.zeros_like(q2)
            s = dot_nt(jnp.where(head, q2, zero), k2) * SCALE
            prob = jnp.exp(s - lsum[:, 2 * p + h : 2 * p + h + 1])
            pg = dot_nt(jnp.where(head, m2, zero), v2)
            inner = jnp.sum(prob * pg, axis=-1, keepdims=True)
            sg = (prob * (pg - inner)).astype(B16)
            parts.append(
                (dot(sg, k2) * SCALE, dot_tn(sg, q2) * SCALE, dot_tn(prob.astype(B16), m2))
            )
        for i in range(3):
            pgrad[:, i * width + 128 * p : i * width + 128 * (p + 1)] = jnp.where(
                low_lane, parts[0][i], parts[1][i]
            ).astype(B16)
    lead = dqkv.shape[:4]
    for i in range(3):
        cols = slice(i * width, (i + 1) * width)
        dqkv[:, :, :, :, cols] = dot_tn(normed[...], pgrad[:, cols]).astype(B16).reshape(lead + (width,))
    core_copy(0).start()
    qkv_load.wait()
    ngrad = dot_nt(pgrad[...], qkv[...])
    n1, r1 = norm_parts(tok[...].astype(F32))
    tgrad_o[...] = rgrad_s[...] + norm_back(ngrad * (1.0 + mod[1:2]), n1, r1)
    per = width // 128
    for i, k in enumerate((0, 2)):
        cut(i, jnp.sum(pgrad[:, k * width : (k + 1) * width].astype(F32), axis=0, keepdims=True))
    mod_rows = [
        jnp.sum(ngrad, axis=0, keepdims=True),
        jnp.sum(ngrad * n1, axis=0, keepdims=True),
    ] + [mg2[i : i + 1, :] for i in range(2, 6)]
    tile[...] = jnp.zeros_like(tile)
    for i, row in enumerate(mod_rows):
        row = row.astype(B16).astype(F32)
        for j in range(per):
            tile[i * per + j : i * per + j + 1, :] = row[:, 128 * j : 128 * (j + 1)]
    tile[40:48, :] = condt[...]
    mine_o[...] = tile[...].astype(B16)
    for i, (half, whole) in enumerate(((qkv_half, dqkv), (out_half, dout))):
        core_copy(i).wait_recv()
        core_add(half, whole)
        core_copy(i).wait_send()
    for f in chunks:
        sout_copy(f).wait_send()
        pl.when(c == 1 - f // (NZ // 2))(lambda: sin_copy(f).wait_send())
    for hop in hops:
        hop.absorb()
    for hop in hops:
        hop.copy().wait_send()

    @pl.when(central)
    def _():
        across().wait()
        across_wide().wait()


def middle(*args):
    second, sin = args[2], args[20]
    length, width = second.shape
    hidden = sin.shape[3]
    rows, tall = width // NZ // 4, hidden // NZ // 4
    dma = pltpu.SemaphoreType.DMA
    vm = pltpu.VMEM
    early = piece_specs(width, hidden)[0]
    return pl.pallas_call(
        middle_kernel,
        out_shape=[
            sds((length, width), B16),
            sds((NZ, NX, 2, rows, width // 2), B16),
            sds((NZ * NX, 24, 128), F32),
            sds((NZ, NX, 2, rows, 3 * width // 2), B16),
            sds((length, width), F32),
            sds((48, 128), B16),
        ]
        + [sds((NZ, 2, spec[2], spec[4]), B16) for _, spec in early]
        + [
            sds((hidden // 2 - CHUNK, width), B16),
            sds((width // 2, hidden // MidSum.COUNT), B16),
        ],
        in_specs=[VM] * 20 + [HB] * 5,
        out_specs=[VM] * 10 + [HB] * 2,
        scratch_shapes=[
            vm(sin.shape, B16),
            vm((NZ, NX, hidden // NZ // NX, width), B16),
            vm((NZ, NX, 2, rows, hidden), B16),
            vm((NZ, NX, 2, tall, width), B16),
            vm((NZ, NX, 2, rows, hidden // 2), B16),
            vm((NZ, NX, 2, tall, width // 2), B16),
            vm((width, 3 * width), B16),
            vm((length, width), F32),
            vm((length, width), F32),
            vm((length, width), B16),
            vm((length, width), F32),
            vm((8, width), F32),
            vm((length, 3 * width), B16),
            vm((48, 128), F32),
            vm((NZ, NX, 2, rows, 3 * width), B16),
            vm((NZ, NX, 2, rows, width), B16),
            dma((2, 2, NZ)),
            dma((2, 2)),
            dma((4,)),
            dma((2, NZ)),
            dma((1,)),
        ]
        + [dma((2,))] * 4,
        compiler_params=params(3),
        name="shared_expert_attention_back",
    )(*args)


class Piece:
    def __init__(self, spec, grad, out, bufs):
        self.z, self.x, self.y, self.c = coords()
        self.half, self.row, self.rows, self.col, self.width, self.y_first = spec
        self.grad, self.out = grad, out
        self.size = out.shape[-1] // 2
        if self.half:
            self.ebuf = grad
        else:
            self.ebuf, bufs = bufs[0], bufs[1:]
        self.fbuf, self.zin, self.one, self.zsem = bufs
        self.inner = jnp.logical_and(self.z > 0, self.z < NZ - 1)
        self.end = jnp.logical_not(self.inner)
        self.mate = NZ - 1 - self.z
        self.beside = self.z + 1 - 2 * lax.rem(self.z, 2)

    @staticmethod
    def scratch(spec):
        half, _, rows, _, width, _ = spec
        vm = lambda *lead: pltpu.VMEM(lead + (rows, width), B16)
        dma = pltpu.SemaphoreType.DMA
        return ([] if half else [vm(NZ, 2)]) + [
            vm(NZ),
            vm(NZ + 3),
            dma((13,)),
            dma((2, 3)),
        ]

    def cols(self, c):
        return pl.ds(pl.multiple_of(c * self.size + self.col, 128), self.width)

    def core(self, *lead):
        return lead + (slice(self.row, self.row + self.rows), slice(self.col, self.col + self.width))

    def to_x(self):
        return dev(self.z, 1 - self.x, self.y, self.c)

    def to_y(self):
        return dev(self.z, self.x, 1 - self.y, self.c)

    def copy1(self):
        every = slice(None)
        if self.y_first:
            source, to = self.grad.at[self.core(every, every, 1 - self.y)], self.to_y()
        else:
            source, to = self.grad.at[self.core(every, 1 - self.x, every)], self.to_x()
        return remote(source, self.ebuf, self.one.at[3], self.one.at[4], to)

    def copy2(self):
        if self.y_first:
            source, to = self.ebuf.at[:, 1 - self.x], self.to_x()
        else:
            source, to = self.ebuf.at[:, 1 - self.y], self.to_y()
        return remote(source, self.fbuf, self.one.at[5], self.one.at[6], to)

    def zcopy(self, step):
        if step == 0:
            at = pl.ds(jnp.where(lax.rem(self.z, NZ - 1) == 0, lax.rem(self.z + 1, NZ), 0), NZ - 1)
            source, target, to = self.fbuf.at[at], self.zin.at[at], self.beside
        elif step == 1:
            at = pl.ds(2 * lax.div(self.mate, 2), 2)
            source, target, to = self.fbuf.at[at], self.zin.at[NZ : NZ + 2], self.mate
        else:
            source, target, to = self.fbuf.at[self.beside], self.zin.at[NZ + 2], self.beside
        return remote(
            source, target, self.zsem.at[0, step], self.zsem.at[1, step], dev(to, self.x, self.y, self.c)
        )

    def plus(self, block, came):
        self.fbuf[block] = (self.fbuf[block].astype(F32) + self.zin[came].astype(F32)).astype(B16)

    def own(self):
        return self.fbuf.at[self.z]

    def place(self, y, c):
        return self.out.at[y, self.row : self.row + self.rows, self.cols(c)]

    def keep(self):
        return pltpu.make_async_copy(self.own(), self.place(self.y, self.c), self.one.at[7])

    def give_y(self, came=False):
        at = self.place(1 - self.y if came else self.y, self.c)
        return remote(self.own(), at, self.one.at[8], self.one.at[9], self.to_y())

    def give_c(self, came=False):
        at = self.place(self.y, 1 - self.c if came else self.c)
        to = dev(self.z, self.x, self.y, 1 - self.c)
        return remote(self.own(), at, self.one.at[10], self.one.at[11], to)

    def pass_c(self, came=False):
        at = self.place(1 - self.y, 1 - self.c if came else self.c)
        to = dev(self.z, self.x, self.y, 1 - self.c)
        return remote(at, at, self.one.at[12], self.one.at[2], to)

    def stage(self, s):
        if s == 0 and not self.half:
            self.copy1().start()
        elif s == 1:
            if not self.half:
                self.copy1().wait_recv()
                if self.y_first:
                    add_into(self.ebuf, lambda i: self.grad[self.core(i[0], i[1], self.y)], (NZ, NX))
                else:
                    add_into(self.ebuf, lambda i: self.grad[self.core(i[0], self.x, i[1])], (NZ, 2))
            self.copy2().start()
        elif s == 2:
            self.copy2().wait_recv()
            side = self.x if self.y_first else self.y
            add_into(self.fbuf, lambda i: self.ebuf[i[0], side], (NZ,))
            pl.when(self.end)(lambda: self.zcopy(0).start())
        elif s == 3:

            @pl.when(self.inner)
            def _():
                self.zcopy(0).wait_recv()
                first = lax.rem(self.z, 2)
                for i in range(NZ - 1):
                    self.plus(first + i, first + i)
                self.zcopy(1).start()

        elif s == 4:

            @pl.when(self.inner)
            def _():
                self.zcopy(1).wait_recv()
                for i in range(2):
                    self.plus(2 * lax.div(self.z, 2) + i, NZ + i)
                self.zcopy(2).start()

        elif s == 5:

            @pl.when(self.end)
            def _():
                self.zcopy(2).wait_recv()
                self.plus(self.z, NZ + 2)

            self.give_y().start()
            self.give_c().start()
            self.keep().start()
        elif s == 6:
            self.give_y(True).wait_recv()
            self.pass_c().start()
        elif s == 7:
            self.keep().wait()
            self.give_c(True).wait_recv()
            self.pass_c(True).wait_recv()
            if not self.half:
                self.copy1().wait_send()
            self.copy2().wait_send()
            self.give_y().wait_send()
            self.give_c().wait_send()
            self.pass_c().wait_send()
            pl.when(self.end)(lambda: self.zcopy(0).wait_send())

            @pl.when(self.inner)
            def _():
                self.zcopy(1).wait_send()
                self.zcopy(2).wait_send()


class MidSum:
    COUNT = 6

    def __init__(self, origin, grad, into, out, total, outer, sems):
        self.z, self.x, self.y, self.c = coords()
        self.origin = origin
        self.grad, self.into, self.out, self.total, self.outer = grad, into, out, total, outer
        self.sems = sems
        self.size = grad.shape[2] // self.COUNT
        self.inner = jnp.logical_and(self.z > 0, self.z < NZ - 1)
        self.end = jnp.logical_not(self.inner)
        self.mate = NZ - 1 - self.z

    @staticmethod
    def scratch(shape):
        vm = pltpu.VMEM
        return [vm(shape[1:], B16), vm(shape[1:], B16), pltpu.SemaphoreType.DMA((9, MidSum.COUNT))]

    def cols(self, p):
        return slice(p * self.size, (p + 1) * self.size)

    @staticmethod
    def beside(z):
        return z + 1 - 2 * lax.rem(z, 2)

    def landing(self, z, block):
        rows = self.grad.shape[1]
        return pl.ds(pl.multiple_of((block - 2 * lax.div(z, 2)) * rows, 16), rows)

    def across(self, i, p, came=False):
        z = self.z if came else self.mate
        block = self.beside(z) if i == 0 else z
        return remote(
            self.origin.at[block, :, self.cols(p)],
            self.into.at[self.landing(z, block), self.cols(p)],
            self.sems.at[i, p],
            self.sems.at[2 + i, p],
            dev(self.mate, self.x, self.y, self.c),
        )

    def came(self, block, p):
        return self.into[self.landing(self.z, block), self.cols(p)].astype(F32)

    def outward(self, p):
        return remote(
            self.outer.at[:, self.cols(p)],
            self.total.at[:, self.cols(p)],
            self.sems.at[4, p],
            self.sems.at[5, p],
            dev(self.beside(self.z), self.x, self.y, self.c),
        )

    def begin(self, i, p):
        pl.when(self.inner)(lambda: self.across(i, p).start())

    def give(self, p, sent=True):
        @pl.when(self.inner)
        def _():
            if sent:
                self.across(0, p, True).wait_recv()
            cols = self.cols(p)
            self.outer[:, cols] = (
                self.grad[self.beside(self.z), :, cols].astype(F32) + self.came(self.beside(self.z), p)
            ).astype(B16)
            self.outward(p).start()

    def swap(self, p, came=False):
        part = self.total.shape[0] // NX
        start = pl.multiple_of((1 - self.x) * part, 16)
        return remote(
            self.total.at[pl.ds(start, part), self.cols(p)],
            self.out.at[1 - self.x if came else self.x, :, self.cols(p)],
            self.sems.at[6, p],
            self.sems.at[7, p],
            dev(self.z, 1 - self.x, self.y, self.c),
        )

    def keep(self, p):
        part = self.total.shape[0] // NX
        start = pl.multiple_of(self.x * part, 16)
        return pltpu.make_async_copy(
            self.total.at[pl.ds(start, part), self.cols(p)],
            self.out.at[self.x, :, self.cols(p)],
            self.sems.at[8, p],
        )

    def final(self, p, sent=True):
        @pl.when(self.inner)
        def _():
            if sent:
                self.across(1, p, True).wait_recv()
            cols = self.cols(p)
            self.total[:, cols] = (
                self.grad[self.z, :, cols].astype(F32) + self.came(self.z, p)
            ).astype(B16)

        pl.when(self.end)(lambda: self.outward(p).wait_recv())
        self.swap(p).start()
        self.keep(p).start()

    def close(self, sent):
        for p in range(self.COUNT):

            @pl.when(self.inner)
            def _():
                self.outward(p).wait_send()
                if p in sent:
                    self.across(0, p).wait_send()
                    self.across(1, p).wait_send()

            self.swap(p, True).wait_recv()
            self.swap(p).wait_send()
            self.keep(p).wait()


def tail_kernel(*refs):
    ebufs, qkv_half, out_half = refs[:4], refs[4], refs[5]
    shares, mine, ada = refs[6:9]
    dwin_h, dwout_h, came_a, came_b, came_w = refs[9:14]
    outs = refs[14:18]
    pair_in, pair_out, small, esum, tiles, cgot = refs[18:24]
    rest = list(refs[24:])
    z, x, y, c = coords()
    dp, ex = lax.axis_index("dp"), lax.axis_index("expert")
    n = NZ * NX
    width = dwout_h.shape[2]
    early_specs, late_specs = piece_specs(width, dwin_h.shape[2])
    dwin, dwout, lsem = rest[:3]
    rest = rest[3:]

    def make(specs, rest, sources):
        made = []
        for (matrix, spec), source in zip(specs, sources):
            count = len(Piece.scratch(spec))
            made.append(Piece(spec, source, outs[matrix], rest[:count]))
            rest = rest[count:]
        return made, rest

    early, rest = make(early_specs, rest, ebufs)
    late, rest = make(late_specs, rest, (qkv_half, qkv_half, out_half))
    wide = MidSum(dwin_h, dwin, rest[0], pair_in, *rest[1:4])
    tall = MidSum(dwout_h, dwout, rest[4], pair_out, *rest[5:8])
    rest = rest[8:]
    first_rows = came_a.shape[0]
    loads = [
        pltpu.make_async_copy(came_a, tall.into.at[0:first_rows, :], lsem.at[0]),
        pltpu.make_async_copy(came_b, tall.into.at[first_rows:, :], lsem.at[1]),
        pltpu.make_async_copy(dwout_h, dwout, lsem.at[2]),
        pltpu.make_async_copy(dwin_h, dwin, lsem.at[3]),
        pltpu.make_async_copy(came_w, wide.into.at[:, 0 : came_w.shape[1]], lsem.at[4]),
    ]
    sgot, dall, floats, csend, dsem, tsem = rest

    barrier = pltpu.get_barrier_semaphore()

    def peers(action):
        for p in range(n):

            @pl.when(p != dp)
            def _():
                action(p)

    peers(lambda p: greet(barrier, (p, ex)))
    mates = (dev(z, x, 1 - y, c), dev(z, x, y, 1 - c), dev(z, x, 1 - y, 1 - c))
    for mate in mates:
        greet(barrier, mate)
    pl.semaphore_wait(barrier, n - 1 + 3)

    def share_copy(p, at):
        return remote(shares.at[p], sgot.at[at], dsem.at[4, p], dsem.at[5, at], (p, ex))

    def tile(p, at):
        return remote(mine, tiles.at[ex, at], dsem.at[0, p], dsem.at[1, at], (p, ex))

    def mate_rank(i):
        return 2 * (1 - y if i != 1 else y) + (1 - c if i != 0 else c)

    def spread(i, theirs=False):
        rows = tiles.at[mate_rank(i) if theirs else ex]
        return remote(rows, rows, tsem.at[0, i], tsem.at[1, i], mates[i])

    def total_copy(i, theirs=False):
        rows = dall.at[mate_rank(i) if theirs else ex]
        return remote(rows, rows, tsem.at[2, i], tsem.at[3, i], mates[i])

    def cond_copy(p, at):
        return remote(csend.at[p], cgot.at[at], dsem.at[2, p], dsem.at[3, at], (p, ex))

    peers(lambda p: share_copy(p, dp).start())
    peers(lambda p: tile(p, dp).start())

    every = range(MidSum.COUNT)
    for piece in early:
        piece.stage(1)
    for piece in late:
        piece.stage(0)
    for p in every[1:]:
        for i in range(2):
            wide.begin(i, p)
    for load in loads:
        load.start()
    sgot[dp] = shares[dp]
    tiles[ex, dp] = mine[...]

    def small1():
        peers(lambda p: share_copy(p, p).wait_recv())
        peers(lambda p: tile(p, p).wait_recv())
        total = sgot[0, 0:16, :]
        for p in range(1, n):
            total = total + sgot[p, 0:16, :]
        dall[ex] = total
        for i in range(NX):
            own = sgot[i, 16:24, :]
            for zb in range(1, NZ):
                own = own + sgot[NX * zb + i, 16:24, :]
            esum[i] = own
        for i in range(3):
            total_copy(i).start()
            spread(i).start()
        floats[...] = tiles[ex].astype(F32)
        acc = jnp.zeros((n, ada.shape[0]), F32)
        for j in range(ada.shape[1] // 128):
            acc = acc + dot_nt(floats[:, j, :].astype(B16), ada[:, 128 * j : 128 * (j + 1)])
        csend[...] = jnp.zeros_like(csend)
        csend[:, 0, 0 : ada.shape[0]] = acc
        peers(lambda p: cond_copy(p, dp).start())
        cgot[dp] = csend[dp]

    def small2():
        for i in range(3):
            total_copy(i, True).wait_recv()
            spread(i, True).wait_recv()
        total = dall[0]
        for i in range(1, 4):
            total = total + dall[i]
        small[...] = total
        peers(lambda p: cond_copy(p, p).wait_recv())
        for i in range(3):
            total_copy(i).wait_send()
            spread(i).wait_send()
        peers(lambda p: share_copy(p, p).wait_send())
        peers(lambda p: tile(p, p).wait_send())
        peers(lambda p: cond_copy(p, p).wait_send())

    def run(pieces, s):
        for piece in pieces:
            piece.stage(s)

    for load in loads[:3]:
        load.wait()
    for p in every:
        tall.give(p, False)
    for load in loads[3:]:
        load.wait()
    wide.give(0, False)
    small1()
    run(early, 2)
    for p in every[1:3]:
        wide.give(p)
    run(late, 1)
    run(early, 3)
    for p in every:
        tall.final(p, False)
    run(early, 4)
    for p in every[3:]:
        wide.give(p)
    run(late, 2)
    run(early, 5)
    wide.final(0, False)
    run(late, 3)
    for p in every[1:3]:
        wide.final(p)
    run(early, 6)
    run(late, 4)
    for p in every[3:]:
        wide.final(p)
    run(late, 5)
    run(early, 7)
    small2()
    run(late, 6)
    run(late, 7)
    tall.close(())
    wide.close(every[1:])


def tail_part(ebufs, qkv_half, out_half, shares, mine, ada, dwin, dwout, came_a, came_b, came_w):
    n = NZ * NX
    dma = pltpu.SemaphoreType.DMA
    vm = pltpu.VMEM
    width, hidden = dwout.shape[2], dwin.shape[2]
    rows, tall = width // NZ // 4, hidden // NZ // 4
    outs = [
        sds((2, rows, 3 * width), B16),
        sds((2, rows, width), B16),
        sds((2, rows, hidden), B16),
        sds((2, tall, width), B16),
    ]
    scratch = [vm(dwin.shape, B16), vm(dwout.shape, B16), dma((5,))]
    for specs in piece_specs(width, hidden):
        for _, spec in specs:
            scratch += Piece.scratch(spec)
    for shape in (dwin.shape, dwout.shape):
        scratch += [vm((2 * shape[1], shape[2]), B16)] + MidSum.scratch(shape)
    scratch += [
        vm(shares.shape, F32),
        vm((4, 16, 128), F32),
        vm((n, 48, 128), F32),
        vm((n, 8, 128), F32),
        dma((6, n)),
        dma((4, 3)),
    ]
    out = pl.pallas_call(
        tail_kernel,
        out_shape=outs
        + [
            sds((NX, dwin.shape[1] // NX, hidden), B16),
            sds((NX, dwout.shape[1] // NX, width), B16),
            sds((16, 128), F32),
            sds((NX, 8, 128), F32),
            sds((4, n, 48, 128), B16),
            sds((n, 8, 128), F32),
        ],
        in_specs=[VM] * 9 + [HB] * 5,
        out_specs=[HB] * 6 + [VM] * 4,
        scratch_shapes=scratch,
        compiler_params=params(4),
        name="device_sums",
    )(
        *ebufs,
        qkv_half,
        out_half,
        shares,
        mine,
        ada,
        dwin,
        dwout,
        came_a,
        came_b,
        came_w,
    )
    return [o.reshape(-1, o.shape[2]) for o in out[:4]], out[4:6], out[6:]


def pick_part(flat, part, dp):
    chosen = jnp.zeros((flat.shape[0], part), flat.dtype)
    for p in range(NZ * NX):
        chosen = jnp.where(dp == p, flat[:, p * part : (p + 1) * part], chosen)
    return chosen


def finish_kernel(*refs):
    large = refs[:6]
    small, esum, tiles, cgot, cond = refs[6:11]
    outs = refs[11:17]
    ada_o, adab_o, qvb_o, outb_o, sinb_o, soutb_o, router_o, einb_o, eoutb_o, cond_o = refs[17:27]
    floats = refs[27]
    dp = lax.axis_index("dp")
    n = NZ * NX
    for source, out in zip(large, outs):
        out[...] = source[...].astype(F32)
    width = cond.shape[1]
    per, part = width // 128, width // n
    hidden = sinb_o.shape[0] * n
    images = tiles.shape[0] * tiles.shape[1]
    floats[...] = tiles[...].astype(F32)
    qvb_o[...] = small[0:2, 0:part]
    outb_o[...] = small[2:3, 0:part]
    soutb_o[...] = small[3:4, 0:part]
    router_o[...] = small[8:16, 0:part]
    for j in range(hidden // n // 128):
        cols = slice(128 * j, 128 * (j + 1))
        sinb_o[cols] = small[4 + j : 5 + j, :].reshape(128)
        for i in range(NX):
            einb_o[i : i + 1, cols] = esum[i, j : j + 1, :]
    for i in range(NX):
        eoutb_o[i : i + 1, :] = esum[i, 3:4, 0:part]

    conds = jnp.concatenate(
        [floats[:, :, 40 + j, :].reshape(images, 128) for j in range(per)], axis=1
    )
    conds = pick_part(conds, part, dp).astype(B16)
    sums = []
    for j in range(6 * per):
        mods = floats[:, :, j, :].reshape(images, 128)
        ada_o[:, 128 * j : 128 * (j + 1)] = dot_tn(conds, mods.astype(B16))
        sums.append(jnp.sum(mods, axis=0, keepdims=True))
    adab_o[...] = pick_part(jnp.concatenate(sums, axis=1), adab_o.shape[0], dp)[0]
    v = cond[...].astype(F32)
    sig = 1.0 / (1.0 + jnp.exp(-v))
    grad = jnp.concatenate([cgot[p, 0:1, 0:part] for p in range(n)], axis=1)
    cond_o[...] = grad * (sig * (1.0 + v * (1.0 - sig)))


def finish(dense, pairs, small, esum, tiles, cgot, cond, hidden):
    n = NZ * NX
    width = cond.shape[1]
    part = width // n
    big = [sds(v.shape, F32) for v in (*dense, *pairs)]
    short = [
        sds((part, 6 * width), F32),
        sds((6 * part,), F32),
        sds((2, part), F32),
        sds((1, part), F32),
        sds((hidden // n,), F32),
        sds((1, part), F32),
        sds((E, part), F32),
        sds((NX, hidden // n), F32),
        sds((NX, part), F32),
        sds((1, width), F32),
    ]
    return pl.pallas_call(
        finish_kernel,
        out_shape=big + short,
        in_specs=[VM] * 11,
        out_specs=[VM] * 16,
        scratch_shapes=[pltpu.VMEM(tiles.shape, F32)],
        compiler_params=params(),
        name="final_form",
    )(*dense, *pairs, small, esum, tiles, cgot, cond)


def on_block(
    tokens, conditioning, routes, cotangent, ada_weight, ada_bias, qkv_weight, qv_bias, out_weight, out_bias,
    shared_in, shared_in_bias, shared_out, shared_out_bias, router,
    expert_in, expert_in_bias, expert_out, expert_out_bias,
):
    n = NZ * NX
    width = tokens.shape[2]
    hidden = shared_in.shape[1]
    part = width // n
    tok, cot, route = tokens[0], cotangent[0], routes[0]
    (
        normed, proj, lsum, mixed, att, resid, second, gates, place, mod, bias, sinb, router_t,
        condt, ebias, ret, retg, qkv_full, out_full, sin_full, sout_full, dwin, dwout, came_a,
    ) = lead_part(
        tok, cot, route.T, conditioning, ada_weight, ada_bias, qv_bias, out_bias[None], shared_out_bias[None],
        shared_in_bias, router.T, expert_in_bias, expert_out_bias,
        (qkv_weight, out_weight, shared_in, shared_out), expert_in, expert_out,
    )
    (output, out_half, shares, qkv_half, tgrad, mine, e0, e1, e2, e3, came_b, came_w) = middle(
        ret, retg, second, resid, att, cot, mod, sinb, bias, router_t, gates, place, mixed, out_full,
        tok, normed, proj, lsum, condt, ebias, sin_full, sout_full, qkv_full, dwout, dwin,
    )
    dense, pairs, (small, esum, tiles, cgot) = tail_part(
        (e0, e1, e2, e3), qkv_half, out_half, shares, mine, ada_weight,
        dwin.reshape(NZ, NX * part, hidden), dwout.reshape(NZ, hidden // NZ, width), came_a, came_b, came_w,
    )
    (
        qkv_grad, out_grad, sin_grad, sout_grad, dwin_sum, dwout_sum, ada_grad, adab_grad, qvb_grad, outb_grad,
        sinb_grad, soutb_grad, router_grad, ein_b, eout_b, cond_grad,
    ) = finish(dense, pairs, small, esum, tiles, cgot, conditioning, hidden)
    return (
        output[None],
        tgrad[None],
        cond_grad,
        ada_grad,
        adab_grad,
        qkv_grad,
        qvb_grad,
        out_grad,
        outb_grad[0],
        sin_grad,
        sinb_grad,
        sout_grad,
        soutb_grad[0],
        router_grad.T,
        dwin_sum,
        ein_b,
        dwout_sum,
        eout_b,
    )


def layer_norm(rows):
    centred = rows - jnp.mean(rows, axis=-1, keepdims=True)
    return centred * lax.rsqrt(jnp.mean(centred * centred, axis=-1, keepdims=True) + 1e-06)


def modulate(rows, shift, scale):
    return layer_norm(rows) * (1.0 + scale) + shift


def gelu_tanh(values_in):
    return jax.nn.gelu(values_in, approximate=True)


def on_device(
    tokens,
    conditioning,
    routes,
    cotangent,
    ada_weight,
    ada_bias,
    qkv_weight,
    qv_bias,
    out_weight,
    out_bias,
    shared_in,
    shared_in_bias,
    shared_out,
    shared_out_bias,
    router,
    expert_in,
    expert_in_bias,
    expert_out,
    expert_out_bias,
):
    f32 = jnp.float32
    b16 = jnp.bfloat16
    gathered_dense = (
        lax.all_gather(ada_weight, "dp", axis=0, tiled=True),
        lax.all_gather(ada_bias, "dp", axis=0, tiled=True),
        lax.all_gather(qkv_weight, "dp", axis=0, tiled=True),
        lax.all_gather(qv_bias, "dp", axis=1, tiled=True),
        lax.all_gather(out_weight, "dp", axis=0, tiled=True),
        lax.all_gather(out_bias, "dp", axis=0, tiled=True),
        lax.all_gather(shared_in, "dp", axis=0, tiled=True),
        lax.all_gather(shared_in_bias, "dp", axis=0, tiled=True),
        lax.all_gather(shared_out, "dp", axis=0, tiled=True),
        lax.all_gather(shared_out_bias, "dp", axis=0, tiled=True),
        lax.all_gather(router, "dp", axis=0, tiled=True),
    )
    (
        ada_full,
        ada_bias_full,
        qkv_full,
        qv_bias_full,
        out_full,
        out_bias_full,
        shared_in_full,
        shared_in_bias_full,
        shared_out_full,
        shared_out_bias_full,
        router_full,
    ) = gathered_dense
    image_count, length, width = tokens.shape
    row_count = image_count * length
    scaling = HEAD_DIM ** (-0.5)
    head_shape = (image_count, length, HEADS, HEAD_DIM)
    cond_float = conditioning.astype(f32)
    cond_act, silu_back = jax.vjp(jax.nn.silu, cond_float)
    cond_low = cond_act.astype(b16)
    modulation = jnp.dot(cond_low, ada_full, preferred_element_type=f32) + ada_bias_full.astype(f32)
    pieces = [modulation[:, None, index * width : (index + 1) * width] for index in range(6)]
    source = tokens.astype(f32)
    first_norm, first_back = jax.vjp(modulate, source, pieces[0], pieces[1])
    normed = first_norm.astype(b16)
    projected = jnp.einsum("isd,de->ise", normed, qkv_full, preferred_element_type=f32)
    query_heads = (
        (projected[..., :width] + qv_bias_full[0].astype(f32)).astype(b16).reshape(head_shape)
    )
    key_heads = projected[..., width : 2 * width].astype(b16).reshape(head_shape)
    value_heads = (
        (projected[..., 2 * width :] + qv_bias_full[1].astype(f32)).astype(b16).reshape(head_shape)
    )
    scores = (
        jnp.einsum("iqhc,ikhc->ihqk", query_heads, key_heads, preferred_element_type=f32) * scaling
    )
    peak_score = jnp.max(scores, axis=-1, keepdims=True)
    unscaled = jnp.exp(scores - peak_score)
    exp_total = jnp.sum(unscaled, axis=-1, keepdims=True)
    log_total = peak_score + jnp.log(exp_total)
    probs_low = (unscaled / exp_total).astype(b16)
    mixed = (
        jnp.einsum("ihqk,ikhc->iqhc", probs_low, value_heads, preferred_element_type=f32)
        .reshape(image_count, length, width)
        .astype(b16)
    )
    attended = jnp.einsum(
        "isd,de->ise", mixed, out_full, preferred_element_type=f32
    ) + out_bias_full.astype(f32)
    resid = source + pieces[2] * attended
    second_float, second_back = jax.vjp(modulate, resid, pieces[3], pieces[4])
    second = second_float.astype(b16)
    shared_pre = jnp.einsum(
        "isd,df->isf", second, shared_in_full, preferred_element_type=f32
    ) + shared_in_bias_full.astype(f32)
    shared_act, shared_gelu_back = jax.vjp(gelu_tanh, shared_pre)
    shared_low = shared_act.astype(b16)
    shared = jnp.einsum(
        "isf,fd->isd", shared_low, shared_out_full, preferred_element_type=f32
    ) + shared_out_bias_full.astype(f32)
    second_rows = second.reshape(row_count, width)
    logits = jnp.dot(second_rows, router_full, preferred_element_type=f32)
    route_flat = routes.reshape(-1)
    one_hot = (route_flat[:, None] == jnp.arange(E, dtype=jnp.int32)).astype(jnp.int32)
    slot_index = jnp.sum(
        (jnp.cumsum(one_hot, axis=0, dtype=jnp.int32) - one_hot) * one_hot, axis=1, dtype=jnp.int32
    )
    position = jnp.where(slot_index < CAP, route_flat * CAP + slot_index, E * CAP)
    pair_rows = jnp.repeat(second_rows, 2, axis=0)
    buffer = (
        jnp.zeros((E * CAP, width), b16)
        .at[position]
        .set(pair_rows, mode="drop")
        .reshape(E, CAP, width)
    )
    received = lax.all_to_all(buffer, "expert", split_axis=0, concat_axis=1, tiled=True)
    expert_pre = (
        jnp.einsum("erd,edf->erf", received, expert_in, preferred_element_type=f32)
        + expert_in_bias.astype(f32)[:, None, :]
    )
    expert_low = gelu_tanh(expert_pre).astype(b16)
    expert_result = (
        jnp.einsum("erf,efd->erd", expert_low, expert_out, preferred_element_type=f32)
        + expert_out_bias.astype(f32)[:, None, :]
    ).astype(b16)
    returned = lax.all_to_all(
        expert_result, "expert", split_axis=1, concat_axis=0, tiled=True
    ).reshape(E * CAP, width)
    gathered = (
        returned.at[position]
        .get(mode="fill", fill_value=0)
        .reshape(row_count, 2, width)
        .astype(f32)
    )
    pair_mask = one_hot.reshape(row_count, 2, E).astype(f32)
    chosen = jnp.sum(logits[:, None, :] * pair_mask, axis=-1)
    gates = jax.nn.softmax(chosen, axis=-1)
    moe = (shared.reshape(row_count, width) + jnp.sum(gates[..., None] * gathered, axis=1)).reshape(
        image_count, length, width
    )
    output = (resid + pieces[5] * moe).astype(b16)
    ada_back, qkv_back, out_back, shared_in_back, shared_out_back, router_back = (
        ada_full,
        qkv_full,
        out_full,
        shared_in_full,
        shared_out_full,
        router_full,
    )
    grad_out = cotangent.astype(f32)
    gate_two_grad = jnp.sum(grad_out * moe, axis=1, keepdims=True)
    moe_grad = (pieces[5] * grad_out).astype(b16)
    moe_rows_grad = moe_grad.reshape(row_count, width)
    moe_rows_float = moe_rows_grad.astype(f32)
    pair_grad = (
        (gates[..., None] * moe_rows_float[:, None, :]).astype(b16).reshape(2 * row_count, width)
    )
    gate_grad = jnp.sum(moe_rows_float[:, None, :] * gathered, axis=-1)
    chosen_grad = gates * (gate_grad - jnp.sum(gates * gate_grad, axis=-1, keepdims=True))
    logits_grad = jnp.sum(chosen_grad[..., None] * pair_mask, axis=1).astype(b16)
    grad_buffer = (
        jnp.zeros((E * CAP, width), b16)
        .at[position]
        .set(pair_grad, mode="drop")
        .reshape(E, CAP, width)
    )
    result_grad = lax.all_to_all(grad_buffer, "expert", split_axis=0, concat_axis=1, tiled=True)
    pre_again = (
        jnp.einsum("erd,edf->erf", received, expert_in, preferred_element_type=f32)
        + expert_in_bias.astype(f32)[:, None, :]
    )
    act_again, expert_gelu_back = jax.vjp(gelu_tanh, pre_again)
    low_again = act_again.astype(b16)
    expert_out_grad = jnp.einsum("erf,erd->efd", low_again, result_grad, preferred_element_type=f32)
    expert_out_bias_grad = jnp.sum(result_grad.astype(f32), axis=1)
    expert_act_grad = jnp.einsum(
        "erd,efd->erf", result_grad, expert_out, preferred_element_type=f32
    )
    pre_grad = expert_gelu_back(expert_act_grad)[0].astype(b16)
    expert_in_grad = jnp.einsum("erd,erf->edf", received, pre_grad, preferred_element_type=f32)
    expert_in_bias_grad = jnp.sum(pre_grad.astype(f32), axis=1)
    received_grad = jnp.einsum(
        "erf,edf->erd", pre_grad, expert_in, preferred_element_type=f32
    ).astype(b16)
    sent_grad = lax.all_to_all(
        received_grad, "expert", split_axis=1, concat_axis=0, tiled=True
    ).reshape(E * CAP, width)
    dispatch_rows_grad = jnp.sum(
        sent_grad.at[position]
        .get(mode="fill", fill_value=0)
        .reshape(row_count, 2, width)
        .astype(f32),
        axis=1,
    )
    shared_out_grad = jnp.einsum("isf,isd->fd", shared_low, moe_grad, preferred_element_type=f32)
    shared_out_bias_grad = jnp.sum(moe_rows_float, axis=0)
    shared_act_grad = jnp.einsum(
        "isd,fd->isf", moe_grad, shared_out_back, preferred_element_type=f32
    )
    shared_pre_grad = shared_gelu_back(shared_act_grad)[0].astype(b16)
    shared_in_grad = jnp.einsum("isd,isf->df", second, shared_pre_grad, preferred_element_type=f32)
    shared_in_bias_grad = jnp.sum(shared_pre_grad.astype(f32), axis=(0, 1))
    router_grad = jnp.einsum("rd,re->de", second_rows, logits_grad, preferred_element_type=f32)
    second_grad = jnp.einsum(
        "isf,df->isd", shared_pre_grad, shared_in_back, preferred_element_type=f32
    )
    side_grad = dispatch_rows_grad + jnp.einsum(
        "re,de->rd", logits_grad, router_back, preferred_element_type=f32
    )
    second_grad = second_grad + side_grad.reshape(image_count, length, width)
    resid_extra, shift_two_grad, scale_two_grad = second_back(second_grad)
    resid_grad = grad_out + resid_extra
    attended_grad = (pieces[2] * resid_grad).astype(b16)
    gate_one_grad = jnp.sum(resid_grad * attended, axis=1, keepdims=True)
    out_weight_grad = jnp.einsum("isd,ise->de", mixed, attended_grad, preferred_element_type=f32)
    out_bias_grad = jnp.sum(attended_grad.astype(f32), axis=(0, 1))
    mixed_grad = (
        jnp.einsum("ise,de->isd", attended_grad, out_back, preferred_element_type=f32)
        .astype(b16)
        .reshape(head_shape)
    )
    again_scores = (
        jnp.einsum("iqhc,ikhc->ihqk", query_heads, key_heads, preferred_element_type=f32) * scaling
    )
    probs_float = jnp.exp(again_scores - log_total)
    again_low = probs_float.astype(b16)
    probs_grad = jnp.einsum("iqhc,ikhc->ihqk", mixed_grad, value_heads, preferred_element_type=f32)
    values_grad = jnp.einsum(
        "ihqk,iqhc->ikhc", again_low, mixed_grad, preferred_element_type=f32
    ).astype(b16)
    scores_grad = (
        probs_float * (probs_grad - jnp.sum(probs_float * probs_grad, axis=-1, keepdims=True))
    ).astype(b16)
    query_grad = (
        jnp.einsum("ihqk,ikhc->iqhc", scores_grad, key_heads, preferred_element_type=f32) * scaling
    ).astype(b16)
    keys_grad = (
        jnp.einsum("ihqk,iqhc->ikhc", scores_grad, query_heads, preferred_element_type=f32)
        * scaling
    ).astype(b16)
    flat_shape = (image_count, length, width)
    projected_grad = jnp.concatenate(
        [
            query_grad.reshape(flat_shape),
            keys_grad.reshape(flat_shape),
            values_grad.reshape(flat_shape),
        ],
        axis=-1,
    )
    qkv_weight_grad = jnp.einsum("isd,ise->de", normed, projected_grad, preferred_element_type=f32)
    qv_bias_grad = jnp.stack(
        [
            jnp.sum(query_grad.astype(f32), axis=(0, 1)).reshape(width),
            jnp.sum(values_grad.astype(f32), axis=(0, 1)).reshape(width),
        ]
    )
    normed_grad = jnp.einsum("ise,de->isd", projected_grad, qkv_back, preferred_element_type=f32)
    token_extra, shift_one_grad, scale_one_grad = first_back(normed_grad)
    tokens_grad = resid_grad + token_extra
    modulation_grad = jnp.concatenate(
        [
            shift_one_grad,
            scale_one_grad,
            gate_one_grad,
            shift_two_grad,
            scale_two_grad,
            gate_two_grad,
        ],
        axis=-1,
    )[:, 0, :].astype(b16)
    ada_weight_grad = jnp.einsum("id,ie->de", cond_low, modulation_grad, preferred_element_type=f32)
    ada_bias_grad = jnp.sum(modulation_grad.astype(f32), axis=0)
    cond_act_grad = jnp.einsum("ie,de->id", modulation_grad, ada_back, preferred_element_type=f32)
    conditioning_grad = silu_back(cond_act_grad)[0]
    expert_sums = (
        lax.psum_scatter(
            expert_in_grad.astype(jnp.bfloat16), "dp", scatter_dimension=1, tiled=True
        ).astype(jnp.float32),
        lax.psum_scatter(
            expert_in_bias_grad.astype(jnp.bfloat16), "dp", scatter_dimension=1, tiled=True
        ).astype(jnp.float32),
        lax.psum_scatter(
            expert_out_grad.astype(jnp.bfloat16), "dp", scatter_dimension=1, tiled=True
        ).astype(jnp.float32),
        lax.psum_scatter(
            expert_out_bias_grad.astype(jnp.bfloat16), "dp", scatter_dimension=1, tiled=True
        ).astype(jnp.float32),
    )
    dense_parts = (
        lax.psum_scatter(
            ada_weight_grad.astype(jnp.bfloat16), "dp", scatter_dimension=0, tiled=True
        ).astype(jnp.float32),
        lax.psum_scatter(
            ada_bias_grad.astype(jnp.bfloat16), "dp", scatter_dimension=0, tiled=True
        ).astype(jnp.float32),
        lax.psum_scatter(
            qkv_weight_grad.astype(jnp.bfloat16), "dp", scatter_dimension=0, tiled=True
        ).astype(jnp.float32),
        lax.psum_scatter(
            qv_bias_grad.astype(jnp.bfloat16), "dp", scatter_dimension=1, tiled=True
        ).astype(jnp.float32),
        lax.psum_scatter(
            out_weight_grad.astype(jnp.bfloat16), "dp", scatter_dimension=0, tiled=True
        ).astype(jnp.float32),
        lax.psum_scatter(
            out_bias_grad.astype(jnp.bfloat16), "dp", scatter_dimension=0, tiled=True
        ).astype(jnp.float32),
        lax.psum_scatter(
            shared_in_grad.astype(jnp.bfloat16), "dp", scatter_dimension=0, tiled=True
        ).astype(jnp.float32),
        lax.psum_scatter(
            shared_in_bias_grad.astype(jnp.bfloat16), "dp", scatter_dimension=0, tiled=True
        ).astype(jnp.float32),
        lax.psum_scatter(
            shared_out_grad.astype(jnp.bfloat16), "dp", scatter_dimension=0, tiled=True
        ).astype(jnp.float32),
        lax.psum_scatter(
            shared_out_bias_grad.astype(jnp.bfloat16), "dp", scatter_dimension=0, tiled=True
        ).astype(jnp.float32),
        lax.psum_scatter(
            router_grad.astype(jnp.bfloat16), "dp", scatter_dimension=0, tiled=True
        ).astype(jnp.float32),
    )
    dense_sums = lax.psum(
        (
            dense_parts[0],
            dense_parts[1],
            dense_parts[2],
            dense_parts[3],
            dense_parts[4],
            dense_parts[5],
            dense_parts[6],
            dense_parts[7],
            dense_parts[8],
            dense_parts[9],
            dense_parts[10],
        ),
        "expert",
    )
    return (
        output,
        tokens_grad,
        conditioning_grad,
        dense_sums[0],
        dense_sums[1],
        dense_sums[2],
        dense_sums[3],
        dense_sums[4],
        dense_sums[5],
        dense_sums[6],
        dense_sums[7],
        dense_sums[8],
        dense_sums[9],
        dense_sums[10],
        expert_sums[0],
        expert_sums[1],
        expert_sums[2],
        expert_sums[3],
    )


def solution(mesh):
    in_specs = (
        P(("dp", "expert"), None, None),
        P(("dp", "expert"), None),
        P(("dp", "expert"), None, None),
        P(("dp", "expert"), None, None),
        P("dp", None),
        P("dp"),
        P("dp", None),
        P(None, "dp"),
        P("dp", None),
        P("dp"),
        P("dp", None),
        P("dp"),
        P("dp", None),
        P("dp"),
        P("dp", None),
        P("expert", None, None),
        P("expert", None),
        P("expert", None, None),
        P("expert", None),
    )
    out_specs = (
        P(("dp", "expert"), None, None),
        P(("dp", "expert"), None, None),
        P(("dp", "expert"), None),
        P("dp", None),
        P("dp"),
        P("dp", None),
        P(None, "dp"),
        P("dp", None),
        P("dp"),
        P("dp", None),
        P("dp"),
        P("dp", None),
        P("dp"),
        P("dp", None),
        P("expert", "dp", None),
        P("expert", "dp"),
        P("expert", "dp", None),
        P("expert", "dp"),
    )
    body = on_device
    if dict(mesh.shape) == {"dp": NZ * NX, "expert": 4}:
        body = on_block
    return jax.shard_map(
        body, mesh=mesh, in_specs=in_specs, out_specs=out_specs, check_vma=False
    )
```

```python
import functools

import jax
import jax.numpy as jnp
from jax import lax
from jax.experimental import pallas as pl
from jax.experimental.pallas import tpu as pltpu
from jax.sharding import PartitionSpec as P

HEADS = 12
HEAD_DIM = 64
E = 8
CAP = 80
MESH = pl.DeviceIdType.MESH
F32 = jnp.float32
B16 = jnp.bfloat16
VMEM_LIMIT = 60 * 1024 * 1024
SCALE = HEAD_DIM ** (-0.5)
GELU_C = 0.7978845608028654
NZ, NX = 4, 2


def coords():
    dp = lax.axis_index("dp")
    ex = lax.axis_index("expert")
    return lax.div(dp, NX), lax.rem(dp, NX), lax.div(ex, 2), lax.rem(ex, 2)


def dev(z, x, y, c):
    return (NX * z + x, 2 * y + c)


def dot(a, b):
    return jnp.dot(a, b, preferred_element_type=F32)


def dot_nt(a, b):
    return lax.dot_general(a, b, (((1,), (1,)), ((), ())), preferred_element_type=F32)


def dot_tn(a, b):
    return lax.dot_general(a, b, (((0,), (0,)), ((), ())), preferred_element_type=F32)


def gelu(v):
    return v * (0.5 + 0.5 * jnp.tanh(v * (GELU_C + GELU_C * 0.044715 * (v * v))))


def gelu_parts(v):
    v2 = v * v
    t = jnp.tanh(GELU_C * v * (1.0 + 0.044715 * v2))
    h = 0.5 * (1.0 + t)
    return v * h, h + 0.5 * v * (1.0 - t * t) * (GELU_C * (1.0 + 0.134145 * v2))


def norm_parts(v):
    centred = v - jnp.mean(v, axis=-1, keepdims=True)
    r = lax.rsqrt(jnp.mean(centred * centred, axis=-1, keepdims=True) + 1e-06)
    return centred * r, r


def norm_back(u, n, r):
    return r * (
        u - jnp.mean(u, axis=-1, keepdims=True) - n * jnp.mean(u * n, axis=-1, keepdims=True)
    )


def remote(src, dst, send, recv, to):
    return pltpu.make_async_remote_copy(
        src_ref=src,
        dst_ref=dst,
        send_sem=send,
        recv_sem=recv,
        device_id=to,
        device_id_type=MESH,
    )


def greet(barrier, to):
    pl.semaphore_signal(barrier, inc=1, device_id=to, device_id_type=MESH)


def params(collective_id=None):
    if collective_id is None:
        return pltpu.CompilerParams(vmem_limit_bytes=VMEM_LIMIT)
    return pltpu.CompilerParams(
        vmem_limit_bytes=VMEM_LIMIT, collective_id=collective_id, has_side_effects=True
    )


VM = pl.BlockSpec(memory_space=pltpu.VMEM)
HB = pl.BlockSpec(memory_space=pl.ANY)


def sds(shape, dtype):
    return jax.ShapeDtypeStruct(shape, dtype)


class Gather:
    def __init__(self, shards, fulls, splits, sems):
        self.z, self.x, self.y, self.c = coords()
        self.mats = list(zip(shards, fulls, splits))
        (self.zs, self.zr, self.xs, self.xr, self.ys, self.yr, self.cs, self.cr, self.loc) = sems

    @staticmethod
    def semaphores(count):
        dma = pltpu.SemaphoreType.DMA
        return [
            dma((count, 2, NZ)),
            dma((count, NZ)),
            dma((count, NZ)),
            dma((count, NZ)),
            dma((count, NZ, NX)),
            dma((count, NZ, NX)),
            dma((count, NZ, NX, 2)),
            dma((count, NZ, NX, 2)),
            dma((count,)),
        ]

    def region(self, m, zb, xb, yh, ch):
        shard, full, split = self.mats[m]
        rows, width = shard.shape[0], shard.shape[1] // 2
        start = (NX * zb + xb) * rows
        if split:
            rows = rows // 2
            start = start + yh * rows
        return full.at[
            pl.ds(pl.multiple_of(start, 16), rows), pl.ds(pl.multiple_of(ch * width, 128), width)
        ]

    def own(self, m):
        shard, full, split = self.mats[m]
        rows, width = shard.shape[0], shard.shape[1] // 2
        start = 0
        if split:
            rows = rows // 2
            start = self.y * rows
        return shard.at[
            pl.ds(pl.multiple_of(start, 16), rows),
            pl.ds(pl.multiple_of(self.c * width, 128), width),
        ]

    def zcopy(self, m, zb, side, mine=False):
        here = self.region(m, zb, self.x, self.y, self.c)
        step = 1 if side else -1
        return remote(
            self.own(m) if mine else here,
            here,
            self.zs.at[m, side, zb],
            self.zr.at[m, zb],
            dev(lax.rem(self.z + step + NZ, NZ), self.x, self.y, self.c),
        )

    def xcopy(self, m, zb, mine=False, xb=None):
        here = self.region(m, zb, self.x if xb is None else xb, self.y, self.c)
        return remote(
            self.own(m) if mine else here,
            here,
            self.xs.at[m, zb],
            self.xr.at[m, zb],
            dev(self.z, 1 - self.x, self.y, self.c),
        )

    def ycopy(self, m, zb, xb, yh=None):
        here = self.region(m, zb, xb, self.y if yh is None else yh, self.c)
        return remote(
            here,
            here,
            self.ys.at[m, zb, xb],
            self.yr.at[m, zb, xb],
            dev(self.z, self.x, 1 - self.y, self.c),
        )

    def ccopy(self, m, zb, xb, yh, ch=None):
        here = self.region(m, zb, xb, yh, self.c if ch is None else ch)
        slot = yh if self.mats[m][2] else 0
        return remote(
            here,
            here,
            self.cs.at[m, zb, xb, slot],
            self.cr.at[m, zb, xb, slot],
            dev(self.z, self.x, self.y, 1 - self.c),
        )

    def local(self, m):
        shard, full, _ = self.mats[m]
        rows = shard.shape[0]
        start = (NX * self.z + self.x) * rows
        return pltpu.make_async_copy(
            shard, full.at[pl.ds(pl.multiple_of(start, 16), rows), :], self.loc.at[m]
        )

    def blocks(self, step):
        if step == 0:
            return [(self.z, None, None)]
        return [
            (self.z - step, self.z - step >= 0, 1),
            (self.z + step, self.z + step < NZ, 0),
        ]

    def more(self, side):
        return self.z + 1 < NZ if side else self.z - 1 >= 0

    def begin(self, m):
        for side in (1, 0):

            @pl.when(self.more(side))
            def _():
                self.zcopy(m, self.z, side, True).start()

        self.xcopy(m, self.z, True).start()
        self.local(m).start()

    def spread(self, m, zb, xb):
        if self.mats[m][2]:
            self.ycopy(m, zb, xb).start()
        self.ccopy(m, zb, xb, self.y).start()

    def take_z(self, m, step):
        for zb, exists, side in self.blocks(step):

            @pl.when(exists)
            def _():
                self.zcopy(m, zb, side).wait_recv()
                if step < NZ - 1:

                    @pl.when(self.more(side))
                    def _():
                        self.zcopy(m, zb, side).start()

                self.xcopy(m, zb).start()
                self.spread(m, zb, self.x)

    def take_x(self, m, step):
        for zb, exists, _ in self.blocks(step):

            def body():
                self.xcopy(m, zb, False, 1 - self.x).wait_recv()
                self.spread(m, zb, 1 - self.x)

            body() if exists is None else pl.when(exists)(body)

    def others(self, m, step, action):
        for zb, exists, _ in self.blocks(step):
            for xb in (self.x, 1 - self.x) if step else (1 - self.x,):
                body = functools.partial(action, m, zb, xb)
                body() if exists is None else pl.when(exists)(body)

    def take_y(self, m, step):
        if not self.mats[m][2]:
            return

        def action(m, zb, xb):
            self.ycopy(m, zb, xb, 1 - self.y).wait_recv()
            self.ccopy(m, zb, xb, 1 - self.y).start()

        self.others(m, step, action)

    def finish(self, m):
        def action(m, zb, xb):
            for yh in (self.y, 1 - self.y) if self.mats[m][2] else (self.y,):
                self.ccopy(m, zb, xb, yh, 1 - self.c).wait_recv()
                self.ccopy(m, zb, xb, yh).wait_send()
            if self.mats[m][2]:
                self.ycopy(m, zb, xb).wait_send()

        for step in range(NZ):
            self.others(m, step, action)
        for side in (1, 0):

            @pl.when(self.more(side))
            def _():
                self.zcopy(m, self.z, side, True).wait_send()

        for step in range(1, NZ):
            for zb, exists, side in self.blocks(step):

                @pl.when(exists)
                def _():
                    self.xcopy(m, zb).wait_send()
                    if step < NZ - 1:

                        @pl.when(self.more(side))
                        def _():
                            self.zcopy(m, zb, side).wait_send()

        self.xcopy(m, self.z, True).wait_send()
        self.local(m).wait()


class Column:
    def __init__(self, shard, column, other, send, recv, local, xsend, xrecv):
        self.z, self.x, self.y, self.c = coords()
        self.shard, self.column, self.other = shard, column, other
        self.send, self.recv, self.local, self.xsend, self.xrecv = send, recv, local, xsend, xrecv

    @staticmethod
    def semaphores():
        dma = pltpu.SemaphoreType.DMA
        return [dma((2, NZ)), dma((NZ,)), dma((1,)), dma((NZ,)), dma((NZ,))]

    def block(self, zb):
        rows = self.shard.shape[0]
        return self.column.at[pl.ds(pl.multiple_of(zb * rows, 16), rows), :]

    def own(self):
        width = self.shard.shape[1] // 2
        return self.shard.at[:, pl.ds(pl.multiple_of(self.c * width, 128), width)]

    def copy(self, zb, side, mine=False):
        here = self.block(zb)
        to = lax.rem(self.z + (1 if side else NZ - 1), NZ)
        return remote(
            self.own() if mine else here,
            here,
            self.send.at[side, zb],
            self.recv.at[zb],
            dev(to, self.x, self.y, self.c),
        )

    def xcopy(self, zb, mine=False):
        rows, width = self.shard.shape[0], self.shard.shape[1] // 2
        part = rows // 2
        start = pl.multiple_of(self.y * part, 16)
        if mine:
            source = self.shard.at[
                pl.ds(start, part), pl.ds(pl.multiple_of(self.c * width, 128), width)
            ]
        else:
            source = self.column.at[pl.ds(pl.multiple_of(zb * rows + start, 16), part), :]
        return remote(
            source,
            self.other.at[pl.ds(pl.multiple_of(zb * part, 16), part), :],
            self.xsend.at[zb],
            self.xrecv.at[zb],
            dev(self.z, 1 - self.x, self.y, self.c),
        )

    def keep(self):
        return pltpu.make_async_copy(self.own(), self.block(self.z), self.local.at[0])

    def more(self, side):
        return self.z + 1 < NZ if side else self.z - 1 >= 0

    def blocks(self, step):
        return [(self.z - step, self.z - step >= 0, 1), (self.z + step, self.z + step < NZ, 0)]

    def begin(self):
        for side in (1, 0):

            @pl.when(self.more(side))
            def _():
                self.copy(self.z, side, True).start()

        self.keep().start()
        self.xcopy(self.z, True).start()

    def take(self, step):
        for zb, exists, side in self.blocks(step):

            @pl.when(exists)
            def _():
                self.copy(zb, side).wait_recv()
                if step < NZ - 1:

                    @pl.when(self.more(side))
                    def _():
                        self.copy(zb, side).start()

    def push(self, step):
        for zb, exists, _ in self.blocks(step):

            @pl.when(exists)
            def _():
                self.xcopy(zb).start()

    def finish(self):
        for side in (1, 0):

            @pl.when(self.more(side))
            def _():
                self.copy(self.z, side, True).wait_send()

        for step in range(1, NZ - 1):
            for zb, exists, side in self.blocks(step):

                @pl.when(jnp.logical_and(exists, self.more(side)))
                def _():
                    self.copy(zb, side).wait_send()

        for zb in range(NZ):
            self.xcopy(zb).wait_send()


class Spread:
    def __init__(self, column, other, full, ys, yr, cs, cr, local):
        self.z, self.x, self.y, self.c = coords()
        self.column, self.other, self.full, self.local = column, other, full, local
        self.ys, self.yr, self.cs, self.cr = ys, yr, cs, cr

    @staticmethod
    def semaphores():
        dma = pltpu.SemaphoreType.DMA
        return [dma((NZ,))] * 2 + [dma((3, NZ))] * 2 + [dma((2, NZ))]

    def cols(self, c):
        width = self.full.shape[3] // 2
        return pl.ds(pl.multiple_of(c * width, 128), width)

    def half(self, y):
        rows = self.full.shape[2] // 2
        return pl.ds(pl.multiple_of(y * rows, 16), rows)

    def source(self, kind, zb):
        rows = self.full.shape[2] // (1 if kind == 0 else 2)
        ref = self.column if kind == 0 else self.other
        return ref.at[pl.ds(pl.multiple_of(zb * rows, 16), rows), :]

    def place(self, kind, zb, c):
        if kind == 0:
            return self.full.at[zb, self.x, :, self.cols(c)]
        return self.full.at[zb, 1 - self.x, self.half(self.y if kind == 1 else 1 - self.y), self.cols(c)]

    def ycopy(self, zb, came=False):
        return remote(
            self.source(1, zb), self.place(2 if came else 1, zb, self.c), self.ys.at[zb], self.yr.at[zb],
            dev(self.z, self.x, 1 - self.y, self.c),
        )

    def ccopy(self, kind, zb, came=False):
        at = self.place(kind, zb, 1 - self.c if came else self.c)
        return remote(
            at if kind == 2 else self.source(kind, zb), at, self.cs.at[kind, zb], self.cr.at[kind, zb],
            dev(self.z, self.x, self.y, 1 - self.c),
        )

    def keep(self, kind, zb):
        return pltpu.make_async_copy(
            self.source(kind, zb), self.place(kind, zb, self.c), self.local.at[kind, zb]
        )

    def near(self):
        for zb in range(NZ):
            self.ccopy(0, zb).start()
            self.keep(0, zb).start()

    def pass_x(self, zb):
        self.ycopy(zb).start()
        self.ccopy(1, zb).start()
        self.keep(1, zb).start()

    def pass_y(self, zb):
        self.ycopy(zb, True).wait_recv()
        self.ccopy(2, zb).start()

    def finish(self):
        for zb in range(NZ):
            for kind in range(3):
                self.ccopy(kind, zb, True).wait_recv()
                self.ccopy(kind, zb).wait_send()
            for kind in range(2):
                self.keep(kind, zb).wait()
            self.ycopy(zb).wait_send()


def choose_rows(place, slots):
    return place == lax.broadcasted_iota(jnp.int32, (place.shape[0], slots), 1)


def plane_peer(k):
    z, x, y, c = coords()
    xt = 1 - x if k & 1 else x
    ct = 1 - c if k & 2 else c
    yt = 1 - y if k & 4 else y
    return dev(z, xt, yt, ct), 4 * yt + 2 * ct + xt


def plane_rank():
    _, x, y, c = coords()
    return 4 * y + 2 * c + x


def slot_rows(ref, rank):
    return ref.at[pl.ds(pl.multiple_of(rank * CAP, 16), CAP), :]


class PlaneExchange:
    ORDER = (7, 5, 6, 4, 3, 1, 2)

    def __init__(self, source, target, send, recv):
        self.source, self.target, self.send, self.recv = source, target, send, recv

    def copy(self, k, into=None):
        peer, other = plane_peer(k)
        return remote(
            slot_rows(self.source, other),
            slot_rows(self.target, plane_rank() if into is None else other),
            self.send.at[k],
            self.recv.at[k],
            peer,
        )

    def mine(self):
        rank = plane_rank()
        return pltpu.make_async_copy(
            slot_rows(self.source, rank), slot_rows(self.target, rank), self.send.at[0]
        )

    def start(self):
        for k in self.ORDER:
            self.copy(k).start()
        self.mine().start()

    def wait_in(self):
        self.mine().wait()
        for k in self.ORDER:
            self.copy(k, True).wait_recv()

    def wait_out(self):
        for k in self.ORDER:
            self.copy(k).wait_send()


CHUNK = 512


def lead_kernel(
    tok, cot, routes, cond, ada, adab, qvb, outb, soutb, sinb_s, router_s, bin_r, bout_r,
    qkv_s, out_s, sin_s, sout_s, win_h, wout_h,
    normed_o, proj_o, lsum_o, mixed_o, att_o, resid_o, second_o, gates_o, place_o, mod_o, bias_o, sinb_o, rt_o,
    condt_o, ebias, ret_o, retg_o, qkv_o, outw_o, sin_o, sout_o, dwin_o, dwout_o, came_o,
    pack, packs, sent, got, qkv, outw, sbuf, gbuf, res, bgr, rows, grads, far_rows, far_grads, win, wout, dwin, dwout,
    pres, acc, turned, sin_c, sout_c, sin_x, sout_x,
    s1, r1, s2, r2, ds0, dr0, ds1, dr1, ds2, dr2, ds3, dr3, wsem, osem, fsem, msem, *gsems,
):
    z, x, y, c = coords()
    dp, ex = lax.axis_index("dp"), lax.axis_index("expert")
    n = NZ * NX
    length, width = tok.shape
    hidden = win.shape[1]
    part = width // n
    per = width // 128
    count = len(Column.semaphores())
    lead = Gather((qkv_s, out_s), (qkv, outw), (True, False), gsems[: len(Gather.semaphores(2))])
    gsems = gsems[len(Gather.semaphores(2)) :]
    later = (
        Column(sin_s, sin_c, sin_x, *gsems[:count]),
        Column(sout_s, sout_c, sout_x, *gsems[count : 2 * count]),
    )
    gsems = gsems[2 * count :]
    count = len(Spread.semaphores())
    spreads = (
        Spread(sin_c, sin_x, sin_o, *gsems[:count]),
        Spread(sout_c, sout_x, sout_o, *gsems[count:]),
    )

    def per_block(step, action):
        for zb, exists in [(z, None)] if step == 0 else [v[:2] for v in later[0].blocks(step)]:
            body = functools.partial(action, zb)
            body() if exists is None else pl.when(exists)(body)

    def pass_x(step):
        def action(zb):
            for column, spread in zip(later, spreads):
                column.xcopy(zb).wait_recv()
                spread.pass_x(zb)

        per_block(step, action)

    def pass_y(step):
        def action(zb):
            for spread in spreads:
                spread.pass_y(zb)

        per_block(step, action)

    loads = [
        pltpu.make_async_copy(win_h.at[x], win, wsem.at[0]),
        pltpu.make_async_copy(wout_h.at[x], wout, wsem.at[1]),
    ]

    def peers(action):
        for p in range(n):

            @pl.when(p != dp)
            def _():
                action(p)

    barrier = pltpu.get_barrier_semaphore()
    peers(lambda p: greet(barrier, (p, ex)))
    for k in range(2, E):
        greet(barrier, plane_peer(k)[0])

    pack[...] = jnp.zeros_like(pack)
    pack[0:2, 0:part] = qvb[...].astype(F32)
    pack[2:3, 0:part] = outb[...].astype(F32)
    pack[3:4, 0:part] = soutb[...].astype(F32)
    for j in range(hidden // n // 128):
        pack[4 + j : 5 + j, :] = sinb_s[128 * j : 128 * (j + 1)].astype(F32).reshape(1, 128)
    long = adab.shape[0]
    for j in range(-(-long // 128)):
        size = min(128, long - 128 * j)
        pack[8 + j : 9 + j, 0:size] = adab[128 * j : 128 * j + size].astype(F32).reshape(1, size)
    pack[16:24, 0:part] = router_s[...].astype(F32)
    cv = cond[...].astype(F32)
    cond_low = (cv / (1.0 + jnp.exp(-cv))).astype(B16).astype(F32)
    for p in range(n):
        pack[24 + p : 25 + p, 0:part] = cond_low[:, part * p : part * (p + 1)]
    condt_o[...] = jnp.zeros_like(condt_o)
    for j in range(per):
        condt_o[j : j + 1, :] = cond_low[:, 128 * j : 128 * (j + 1)]

    pl.semaphore_wait(barrier, n - 1 + E - 2)

    def first(p, at):
        return remote(pack, packs.at[at], s1.at[p], r1.at[at], (p, ex))

    def second_hop(p, at):
        return remote(sent.at[p], got.at[at], s2.at[p], r2.at[at], (p, ex))

    peers(lambda p: first(p, dp).start())
    lead.begin(0)
    lead.begin(1)
    for load in loads:
        load.start()
    packs[dp] = pack[...]
    peers(lambda p: first(p, p).wait_recv())
    cond_rows = jnp.concatenate([packs[p, pl.ds(24 + dp, 1), :] for p in range(n)], axis=0)
    partial = dot(cond_rows[:, :part].astype(B16), ada[...])
    for j in range(partial.shape[1] // 128):
        sent[:, j, :] = partial[:, 128 * j : 128 * (j + 1)]
    peers(lambda p: second_hop(p, dp).start())
    got[dp] = sent[dp]

    both_mats = (0, 1)

    def step_of(plan, step):
        for m in both_mats:
            if step:
                plan.take_z(m, step)
            plan.take_x(m, step)
        if step:
            for m in both_mats:
                plan.take_y(m, step - 1)

    for step in range(NZ):
        step_of(lead, step)

    for column in later:
        column.begin()

    bias_o[...] = jnp.zeros_like(bias_o)
    for p in range(n):
        bias_o[0:4, part * p : part * (p + 1)] = packs[p, 0:4, 0:part]
        rt_o[:, part * p : part * (p + 1)] = packs[p, 16:24, 0:part]
        for j in range(hidden // n // 128):
            at = hidden // n * p + 128 * j
            sinb_o[:, at : at + 128] = packs[p, 4 + j : 5 + j, :]
    peers(lambda p: second_hop(p, p).wait_recv())
    total = got[0]
    for p in range(1, n):
        total = total + got[p]
    mod_o[...] = jnp.zeros_like(mod_o)
    for i in range(6):
        for b in range(per):
            mod_o[i : i + 1, 128 * b : 128 * (b + 1)] = total[per * i + b : per * i + b + 1, :]
    unit = 64
    for p in range(n):
        for u in range(long // unit):
            at = long * p + unit * u
            i, b = at // width, at % width
            mod_o[i : i + 1, b : b + unit] += packs[
                p, 8 + unit * u // 128 : 9 + unit * u // 128, unit * u % 128 : unit * u % 128 + unit
            ]

    mod = mod_o[...]
    source = tok[...].astype(F32)
    n1, _ = norm_parts(source)
    normed = (n1 * (1.0 + mod[1:2]) + mod[0:1]).astype(B16)
    normed_o[...] = normed
    for m in both_mats:
        lead.take_y(m, NZ - 1)
    for m in both_mats:
        lead.finish(m)
    keep = [
        pltpu.make_async_copy(qkv, qkv_o, wsem.at[2]),
        pltpu.make_async_copy(outw, outw_o, wsem.at[3]),
    ]
    for copy in keep:
        copy.start()

    for k in range(3):
        part_k = dot(normed, qkv[:, k * width : (k + 1) * width])
        if k != 1:
            part_k = part_k + bias_o[k // 2 : k // 2 + 1, :]
        proj_o[:, k * width : (k + 1) * width] = part_k.astype(B16)
    lane = lax.broadcasted_iota(jnp.int32, (length, 128), 1)
    low_lane = lane < HEAD_DIM
    lsum = jnp.zeros((length, 128), F32)
    for p in range(HEADS // 2):
        q2 = proj_o[:, 128 * p : 128 * (p + 1)]
        k2 = proj_o[:, width + 128 * p : width + 128 * (p + 1)]
        v2 = proj_o[:, 2 * width + 128 * p : 2 * width + 128 * (p + 1)]
        outs = []
        for h in range(2):
            mine = low_lane if h == 0 else jnp.logical_not(low_lane)
            s = dot_nt(jnp.where(mine, q2, jnp.zeros_like(q2)), k2) * SCALE
            peak = jnp.max(s, axis=-1, keepdims=True)
            e = jnp.exp(s - peak)
            tot = jnp.sum(e, axis=-1, keepdims=True)
            lsum = jnp.where(lane == 2 * p + h, peak + jnp.log(tot), lsum)
            outs.append(dot((e / tot).astype(B16), v2))
        mixed_o[:, 128 * p : 128 * (p + 1)] = jnp.where(low_lane, outs[0], outs[1]).astype(B16)
    lsum_o[...] = lsum
    att = dot(mixed_o[...], outw[...]) + bias_o[2:3, :]
    att_o[...] = att
    resid = source + mod[2:3] * att
    resid_o[...] = resid
    n2, _ = norm_parts(resid)
    second = (n2 * (1.0 + mod[4:5]) + mod[3:4]).astype(B16)
    second_o[...] = second

    lane8 = lax.broadcasted_iota(jnp.int32, (length, E), 1)
    two = (
        lax.broadcasted_iota(jnp.int32, (2, 128), 0) == lax.broadcasted_iota(jnp.int32, (2, 128), 1)
    )
    route_cols = dot_tn(
        routes[...].astype(F32).astype(B16), jnp.where(two, 1.0, 0.0).astype(B16)
    ).astype(jnp.int32)
    route = [route_cols[:, k : k + 1] for k in range(2)]
    picks = [(r == lane8) for r in route]
    both = jnp.where(picks[0], 1.0, 0.0) + jnp.where(picks[1], 1.0, 0.0)
    earlier = (
        lax.broadcasted_iota(jnp.int32, (length, length), 1)
        < lax.broadcasted_iota(jnp.int32, (length, length), 0)
    )
    rank = dot(jnp.where(earlier, 1.0, 0.0).astype(B16), both.astype(B16))
    places = []
    for k in range(2):
        slot = jnp.sum(jnp.where(picks[k], rank, 0.0), axis=-1, keepdims=True).astype(jnp.int32)
        places.append(jnp.where(slot < CAP, route[k] * CAP + slot, -1))
    place_o[...] = jnp.where(
        lane == 0,
        places[0],
        jnp.where(lane == 1, places[1], jnp.where(lane == 2, route[0], route[1])),
    )
    maps = [jnp.where(choose_rows(v, E * CAP), 1.0, 0.0) for v in places]
    sbuf[...] = dot_tn((maps[0] + maps[1]).astype(B16), second).astype(B16)
    give_rows = PlaneExchange(sbuf, rows, ds0, dr0)
    give_rows.start()
    logits = dot_nt(second, rt_o[...].astype(B16))
    chosen = [jnp.sum(jnp.where(pick, logits, 0.0), axis=-1, keepdims=True) for pick in picks]
    top = jnp.maximum(chosen[0], chosen[1])
    e2 = [jnp.exp(v - top) for v in chosen]
    gates = [v / (e2[0] + e2[1]) for v in e2]
    gates_o[...] = jnp.where(lane == 0, gates[0], jnp.where(lane == 1, gates[1], 0.0))
    moe_grad = (mod[5:6] * cot[...].astype(F32)).astype(B16).astype(F32)
    pair = [(g * moe_grad).astype(B16) for g in gates]
    gbuf[...] = (
        dot_tn(maps[0].astype(B16), pair[0]) + dot_tn(maps[1].astype(B16), pair[1])
    ).astype(B16)
    give_grads = PlaneExchange(gbuf, grads, ds1, dr1)
    give_grads.start()
    for column in later:
        column.take(1)

    first_x = x == 0
    acc[...] = jnp.zeros_like(acc) + jnp.where(first_x, bout_r[0:1, :], bout_r[1:2, :]).astype(F32)
    for load in loads:
        load.wait()
    for column in later:
        column.take(2)
    give_rows.wait_in()

    end = jnp.logical_or(z == 0, z == NZ - 1)
    inner = jnp.logical_not(end)
    partner = dev(z + 1 - 2 * lax.rem(z, 2), x, y, c)

    def far_copy(i):
        source, target = ((rows, far_rows), (grads, far_grads))[i]
        return remote(source, target, fsem.at[0, i], fsem.at[1, i], partner)

    pl.when(end)(lambda: far_copy(0).start())
    for column in later:
        column.push(1)

    def span(f):
        return pl.ds(pl.multiple_of(f * CHUNK, 128), CHUNK)

    def put_in(f):
        return pltpu.make_async_copy(dwin.at[:, span(f)], dwin_o.at[:, span(f)], osem.at[1, f])

    def put_out(f):
        return pltpu.make_async_copy(dwout.at[span(f), :], dwout_o.at[span(f), :], osem.at[0, f])

    def bias_of(cols):
        return jnp.where(first_x, bin_r[0:1, cols], bin_r[1:2, cols]).astype(F32)

    def forward(f, carry):
        cols = span(f)
        pre = dot(rows[...], win[:, cols]) + bias_of(cols)
        pres[:, cols] = pre
        low = gelu(pre).astype(B16)
        acc[...] += dot(low, wout[cols, :])
        return carry

    count = hidden // CHUNK
    lax.fori_loop(0, count, forward, 0)
    res[...] = acc[...].astype(B16)
    give_res = PlaneExchange(res, ret_o, ds2, dr2)
    give_res.start()
    for column in later:
        column.push(2)
        column.take(3)
        column.push(3)
    for column, spread in zip(later, spreads):
        column.keep().wait()
        spread.near()
    pass_x(0)
    pass_x(1)
    give_grads.wait_in()
    pl.when(end)(lambda: far_copy(1).start())
    acc[...] = jnp.zeros_like(acc)
    ebias[...] = jnp.zeros_like(ebias)
    column_sum = jnp.sum(grads[...].astype(F32), axis=0, keepdims=True)
    for p in range(n):
        at = hidden // 128 + p
        ebias[at : at + 1, 0:part] = column_sum[:, part * p : part * (p + 1)]

    def backward(f, carry):
        cols = span(f)
        act, slope = gelu_parts(pres[:, cols])
        pre = (dot_nt(grads[...], wout[cols, :]) * slope).astype(B16)
        acc[...] += dot_nt(pre, win[:, cols])
        col = jnp.sum(pre.astype(F32), axis=0, keepdims=True)
        for j in range(CHUNK // 128):
            ebias[pl.ds(f * (CHUNK // 128) + j, 1), :] = col[:, 128 * j : 128 * (j + 1)]

        @pl.when(inner)
        def _():
            dwout[cols, :] = dot_tn(act.astype(B16), grads[...]).astype(B16)
            dwin[:, cols] = dot(turned[...], pre).astype(B16)

        return carry

    turned[...] = rows[...].T
    lax.fori_loop(0, count, backward, 0)
    bgr[...] = acc[...].astype(B16)
    give_bgr = PlaneExchange(bgr, retg_o, ds3, dr3)
    give_bgr.start()

    mate = NZ - 1 - z

    def across():
        start = lax.div(mate, 2) * (hidden // 2)
        return remote(
            dwout.at[pl.ds(pl.multiple_of(start, 16), CHUNK), :], came_o, msem.at[0], msem.at[1], dev(mate, x, y, c)
        )

    def far(i, carry):
        f = lax.rem(i + lax.div(mate, 2) * (count // 2), count)
        cols = span(f)
        data, grad = far_rows[...], far_grads[...]
        act, slope = gelu_parts(dot(data, win[:, cols]) + bias_of(cols))
        pre = (dot_nt(grad, wout[cols, :]) * slope).astype(B16)
        dwout[cols, :] = (dwout[cols, :].astype(F32) + dot_tn(act.astype(B16), grad)).astype(B16)
        put_out(f).start()
        dwin[:, cols] = (dwin[:, cols].astype(F32) + dot(turned[...], pre)).astype(B16)
        put_in(f).start()
        pl.when(i == 0)(lambda: across().start())
        return carry

    pass_x(2)
    pass_x(3)
    pass_y(0)
    pass_y(1)

    @pl.when(inner)
    def _():
        far_copy(0).wait_recv()
        turned[...] = far_rows[...].T
        far_copy(1).wait_recv()
        lax.fori_loop(0, count, far, 0)

    pass_y(2)
    pass_y(3)
    for spread in spreads:
        spread.finish()

    @pl.when(inner)
    def _():
        across().wait()

    for column in later:
        column.finish()
    for exchange in (give_res, give_bgr):
        exchange.wait_in()
    for exchange in (give_rows, give_grads, give_res, give_bgr):
        exchange.wait_out()
    peers(lambda p: first(p, p).wait_send())
    peers(lambda p: second_hop(p, p).wait_send())
    for copy in keep:
        copy.wait()

    @pl.when(end)
    def _():
        far_copy(0).wait_send()
        far_copy(1).wait_send()

    @pl.when(inner)
    def _():
        for f in range(count):
            put_out(f).wait()
            put_in(f).wait()


def lead_part(tok, cot, route, cond, ada, adab, qvb, outb, soutb, sinb, router, bin_r, bout_r, shards, win, wout):
    n = NZ * NX
    length, width = tok.shape
    hidden = win.shape[2]
    slots = E * CAP
    dma = pltpu.SemaphoreType.DMA
    vm = pltpu.VMEM
    tiles = (ada.shape[1] // 128 + 7) // 8 * 8
    wide = [sds((n * s.shape[0], s.shape[1]), B16) for s in shards[:2]]
    outs = [
        sds((length, width), B16),
        sds((length, 3 * width), B16),
        sds((length, 128), F32),
        sds((length, width), B16),
        sds((length, width), F32),
        sds((length, width), F32),
        sds((length, width), B16),
        sds((length, 128), F32),
        sds((length, 128), jnp.int32),
        sds((8, width), F32),
        sds((8, width), F32),
        sds((1, hidden), F32),
        sds((E, width), F32),
        sds((8, 128), F32),
        sds((32, 128), F32),
    ]
    back = [sds((slots, width), B16)] * 2
    wide += [sds((NZ, NX) + s.shape, B16) for s in shards[2:]]
    far = back + wide + [
        sds((width, hidden), B16),
        sds((hidden, width), B16),
        sds((CHUNK, width), B16),
    ]
    return pl.pallas_call(
        lead_kernel,
        out_shape=outs + far,
        in_specs=[VM] * 13 + [HB] * 6,
        out_specs=[VM] * len(outs) + [HB] * len(far),
        scratch_shapes=[
            vm((32, 128), F32),
            vm((n, 32, 128), F32),
            vm((n, tiles, 128), F32),
            vm((n, tiles, 128), F32),
            vm(wide[0].shape, B16),
            vm(wide[1].shape, B16),
            vm((slots, width), B16),
            vm((slots, width), B16),
            vm((slots, width), B16),
            vm((slots, width), B16),
            vm((slots, width), B16),
            vm((slots, width), B16),
            vm((slots, width), B16),
            vm((slots, width), B16),
            vm((width, hidden), B16),
            vm((hidden, width), B16),
            vm((width, hidden), B16),
            vm((hidden, width), B16),
            vm((slots, hidden), F32),
            vm((slots, width), F32),
            vm((width, slots), B16),
        ]
        + [vm((NZ * s.shape[0], s.shape[1] // 2), B16) for s in shards[2:]]
        + [vm((NZ * s.shape[0] // 2, s.shape[1] // 2), B16) for s in shards[2:]]
        + [
            dma((n,)),
            dma((n,)),
            dma((n,)),
            dma((n,)),
        ]
        + [dma((E,))] * 8
        + [dma((4,)), dma((2, hidden // CHUNK)), dma((2, 2)), dma((2,))]
        + Gather.semaphores(2)
        + Column.semaphores()
        + Column.semaphores()
        + Spread.semaphores()
        + Spread.semaphores(),
        compiler_params=params(1),
        name="front_and_expert",
    )(tok, cot, route, cond, ada, adab, qvb, outb, soutb, sinb, router, bin_r, bout_r, *shards, win, wout)


def add_into(target, source, lead):
    count = 1
    for n in lead:
        count *= n

    def body(i, carry):
        at = []
        rest = i
        for n in reversed(lead):
            at.append(lax.rem(rest, n))
            rest = lax.div(rest, n)
        at = tuple(reversed(at))
        target[at] = (target[at].astype(F32) + source(at).astype(F32)).astype(B16)
        return carry

    lax.fori_loop(0, count, body, 0)


def piece_specs(width, hidden):
    rows, tall = width // NZ // 4, hidden // NZ // 4
    qkv = 3 * width // 2
    left = (qkv // 128 + 1) // 2 * 128
    early = (
        (2, (True, 0, rows, 0, hidden // 4, True)),
        (3, (True, 0, tall // 2, 0, width // 2, False)),
        (2, (True, 0, rows, hidden // 4, hidden // 4, False)),
        (3, (True, tall // 2, tall // 2, 0, width // 2, True)),
    )
    late = (
        (0, (False, 0, rows, 0, left, True)),
        (0, (False, 0, rows, left, qkv - left, False)),
        (1, (False, 0, rows, 0, width // 2, False)),
    )
    return early, late


class FirstHop:
    def __init__(self, spec, half, ebuf, sems):
        self.z, self.x, self.y, self.c = coords()
        _, self.row, self.rows, self.col, self.width, self.y_first = spec
        self.half, self.ebuf, self.sems = half, ebuf, sems

    def inner(self, *lead):
        return lead + (slice(self.row, self.row + self.rows), slice(self.col, self.col + self.width))

    def copy(self):
        every = slice(None)
        if self.y_first:
            at, to = self.inner(every, every, 1 - self.y), dev(self.z, self.x, 1 - self.y, self.c)
        else:
            at, to = self.inner(every, 1 - self.x, every), dev(self.z, 1 - self.x, self.y, self.c)
        return remote(self.half.at[at], self.ebuf, self.sems.at[0], self.sems.at[1], to)

    def absorb(self):
        self.copy().wait_recv()
        if self.y_first:
            source = lambda i: self.half[self.inner(i[0], i[1], self.y)]
        else:
            source = lambda i: self.half[self.inner(i[0], self.x, i[1])]
        add_into(self.ebuf, source, (NZ, 2))


def middle_kernel(
    ret, retg, second_r, resid_r, att_r, cot, mod, sinb, bias, router, gates_r, place_r, mixed, outw,
    tok, normed, proj, lsum, condt, ebias, sin_h, sout_h, qkv_h, dwout, dwin,
    out_o, out_half, shares, qkv_half, tgrad_o, mine_o, e0, e1, e2, e3, came_o, came_w,
    sin, sout, dsin, dsout, sin_half, sout_half, qkv, shared, sgrad, mgrad, rgrad_s, mg2, pgrad, tile, dqkv, dout,
    hsem, gsem, msem, lsem, qsem, s0, s1, s2, s3,
):
    chunks = range(NZ)
    size = sin.shape[3] // NZ
    loads = []
    for f in chunks:
        cols = slice(f * size, (f + 1) * size)
        loads.append(
            (
                pltpu.make_async_copy(sin_h.at[:, :, :, cols], sin.at[:, :, :, cols], lsem.at[0, f]),
                pltpu.make_async_copy(sout_h.at[f], sout.at[f], lsem.at[1, f]),
            )
        )
        for load in loads[-1]:
            load.start()
    qkv_load = pltpu.make_async_copy(qkv_h, qkv, qsem.at[0])
    qkv_load.start()
    barrier = pltpu.get_barrier_semaphore()
    z, x, y, c = coords()
    mate = NZ - 1 - z
    for to in (dev(mate, x, y, c), dev(z, x, y, 1 - c), dev(z, x, 1 - y, c), dev(z, 1 - x, y, c)):
        greet(barrier, to)
    pl.semaphore_wait(barrier, 4)
    central = jnp.logical_and(z > 0, z < NZ - 1)

    def across():
        rows = dwout.shape[0] // 2
        start = pl.multiple_of(lax.div(mate, 2) * rows + CHUNK, 16)
        return remote(
            dwout.at[pl.ds(start, rows - CHUNK), :], came_o, msem.at[0], msem.at[1], dev(mate, x, y, c)
        )

    def across_wide():
        rows = dwin.shape[0] // 2
        start = pl.multiple_of(lax.div(mate, 2) * rows, 16)
        return remote(
            dwin.at[pl.ds(start, rows), 0 : came_w.shape[1]], came_w, msem.at[2], msem.at[3], dev(mate, x, y, c)
        )

    @pl.when(central)
    def _():
        across().start()
        across_wide().start()

    length, width = second_r.shape
    hidden = sin.shape[3]
    chunk = hidden // NZ
    second = second_r[...]
    grad_out = cot[...].astype(F32)
    moe_low = (mod[5:6] * grad_out).astype(B16)
    moe_grad = moe_low.astype(F32)
    shared[...] = jnp.zeros_like(shared) + bias[3:4, :]
    sgrad[...] = jnp.zeros_like(sgrad)
    shares[...] = jnp.zeros_like(shares)
    n = NZ * NX
    part = width // n
    own_tiles = hidden // n // 128

    def cut(at, rows):
        for p in range(n):
            shares[p, at : at + rows.shape[0], 0:part] = rows[:, part * p : part * (p + 1)]

    for p in range(n):
        shares[p, 16 : 16 + own_tiles, :] = ebias[own_tiles * p : own_tiles * (p + 1), :]
        at = hidden // 128 + p
        shares[p, 19:20, 0:part] = ebias[at : at + 1, 0:part]

    other_core = dev(z, x, y, 1 - c)

    def half_cols(size, core):
        return pl.ds(pl.multiple_of(core * size, 128), size)

    def sout_copy(f):
        cols = half_cols(width // 2, 1 - c)
        return remote(
            dsout.at[f, :, :, :, cols], sout_half.at[f], hsem.at[0, 1, f], hsem.at[1, 1, f], other_core
        )

    def sin_copy(f):
        at = f % (NZ // 2)
        return remote(
            dsin.at[:, :, :, :, f * chunk : (f + 1) * chunk],
            sin_half.at[:, :, :, :, at * chunk : (at + 1) * chunk],
            hsem.at[0, 0, at],
            hsem.at[1, 0, at],
            other_core,
        )

    def core_copy(i):
        whole, half = ((dqkv, qkv_half), (dout, out_half))[i]
        cols = half_cols(half.shape[4], 1 - c)
        return remote(whole.at[:, :, :, :, cols], half, gsem.at[0, i], gsem.at[1, i], other_core)

    def core_add(half, whole):
        own = half_cols(half.shape[4], c)
        add_into(half, lambda at: whole[at[0], at[1], at[2], :, own], (NZ, NX, 2))

    def body(f):
        for load in loads[f]:
            load.wait()
        cols = slice(f * chunk, (f + 1) * chunk)
        w1 = sin[:, :, :, cols].reshape(width, chunk)
        w2 = sout[f].reshape(chunk, width)
        act, slope = gelu_parts(dot(second, w1) + sinb[:, cols])
        low = act.astype(B16)
        shared[...] += dot(low, w2)
        pre = (dot_nt(moe_low, w2) * slope).astype(B16)
        dsout[f] = dot_tn(low, moe_low).astype(B16).reshape(dsout.shape[1:])
        dsin[:, :, :, :, cols] = dot_tn(second, pre).astype(B16).reshape(dsin.shape[:4] + (chunk,))
        sout_copy(f).start()
        pl.when(c == 1 - f // (NZ // 2))(lambda: sin_copy(f).start())
        sgrad[...] += dot_nt(pre, w1)
        col = jnp.sum(pre.astype(F32), axis=0, keepdims=True)
        for j in range(chunk // 128):
            at = f * (chunk // 128) + j
            shares[at // own_tiles, 4 + at % own_tiles : 5 + at % own_tiles, :] = col[
                :, 128 * j : 128 * (j + 1)
            ]

    for f in chunks:
        body(f)
    lane = lax.broadcasted_iota(jnp.int32, (length, E), 1)
    gates = [gates_r[:, k : k + 1] for k in range(2)]
    maps = [
        jnp.where(choose_rows(place_r[:, k : k + 1], E * CAP), 1.0, 0.0) for k in range(2)
    ]
    back = ret[...]
    rows = [dot(m.astype(B16), back) for m in maps]
    moe = shared[...] + (gates[0] * rows[0] + gates[1] * rows[1])
    for f in range(NZ // 2):
        sin_copy(f).wait_recv()
    for f in chunks:
        sout_copy(f).wait_recv()
    core_add(sin_half, dsin)
    core_add(sout_half, dsout)
    hops = [
        FirstHop(spec, sin_half if matrix == 2 else sout_half, ebuf, sem)
        for (matrix, spec), ebuf, sem in zip(
            piece_specs(width, hidden)[0], (e0, e1, e2, e3), (s0, s1, s2, s3)
        )
    ]
    for hop in hops:
        hop.copy().start()

    resid = resid_r[...]
    out_o[...] = (resid + mod[5:6] * moe).astype(B16)
    mg2[...] = jnp.zeros_like(mg2)
    mg2[5:6, :] = jnp.sum(grad_out * moe, axis=0, keepdims=True)
    ggrad = [jnp.sum(moe_grad * r, axis=-1, keepdims=True) for r in rows]
    inner = gates[0] * ggrad[0] + gates[1] * ggrad[1]
    lgrad = jnp.zeros((length, E), F32)
    for k in range(2):
        pick = place_r[:, 2 + k : 3 + k] == lane
        lgrad = lgrad + jnp.where(pick, gates[k] * (ggrad[k] - inner), 0.0)
    lgrad = lgrad.astype(B16)
    cut(8, dot_tn(lgrad, second))
    grad = (
        sgrad[...]
        + dot((maps[0] + maps[1]).astype(B16), retg[...])
        + dot(lgrad, router[...].astype(B16))
    )
    n2, r2 = norm_parts(resid)
    mg2[3:4, :] = jnp.sum(grad, axis=0, keepdims=True)
    mg2[4:5, :] = jnp.sum(grad * n2, axis=0, keepdims=True)
    rgrad = grad_out + norm_back(grad * (1.0 + mod[4:5]), n2, r2)
    rgrad_s[...] = rgrad
    agrad = (mod[2:3] * rgrad).astype(B16)
    mg2[2:3, :] = jnp.sum(rgrad * att_r[...], axis=0, keepdims=True)
    dout[...] = dot_tn(mixed[...], agrad).astype(B16).reshape(dout.shape)
    core_copy(1).start()
    mgrad[...] = dot_nt(agrad, outw[...]).astype(B16)
    cut(3, jnp.sum(moe_grad, axis=0, keepdims=True))
    cut(2, jnp.sum(agrad.astype(F32), axis=0, keepdims=True))
    low_lane = lax.broadcasted_iota(jnp.int32, (length, 128), 1) < HEAD_DIM
    for p in range(HEADS // 2):
        q2 = proj[:, 128 * p : 128 * (p + 1)]
        k2 = proj[:, width + 128 * p : width + 128 * (p + 1)]
        v2 = proj[:, 2 * width + 128 * p : 2 * width + 128 * (p + 1)]
        m2 = mgrad[:, 128 * p : 128 * (p + 1)]
        parts = []
        for h in range(2):
            head = low_lane if h == 0 else jnp.logical_not(low_lane)
            zero = jnp.zeros_like(q2)
            s = dot_nt(jnp.where(head, q2, zero), k2) * SCALE
            prob = jnp.exp(s - lsum[:, 2 * p + h : 2 * p + h + 1])
            pg = dot_nt(jnp.where(head, m2, zero), v2)
            inner = jnp.sum(prob * pg, axis=-1, keepdims=True)
            sg = (prob * (pg - inner)).astype(B16)
            parts.append(
                (dot(sg, k2) * SCALE, dot_tn(sg, q2) * SCALE, dot_tn(prob.astype(B16), m2))
            )
        for i in range(3):
            pgrad[:, i * width + 128 * p : i * width + 128 * (p + 1)] = jnp.where(
                low_lane, parts[0][i], parts[1][i]
            ).astype(B16)
    lead = dqkv.shape[:4]
    for i in range(3):
        cols = slice(i * width, (i + 1) * width)
        dqkv[:, :, :, :, cols] = dot_tn(normed[...], pgrad[:, cols]).astype(B16).reshape(lead + (width,))
    core_copy(0).start()
    qkv_load.wait()
    ngrad = dot_nt(pgrad[...], qkv[...])
    n1, r1 = norm_parts(tok[...].astype(F32))
    tgrad_o[...] = rgrad_s[...] + norm_back(ngrad * (1.0 + mod[1:2]), n1, r1)
    per = width // 128
    for i, k in enumerate((0, 2)):
        cut(i, jnp.sum(pgrad[:, k * width : (k + 1) * width].astype(F32), axis=0, keepdims=True))
    mod_rows = [
        jnp.sum(ngrad, axis=0, keepdims=True),
        jnp.sum(ngrad * n1, axis=0, keepdims=True),
    ] + [mg2[i : i + 1, :] for i in range(2, 6)]
    tile[...] = jnp.zeros_like(tile)
    for i, row in enumerate(mod_rows):
        row = row.astype(B16).astype(F32)
        for j in range(per):
            tile[i * per + j : i * per + j + 1, :] = row[:, 128 * j : 128 * (j + 1)]
    tile[40:48, :] = condt[...]
    mine_o[...] = tile[...].astype(B16)
    for i, (half, whole) in enumerate(((qkv_half, dqkv), (out_half, dout))):
        core_copy(i).wait_recv()
        core_add(half, whole)
        core_copy(i).wait_send()
    for f in chunks:
        sout_copy(f).wait_send()
        pl.when(c == 1 - f // (NZ // 2))(lambda: sin_copy(f).wait_send())
    for hop in hops:
        hop.absorb()
    for hop in hops:
        hop.copy().wait_send()

    @pl.when(central)
    def _():
        across().wait()
        across_wide().wait()


def middle(*args):
    second, sin = args[2], args[20]
    length, width = second.shape
    hidden = sin.shape[3]
    rows, tall = width // NZ // 4, hidden // NZ // 4
    dma = pltpu.SemaphoreType.DMA
    vm = pltpu.VMEM
    early = piece_specs(width, hidden)[0]
    return pl.pallas_call(
        middle_kernel,
        out_shape=[
            sds((length, width), B16),
            sds((NZ, NX, 2, rows, width // 2), B16),
            sds((NZ * NX, 24, 128), F32),
            sds((NZ, NX, 2, rows, 3 * width // 2), B16),
            sds((length, width), F32),
            sds((48, 128), B16),
        ]
        + [sds((NZ, 2, spec[2], spec[4]), B16) for _, spec in early]
        + [
            sds((hidden // 2 - CHUNK, width), B16),
            sds((width // 2, hidden // MidSum.COUNT), B16),
        ],
        in_specs=[VM] * 20 + [HB] * 5,
        out_specs=[VM] * 10 + [HB] * 2,
        scratch_shapes=[
            vm(sin.shape, B16),
            vm((NZ, NX, hidden // NZ // NX, width), B16),
            vm((NZ, NX, 2, rows, hidden), B16),
            vm((NZ, NX, 2, tall, width), B16),
            vm((NZ, NX, 2, rows, hidden // 2), B16),
            vm((NZ, NX, 2, tall, width // 2), B16),
            vm((width, 3 * width), B16),
            vm((length, width), F32),
            vm((length, width), F32),
            vm((length, width), B16),
            vm((length, width), F32),
            vm((8, width), F32),
            vm((length, 3 * width), B16),
            vm((48, 128), F32),
            vm((NZ, NX, 2, rows, 3 * width), B16),
            vm((NZ, NX, 2, rows, width), B16),
            dma((2, 2, NZ)),
            dma((2, 2)),
            dma((4,)),
            dma((2, NZ)),
            dma((1,)),
        ]
        + [dma((2,))] * 4,
        compiler_params=params(3),
        name="shared_expert_attention_back",
    )(*args)


class Piece:
    def __init__(self, spec, grad, out, bufs):
        self.z, self.x, self.y, self.c = coords()
        self.half, self.row, self.rows, self.col, self.width, self.y_first = spec
        self.grad, self.out = grad, out
        self.size = out.shape[-1] // 2
        if self.half:
            self.ebuf = grad
        else:
            self.ebuf, bufs = bufs[0], bufs[1:]
        self.fbuf, self.zin, self.one, self.zsem = bufs
        self.inner = jnp.logical_and(self.z > 0, self.z < NZ - 1)
        self.end = jnp.logical_not(self.inner)
        self.mate = NZ - 1 - self.z
        self.beside = self.z + 1 - 2 * lax.rem(self.z, 2)

    @staticmethod
    def scratch(spec):
        half, _, rows, _, width, _ = spec
        vm = lambda *lead: pltpu.VMEM(lead + (rows, width), B16)
        dma = pltpu.SemaphoreType.DMA
        return ([] if half else [vm(NZ, 2)]) + [
            vm(NZ),
            vm(NZ + 3),
            dma((13,)),
            dma((2, 3)),
        ]

    def cols(self, c):
        return pl.ds(pl.multiple_of(c * self.size + self.col, 128), self.width)

    def core(self, *lead):
        return lead + (slice(self.row, self.row + self.rows), slice(self.col, self.col + self.width))

    def to_x(self):
        return dev(self.z, 1 - self.x, self.y, self.c)

    def to_y(self):
        return dev(self.z, self.x, 1 - self.y, self.c)

    def copy1(self):
        every = slice(None)
        if self.y_first:
            source, to = self.grad.at[self.core(every, every, 1 - self.y)], self.to_y()
        else:
            source, to = self.grad.at[self.core(every, 1 - self.x, every)], self.to_x()
        return remote(source, self.ebuf, self.one.at[3], self.one.at[4], to)

    def copy2(self):
        if self.y_first:
            source, to = self.ebuf.at[:, 1 - self.x], self.to_x()
        else:
            source, to = self.ebuf.at[:, 1 - self.y], self.to_y()
        return remote(source, self.fbuf, self.one.at[5], self.one.at[6], to)

    def zcopy(self, step):
        if step == 0:
            at = pl.ds(jnp.where(lax.rem(self.z, NZ - 1) == 0, lax.rem(self.z + 1, NZ), 0), NZ - 1)
            source, target, to = self.fbuf.at[at], self.zin.at[at], self.beside
        elif step == 1:
            at = pl.ds(2 * lax.div(self.mate, 2), 2)
            source, target, to = self.fbuf.at[at], self.zin.at[NZ : NZ + 2], self.mate
        else:
            source, target, to = self.fbuf.at[self.beside], self.zin.at[NZ + 2], self.beside
        return remote(
            source, target, self.zsem.at[0, step], self.zsem.at[1, step], dev(to, self.x, self.y, self.c)
        )

    def plus(self, block, came):
        self.fbuf[block] = (self.fbuf[block].astype(F32) + self.zin[came].astype(F32)).astype(B16)

    def own(self):
        return self.fbuf.at[self.z]

    def place(self, y, c):
        return self.out.at[y, self.row : self.row + self.rows, self.cols(c)]

    def keep(self):
        return pltpu.make_async_copy(self.own(), self.place(self.y, self.c), self.one.at[7])

    def give_y(self, came=False):
        at = self.place(1 - self.y if came else self.y, self.c)
        return remote(self.own(), at, self.one.at[8], self.one.at[9], self.to_y())

    def give_c(self, came=False):
        at = self.place(self.y, 1 - self.c if came else self.c)
        to = dev(self.z, self.x, self.y, 1 - self.c)
        return remote(self.own(), at, self.one.at[10], self.one.at[11], to)

    def pass_c(self, came=False):
        at = self.place(1 - self.y, 1 - self.c if came else self.c)
        to = dev(self.z, self.x, self.y, 1 - self.c)
        return remote(at, at, self.one.at[12], self.one.at[2], to)

    def stage(self, s):
        if s == 0 and not self.half:
            self.copy1().start()
        elif s == 1:
            if not self.half:
                self.copy1().wait_recv()
                if self.y_first:
                    add_into(self.ebuf, lambda i: self.grad[self.core(i[0], i[1], self.y)], (NZ, NX))
                else:
                    add_into(self.ebuf, lambda i: self.grad[self.core(i[0], self.x, i[1])], (NZ, 2))
            self.copy2().start()
        elif s == 2:
            self.copy2().wait_recv()
            side = self.x if self.y_first else self.y
            add_into(self.fbuf, lambda i: self.ebuf[i[0], side], (NZ,))
            pl.when(self.end)(lambda: self.zcopy(0).start())
        elif s == 3:

            @pl.when(self.inner)
            def _():
                self.zcopy(0).wait_recv()
                first = lax.rem(self.z, 2)
                for i in range(NZ - 1):
                    self.plus(first + i, first + i)
                self.zcopy(1).start()

        elif s == 4:

            @pl.when(self.inner)
            def _():
                self.zcopy(1).wait_recv()
                for i in range(2):
                    self.plus(2 * lax.div(self.z, 2) + i, NZ + i)
                self.zcopy(2).start()

        elif s == 5:

            @pl.when(self.end)
            def _():
                self.zcopy(2).wait_recv()
                self.plus(self.z, NZ + 2)

            self.give_y().start()
            self.give_c().start()
            self.keep().start()
        elif s == 6:
            self.give_y(True).wait_recv()
            self.pass_c().start()
        elif s == 7:
            self.keep().wait()
            self.give_c(True).wait_recv()
            self.pass_c(True).wait_recv()
            if not self.half:
                self.copy1().wait_send()
            self.copy2().wait_send()
            self.give_y().wait_send()
            self.give_c().wait_send()
            self.pass_c().wait_send()
            pl.when(self.end)(lambda: self.zcopy(0).wait_send())

            @pl.when(self.inner)
            def _():
                self.zcopy(1).wait_send()
                self.zcopy(2).wait_send()


class MidSum:
    COUNT = 6

    def __init__(self, origin, grad, into, out, total, outer, sems):
        self.z, self.x, self.y, self.c = coords()
        self.origin = origin
        self.grad, self.into, self.out, self.total, self.outer = grad, into, out, total, outer
        self.sems = sems
        self.size = grad.shape[2] // self.COUNT
        self.inner = jnp.logical_and(self.z > 0, self.z < NZ - 1)
        self.end = jnp.logical_not(self.inner)
        self.mate = NZ - 1 - self.z

    @staticmethod
    def scratch(shape):
        vm = pltpu.VMEM
        return [vm(shape[1:], B16), vm(shape[1:], B16), pltpu.SemaphoreType.DMA((9, MidSum.COUNT))]

    def cols(self, p):
        return slice(p * self.size, (p + 1) * self.size)

    @staticmethod
    def beside(z):
        return z + 1 - 2 * lax.rem(z, 2)

    def landing(self, z, block):
        rows = self.grad.shape[1]
        return pl.ds(pl.multiple_of((block - 2 * lax.div(z, 2)) * rows, 16), rows)

    def across(self, i, p, came=False):
        z = self.z if came else self.mate
        block = self.beside(z) if i == 0 else z
        return remote(
            self.origin.at[block, :, self.cols(p)],
            self.into.at[self.landing(z, block), self.cols(p)],
            self.sems.at[i, p],
            self.sems.at[2 + i, p],
            dev(self.mate, self.x, self.y, self.c),
        )

    def came(self, block, p):
        return self.into[self.landing(self.z, block), self.cols(p)].astype(F32)

    def outward(self, p):
        return remote(
            self.outer.at[:, self.cols(p)],
            self.total.at[:, self.cols(p)],
            self.sems.at[4, p],
            self.sems.at[5, p],
            dev(self.beside(self.z), self.x, self.y, self.c),
        )

    def begin(self, i, p):
        pl.when(self.inner)(lambda: self.across(i, p).start())

    def give(self, p, sent=True):
        @pl.when(self.inner)
        def _():
            if sent:
                self.across(0, p, True).wait_recv()
            cols = self.cols(p)
            self.outer[:, cols] = (
                self.grad[self.beside(self.z), :, cols].astype(F32) + self.came(self.beside(self.z), p)
            ).astype(B16)
            self.outward(p).start()

    def swap(self, p, came=False):
        part = self.total.shape[0] // NX
        start = pl.multiple_of((1 - self.x) * part, 16)
        return remote(
            self.total.at[pl.ds(start, part), self.cols(p)],
            self.out.at[1 - self.x if came else self.x, :, self.cols(p)],
            self.sems.at[6, p],
            self.sems.at[7, p],
            dev(self.z, 1 - self.x, self.y, self.c),
        )

    def keep(self, p):
        part = self.total.shape[0] // NX
        start = pl.multiple_of(self.x * part, 16)
        return pltpu.make_async_copy(
            self.total.at[pl.ds(start, part), self.cols(p)],
            self.out.at[self.x, :, self.cols(p)],
            self.sems.at[8, p],
        )

    def final(self, p, sent=True):
        @pl.when(self.inner)
        def _():
            if sent:
                self.across(1, p, True).wait_recv()
            cols = self.cols(p)
            self.total[:, cols] = (
                self.grad[self.z, :, cols].astype(F32) + self.came(self.z, p)
            ).astype(B16)

        pl.when(self.end)(lambda: self.outward(p).wait_recv())
        self.swap(p).start()
        self.keep(p).start()

    def close(self, sent):
        for p in range(self.COUNT):

            @pl.when(self.inner)
            def _():
                self.outward(p).wait_send()
                if p in sent:
                    self.across(0, p).wait_send()
                    self.across(1, p).wait_send()

            self.swap(p, True).wait_recv()
            self.swap(p).wait_send()
            self.keep(p).wait()


def tail_kernel(*refs):
    ebufs, qkv_half, out_half = refs[:4], refs[4], refs[5]
    shares, mine, ada = refs[6:9]
    dwin_h, dwout_h, came_a, came_b, came_w = refs[9:14]
    outs = refs[14:18]
    pair_in, pair_out, small, esum, tiles, cgot = refs[18:24]
    rest = list(refs[24:])
    z, x, y, c = coords()
    dp, ex = lax.axis_index("dp"), lax.axis_index("expert")
    n = NZ * NX
    width = dwout_h.shape[2]
    early_specs, late_specs = piece_specs(width, dwin_h.shape[2])
    dwin, dwout, lsem = rest[:3]
    rest = rest[3:]

    def make(specs, rest, sources):
        made = []
        for (matrix, spec), source in zip(specs, sources):
            count = len(Piece.scratch(spec))
            made.append(Piece(spec, source, outs[matrix], rest[:count]))
            rest = rest[count:]
        return made, rest

    early, rest = make(early_specs, rest, ebufs)
    late, rest = make(late_specs, rest, (qkv_half, qkv_half, out_half))
    wide = MidSum(dwin_h, dwin, rest[0], pair_in, *rest[1:4])
    tall = MidSum(dwout_h, dwout, rest[4], pair_out, *rest[5:8])
    rest = rest[8:]
    first_rows = came_a.shape[0]
    loads = [
        pltpu.make_async_copy(came_a, tall.into.at[0:first_rows, :], lsem.at[0]),
        pltpu.make_async_copy(came_b, tall.into.at[first_rows:, :], lsem.at[1]),
        pltpu.make_async_copy(dwout_h, dwout, lsem.at[2]),
        pltpu.make_async_copy(dwin_h, dwin, lsem.at[3]),
        pltpu.make_async_copy(came_w, wide.into.at[:, 0 : came_w.shape[1]], lsem.at[4]),
    ]
    sgot, dall, floats, csend, dsem, tsem = rest

    barrier = pltpu.get_barrier_semaphore()

    def peers(action):
        for p in range(n):

            @pl.when(p != dp)
            def _():
                action(p)

    peers(lambda p: greet(barrier, (p, ex)))
    mates = (dev(z, x, 1 - y, c), dev(z, x, y, 1 - c), dev(z, x, 1 - y, 1 - c))
    for mate in mates:
        greet(barrier, mate)
    pl.semaphore_wait(barrier, n - 1 + 3)

    def share_copy(p, at):
        return remote(shares.at[p], sgot.at[at], dsem.at[4, p], dsem.at[5, at], (p, ex))

    def tile(p, at):
        return remote(mine, tiles.at[ex, at], dsem.at[0, p], dsem.at[1, at], (p, ex))

    def mate_rank(i):
        return 2 * (1 - y if i != 1 else y) + (1 - c if i != 0 else c)

    def spread(i, theirs=False):
        rows = tiles.at[mate_rank(i) if theirs else ex]
        return remote(rows, rows, tsem.at[0, i], tsem.at[1, i], mates[i])

    def total_copy(i, theirs=False):
        rows = dall.at[mate_rank(i) if theirs else ex]
        return remote(rows, rows, tsem.at[2, i], tsem.at[3, i], mates[i])

    def cond_copy(p, at):
        return remote(csend.at[p], cgot.at[at], dsem.at[2, p], dsem.at[3, at], (p, ex))

    peers(lambda p: share_copy(p, dp).start())
    peers(lambda p: tile(p, dp).start())

    every = range(MidSum.COUNT)
    for piece in early:
        piece.stage(1)
    for piece in late:
        piece.stage(0)
    for p in every[1:]:
        for i in range(2):
            wide.begin(i, p)
    for load in loads:
        load.start()
    sgot[dp] = shares[dp]
    tiles[ex, dp] = mine[...]

    def small1():
        peers(lambda p: share_copy(p, p).wait_recv())
        peers(lambda p: tile(p, p).wait_recv())
        total = sgot[0, 0:16, :]
        for p in range(1, n):
            total = total + sgot[p, 0:16, :]
        dall[ex] = total
        for i in range(NX):
            own = sgot[i, 16:24, :]
            for zb in range(1, NZ):
                own = own + sgot[NX * zb + i, 16:24, :]
            esum[i] = own
        for i in range(3):
            total_copy(i).start()
            spread(i).start()
        floats[...] = tiles[ex].astype(F32)
        acc = jnp.zeros((n, ada.shape[0]), F32)
        for j in range(ada.shape[1] // 128):
            acc = acc + dot_nt(floats[:, j, :].astype(B16), ada[:, 128 * j : 128 * (j + 1)])
        csend[...] = jnp.zeros_like(csend)
        csend[:, 0, 0 : ada.shape[0]] = acc
        peers(lambda p: cond_copy(p, dp).start())
        cgot[dp] = csend[dp]

    def small2():
        for i in range(3):
            total_copy(i, True).wait_recv()
            spread(i, True).wait_recv()
        total = dall[0]
        for i in range(1, 4):
            total = total + dall[i]
        small[...] = total
        peers(lambda p: cond_copy(p, p).wait_recv())
        for i in range(3):
            total_copy(i).wait_send()
            spread(i).wait_send()
        peers(lambda p: share_copy(p, p).wait_send())
        peers(lambda p: tile(p, p).wait_send())
        peers(lambda p: cond_copy(p, p).wait_send())

    def run(pieces, s):
        for piece in pieces:
            piece.stage(s)

    for load in loads[:3]:
        load.wait()
    for p in every:
        tall.give(p, False)
    for load in loads[3:]:
        load.wait()
    wide.give(0, False)
    small1()
    run(early, 2)
    for p in every[1:3]:
        wide.give(p)
    run(late, 1)
    run(early, 3)
    for p in every:
        tall.final(p, False)
    run(early, 4)
    for p in every[3:]:
        wide.give(p)
    run(late, 2)
    run(early, 5)
    wide.final(0, False)
    run(late, 3)
    for p in every[1:3]:
        wide.final(p)
    run(early, 6)
    run(late, 4)
    for p in every[3:]:
        wide.final(p)
    run(late, 5)
    run(early, 7)
    small2()
    run(late, 6)
    run(late, 7)
    tall.close(())
    wide.close(every[1:])


def tail_part(ebufs, qkv_half, out_half, shares, mine, ada, dwin, dwout, came_a, came_b, came_w):
    n = NZ * NX
    dma = pltpu.SemaphoreType.DMA
    vm = pltpu.VMEM
    width, hidden = dwout.shape[2], dwin.shape[2]
    rows, tall = width // NZ // 4, hidden // NZ // 4
    outs = [
        sds((2, rows, 3 * width), B16),
        sds((2, rows, width), B16),
        sds((2, rows, hidden), B16),
        sds((2, tall, width), B16),
    ]
    scratch = [vm(dwin.shape, B16), vm(dwout.shape, B16), dma((5,))]
    for specs in piece_specs(width, hidden):
        for _, spec in specs:
            scratch += Piece.scratch(spec)
    for shape in (dwin.shape, dwout.shape):
        scratch += [vm((2 * shape[1], shape[2]), B16)] + MidSum.scratch(shape)
    scratch += [
        vm(shares.shape, F32),
        vm((4, 16, 128), F32),
        vm((n, 48, 128), F32),
        vm((n, 8, 128), F32),
        dma((6, n)),
        dma((4, 3)),
    ]
    out = pl.pallas_call(
        tail_kernel,
        out_shape=outs
        + [
            sds((NX, dwin.shape[1] // NX, hidden), B16),
            sds((NX, dwout.shape[1] // NX, width), B16),
            sds((16, 128), F32),
            sds((NX, 8, 128), F32),
            sds((4, n, 48, 128), B16),
            sds((n, 8, 128), F32),
        ],
        in_specs=[VM] * 9 + [HB] * 5,
        out_specs=[HB] * 6 + [VM] * 4,
        scratch_shapes=scratch,
        compiler_params=params(4),
        name="device_sums",
    )(
        *ebufs,
        qkv_half,
        out_half,
        shares,
        mine,
        ada,
        dwin,
        dwout,
        came_a,
        came_b,
        came_w,
    )
    return [o.reshape(-1, o.shape[2]) for o in out[:4]], out[4:6], out[6:]


def pick_part(flat, part, dp):
    chosen = jnp.zeros((flat.shape[0], part), flat.dtype)
    for p in range(NZ * NX):
        chosen = jnp.where(dp == p, flat[:, p * part : (p + 1) * part], chosen)
    return chosen


def finish_kernel(*refs):
    large = refs[:6]
    small, esum, tiles, cgot, cond, out_r, tgrad_r = refs[6:13]
    outs = refs[13:19]
    ada_o, adab_o, qvb_o, outb_o, sinb_o, soutb_o, router_o, einb_o, eoutb_o, cond_o = refs[19:29]
    out_o, tgrad_o, floats = refs[29:32]
    out_o[...] = out_r[...]
    tgrad_o[...] = tgrad_r[...]
    dp = lax.axis_index("dp")
    n = NZ * NX
    for source, out in zip(large, outs):
        out[...] = source[...].astype(F32)
    width = cond.shape[1]
    per, part = width // 128, width // n
    hidden = sinb_o.shape[0] * n
    images = tiles.shape[0] * tiles.shape[1]
    floats[...] = tiles[...].astype(F32)
    qvb_o[...] = small[0:2, 0:part]
    outb_o[...] = small[2:3, 0:part]
    soutb_o[...] = small[3:4, 0:part]
    router_o[...] = small[8:16, 0:part]
    for j in range(hidden // n // 128):
        cols = slice(128 * j, 128 * (j + 1))
        sinb_o[cols] = small[4 + j : 5 + j, :].reshape(128)
        for i in range(NX):
            einb_o[i : i + 1, cols] = esum[i, j : j + 1, :]
    for i in range(NX):
        eoutb_o[i : i + 1, :] = esum[i, 3:4, 0:part]

    conds = jnp.concatenate(
        [floats[:, :, 40 + j, :].reshape(images, 128) for j in range(per)], axis=1
    )
    conds = pick_part(conds, part, dp).astype(B16)
    sums = []
    for j in range(6 * per):
        mods = floats[:, :, j, :].reshape(images, 128)
        ada_o[:, 128 * j : 128 * (j + 1)] = dot_tn(conds, mods.astype(B16))
        sums.append(jnp.sum(mods, axis=0, keepdims=True))
    adab_o[...] = pick_part(jnp.concatenate(sums, axis=1), adab_o.shape[0], dp)[0]
    v = cond[...].astype(F32)
    sig = 1.0 / (1.0 + jnp.exp(-v))
    grad = jnp.concatenate([cgot[p, 0:1, 0:part] for p in range(n)], axis=1)
    cond_o[...] = grad * (sig * (1.0 + v * (1.0 - sig)))


def finish(dense, pairs, small, esum, tiles, cgot, cond, output, tgrad, hidden):
    n = NZ * NX
    width = cond.shape[1]
    part = width // n
    big = [sds(v.shape, F32) for v in (*dense, *pairs)]
    short = [
        sds((part, 6 * width), F32),
        sds((6 * part,), F32),
        sds((2, part), F32),
        sds((1, part), F32),
        sds((hidden // n,), F32),
        sds((1, part), F32),
        sds((E, part), F32),
        sds((NX, hidden // n), F32),
        sds((NX, part), F32),
        sds((1, width), F32),
        sds(output.shape, output.dtype),
        sds(tgrad.shape, tgrad.dtype),
    ]
    return pl.pallas_call(
        finish_kernel,
        out_shape=big + short,
        in_specs=[VM] * 13,
        out_specs=[VM] * 18,
        scratch_shapes=[pltpu.VMEM(tiles.shape, F32)],
        compiler_params=params(),
        name="final_form",
    )(*dense, *pairs, small, esum, tiles, cgot, cond, output, tgrad)


def on_block(
    tokens, conditioning, routes, cotangent, ada_weight, ada_bias, qkv_weight, qv_bias, out_weight, out_bias,
    shared_in, shared_in_bias, shared_out, shared_out_bias, router,
    expert_in, expert_in_bias, expert_out, expert_out_bias,
):
    n = NZ * NX
    width = tokens.shape[2]
    hidden = shared_in.shape[1]
    part = width // n
    tok, cot, route = tokens[0], cotangent[0], routes[0]
    (
        normed, proj, lsum, mixed, att, resid, second, gates, place, mod, bias, sinb, router_t,
        condt, ebias, ret, retg, qkv_full, out_full, sin_full, sout_full, dwin, dwout, came_a,
    ) = lead_part(
        tok, cot, route.T, conditioning, ada_weight, ada_bias, qv_bias, out_bias[None], shared_out_bias[None],
        shared_in_bias, router.T, expert_in_bias, expert_out_bias,
        (qkv_weight, out_weight, shared_in, shared_out), expert_in, expert_out,
    )
    (output, out_half, shares, qkv_half, tgrad, mine, e0, e1, e2, e3, came_b, came_w) = middle(
        ret, retg, second, resid, att, cot, mod, sinb, bias, router_t, gates, place, mixed, out_full,
        tok, normed, proj, lsum, condt, ebias, sin_full, sout_full, qkv_full, dwout, dwin,
    )
    dense, pairs, (small, esum, tiles, cgot) = tail_part(
        (e0, e1, e2, e3), qkv_half, out_half, shares, mine, ada_weight,
        dwin.reshape(NZ, NX * part, hidden), dwout.reshape(NZ, hidden // NZ, width), came_a, came_b, came_w,
    )
    (
        qkv_grad, out_grad, sin_grad, sout_grad, dwin_sum, dwout_sum, ada_grad, adab_grad, qvb_grad, outb_grad,
        sinb_grad, soutb_grad, router_grad, ein_b, eout_b, cond_grad, output, tgrad,
    ) = finish(dense, pairs, small, esum, tiles, cgot, conditioning, output, tgrad, hidden)
    return (
        output[None],
        tgrad[None],
        cond_grad,
        ada_grad,
        adab_grad,
        qkv_grad,
        qvb_grad,
        out_grad,
        outb_grad[0],
        sin_grad,
        sinb_grad,
        sout_grad,
        soutb_grad[0],
        router_grad.T,
        dwin_sum,
        ein_b,
        dwout_sum,
        eout_b,
    )


def layer_norm(rows):
    centred = rows - jnp.mean(rows, axis=-1, keepdims=True)
    return centred * lax.rsqrt(jnp.mean(centred * centred, axis=-1, keepdims=True) + 1e-06)


def modulate(rows, shift, scale):
    return layer_norm(rows) * (1.0 + scale) + shift


def gelu_tanh(values_in):
    return jax.nn.gelu(values_in, approximate=True)


def on_device(
    tokens,
    conditioning,
    routes,
    cotangent,
    ada_weight,
    ada_bias,
    qkv_weight,
    qv_bias,
    out_weight,
    out_bias,
    shared_in,
    shared_in_bias,
    shared_out,
    shared_out_bias,
    router,
    expert_in,
    expert_in_bias,
    expert_out,
    expert_out_bias,
):
    f32 = jnp.float32
    b16 = jnp.bfloat16
    gathered_dense = (
        lax.all_gather(ada_weight, "dp", axis=0, tiled=True),
        lax.all_gather(ada_bias, "dp", axis=0, tiled=True),
        lax.all_gather(qkv_weight, "dp", axis=0, tiled=True),
        lax.all_gather(qv_bias, "dp", axis=1, tiled=True),
        lax.all_gather(out_weight, "dp", axis=0, tiled=True),
        lax.all_gather(out_bias, "dp", axis=0, tiled=True),
        lax.all_gather(shared_in, "dp", axis=0, tiled=True),
        lax.all_gather(shared_in_bias, "dp", axis=0, tiled=True),
        lax.all_gather(shared_out, "dp", axis=0, tiled=True),
        lax.all_gather(shared_out_bias, "dp", axis=0, tiled=True),
        lax.all_gather(router, "dp", axis=0, tiled=True),
    )
    (
        ada_full,
        ada_bias_full,
        qkv_full,
        qv_bias_full,
        out_full,
        out_bias_full,
        shared_in_full,
        shared_in_bias_full,
        shared_out_full,
        shared_out_bias_full,
        router_full,
    ) = gathered_dense
    image_count, length, width = tokens.shape
    row_count = image_count * length
    scaling = HEAD_DIM ** (-0.5)
    head_shape = (image_count, length, HEADS, HEAD_DIM)
    cond_float = conditioning.astype(f32)
    cond_act, silu_back = jax.vjp(jax.nn.silu, cond_float)
    cond_low = cond_act.astype(b16)
    modulation = jnp.dot(cond_low, ada_full, preferred_element_type=f32) + ada_bias_full.astype(f32)
    pieces = [modulation[:, None, index * width : (index + 1) * width] for index in range(6)]
    source = tokens.astype(f32)
    first_norm, first_back = jax.vjp(modulate, source, pieces[0], pieces[1])
    normed = first_norm.astype(b16)
    projected = jnp.einsum("isd,de->ise", normed, qkv_full, preferred_element_type=f32)
    query_heads = (
        (projected[..., :width] + qv_bias_full[0].astype(f32)).astype(b16).reshape(head_shape)
    )
    key_heads = projected[..., width : 2 * width].astype(b16).reshape(head_shape)
    value_heads = (
        (projected[..., 2 * width :] + qv_bias_full[1].astype(f32)).astype(b16).reshape(head_shape)
    )
    scores = (
        jnp.einsum("iqhc,ikhc->ihqk", query_heads, key_heads, preferred_element_type=f32) * scaling
    )
    peak_score = jnp.max(scores, axis=-1, keepdims=True)
    unscaled = jnp.exp(scores - peak_score)
    exp_total = jnp.sum(unscaled, axis=-1, keepdims=True)
    log_total = peak_score + jnp.log(exp_total)
    probs_low = (unscaled / exp_total).astype(b16)
    mixed = (
        jnp.einsum("ihqk,ikhc->iqhc", probs_low, value_heads, preferred_element_type=f32)
        .reshape(image_count, length, width)
        .astype(b16)
    )
    attended = jnp.einsum(
        "isd,de->ise", mixed, out_full, preferred_element_type=f32
    ) + out_bias_full.astype(f32)
    resid = source + pieces[2] * attended
    second_float, second_back = jax.vjp(modulate, resid, pieces[3], pieces[4])
    second = second_float.astype(b16)
    shared_pre = jnp.einsum(
        "isd,df->isf", second, shared_in_full, preferred_element_type=f32
    ) + shared_in_bias_full.astype(f32)
    shared_act, shared_gelu_back = jax.vjp(gelu_tanh, shared_pre)
    shared_low = shared_act.astype(b16)
    shared = jnp.einsum(
        "isf,fd->isd", shared_low, shared_out_full, preferred_element_type=f32
    ) + shared_out_bias_full.astype(f32)
    second_rows = second.reshape(row_count, width)
    logits = jnp.dot(second_rows, router_full, preferred_element_type=f32)
    route_flat = routes.reshape(-1)
    one_hot = (route_flat[:, None] == jnp.arange(E, dtype=jnp.int32)).astype(jnp.int32)
    slot_index = jnp.sum(
        (jnp.cumsum(one_hot, axis=0, dtype=jnp.int32) - one_hot) * one_hot, axis=1, dtype=jnp.int32
    )
    position = jnp.where(slot_index < CAP, route_flat * CAP + slot_index, E * CAP)
    pair_rows = jnp.repeat(second_rows, 2, axis=0)
    buffer = (
        jnp.zeros((E * CAP, width), b16)
        .at[position]
        .set(pair_rows, mode="drop")
        .reshape(E, CAP, width)
    )
    received = lax.all_to_all(buffer, "expert", split_axis=0, concat_axis=1, tiled=True)
    expert_pre = (
        jnp.einsum("erd,edf->erf", received, expert_in, preferred_element_type=f32)
        + expert_in_bias.astype(f32)[:, None, :]
    )
    expert_low = gelu_tanh(expert_pre).astype(b16)
    expert_result = (
        jnp.einsum("erf,efd->erd", expert_low, expert_out, preferred_element_type=f32)
        + expert_out_bias.astype(f32)[:, None, :]
    ).astype(b16)
    returned = lax.all_to_all(
        expert_result, "expert", split_axis=1, concat_axis=0, tiled=True
    ).reshape(E * CAP, width)
    gathered = (
        returned.at[position]
        .get(mode="fill", fill_value=0)
        .reshape(row_count, 2, width)
        .astype(f32)
    )
    pair_mask = one_hot.reshape(row_count, 2, E).astype(f32)
    chosen = jnp.sum(logits[:, None, :] * pair_mask, axis=-1)
    gates = jax.nn.softmax(chosen, axis=-1)
    moe = (shared.reshape(row_count, width) + jnp.sum(gates[..., None] * gathered, axis=1)).reshape(
        image_count, length, width
    )
    output = (resid + pieces[5] * moe).astype(b16)
    ada_back, qkv_back, out_back, shared_in_back, shared_out_back, router_back = (
        ada_full,
        qkv_full,
        out_full,
        shared_in_full,
        shared_out_full,
        router_full,
    )
    grad_out = cotangent.astype(f32)
    gate_two_grad = jnp.sum(grad_out * moe, axis=1, keepdims=True)
    moe_grad = (pieces[5] * grad_out).astype(b16)
    moe_rows_grad = moe_grad.reshape(row_count, width)
    moe_rows_float = moe_rows_grad.astype(f32)
    pair_grad = (
        (gates[..., None] * moe_rows_float[:, None, :]).astype(b16).reshape(2 * row_count, width)
    )
    gate_grad = jnp.sum(moe_rows_float[:, None, :] * gathered, axis=-1)
    chosen_grad = gates * (gate_grad - jnp.sum(gates * gate_grad, axis=-1, keepdims=True))
    logits_grad = jnp.sum(chosen_grad[..., None] * pair_mask, axis=1).astype(b16)
    grad_buffer = (
        jnp.zeros((E * CAP, width), b16)
        .at[position]
        .set(pair_grad, mode="drop")
        .reshape(E, CAP, width)
    )
    result_grad = lax.all_to_all(grad_buffer, "expert", split_axis=0, concat_axis=1, tiled=True)
    pre_again = (
        jnp.einsum("erd,edf->erf", received, expert_in, preferred_element_type=f32)
        + expert_in_bias.astype(f32)[:, None, :]
    )
    act_again, expert_gelu_back = jax.vjp(gelu_tanh, pre_again)
    low_again = act_again.astype(b16)
    expert_out_grad = jnp.einsum("erf,erd->efd", low_again, result_grad, preferred_element_type=f32)
    expert_out_bias_grad = jnp.sum(result_grad.astype(f32), axis=1)
    expert_act_grad = jnp.einsum(
        "erd,efd->erf", result_grad, expert_out, preferred_element_type=f32
    )
    pre_grad = expert_gelu_back(expert_act_grad)[0].astype(b16)
    expert_in_grad = jnp.einsum("erd,erf->edf", received, pre_grad, preferred_element_type=f32)
    expert_in_bias_grad = jnp.sum(pre_grad.astype(f32), axis=1)
    received_grad = jnp.einsum(
        "erf,edf->erd", pre_grad, expert_in, preferred_element_type=f32
    ).astype(b16)
    sent_grad = lax.all_to_all(
        received_grad, "expert", split_axis=1, concat_axis=0, tiled=True
    ).reshape(E * CAP, width)
    dispatch_rows_grad = jnp.sum(
        sent_grad.at[position]
        .get(mode="fill", fill_value=0)
        .reshape(row_count, 2, width)
        .astype(f32),
        axis=1,
    )
    shared_out_grad = jnp.einsum("isf,isd->fd", shared_low, moe_grad, preferred_element_type=f32)
    shared_out_bias_grad = jnp.sum(moe_rows_float, axis=0)
    shared_act_grad = jnp.einsum(
        "isd,fd->isf", moe_grad, shared_out_back, preferred_element_type=f32
    )
    shared_pre_grad = shared_gelu_back(shared_act_grad)[0].astype(b16)
    shared_in_grad = jnp.einsum("isd,isf->df", second, shared_pre_grad, preferred_element_type=f32)
    shared_in_bias_grad = jnp.sum(shared_pre_grad.astype(f32), axis=(0, 1))
    router_grad = jnp.einsum("rd,re->de", second_rows, logits_grad, preferred_element_type=f32)
    second_grad = jnp.einsum(
        "isf,df->isd", shared_pre_grad, shared_in_back, preferred_element_type=f32
    )
    side_grad = dispatch_rows_grad + jnp.einsum(
        "re,de->rd", logits_grad, router_back, preferred_element_type=f32
    )
    second_grad = second_grad + side_grad.reshape(image_count, length, width)
    resid_extra, shift_two_grad, scale_two_grad = second_back(second_grad)
    resid_grad = grad_out + resid_extra
    attended_grad = (pieces[2] * resid_grad).astype(b16)
    gate_one_grad = jnp.sum(resid_grad * attended, axis=1, keepdims=True)
    out_weight_grad = jnp.einsum("isd,ise->de", mixed, attended_grad, preferred_element_type=f32)
    out_bias_grad = jnp.sum(attended_grad.astype(f32), axis=(0, 1))
    mixed_grad = (
        jnp.einsum("ise,de->isd", attended_grad, out_back, preferred_element_type=f32)
        .astype(b16)
        .reshape(head_shape)
    )
    again_scores = (
        jnp.einsum("iqhc,ikhc->ihqk", query_heads, key_heads, preferred_element_type=f32) * scaling
    )
    probs_float = jnp.exp(again_scores - log_total)
    again_low = probs_float.astype(b16)
    probs_grad = jnp.einsum("iqhc,ikhc->ihqk", mixed_grad, value_heads, preferred_element_type=f32)
    values_grad = jnp.einsum(
        "ihqk,iqhc->ikhc", again_low, mixed_grad, preferred_element_type=f32
    ).astype(b16)
    scores_grad = (
        probs_float * (probs_grad - jnp.sum(probs_float * probs_grad, axis=-1, keepdims=True))
    ).astype(b16)
    query_grad = (
        jnp.einsum("ihqk,ikhc->iqhc", scores_grad, key_heads, preferred_element_type=f32) * scaling
    ).astype(b16)
    keys_grad = (
        jnp.einsum("ihqk,iqhc->ikhc", scores_grad, query_heads, preferred_element_type=f32)
        * scaling
    ).astype(b16)
    flat_shape = (image_count, length, width)
    projected_grad = jnp.concatenate(
        [
            query_grad.reshape(flat_shape),
            keys_grad.reshape(flat_shape),
            values_grad.reshape(flat_shape),
        ],
        axis=-1,
    )
    qkv_weight_grad = jnp.einsum("isd,ise->de", normed, projected_grad, preferred_element_type=f32)
    qv_bias_grad = jnp.stack(
        [
            jnp.sum(query_grad.astype(f32), axis=(0, 1)).reshape(width),
            jnp.sum(values_grad.astype(f32), axis=(0, 1)).reshape(width),
        ]
    )
    normed_grad = jnp.einsum("ise,de->isd", projected_grad, qkv_back, preferred_element_type=f32)
    token_extra, shift_one_grad, scale_one_grad = first_back(normed_grad)
    tokens_grad = resid_grad + token_extra
    modulation_grad = jnp.concatenate(
        [
            shift_one_grad,
            scale_one_grad,
            gate_one_grad,
            shift_two_grad,
            scale_two_grad,
            gate_two_grad,
        ],
        axis=-1,
    )[:, 0, :].astype(b16)
    ada_weight_grad = jnp.einsum("id,ie->de", cond_low, modulation_grad, preferred_element_type=f32)
    ada_bias_grad = jnp.sum(modulation_grad.astype(f32), axis=0)
    cond_act_grad = jnp.einsum("ie,de->id", modulation_grad, ada_back, preferred_element_type=f32)
    conditioning_grad = silu_back(cond_act_grad)[0]
    expert_sums = (
        lax.psum_scatter(
            expert_in_grad.astype(jnp.bfloat16), "dp", scatter_dimension=1, tiled=True
        ).astype(jnp.float32),
        lax.psum_scatter(
            expert_in_bias_grad.astype(jnp.bfloat16), "dp", scatter_dimension=1, tiled=True
        ).astype(jnp.float32),
        lax.psum_scatter(
            expert_out_grad.astype(jnp.bfloat16), "dp", scatter_dimension=1, tiled=True
        ).astype(jnp.float32),
        lax.psum_scatter(
            expert_out_bias_grad.astype(jnp.bfloat16), "dp", scatter_dimension=1, tiled=True
        ).astype(jnp.float32),
    )
    dense_parts = (
        lax.psum_scatter(
            ada_weight_grad.astype(jnp.bfloat16), "dp", scatter_dimension=0, tiled=True
        ).astype(jnp.float32),
        lax.psum_scatter(
            ada_bias_grad.astype(jnp.bfloat16), "dp", scatter_dimension=0, tiled=True
        ).astype(jnp.float32),
        lax.psum_scatter(
            qkv_weight_grad.astype(jnp.bfloat16), "dp", scatter_dimension=0, tiled=True
        ).astype(jnp.float32),
        lax.psum_scatter(
            qv_bias_grad.astype(jnp.bfloat16), "dp", scatter_dimension=1, tiled=True
        ).astype(jnp.float32),
        lax.psum_scatter(
            out_weight_grad.astype(jnp.bfloat16), "dp", scatter_dimension=0, tiled=True
        ).astype(jnp.float32),
        lax.psum_scatter(
            out_bias_grad.astype(jnp.bfloat16), "dp", scatter_dimension=0, tiled=True
        ).astype(jnp.float32),
        lax.psum_scatter(
            shared_in_grad.astype(jnp.bfloat16), "dp", scatter_dimension=0, tiled=True
        ).astype(jnp.float32),
        lax.psum_scatter(
            shared_in_bias_grad.astype(jnp.bfloat16), "dp", scatter_dimension=0, tiled=True
        ).astype(jnp.float32),
        lax.psum_scatter(
            shared_out_grad.astype(jnp.bfloat16), "dp", scatter_dimension=0, tiled=True
        ).astype(jnp.float32),
        lax.psum_scatter(
            shared_out_bias_grad.astype(jnp.bfloat16), "dp", scatter_dimension=0, tiled=True
        ).astype(jnp.float32),
        lax.psum_scatter(
            router_grad.astype(jnp.bfloat16), "dp", scatter_dimension=0, tiled=True
        ).astype(jnp.float32),
    )
    dense_sums = lax.psum(
        (
            dense_parts[0],
            dense_parts[1],
            dense_parts[2],
            dense_parts[3],
            dense_parts[4],
            dense_parts[5],
            dense_parts[6],
            dense_parts[7],
            dense_parts[8],
            dense_parts[9],
            dense_parts[10],
        ),
        "expert",
    )
    return (
        output,
        tokens_grad,
        conditioning_grad,
        dense_sums[0],
        dense_sums[1],
        dense_sums[2],
        dense_sums[3],
        dense_sums[4],
        dense_sums[5],
        dense_sums[6],
        dense_sums[7],
        dense_sums[8],
        dense_sums[9],
        dense_sums[10],
        expert_sums[0],
        expert_sums[1],
        expert_sums[2],
        expert_sums[3],
    )


def solution(mesh):
    in_specs = (
        P(("dp", "expert"), None, None),
        P(("dp", "expert"), None),
        P(("dp", "expert"), None, None),
        P(("dp", "expert"), None, None),
        P("dp", None),
        P("dp"),
        P("dp", None),
        P(None, "dp"),
        P("dp", None),
        P("dp"),
        P("dp", None),
        P("dp"),
        P("dp", None),
        P("dp"),
        P("dp", None),
        P("expert", None, None),
        P("expert", None),
        P("expert", None, None),
        P("expert", None),
    )
    out_specs = (
        P(("dp", "expert"), None, None),
        P(("dp", "expert"), None, None),
        P(("dp", "expert"), None),
        P("dp", None),
        P("dp"),
        P("dp", None),
        P(None, "dp"),
        P("dp", None),
        P("dp"),
        P("dp", None),
        P("dp"),
        P("dp", None),
        P("dp"),
        P("dp", None),
        P("expert", "dp", None),
        P("expert", "dp"),
        P("expert", "dp", None),
        P("expert", "dp"),
    )
    body = on_device
    if dict(mesh.shape) == {"dp": NZ * NX, "expert": 4}:
        body = on_block
    return jax.shard_map(
        body, mesh=mesh, in_specs=in_specs, out_specs=out_specs, check_vma=False
    )
```

```python
import functools

import jax
import jax.numpy as jnp
from jax import lax
from jax.experimental import pallas as pl
from jax.experimental.pallas import tpu as pltpu
from jax.sharding import PartitionSpec as P

HEADS = 12
HEAD_DIM = 64
E = 8
CAP = 80
MESH = pl.DeviceIdType.MESH
F32 = jnp.float32
B16 = jnp.bfloat16
VMEM_LIMIT = 60 * 1024 * 1024
SCALE = HEAD_DIM ** (-0.5)
GELU_C = 0.7978845608028654
NZ, NX = 4, 2


def coords():
    dp = lax.axis_index("dp")
    ex = lax.axis_index("expert")
    return lax.div(dp, NX), lax.rem(dp, NX), lax.div(ex, 2), lax.rem(ex, 2)


def dev(z, x, y, c):
    return (NX * z + x, 2 * y + c)


def dot(a, b):
    return jnp.dot(a, b, preferred_element_type=F32)


def dot_nt(a, b):
    return lax.dot_general(a, b, (((1,), (1,)), ((), ())), preferred_element_type=F32)


def dot_tn(a, b):
    return lax.dot_general(a, b, (((0,), (0,)), ((), ())), preferred_element_type=F32)


def gelu(v):
    return v * (0.5 + 0.5 * jnp.tanh(v * (GELU_C + GELU_C * 0.044715 * (v * v))))


def gelu_parts(v):
    v2 = v * v
    t = jnp.tanh(GELU_C * v * (1.0 + 0.044715 * v2))
    h = 0.5 * (1.0 + t)
    return v * h, h + 0.5 * v * (1.0 - t * t) * (GELU_C * (1.0 + 0.134145 * v2))


def norm_parts(v):
    centred = v - jnp.mean(v, axis=-1, keepdims=True)
    r = lax.rsqrt(jnp.mean(centred * centred, axis=-1, keepdims=True) + 1e-06)
    return centred * r, r


def norm_back(u, n, r):
    return r * (
        u - jnp.mean(u, axis=-1, keepdims=True) - n * jnp.mean(u * n, axis=-1, keepdims=True)
    )


def remote(src, dst, send, recv, to):
    return pltpu.make_async_remote_copy(
        src_ref=src,
        dst_ref=dst,
        send_sem=send,
        recv_sem=recv,
        device_id=to,
        device_id_type=MESH,
    )


def greet(barrier, to):
    pl.semaphore_signal(barrier, inc=1, device_id=to, device_id_type=MESH)


def params(collective_id=None):
    if collective_id is None:
        return pltpu.CompilerParams(vmem_limit_bytes=VMEM_LIMIT)
    return pltpu.CompilerParams(
        vmem_limit_bytes=VMEM_LIMIT, collective_id=collective_id, has_side_effects=True
    )


VM = pl.BlockSpec(memory_space=pltpu.VMEM)
HB = pl.BlockSpec(memory_space=pl.ANY)


def sds(shape, dtype):
    return jax.ShapeDtypeStruct(shape, dtype)


class Gather:
    def __init__(self, shards, fulls, splits, sems):
        self.z, self.x, self.y, self.c = coords()
        self.mats = list(zip(shards, fulls, splits))
        (self.zs, self.zr, self.xs, self.xr, self.ys, self.yr, self.cs, self.cr, self.loc) = sems

    @staticmethod
    def semaphores(count):
        dma = pltpu.SemaphoreType.DMA
        return [
            dma((count, 2, NZ)),
            dma((count, NZ)),
            dma((count, NZ)),
            dma((count, NZ)),
            dma((count, NZ, NX)),
            dma((count, NZ, NX)),
            dma((count, NZ, NX, 2)),
            dma((count, NZ, NX, 2)),
            dma((count,)),
        ]

    def region(self, m, zb, xb, yh, ch):
        shard, full, split = self.mats[m]
        rows, width = shard.shape[0], shard.shape[1] // 2
        start = (NX * zb + xb) * rows
        if split:
            rows = rows // 2
            start = start + yh * rows
        return full.at[
            pl.ds(pl.multiple_of(start, 16), rows), pl.ds(pl.multiple_of(ch * width, 128), width)
        ]

    def own(self, m):
        shard, full, split = self.mats[m]
        rows, width = shard.shape[0], shard.shape[1] // 2
        start = 0
        if split:
            rows = rows // 2
            start = self.y * rows
        return shard.at[
            pl.ds(pl.multiple_of(start, 16), rows),
            pl.ds(pl.multiple_of(self.c * width, 128), width),
        ]

    def zcopy(self, m, zb, side, mine=False):
        here = self.region(m, zb, self.x, self.y, self.c)
        step = 1 if side else -1
        return remote(
            self.own(m) if mine else here,
            here,
            self.zs.at[m, side, zb],
            self.zr.at[m, zb],
            dev(lax.rem(self.z + step + NZ, NZ), self.x, self.y, self.c),
        )

    def xcopy(self, m, zb, mine=False, xb=None):
        here = self.region(m, zb, self.x if xb is None else xb, self.y, self.c)
        return remote(
            self.own(m) if mine else here,
            here,
            self.xs.at[m, zb],
            self.xr.at[m, zb],
            dev(self.z, 1 - self.x, self.y, self.c),
        )

    def ycopy(self, m, zb, xb, yh=None):
        here = self.region(m, zb, xb, self.y if yh is None else yh, self.c)
        return remote(
            here,
            here,
            self.ys.at[m, zb, xb],
            self.yr.at[m, zb, xb],
            dev(self.z, self.x, 1 - self.y, self.c),
        )

    def ccopy(self, m, zb, xb, yh, ch=None):
        here = self.region(m, zb, xb, yh, self.c if ch is None else ch)
        slot = yh if self.mats[m][2] else 0
        return remote(
            here,
            here,
            self.cs.at[m, zb, xb, slot],
            self.cr.at[m, zb, xb, slot],
            dev(self.z, self.x, self.y, 1 - self.c),
        )

    def local(self, m):
        shard, full, _ = self.mats[m]
        rows = shard.shape[0]
        start = (NX * self.z + self.x) * rows
        return pltpu.make_async_copy(
            shard, full.at[pl.ds(pl.multiple_of(start, 16), rows), :], self.loc.at[m]
        )

    def blocks(self, step):
        if step == 0:
            return [(self.z, None, None)]
        return [
            (self.z - step, self.z - step >= 0, 1),
            (self.z + step, self.z + step < NZ, 0),
        ]

    def more(self, side):
        return self.z + 1 < NZ if side else self.z - 1 >= 0

    def begin(self, m):
        for side in (1, 0):

            @pl.when(self.more(side))
            def _():
                self.zcopy(m, self.z, side, True).start()

        self.xcopy(m, self.z, True).start()
        self.local(m).start()

    def spread(self, m, zb, xb):
        if self.mats[m][2]:
            self.ycopy(m, zb, xb).start()
        self.ccopy(m, zb, xb, self.y).start()

    def take_z(self, m, step):
        for zb, exists, side in self.blocks(step):

            @pl.when(exists)
            def _():
                self.zcopy(m, zb, side).wait_recv()
                if step < NZ - 1:

                    @pl.when(self.more(side))
                    def _():
                        self.zcopy(m, zb, side).start()

                self.xcopy(m, zb).start()
                self.spread(m, zb, self.x)

    def take_x(self, m, step):
        for zb, exists, _ in self.blocks(step):

            def body():
                self.xcopy(m, zb, False, 1 - self.x).wait_recv()
                self.spread(m, zb, 1 - self.x)

            body() if exists is None else pl.when(exists)(body)

    def others(self, m, step, action):
        for zb, exists, _ in self.blocks(step):
            for xb in (self.x, 1 - self.x) if step else (1 - self.x,):
                body = functools.partial(action, m, zb, xb)
                body() if exists is None else pl.when(exists)(body)

    def take_y(self, m, step):
        if not self.mats[m][2]:
            return

        def action(m, zb, xb):
            self.ycopy(m, zb, xb, 1 - self.y).wait_recv()
            self.ccopy(m, zb, xb, 1 - self.y).start()

        self.others(m, step, action)

    def finish(self, m):
        def action(m, zb, xb):
            for yh in (self.y, 1 - self.y) if self.mats[m][2] else (self.y,):
                self.ccopy(m, zb, xb, yh, 1 - self.c).wait_recv()
                self.ccopy(m, zb, xb, yh).wait_send()
            if self.mats[m][2]:
                self.ycopy(m, zb, xb).wait_send()

        for step in range(NZ):
            self.others(m, step, action)
        for side in (1, 0):

            @pl.when(self.more(side))
            def _():
                self.zcopy(m, self.z, side, True).wait_send()

        for step in range(1, NZ):
            for zb, exists, side in self.blocks(step):

                @pl.when(exists)
                def _():
                    self.xcopy(m, zb).wait_send()
                    if step < NZ - 1:

                        @pl.when(self.more(side))
                        def _():
                            self.zcopy(m, zb, side).wait_send()

        self.xcopy(m, self.z, True).wait_send()
        self.local(m).wait()


class Column:
    def __init__(self, shard, column, other, send, recv, local, xsend, xrecv):
        self.z, self.x, self.y, self.c = coords()
        self.shard, self.column, self.other = shard, column, other
        self.send, self.recv, self.local, self.xsend, self.xrecv = send, recv, local, xsend, xrecv

    @staticmethod
    def semaphores():
        dma = pltpu.SemaphoreType.DMA
        return [dma((2, NZ)), dma((NZ,)), dma((1,)), dma((NZ,)), dma((NZ,))]

    def block(self, zb):
        rows = self.shard.shape[0]
        return self.column.at[pl.ds(pl.multiple_of(zb * rows, 16), rows), :]

    def own(self):
        width = self.shard.shape[1] // 2
        return self.shard.at[:, pl.ds(pl.multiple_of(self.c * width, 128), width)]

    def copy(self, zb, side, mine=False):
        here = self.block(zb)
        to = lax.rem(self.z + (1 if side else NZ - 1), NZ)
        return remote(
            self.own() if mine else here,
            here,
            self.send.at[side, zb],
            self.recv.at[zb],
            dev(to, self.x, self.y, self.c),
        )

    def xcopy(self, zb, mine=False):
        rows, width = self.shard.shape[0], self.shard.shape[1] // 2
        part = rows // 2
        start = pl.multiple_of(self.y * part, 16)
        if mine:
            source = self.shard.at[
                pl.ds(start, part), pl.ds(pl.multiple_of(self.c * width, 128), width)
            ]
        else:
            source = self.column.at[pl.ds(pl.multiple_of(zb * rows + start, 16), part), :]
        return remote(
            source,
            self.other.at[pl.ds(pl.multiple_of(zb * part, 16), part), :],
            self.xsend.at[zb],
            self.xrecv.at[zb],
            dev(self.z, 1 - self.x, self.y, self.c),
        )

    def keep(self):
        return pltpu.make_async_copy(self.own(), self.block(self.z), self.local.at[0])

    def more(self, side):
        return self.z + 1 < NZ if side else self.z - 1 >= 0

    def blocks(self, step):
        return [(self.z - step, self.z - step >= 0, 1), (self.z + step, self.z + step < NZ, 0)]

    def begin(self):
        for side in (1, 0):

            @pl.when(self.more(side))
            def _():
                self.copy(self.z, side, True).start()

        self.keep().start()
        self.xcopy(self.z, True).start()

    def take(self, step):
        for zb, exists, side in self.blocks(step):

            @pl.when(exists)
            def _():
                self.copy(zb, side).wait_recv()
                if step < NZ - 1:

                    @pl.when(self.more(side))
                    def _():
                        self.copy(zb, side).start()

    def push(self, step):
        for zb, exists, _ in self.blocks(step):

            @pl.when(exists)
            def _():
                self.xcopy(zb).start()

    def finish(self):
        for side in (1, 0):

            @pl.when(self.more(side))
            def _():
                self.copy(self.z, side, True).wait_send()

        for step in range(1, NZ - 1):
            for zb, exists, side in self.blocks(step):

                @pl.when(jnp.logical_and(exists, self.more(side)))
                def _():
                    self.copy(zb, side).wait_send()

        for zb in range(NZ):
            self.xcopy(zb).wait_send()


class Spread:
    def __init__(self, column, other, full, ys, yr, cs, cr, local):
        self.z, self.x, self.y, self.c = coords()
        self.column, self.other, self.full, self.local = column, other, full, local
        self.ys, self.yr, self.cs, self.cr = ys, yr, cs, cr

    @staticmethod
    def semaphores():
        dma = pltpu.SemaphoreType.DMA
        return [dma((NZ,))] * 2 + [dma((3, NZ))] * 2 + [dma((2, NZ))]

    def cols(self, c):
        width = self.full.shape[3] // 2
        return pl.ds(pl.multiple_of(c * width, 128), width)

    def half(self, y):
        rows = self.full.shape[2] // 2
        return pl.ds(pl.multiple_of(y * rows, 16), rows)

    def source(self, kind, zb):
        rows = self.full.shape[2] // (1 if kind == 0 else 2)
        ref = self.column if kind == 0 else self.other
        return ref.at[pl.ds(pl.multiple_of(zb * rows, 16), rows), :]

    def place(self, kind, zb, c):
        if kind == 0:
            return self.full.at[zb, self.x, :, self.cols(c)]
        return self.full.at[zb, 1 - self.x, self.half(self.y if kind == 1 else 1 - self.y), self.cols(c)]

    def ycopy(self, zb, came=False):
        return remote(
            self.source(1, zb), self.place(2 if came else 1, zb, self.c), self.ys.at[zb], self.yr.at[zb],
            dev(self.z, self.x, 1 - self.y, self.c),
        )

    def ccopy(self, kind, zb, came=False):
        at = self.place(kind, zb, 1 - self.c if came else self.c)
        return remote(
            at if kind == 2 else self.source(kind, zb), at, self.cs.at[kind, zb], self.cr.at[kind, zb],
            dev(self.z, self.x, self.y, 1 - self.c),
        )

    def keep(self, kind, zb):
        return pltpu.make_async_copy(
            self.source(kind, zb), self.place(kind, zb, self.c), self.local.at[kind, zb]
        )

    def near(self):
        for zb in range(NZ):
            self.ccopy(0, zb).start()
            self.keep(0, zb).start()

    def pass_x(self, zb):
        self.ycopy(zb).start()
        self.ccopy(1, zb).start()
        self.keep(1, zb).start()

    def pass_y(self, zb):
        self.ycopy(zb, True).wait_recv()
        self.ccopy(2, zb).start()

    def finish(self):
        for zb in range(NZ):
            for kind in range(3):
                self.ccopy(kind, zb, True).wait_recv()
                self.ccopy(kind, zb).wait_send()
            for kind in range(2):
                self.keep(kind, zb).wait()
            self.ycopy(zb).wait_send()


def choose_rows(place, slots):
    return place == lax.broadcasted_iota(jnp.int32, (place.shape[0], slots), 1)


def plane_peer(k):
    z, x, y, c = coords()
    xt = 1 - x if k & 1 else x
    ct = 1 - c if k & 2 else c
    yt = 1 - y if k & 4 else y
    return dev(z, xt, yt, ct), 4 * yt + 2 * ct + xt


def plane_rank():
    _, x, y, c = coords()
    return 4 * y + 2 * c + x


def slot_rows(ref, rank):
    return ref.at[pl.ds(pl.multiple_of(rank * CAP, 16), CAP), :]


class PlaneExchange:
    ORDER = (7, 5, 6, 4, 3, 1, 2)

    def __init__(self, source, target, send, recv):
        self.source, self.target, self.send, self.recv = source, target, send, recv

    def copy(self, k, into=None):
        peer, other = plane_peer(k)
        return remote(
            slot_rows(self.source, other),
            slot_rows(self.target, plane_rank() if into is None else other),
            self.send.at[k],
            self.recv.at[k],
            peer,
        )

    def mine(self):
        rank = plane_rank()
        return pltpu.make_async_copy(
            slot_rows(self.source, rank), slot_rows(self.target, rank), self.send.at[0]
        )

    def start(self):
        for k in self.ORDER:
            self.copy(k).start()
        self.mine().start()

    def wait_in(self):
        self.mine().wait()
        for k in self.ORDER:
            self.copy(k, True).wait_recv()

    def wait_out(self):
        for k in self.ORDER:
            self.copy(k).wait_send()


CHUNK = 512


def lead_kernel(
    tok, cot, routes, cond, ada, adab, qvb, outb, soutb, sinb_s, router_s, bin_r, bout_r,
    qkv_s, out_s, sin_s, sout_s, win_h, wout_h,
    normed_o, proj_o, lsum_o, mixed_o, att_o, resid_o, second_o, gates_o, place_o, mod_o, bias_o, sinb_o, rt_o,
    condt_o, ebias, ret_o, retg_o, qkv_o, outw_o, sin_o, sout_o, dwin_o, dwout_o, came_o,
    pack, packs, sent, got, qkv, outw, sbuf, gbuf, res, bgr, rows, grads, far_rows, far_grads, win, wout, dwin, dwout,
    pres, acc, turned, sin_c, sout_c, sin_x, sout_x,
    s1, r1, s2, r2, ds0, dr0, ds1, dr1, ds2, dr2, ds3, dr3, wsem, osem, fsem, msem, *gsems,
):
    z, x, y, c = coords()
    dp, ex = lax.axis_index("dp"), lax.axis_index("expert")
    n = NZ * NX
    length, width = tok.shape
    hidden = win.shape[1]
    part = width // n
    per = width // 128
    count = len(Column.semaphores())
    lead = Gather((qkv_s, out_s), (qkv, outw), (True, False), gsems[: len(Gather.semaphores(2))])
    gsems = gsems[len(Gather.semaphores(2)) :]
    later = (
        Column(sin_s, sin_c, sin_x, *gsems[:count]),
        Column(sout_s, sout_c, sout_x, *gsems[count : 2 * count]),
    )
    gsems = gsems[2 * count :]
    count = len(Spread.semaphores())
    spreads = (
        Spread(sin_c, sin_x, sin_o, *gsems[:count]),
        Spread(sout_c, sout_x, sout_o, *gsems[count:]),
    )

    def per_block(step, action):
        for zb, exists in [(z, None)] if step == 0 else [v[:2] for v in later[0].blocks(step)]:
            body = functools.partial(action, zb)
            body() if exists is None else pl.when(exists)(body)

    def pass_x(step):
        def action(zb):
            for column, spread in zip(later, spreads):
                column.xcopy(zb).wait_recv()
                spread.pass_x(zb)

        per_block(step, action)

    def pass_y(step):
        def action(zb):
            for spread in spreads:
                spread.pass_y(zb)

        per_block(step, action)

    loads = [
        pltpu.make_async_copy(win_h.at[x], win, wsem.at[0]),
        pltpu.make_async_copy(wout_h.at[x], wout, wsem.at[1]),
    ]

    def peers(action):
        for p in range(n):

            @pl.when(p != dp)
            def _():
                action(p)

    barrier = pltpu.get_barrier_semaphore()
    peers(lambda p: greet(barrier, (p, ex)))
    for k in range(2, E):
        greet(barrier, plane_peer(k)[0])

    pack[...] = jnp.zeros_like(pack)
    pack[0:2, 0:part] = qvb[...].astype(F32)
    pack[2:3, 0:part] = outb[...].astype(F32)
    pack[3:4, 0:part] = soutb[...].astype(F32)
    for j in range(hidden // n // 128):
        pack[4 + j : 5 + j, :] = sinb_s[128 * j : 128 * (j + 1)].astype(F32).reshape(1, 128)
    long = adab.shape[0]
    for j in range(-(-long // 128)):
        size = min(128, long - 128 * j)
        pack[8 + j : 9 + j, 0:size] = adab[128 * j : 128 * j + size].astype(F32).reshape(1, size)
    pack[16:24, 0:part] = router_s[...].astype(F32)
    cv = cond[...].astype(F32)
    cond_low = (cv / (1.0 + jnp.exp(-cv))).astype(B16).astype(F32)
    for p in range(n):
        pack[24 + p : 25 + p, 0:part] = cond_low[:, part * p : part * (p + 1)]
    condt_o[...] = jnp.zeros_like(condt_o)
    for j in range(per):
        condt_o[j : j + 1, :] = cond_low[:, 128 * j : 128 * (j + 1)]

    pl.semaphore_wait(barrier, n - 1 + E - 2)

    def first(p, at):
        return remote(pack, packs.at[at], s1.at[p], r1.at[at], (p, ex))

    def second_hop(p, at):
        return remote(sent.at[p], got.at[at], s2.at[p], r2.at[at], (p, ex))

    peers(lambda p: first(p, dp).start())
    lead.begin(0)
    lead.begin(1)
    for load in loads:
        load.start()
    packs[dp] = pack[...]
    peers(lambda p: first(p, p).wait_recv())
    cond_rows = jnp.concatenate([packs[p, pl.ds(24 + dp, 1), :] for p in range(n)], axis=0)
    partial = dot(cond_rows[:, :part].astype(B16), ada[...])
    for j in range(partial.shape[1] // 128):
        sent[:, j, :] = partial[:, 128 * j : 128 * (j + 1)]
    peers(lambda p: second_hop(p, dp).start())
    got[dp] = sent[dp]

    both_mats = (0, 1)

    def step_of(plan, step):
        for m in both_mats:
            if step:
                plan.take_z(m, step)
            plan.take_x(m, step)
        if step:
            for m in both_mats:
                plan.take_y(m, step - 1)

    for step in range(NZ):
        step_of(lead, step)

    for column in later:
        column.begin()

    bias_o[...] = jnp.zeros_like(bias_o)
    for p in range(n):
        bias_o[0:4, part * p : part * (p + 1)] = packs[p, 0:4, 0:part]
        rt_o[:, part * p : part * (p + 1)] = packs[p, 16:24, 0:part]
        for j in range(hidden // n // 128):
            at = hidden // n * p + 128 * j
            sinb_o[:, at : at + 128] = packs[p, 4 + j : 5 + j, :]
    peers(lambda p: second_hop(p, p).wait_recv())
    total = got[0]
    for p in range(1, n):
        total = total + got[p]
    mod_o[...] = jnp.zeros_like(mod_o)
    for i in range(6):
        for b in range(per):
            mod_o[i : i + 1, 128 * b : 128 * (b + 1)] = total[per * i + b : per * i + b + 1, :]
    unit = 64
    for p in range(n):
        for u in range(long // unit):
            at = long * p + unit * u
            i, b = at // width, at % width
            mod_o[i : i + 1, b : b + unit] += packs[
                p, 8 + unit * u // 128 : 9 + unit * u // 128, unit * u % 128 : unit * u % 128 + unit
            ]

    mod = mod_o[...]
    source = tok[...].astype(F32)
    n1, _ = norm_parts(source)
    normed = (n1 * (1.0 + mod[1:2]) + mod[0:1]).astype(B16)
    normed_o[...] = normed
    for m in both_mats:
        lead.take_y(m, NZ - 1)
    for m in both_mats:
        lead.finish(m)
    keep = [
        pltpu.make_async_copy(qkv, qkv_o, wsem.at[2]),
        pltpu.make_async_copy(outw, outw_o, wsem.at[3]),
    ]
    for copy in keep:
        copy.start()

    for k in range(3):
        part_k = dot(normed, qkv[:, k * width : (k + 1) * width])
        if k != 1:
            part_k = part_k + bias_o[k // 2 : k // 2 + 1, :]
        proj_o[:, k * width : (k + 1) * width] = part_k.astype(B16)
    lane = lax.broadcasted_iota(jnp.int32, (length, 128), 1)
    low_lane = lane < HEAD_DIM
    lsum = jnp.zeros((length, 128), F32)
    for p in range(HEADS // 2):
        q2 = proj_o[:, 128 * p : 128 * (p + 1)]
        k2 = proj_o[:, width + 128 * p : width + 128 * (p + 1)]
        v2 = proj_o[:, 2 * width + 128 * p : 2 * width + 128 * (p + 1)]
        outs = []
        for h in range(2):
            mine = low_lane if h == 0 else jnp.logical_not(low_lane)
            s = dot_nt(jnp.where(mine, q2, jnp.zeros_like(q2)), k2) * SCALE
            peak = jnp.max(s, axis=-1, keepdims=True)
            e = jnp.exp(s - peak)
            tot = jnp.sum(e, axis=-1, keepdims=True)
            lsum = jnp.where(lane == 2 * p + h, peak + jnp.log(tot), lsum)
            outs.append(dot((e / tot).astype(B16), v2))
        mixed_o[:, 128 * p : 128 * (p + 1)] = jnp.where(low_lane, outs[0], outs[1]).astype(B16)
    lsum_o[...] = lsum
    att = dot(mixed_o[...], outw[...]) + bias_o[2:3, :]
    att_o[...] = att
    resid = source + mod[2:3] * att
    resid_o[...] = resid
    n2, _ = norm_parts(resid)
    second = (n2 * (1.0 + mod[4:5]) + mod[3:4]).astype(B16)
    second_o[...] = second

    lane8 = lax.broadcasted_iota(jnp.int32, (length, E), 1)
    two = (
        lax.broadcasted_iota(jnp.int32, (2, 128), 0) == lax.broadcasted_iota(jnp.int32, (2, 128), 1)
    )
    route_cols = dot_tn(
        routes[...].astype(F32).astype(B16), jnp.where(two, 1.0, 0.0).astype(B16)
    ).astype(jnp.int32)
    route = [route_cols[:, k : k + 1] for k in range(2)]
    picks = [(r == lane8) for r in route]
    both = jnp.where(picks[0], 1.0, 0.0) + jnp.where(picks[1], 1.0, 0.0)
    earlier = (
        lax.broadcasted_iota(jnp.int32, (length, length), 1)
        < lax.broadcasted_iota(jnp.int32, (length, length), 0)
    )
    rank = dot(jnp.where(earlier, 1.0, 0.0).astype(B16), both.astype(B16))
    places = []
    for k in range(2):
        slot = jnp.sum(jnp.where(picks[k], rank, 0.0), axis=-1, keepdims=True).astype(jnp.int32)
        places.append(jnp.where(slot < CAP, route[k] * CAP + slot, -1))
    place_o[...] = jnp.where(
        lane == 0,
        places[0],
        jnp.where(lane == 1, places[1], jnp.where(lane == 2, route[0], route[1])),
    )
    maps = [jnp.where(choose_rows(v, E * CAP), 1.0, 0.0) for v in places]
    sbuf[...] = dot_tn((maps[0] + maps[1]).astype(B16), second).astype(B16)
    give_rows = PlaneExchange(sbuf, rows, ds0, dr0)
    give_rows.start()
    logits = dot_nt(second, rt_o[...].astype(B16))
    chosen = [jnp.sum(jnp.where(pick, logits, 0.0), axis=-1, keepdims=True) for pick in picks]
    top = jnp.maximum(chosen[0], chosen[1])
    e2 = [jnp.exp(v - top) for v in chosen]
    gates = [v / (e2[0] + e2[1]) for v in e2]
    gates_o[...] = jnp.where(lane == 0, gates[0], jnp.where(lane == 1, gates[1], 0.0))
    moe_grad = (mod[5:6] * cot[...].astype(F32)).astype(B16).astype(F32)
    pair = [(g * moe_grad).astype(B16) for g in gates]
    gbuf[...] = (
        dot_tn(maps[0].astype(B16), pair[0]) + dot_tn(maps[1].astype(B16), pair[1])
    ).astype(B16)
    give_grads = PlaneExchange(gbuf, grads, ds1, dr1)
    give_grads.start()
    for column in later:
        column.take(1)

    first_x = x == 0
    acc[...] = jnp.zeros_like(acc) + jnp.where(first_x, bout_r[0:1, :], bout_r[1:2, :]).astype(F32)
    for load in loads:
        load.wait()
    for column in later:
        column.take(2)
    give_rows.wait_in()

    end = jnp.logical_or(z == 0, z == NZ - 1)
    inner = jnp.logical_not(end)
    partner = dev(z + 1 - 2 * lax.rem(z, 2), x, y, c)

    def far_copy(i):
        source, target = ((rows, far_rows), (grads, far_grads))[i]
        return remote(source, target, fsem.at[0, i], fsem.at[1, i], partner)

    pl.when(end)(lambda: far_copy(0).start())
    for column in later:
        column.push(1)

    def span(f):
        return pl.ds(pl.multiple_of(f * CHUNK, 128), CHUNK)

    def put_in(f):
        return pltpu.make_async_copy(dwin.at[:, span(f)], dwin_o.at[:, span(f)], osem.at[1, f])

    def put_out(f):
        return pltpu.make_async_copy(dwout.at[span(f), :], dwout_o.at[span(f), :], osem.at[0, f])

    def bias_of(cols):
        return jnp.where(first_x, bin_r[0:1, cols], bin_r[1:2, cols]).astype(F32)

    def forward(f, carry):
        cols = span(f)
        pre = dot(rows[...], win[:, cols]) + bias_of(cols)
        pres[:, cols] = pre
        low = gelu(pre).astype(B16)
        acc[...] += dot(low, wout[cols, :])
        return carry

    count = hidden // CHUNK
    lax.fori_loop(0, count, forward, 0)
    res[...] = acc[...].astype(B16)
    give_res = PlaneExchange(res, ret_o, ds2, dr2)
    give_res.start()
    for column in later:
        column.push(2)
        column.take(3)
        column.push(3)
    for column, spread in zip(later, spreads):
        column.keep().wait()
        spread.near()
    pass_x(0)
    pass_x(1)
    give_grads.wait_in()
    pl.when(end)(lambda: far_copy(1).start())
    acc[...] = jnp.zeros_like(acc)
    ebias[...] = jnp.zeros_like(ebias)
    column_sum = jnp.sum(grads[...].astype(F32), axis=0, keepdims=True)
    for p in range(n):
        at = hidden // 128 + p
        ebias[at : at + 1, 0:part] = column_sum[:, part * p : part * (p + 1)]

    def backward(f, carry):
        cols = span(f)
        act, slope = gelu_parts(pres[:, cols])
        pre = (dot_nt(grads[...], wout[cols, :]) * slope).astype(B16)
        acc[...] += dot_nt(pre, win[:, cols])
        col = jnp.sum(pre.astype(F32), axis=0, keepdims=True)
        for j in range(CHUNK // 128):
            ebias[pl.ds(f * (CHUNK // 128) + j, 1), :] = col[:, 128 * j : 128 * (j + 1)]

        @pl.when(inner)
        def _():
            dwout[cols, :] = dot_tn(act.astype(B16), grads[...]).astype(B16)
            dwin[:, cols] = dot(turned[...], pre).astype(B16)

        return carry

    turned[...] = rows[...].T
    lax.fori_loop(0, count, backward, 0)
    bgr[...] = acc[...].astype(B16)
    give_bgr = PlaneExchange(bgr, retg_o, ds3, dr3)
    give_bgr.start()

    mate = NZ - 1 - z

    def across():
        start = lax.div(mate, 2) * (hidden // 2)
        return remote(
            dwout.at[pl.ds(pl.multiple_of(start, 16), CHUNK), :], came_o, msem.at[0], msem.at[1], dev(mate, x, y, c)
        )

    def far(i, carry):
        f = lax.rem(i + lax.div(mate, 2) * (count // 2), count)
        cols = span(f)
        data, grad = far_rows[...], far_grads[...]
        act, slope = gelu_parts(dot(data, win[:, cols]) + bias_of(cols))
        pre = (dot_nt(grad, wout[cols, :]) * slope).astype(B16)
        dwout[cols, :] = (dwout[cols, :].astype(F32) + dot_tn(act.astype(B16), grad)).astype(B16)
        put_out(f).start()
        dwin[:, cols] = (dwin[:, cols].astype(F32) + dot(turned[...], pre)).astype(B16)
        put_in(f).start()
        pl.when(i == 0)(lambda: across().start())
        return carry

    pass_x(2)
    pass_x(3)
    pass_y(0)
    pass_y(1)

    @pl.when(inner)
    def _():
        far_copy(0).wait_recv()
        turned[...] = far_rows[...].T
        far_copy(1).wait_recv()
        lax.fori_loop(0, count, far, 0)

    pass_y(2)
    pass_y(3)
    for spread in spreads:
        spread.finish()

    @pl.when(inner)
    def _():
        across().wait()

    for column in later:
        column.finish()
    for exchange in (give_res, give_bgr):
        exchange.wait_in()
    for exchange in (give_rows, give_grads, give_res, give_bgr):
        exchange.wait_out()
    peers(lambda p: first(p, p).wait_send())
    peers(lambda p: second_hop(p, p).wait_send())
    for copy in keep:
        copy.wait()

    @pl.when(end)
    def _():
        far_copy(0).wait_send()
        far_copy(1).wait_send()

    @pl.when(inner)
    def _():
        for f in range(count):
            put_out(f).wait()
            put_in(f).wait()


def lead_part(tok, cot, route, cond, ada, adab, qvb, outb, soutb, sinb, router, bin_r, bout_r, shards, win, wout):
    n = NZ * NX
    length, width = tok.shape
    hidden = win.shape[2]
    slots = E * CAP
    dma = pltpu.SemaphoreType.DMA
    vm = pltpu.VMEM
    tiles = (ada.shape[1] // 128 + 7) // 8 * 8
    wide = [sds((n * s.shape[0], s.shape[1]), B16) for s in shards[:2]]
    outs = [
        sds((length, width), B16),
        sds((length, 3 * width), B16),
        sds((length, 128), F32),
        sds((length, width), B16),
        sds((length, width), F32),
        sds((length, width), F32),
        sds((length, width), B16),
        sds((length, 128), F32),
        sds((length, 128), jnp.int32),
        sds((8, width), F32),
        sds((8, width), F32),
        sds((1, hidden), F32),
        sds((E, width), F32),
        sds((8, 128), F32),
        sds((32, 128), F32),
    ]
    back = [sds((slots, width), B16)] * 2
    wide += [sds((NZ, NX) + s.shape, B16) for s in shards[2:]]
    far = back + wide + [
        sds((width, hidden), B16),
        sds((hidden, width), B16),
        sds((CHUNK, width), B16),
    ]
    return pl.pallas_call(
        lead_kernel,
        out_shape=outs + far,
        in_specs=[VM] * 13 + [HB] * 6,
        out_specs=[VM] * len(outs) + [HB] * len(far),
        scratch_shapes=[
            vm((32, 128), F32),
            vm((n, 32, 128), F32),
            vm((n, tiles, 128), F32),
            vm((n, tiles, 128), F32),
            vm(wide[0].shape, B16),
            vm(wide[1].shape, B16),
            vm((slots, width), B16),
            vm((slots, width), B16),
            vm((slots, width), B16),
            vm((slots, width), B16),
            vm((slots, width), B16),
            vm((slots, width), B16),
            vm((slots, width), B16),
            vm((slots, width), B16),
            vm((width, hidden), B16),
            vm((hidden, width), B16),
            vm((width, hidden), B16),
            vm((hidden, width), B16),
            vm((slots, hidden), F32),
            vm((slots, width), F32),
            vm((width, slots), B16),
        ]
        + [vm((NZ * s.shape[0], s.shape[1] // 2), B16) for s in shards[2:]]
        + [vm((NZ * s.shape[0] // 2, s.shape[1] // 2), B16) for s in shards[2:]]
        + [
            dma((n,)),
            dma((n,)),
            dma((n,)),
            dma((n,)),
        ]
        + [dma((E,))] * 8
        + [dma((4,)), dma((2, hidden // CHUNK)), dma((2, 2)), dma((2,))]
        + Gather.semaphores(2)
        + Column.semaphores()
        + Column.semaphores()
        + Spread.semaphores()
        + Spread.semaphores(),
        compiler_params=params(1),
        name="front_and_expert",
    )(tok, cot, route, cond, ada, adab, qvb, outb, soutb, sinb, router, bin_r, bout_r, *shards, win, wout)


def add_into(target, source, lead):
    count = 1
    for n in lead:
        count *= n

    def body(i, carry):
        at = []
        rest = i
        for n in reversed(lead):
            at.append(lax.rem(rest, n))
            rest = lax.div(rest, n)
        at = tuple(reversed(at))
        target[at] = (target[at].astype(F32) + source(at).astype(F32)).astype(B16)
        return carry

    lax.fori_loop(0, count, body, 0)


def piece_specs(width, hidden):
    rows, tall = width // NZ // 4, hidden // NZ // 4
    qkv = 3 * width // 2
    left = (qkv // 128 + 1) // 2 * 128
    early = (
        (2, (True, 0, rows, 0, hidden // 4, True)),
        (3, (True, 0, tall // 2, 0, width // 2, False)),
        (2, (True, 0, rows, hidden // 4, hidden // 4, False)),
        (3, (True, tall // 2, tall // 2, 0, width // 2, True)),
    )
    late = (
        (0, (False, 0, rows, 0, left, True)),
        (0, (False, 0, rows, left, qkv - left, False)),
        (1, (False, 0, rows, 0, width // 2, False)),
    )
    return early, late


class FirstHop:
    def __init__(self, spec, half, ebuf, sems):
        self.z, self.x, self.y, self.c = coords()
        _, self.row, self.rows, self.col, self.width, self.y_first = spec
        self.half, self.ebuf, self.sems = half, ebuf, sems

    def inner(self, *lead):
        return lead + (slice(self.row, self.row + self.rows), slice(self.col, self.col + self.width))

    def copy(self):
        every = slice(None)
        if self.y_first:
            at, to = self.inner(every, every, 1 - self.y), dev(self.z, self.x, 1 - self.y, self.c)
        else:
            at, to = self.inner(every, 1 - self.x, every), dev(self.z, 1 - self.x, self.y, self.c)
        return remote(self.half.at[at], self.ebuf, self.sems.at[0], self.sems.at[1], to)

    def absorb(self):
        self.copy().wait_recv()
        if self.y_first:
            source = lambda i: self.half[self.inner(i[0], i[1], self.y)]
        else:
            source = lambda i: self.half[self.inner(i[0], self.x, i[1])]
        add_into(self.ebuf, source, (NZ, 2))


def middle_kernel(
    ret, retg, second_r, resid_r, att_r, cot, mod, sinb, bias, router, gates_r, place_r, mixed, outw,
    tok, normed, proj, lsum, condt, ebias, sin_h, sout_h, qkv_h, dwout, dwin,
    out_o, out_half, shares, qkv_half, tgrad_o, mine_o, e0, e1, e2, e3, came_o, came_w,
    sin, sout, dsin, dsout, sin_half, sout_half, qkv, shared, sgrad, mgrad, rgrad_s, mg2, pgrad, tile, dqkv, dout,
    hsem, gsem, msem, lsem, qsem, s0, s1, s2, s3,
):
    chunks = range(NZ)
    size = sin.shape[3] // NZ
    loads = []
    for f in chunks:
        cols = slice(f * size, (f + 1) * size)
        loads.append(
            (
                pltpu.make_async_copy(sin_h.at[:, :, :, cols], sin.at[:, :, :, cols], lsem.at[0, f]),
                pltpu.make_async_copy(sout_h.at[f], sout.at[f], lsem.at[1, f]),
            )
        )
        for load in loads[-1]:
            load.start()
    qkv_load = pltpu.make_async_copy(qkv_h, qkv, qsem.at[0])
    qkv_load.start()
    barrier = pltpu.get_barrier_semaphore()
    z, x, y, c = coords()
    mate = NZ - 1 - z
    for to in (dev(mate, x, y, c), dev(z, x, y, 1 - c), dev(z, x, 1 - y, c), dev(z, 1 - x, y, c)):
        greet(barrier, to)
    pl.semaphore_wait(barrier, 4)
    central = jnp.logical_and(z > 0, z < NZ - 1)

    def across():
        rows = dwout.shape[0] // 2
        start = pl.multiple_of(lax.div(mate, 2) * rows + CHUNK, 16)
        return remote(
            dwout.at[pl.ds(start, rows - CHUNK), :], came_o, msem.at[0], msem.at[1], dev(mate, x, y, c)
        )

    def across_wide():
        rows = dwin.shape[0] // 2
        start = pl.multiple_of(lax.div(mate, 2) * rows, 16)
        return remote(
            dwin.at[pl.ds(start, rows), 0 : came_w.shape[1]], came_w, msem.at[2], msem.at[3], dev(mate, x, y, c)
        )

    @pl.when(central)
    def _():
        across().start()
        across_wide().start()

    length, width = second_r.shape
    hidden = sin.shape[3]
    chunk = hidden // NZ
    second = second_r[...]
    grad_out = cot[...].astype(F32)
    moe_low = (mod[5:6] * grad_out).astype(B16)
    moe_grad = moe_low.astype(F32)
    shared[...] = jnp.zeros_like(shared) + bias[3:4, :]
    sgrad[...] = jnp.zeros_like(sgrad)
    shares[...] = jnp.zeros_like(shares)
    n = NZ * NX
    part = width // n
    own_tiles = hidden // n // 128

    def cut(at, rows):
        for p in range(n):
            shares[p, at : at + rows.shape[0], 0:part] = rows[:, part * p : part * (p + 1)]

    for p in range(n):
        shares[p, 16 : 16 + own_tiles, :] = ebias[own_tiles * p : own_tiles * (p + 1), :]
        at = hidden // 128 + p
        shares[p, 19:20, 0:part] = ebias[at : at + 1, 0:part]

    other_core = dev(z, x, y, 1 - c)

    def half_cols(size, core):
        return pl.ds(pl.multiple_of(core * size, 128), size)

    def sout_copy(f):
        cols = half_cols(width // 2, 1 - c)
        return remote(
            dsout.at[f, :, :, :, cols], sout_half.at[f], hsem.at[0, 1, f], hsem.at[1, 1, f], other_core
        )

    def sin_copy(f):
        at = f % (NZ // 2)
        return remote(
            dsin.at[:, :, :, :, f * chunk : (f + 1) * chunk],
            sin_half.at[:, :, :, :, at * chunk : (at + 1) * chunk],
            hsem.at[0, 0, at],
            hsem.at[1, 0, at],
            other_core,
        )

    def core_copy(i):
        whole, half = ((dqkv, qkv_half), (dout, out_half))[i]
        cols = half_cols(half.shape[4], 1 - c)
        return remote(whole.at[:, :, :, :, cols], half, gsem.at[0, i], gsem.at[1, i], other_core)

    def core_add(half, whole):
        own = half_cols(half.shape[4], c)
        add_into(half, lambda at: whole[at[0], at[1], at[2], :, own], (NZ, NX, 2))

    def body(f):
        for load in loads[f]:
            load.wait()
        cols = slice(f * chunk, (f + 1) * chunk)
        w1 = sin[:, :, :, cols].reshape(width, chunk)
        w2 = sout[f].reshape(chunk, width)
        act, slope = gelu_parts(dot(second, w1) + sinb[:, cols])
        low = act.astype(B16)
        shared[...] += dot(low, w2)
        pre = (dot_nt(moe_low, w2) * slope).astype(B16)
        dsout[f] = dot_tn(low, moe_low).astype(B16).reshape(dsout.shape[1:])
        dsin[:, :, :, :, cols] = dot_tn(second, pre).astype(B16).reshape(dsin.shape[:4] + (chunk,))
        sout_copy(f).start()
        pl.when(c == 1 - f // (NZ // 2))(lambda: sin_copy(f).start())
        sgrad[...] += dot_nt(pre, w1)
        col = jnp.sum(pre.astype(F32), axis=0, keepdims=True)
        for j in range(chunk // 128):
            at = f * (chunk // 128) + j
            shares[at // own_tiles, 4 + at % own_tiles : 5 + at % own_tiles, :] = col[
                :, 128 * j : 128 * (j + 1)
            ]

    for f in chunks:
        body(f)
    lane = lax.broadcasted_iota(jnp.int32, (length, E), 1)
    gates = [gates_r[:, k : k + 1] for k in range(2)]
    maps = [
        jnp.where(choose_rows(place_r[:, k : k + 1], E * CAP), 1.0, 0.0) for k in range(2)
    ]
    back = ret[...]
    rows = [dot(m.astype(B16), back) for m in maps]
    moe = shared[...] + (gates[0] * rows[0] + gates[1] * rows[1])
    for f in range(NZ // 2):
        sin_copy(f).wait_recv()
    for f in chunks:
        sout_copy(f).wait_recv()
    core_add(sin_half, dsin)
    core_add(sout_half, dsout)
    hops = [
        FirstHop(spec, sin_half if matrix == 2 else sout_half, ebuf, sem)
        for (matrix, spec), ebuf, sem in zip(
            piece_specs(width, hidden)[0], (e0, e1, e2, e3), (s0, s1, s2, s3)
        )
    ]
    for hop in hops:
        hop.copy().start()

    resid = resid_r[...]
    out_o[...] = (resid + mod[5:6] * moe).astype(B16)
    mg2[...] = jnp.zeros_like(mg2)
    mg2[5:6, :] = jnp.sum(grad_out * moe, axis=0, keepdims=True)
    ggrad = [jnp.sum(moe_grad * r, axis=-1, keepdims=True) for r in rows]
    inner = gates[0] * ggrad[0] + gates[1] * ggrad[1]
    lgrad = jnp.zeros((length, E), F32)
    for k in range(2):
        pick = place_r[:, 2 + k : 3 + k] == lane
        lgrad = lgrad + jnp.where(pick, gates[k] * (ggrad[k] - inner), 0.0)
    lgrad = lgrad.astype(B16)
    cut(8, dot_tn(lgrad, second))
    grad = (
        sgrad[...]
        + dot((maps[0] + maps[1]).astype(B16), retg[...])
        + dot(lgrad, router[...].astype(B16))
    )
    n2, r2 = norm_parts(resid)
    mg2[3:4, :] = jnp.sum(grad, axis=0, keepdims=True)
    mg2[4:5, :] = jnp.sum(grad * n2, axis=0, keepdims=True)
    rgrad = grad_out + norm_back(grad * (1.0 + mod[4:5]), n2, r2)
    rgrad_s[...] = rgrad
    agrad = (mod[2:3] * rgrad).astype(B16)
    mg2[2:3, :] = jnp.sum(rgrad * att_r[...], axis=0, keepdims=True)
    dout[...] = dot_tn(mixed[...], agrad).astype(B16).reshape(dout.shape)
    core_copy(1).start()
    mgrad[...] = dot_nt(agrad, outw[...]).astype(B16)
    cut(3, jnp.sum(moe_grad, axis=0, keepdims=True))
    cut(2, jnp.sum(agrad.astype(F32), axis=0, keepdims=True))
    low_lane = lax.broadcasted_iota(jnp.int32, (length, 128), 1) < HEAD_DIM
    for p in range(HEADS // 2):
        q2 = proj[:, 128 * p : 128 * (p + 1)]
        k2 = proj[:, width + 128 * p : width + 128 * (p + 1)]
        v2 = proj[:, 2 * width + 128 * p : 2 * width + 128 * (p + 1)]
        m2 = mgrad[:, 128 * p : 128 * (p + 1)]
        parts = []
        for h in range(2):
            head = low_lane if h == 0 else jnp.logical_not(low_lane)
            zero = jnp.zeros_like(q2)
            s = dot_nt(jnp.where(head, q2, zero), k2) * SCALE
            prob = jnp.exp(s - lsum[:, 2 * p + h : 2 * p + h + 1])
            pg = dot_nt(jnp.where(head, m2, zero), v2)
            inner = jnp.sum(prob * pg, axis=-1, keepdims=True)
            sg = (prob * (pg - inner)).astype(B16)
            parts.append(
                (dot(sg, k2) * SCALE, dot_tn(sg, q2) * SCALE, dot_tn(prob.astype(B16), m2))
            )
        for i in range(3):
            pgrad[:, i * width + 128 * p : i * width + 128 * (p + 1)] = jnp.where(
                low_lane, parts[0][i], parts[1][i]
            ).astype(B16)
    lead = dqkv.shape[:4]
    for i in range(3):
        cols = slice(i * width, (i + 1) * width)
        dqkv[:, :, :, :, cols] = dot_tn(normed[...], pgrad[:, cols]).astype(B16).reshape(lead + (width,))
    core_copy(0).start()
    qkv_load.wait()
    ngrad = dot_nt(pgrad[...], qkv[...])
    n1, r1 = norm_parts(tok[...].astype(F32))
    tgrad_o[...] = rgrad_s[...] + norm_back(ngrad * (1.0 + mod[1:2]), n1, r1)
    per = width // 128
    for i, k in enumerate((0, 2)):
        cut(i, jnp.sum(pgrad[:, k * width : (k + 1) * width].astype(F32), axis=0, keepdims=True))
    mod_rows = [
        jnp.sum(ngrad, axis=0, keepdims=True),
        jnp.sum(ngrad * n1, axis=0, keepdims=True),
    ] + [mg2[i : i + 1, :] for i in range(2, 6)]
    tile[...] = jnp.zeros_like(tile)
    for i, row in enumerate(mod_rows):
        row = row.astype(B16).astype(F32)
        for j in range(per):
            tile[i * per + j : i * per + j + 1, :] = row[:, 128 * j : 128 * (j + 1)]
    tile[40:48, :] = condt[...]
    mine_o[...] = tile[...].astype(B16)
    for i, (half, whole) in enumerate(((qkv_half, dqkv), (out_half, dout))):
        core_copy(i).wait_recv()
        core_add(half, whole)
        core_copy(i).wait_send()
    for f in chunks:
        sout_copy(f).wait_send()
        pl.when(c == 1 - f // (NZ // 2))(lambda: sin_copy(f).wait_send())
    for hop in hops:
        hop.absorb()
    for hop in hops:
        hop.copy().wait_send()

    @pl.when(central)
    def _():
        across().wait()
        across_wide().wait()


def middle(*args):
    second, sin = args[2], args[20]
    length, width = second.shape
    hidden = sin.shape[3]
    rows, tall = width // NZ // 4, hidden // NZ // 4
    dma = pltpu.SemaphoreType.DMA
    vm = pltpu.VMEM
    early = piece_specs(width, hidden)[0]
    return pl.pallas_call(
        middle_kernel,
        out_shape=[
            sds((length, width), B16),
            sds((NZ, NX, 2, rows, width // 2), B16),
            sds((NZ * NX, 24, 128), F32),
            sds((NZ, NX, 2, rows, 3 * width // 2), B16),
            sds((length, width), F32),
            sds((48, 128), B16),
        ]
        + [sds((NZ, 2, spec[2], spec[4]), B16) for _, spec in early]
        + [
            sds((hidden // 2 - CHUNK, width), B16),
            sds((width // 2, hidden // MidSum.COUNT), B16),
        ],
        in_specs=[VM] * 20 + [HB] * 5,
        out_specs=[VM] * 10 + [HB] * 2,
        scratch_shapes=[
            vm(sin.shape, B16),
            vm((NZ, NX, hidden // NZ // NX, width), B16),
            vm((NZ, NX, 2, rows, hidden), B16),
            vm((NZ, NX, 2, tall, width), B16),
            vm((NZ, NX, 2, rows, hidden // 2), B16),
            vm((NZ, NX, 2, tall, width // 2), B16),
            vm((width, 3 * width), B16),
            vm((length, width), F32),
            vm((length, width), F32),
            vm((length, width), B16),
            vm((length, width), F32),
            vm((8, width), F32),
            vm((length, 3 * width), B16),
            vm((48, 128), F32),
            vm((NZ, NX, 2, rows, 3 * width), B16),
            vm((NZ, NX, 2, rows, width), B16),
            dma((2, 2, NZ)),
            dma((2, 2)),
            dma((4,)),
            dma((2, NZ)),
            dma((1,)),
        ]
        + [dma((2,))] * 4,
        compiler_params=params(3),
        name="shared_expert_attention_back",
    )(*args)


class Piece:
    def __init__(self, spec, grad, out, bufs):
        self.z, self.x, self.y, self.c = coords()
        self.half, self.row, self.rows, self.col, self.width, self.y_first = spec
        self.grad, self.out = grad, out
        self.size = out.shape[-1] // 2
        if self.half:
            self.ebuf = grad
        else:
            self.ebuf, bufs = bufs[0], bufs[1:]
        self.fbuf, self.zin, self.one, self.zsem = bufs
        self.inner = jnp.logical_and(self.z > 0, self.z < NZ - 1)
        self.end = jnp.logical_not(self.inner)
        self.mate = NZ - 1 - self.z
        self.beside = self.z + 1 - 2 * lax.rem(self.z, 2)

    @staticmethod
    def scratch(spec):
        half, _, rows, _, width, _ = spec
        vm = lambda *lead: pltpu.VMEM(lead + (rows, width), B16)
        dma = pltpu.SemaphoreType.DMA
        return ([] if half else [vm(NZ, 2)]) + [
            vm(NZ),
            vm(NZ + 3),
            dma((13,)),
            dma((2, 3)),
        ]

    def cols(self, c):
        return pl.ds(pl.multiple_of(c * self.size + self.col, 128), self.width)

    def core(self, *lead):
        return lead + (slice(self.row, self.row + self.rows), slice(self.col, self.col + self.width))

    def to_x(self):
        return dev(self.z, 1 - self.x, self.y, self.c)

    def to_y(self):
        return dev(self.z, self.x, 1 - self.y, self.c)

    def copy1(self):
        every = slice(None)
        if self.y_first:
            source, to = self.grad.at[self.core(every, every, 1 - self.y)], self.to_y()
        else:
            source, to = self.grad.at[self.core(every, 1 - self.x, every)], self.to_x()
        return remote(source, self.ebuf, self.one.at[3], self.one.at[4], to)

    def copy2(self):
        if self.y_first:
            source, to = self.ebuf.at[:, 1 - self.x], self.to_x()
        else:
            source, to = self.ebuf.at[:, 1 - self.y], self.to_y()
        return remote(source, self.fbuf, self.one.at[5], self.one.at[6], to)

    def zcopy(self, step):
        if step == 0:
            at = pl.ds(jnp.where(lax.rem(self.z, NZ - 1) == 0, lax.rem(self.z + 1, NZ), 0), NZ - 1)
            source, target, to = self.fbuf.at[at], self.zin.at[at], self.beside
        elif step == 1:
            at = pl.ds(2 * lax.div(self.mate, 2), 2)
            source, target, to = self.fbuf.at[at], self.zin.at[NZ : NZ + 2], self.mate
        else:
            source, target, to = self.fbuf.at[self.beside], self.zin.at[NZ + 2], self.beside
        return remote(
            source, target, self.zsem.at[0, step], self.zsem.at[1, step], dev(to, self.x, self.y, self.c)
        )

    def plus(self, block, came):
        self.fbuf[block] = (self.fbuf[block].astype(F32) + self.zin[came].astype(F32)).astype(B16)

    def own(self):
        return self.fbuf.at[self.z]

    def place(self, y, c):
        return self.out.at[y, self.row : self.row + self.rows, self.cols(c)]

    def keep(self):
        return pltpu.make_async_copy(self.own(), self.place(self.y, self.c), self.one.at[7])

    def give_y(self, came=False):
        at = self.place(1 - self.y if came else self.y, self.c)
        return remote(self.own(), at, self.one.at[8], self.one.at[9], self.to_y())

    def give_c(self, came=False):
        at = self.place(self.y, 1 - self.c if came else self.c)
        to = dev(self.z, self.x, self.y, 1 - self.c)
        return remote(self.own(), at, self.one.at[10], self.one.at[11], to)

    def pass_c(self, came=False):
        at = self.place(1 - self.y, 1 - self.c if came else self.c)
        to = dev(self.z, self.x, self.y, 1 - self.c)
        return remote(at, at, self.one.at[12], self.one.at[2], to)

    def stage(self, s):
        if s == 0 and not self.half:
            self.copy1().start()
        elif s == 1:
            if not self.half:
                self.copy1().wait_recv()
                if self.y_first:
                    add_into(self.ebuf, lambda i: self.grad[self.core(i[0], i[1], self.y)], (NZ, NX))
                else:
                    add_into(self.ebuf, lambda i: self.grad[self.core(i[0], self.x, i[1])], (NZ, 2))
            self.copy2().start()
        elif s == 2:
            self.copy2().wait_recv()
            side = self.x if self.y_first else self.y
            add_into(self.fbuf, lambda i: self.ebuf[i[0], side], (NZ,))
            pl.when(self.end)(lambda: self.zcopy(0).start())
        elif s == 3:

            @pl.when(self.inner)
            def _():
                self.zcopy(0).wait_recv()
                first = lax.rem(self.z, 2)
                for i in range(NZ - 1):
                    self.plus(first + i, first + i)
                self.zcopy(1).start()

        elif s == 4:

            @pl.when(self.inner)
            def _():
                self.zcopy(1).wait_recv()
                for i in range(2):
                    self.plus(2 * lax.div(self.z, 2) + i, NZ + i)
                self.zcopy(2).start()

        elif s == 5:

            @pl.when(self.end)
            def _():
                self.zcopy(2).wait_recv()
                self.plus(self.z, NZ + 2)

            self.give_y().start()
            self.give_c().start()
            self.keep().start()
        elif s == 6:
            self.give_y(True).wait_recv()
            self.pass_c().start()
        elif s == 7:
            self.keep().wait()
            self.give_c(True).wait_recv()
            self.pass_c(True).wait_recv()
            if not self.half:
                self.copy1().wait_send()
            self.copy2().wait_send()
            self.give_y().wait_send()
            self.give_c().wait_send()
            self.pass_c().wait_send()
            pl.when(self.end)(lambda: self.zcopy(0).wait_send())

            @pl.when(self.inner)
            def _():
                self.zcopy(1).wait_send()
                self.zcopy(2).wait_send()


class MidSum:
    COUNT = 3

    def __init__(self, origin, grad, into, out, total, outer, sems):
        self.z, self.x, self.y, self.c = coords()
        self.origin = origin
        self.grad, self.into, self.out, self.total, self.outer = grad, into, out, total, outer
        self.sems = sems
        self.size = grad.shape[2] // self.COUNT
        self.inner = jnp.logical_and(self.z > 0, self.z < NZ - 1)
        self.end = jnp.logical_not(self.inner)
        self.mate = NZ - 1 - self.z

    @staticmethod
    def scratch(shape):
        vm = pltpu.VMEM
        return [vm(shape[1:], B16), vm(shape[1:], B16), pltpu.SemaphoreType.DMA((9, MidSum.COUNT))]

    def cols(self, p):
        return slice(p * self.size, (p + 1) * self.size)

    @staticmethod
    def beside(z):
        return z + 1 - 2 * lax.rem(z, 2)

    def landing(self, z, block):
        rows = self.grad.shape[1]
        return pl.ds(pl.multiple_of((block - 2 * lax.div(z, 2)) * rows, 16), rows)

    def across(self, i, p, came=False):
        z = self.z if came else self.mate
        block = self.beside(z) if i == 0 else z
        return remote(
            self.origin.at[block, :, self.cols(p)],
            self.into.at[self.landing(z, block), self.cols(p)],
            self.sems.at[i, p],
            self.sems.at[2 + i, p],
            dev(self.mate, self.x, self.y, self.c),
        )

    def came(self, block, p):
        return self.into[self.landing(self.z, block), self.cols(p)].astype(F32)

    def outward(self, p):
        return remote(
            self.outer.at[:, self.cols(p)],
            self.total.at[:, self.cols(p)],
            self.sems.at[4, p],
            self.sems.at[5, p],
            dev(self.beside(self.z), self.x, self.y, self.c),
        )

    def begin(self, i, p):
        pl.when(self.inner)(lambda: self.across(i, p).start())

    def give(self, p, sent=True):
        @pl.when(self.inner)
        def _():
            if sent:
                self.across(0, p, True).wait_recv()
            cols = self.cols(p)
            self.outer[:, cols] = (
                self.grad[self.beside(self.z), :, cols].astype(F32) + self.came(self.beside(self.z), p)
            ).astype(B16)
            self.outward(p).start()

    def swap(self, p, came=False):
        part = self.total.shape[0] // NX
        start = pl.multiple_of((1 - self.x) * part, 16)
        return remote(
            self.total.at[pl.ds(start, part), self.cols(p)],
            self.out.at[1 - self.x if came else self.x, :, self.cols(p)],
            self.sems.at[6, p],
            self.sems.at[7, p],
            dev(self.z, 1 - self.x, self.y, self.c),
        )

    def keep(self, p):
        part = self.total.shape[0] // NX
        start = pl.multiple_of(self.x * part, 16)
        return pltpu.make_async_copy(
            self.total.at[pl.ds(start, part), self.cols(p)],
            self.out.at[self.x, :, self.cols(p)],
            self.sems.at[8, p],
        )

    def final(self, p, sent=True):
        @pl.when(self.inner)
        def _():
            if sent:
                self.across(1, p, True).wait_recv()
            cols = self.cols(p)
            self.total[:, cols] = (
                self.grad[self.z, :, cols].astype(F32) + self.came(self.z, p)
            ).astype(B16)

        pl.when(self.end)(lambda: self.outward(p).wait_recv())
        self.swap(p).start()
        self.keep(p).start()

    def close(self, sent):
        for p in range(self.COUNT):

            @pl.when(self.inner)
            def _():
                self.outward(p).wait_send()
                if p in sent:
                    self.across(0, p).wait_send()
                    self.across(1, p).wait_send()

            self.swap(p, True).wait_recv()
            self.swap(p).wait_send()
            self.keep(p).wait()


def tail_kernel(*refs):
    ebufs, qkv_half, out_half = refs[:4], refs[4], refs[5]
    shares, mine, ada = refs[6:9]
    dwin_h, dwout_h, came_a, came_b, came_w = refs[9:14]
    outs = refs[14:18]
    pair_in, pair_out, small, esum, tiles, cgot = refs[18:24]
    rest = list(refs[24:])
    z, x, y, c = coords()
    dp, ex = lax.axis_index("dp"), lax.axis_index("expert")
    n = NZ * NX
    width = dwout_h.shape[2]
    early_specs, late_specs = piece_specs(width, dwin_h.shape[2])
    dwin, dwout, lsem = rest[:3]
    rest = rest[3:]

    def make(specs, rest, sources):
        made = []
        for (matrix, spec), source in zip(specs, sources):
            count = len(Piece.scratch(spec))
            made.append(Piece(spec, source, outs[matrix], rest[:count]))
            rest = rest[count:]
        return made, rest

    early, rest = make(early_specs, rest, ebufs)
    late, rest = make(late_specs, rest, (qkv_half, qkv_half, out_half))
    wide = MidSum(dwin_h, dwin, rest[0], pair_in, *rest[1:4])
    tall = MidSum(dwout_h, dwout, rest[4], pair_out, *rest[5:8])
    rest = rest[8:]
    first_rows = came_a.shape[0]
    loads = [
        pltpu.make_async_copy(came_a, tall.into.at[0:first_rows, :], lsem.at[0]),
        pltpu.make_async_copy(came_b, tall.into.at[first_rows:, :], lsem.at[1]),
        pltpu.make_async_copy(dwout_h, dwout, lsem.at[2]),
        pltpu.make_async_copy(dwin_h, dwin, lsem.at[3]),
        pltpu.make_async_copy(came_w, wide.into.at[:, 0 : came_w.shape[1]], lsem.at[4]),
    ]
    sgot, dall, floats, csend, dsem, tsem = rest

    barrier = pltpu.get_barrier_semaphore()

    def peers(action):
        for p in range(n):

            @pl.when(p != dp)
            def _():
                action(p)

    peers(lambda p: greet(barrier, (p, ex)))
    mates = (dev(z, x, 1 - y, c), dev(z, x, y, 1 - c), dev(z, x, 1 - y, 1 - c))
    for mate in mates:
        greet(barrier, mate)
    pl.semaphore_wait(barrier, n - 1 + 3)

    def share_copy(p, at):
        return remote(shares.at[p], sgot.at[at], dsem.at[4, p], dsem.at[5, at], (p, ex))

    def tile(p, at):
        return remote(mine, tiles.at[ex, at], dsem.at[0, p], dsem.at[1, at], (p, ex))

    def mate_rank(i):
        return 2 * (1 - y if i != 1 else y) + (1 - c if i != 0 else c)

    def spread(i, theirs=False):
        rows = tiles.at[mate_rank(i) if theirs else ex]
        return remote(rows, rows, tsem.at[0, i], tsem.at[1, i], mates[i])

    def total_copy(i, theirs=False):
        rows = dall.at[mate_rank(i) if theirs else ex]
        return remote(rows, rows, tsem.at[2, i], tsem.at[3, i], mates[i])

    def cond_copy(p, at):
        return remote(csend.at[p], cgot.at[at], dsem.at[2, p], dsem.at[3, at], (p, ex))

    peers(lambda p: share_copy(p, dp).start())
    peers(lambda p: tile(p, dp).start())

    every = range(MidSum.COUNT)
    for piece in early:
        piece.stage(1)
    for piece in late:
        piece.stage(0)
    for p in every[1:]:
        for i in range(2):
            wide.begin(i, p)
    for load in loads:
        load.start()
    sgot[dp] = shares[dp]
    tiles[ex, dp] = mine[...]

    def small1():
        peers(lambda p: share_copy(p, p).wait_recv())
        peers(lambda p: tile(p, p).wait_recv())
        total = sgot[0, 0:16, :]
        for p in range(1, n):
            total = total + sgot[p, 0:16, :]
        dall[ex] = total
        for i in range(NX):
            own = sgot[i, 16:24, :]
            for zb in range(1, NZ):
                own = own + sgot[NX * zb + i, 16:24, :]
            esum[i] = own
        for i in range(3):
            total_copy(i).start()
            spread(i).start()
        floats[...] = tiles[ex].astype(F32)
        acc = jnp.zeros((n, ada.shape[0]), F32)
        for j in range(ada.shape[1] // 128):
            acc = acc + dot_nt(floats[:, j, :].astype(B16), ada[:, 128 * j : 128 * (j + 1)])
        csend[...] = jnp.zeros_like(csend)
        csend[:, 0, 0 : ada.shape[0]] = acc
        peers(lambda p: cond_copy(p, dp).start())
        cgot[dp] = csend[dp]

    def small2():
        for i in range(3):
            total_copy(i, True).wait_recv()
            spread(i, True).wait_recv()
        total = dall[0]
        for i in range(1, 4):
            total = total + dall[i]
        small[...] = total
        peers(lambda p: cond_copy(p, p).wait_recv())
        for i in range(3):
            total_copy(i).wait_send()
            spread(i).wait_send()
        peers(lambda p: share_copy(p, p).wait_send())
        peers(lambda p: tile(p, p).wait_send())
        peers(lambda p: cond_copy(p, p).wait_send())

    def run(pieces, s):
        for piece in pieces:
            piece.stage(s)

    for load in loads[:3]:
        load.wait()
    for p in every:
        tall.give(p, False)
    for load in loads[3:]:
        load.wait()
    wide.give(0, False)
    small1()
    run(early, 2)
    for p in every[1:2]:
        wide.give(p)
    run(late, 1)
    run(early, 3)
    for p in every:
        tall.final(p, False)
    run(early, 4)
    for p in every[2:]:
        wide.give(p)
    run(late, 2)
    run(early, 5)
    wide.final(0, False)
    run(late, 3)
    for p in every[1:2]:
        wide.final(p)
    run(early, 6)
    run(late, 4)
    for p in every[2:]:
        wide.final(p)
    run(late, 5)
    run(early, 7)
    small2()
    run(late, 6)
    run(late, 7)
    tall.close(())
    wide.close(every[1:])


def tail_part(ebufs, qkv_half, out_half, shares, mine, ada, dwin, dwout, came_a, came_b, came_w):
    n = NZ * NX
    dma = pltpu.SemaphoreType.DMA
    vm = pltpu.VMEM
    width, hidden = dwout.shape[2], dwin.shape[2]
    rows, tall = width // NZ // 4, hidden // NZ // 4
    outs = [
        sds((2, rows, 3 * width), B16),
        sds((2, rows, width), B16),
        sds((2, rows, hidden), B16),
        sds((2, tall, width), B16),
    ]
    scratch = [vm(dwin.shape, B16), vm(dwout.shape, B16), dma((5,))]
    for specs in piece_specs(width, hidden):
        for _, spec in specs:
            scratch += Piece.scratch(spec)
    for shape in (dwin.shape, dwout.shape):
        scratch += [vm((2 * shape[1], shape[2]), B16)] + MidSum.scratch(shape)
    scratch += [
        vm(shares.shape, F32),
        vm((4, 16, 128), F32),
        vm((n, 48, 128), F32),
        vm((n, 8, 128), F32),
        dma((6, n)),
        dma((4, 3)),
    ]
    out = pl.pallas_call(
        tail_kernel,
        out_shape=outs
        + [
            sds((NX, dwin.shape[1] // NX, hidden), B16),
            sds((NX, dwout.shape[1] // NX, width), B16),
            sds((16, 128), F32),
            sds((NX, 8, 128), F32),
            sds((4, n, 48, 128), B16),
            sds((n, 8, 128), F32),
        ],
        in_specs=[VM] * 9 + [HB] * 5,
        out_specs=[HB] * 6 + [VM] * 4,
        scratch_shapes=scratch,
        compiler_params=params(4),
        name="device_sums",
    )(
        *ebufs,
        qkv_half,
        out_half,
        shares,
        mine,
        ada,
        dwin,
        dwout,
        came_a,
        came_b,
        came_w,
    )
    return [o.reshape(-1, o.shape[2]) for o in out[:4]], out[4:6], out[6:]


def pick_part(flat, part, dp):
    chosen = jnp.zeros((flat.shape[0], part), flat.dtype)
    for p in range(NZ * NX):
        chosen = jnp.where(dp == p, flat[:, p * part : (p + 1) * part], chosen)
    return chosen


def finish_kernel(*refs):
    large = refs[:6]
    small, esum, tiles, cgot, cond, out_r, tgrad_r = refs[6:13]
    outs = refs[13:19]
    ada_o, adab_o, qvb_o, outb_o, sinb_o, soutb_o, router_o, einb_o, eoutb_o, cond_o = refs[19:29]
    out_o, tgrad_o, floats = refs[29:32]
    out_o[...] = out_r[...]
    tgrad_o[...] = tgrad_r[...]
    dp = lax.axis_index("dp")
    n = NZ * NX
    for source, out in zip(large, outs):
        out[...] = source[...].astype(F32)
    width = cond.shape[1]
    per, part = width // 128, width // n
    hidden = sinb_o.shape[0] * n
    images = tiles.shape[0] * tiles.shape[1]
    floats[...] = tiles[...].astype(F32)
    qvb_o[...] = small[0:2, 0:part]
    outb_o[...] = small[2:3, 0:part]
    soutb_o[...] = small[3:4, 0:part]
    router_o[...] = small[8:16, 0:part]
    for j in range(hidden // n // 128):
        cols = slice(128 * j, 128 * (j + 1))
        sinb_o[cols] = small[4 + j : 5 + j, :].reshape(128)
        for i in range(NX):
            einb_o[i : i + 1, cols] = esum[i, j : j + 1, :]
    for i in range(NX):
        eoutb_o[i : i + 1, :] = esum[i, 3:4, 0:part]

    conds = jnp.concatenate(
        [floats[:, :, 40 + j, :].reshape(images, 128) for j in range(per)], axis=1
    )
    conds = pick_part(conds, part, dp).astype(B16)
    sums = []
    for j in range(6 * per):
        mods = floats[:, :, j, :].reshape(images, 128)
        ada_o[:, 128 * j : 128 * (j + 1)] = dot_tn(conds, mods.astype(B16))
        sums.append(jnp.sum(mods, axis=0, keepdims=True))
    adab_o[...] = pick_part(jnp.concatenate(sums, axis=1), adab_o.shape[0], dp)[0]
    v = cond[...].astype(F32)
    sig = 1.0 / (1.0 + jnp.exp(-v))
    grad = jnp.concatenate([cgot[p, 0:1, 0:part] for p in range(n)], axis=1)
    cond_o[...] = grad * (sig * (1.0 + v * (1.0 - sig)))


def finish(dense, pairs, small, esum, tiles, cgot, cond, output, tgrad, hidden):
    n = NZ * NX
    width = cond.shape[1]
    part = width // n
    big = [sds(v.shape, F32) for v in (*dense, *pairs)]
    short = [
        sds((part, 6 * width), F32),
        sds((6 * part,), F32),
        sds((2, part), F32),
        sds((1, part), F32),
        sds((hidden // n,), F32),
        sds((1, part), F32),
        sds((E, part), F32),
        sds((NX, hidden // n), F32),
        sds((NX, part), F32),
        sds((1, width), F32),
        sds(output.shape, output.dtype),
        sds(tgrad.shape, tgrad.dtype),
    ]
    return pl.pallas_call(
        finish_kernel,
        out_shape=big + short,
        in_specs=[VM] * 13,
        out_specs=[VM] * 18,
        scratch_shapes=[pltpu.VMEM(tiles.shape, F32)],
        compiler_params=params(),
        name="final_form",
    )(*dense, *pairs, small, esum, tiles, cgot, cond, output, tgrad)


def on_block(
    tokens, conditioning, routes, cotangent, ada_weight, ada_bias, qkv_weight, qv_bias, out_weight, out_bias,
    shared_in, shared_in_bias, shared_out, shared_out_bias, router,
    expert_in, expert_in_bias, expert_out, expert_out_bias,
):
    n = NZ * NX
    width = tokens.shape[2]
    hidden = shared_in.shape[1]
    part = width // n
    tok, cot, route = tokens[0], cotangent[0], routes[0]
    (
        normed, proj, lsum, mixed, att, resid, second, gates, place, mod, bias, sinb, router_t,
        condt, ebias, ret, retg, qkv_full, out_full, sin_full, sout_full, dwin, dwout, came_a,
    ) = lead_part(
        tok, cot, route.T, conditioning, ada_weight, ada_bias, qv_bias, out_bias[None], shared_out_bias[None],
        shared_in_bias, router.T, expert_in_bias, expert_out_bias,
        (qkv_weight, out_weight, shared_in, shared_out), expert_in, expert_out,
    )
    (output, out_half, shares, qkv_half, tgrad, mine, e0, e1, e2, e3, came_b, came_w) = middle(
        ret, retg, second, resid, att, cot, mod, sinb, bias, router_t, gates, place, mixed, out_full,
        tok, normed, proj, lsum, condt, ebias, sin_full, sout_full, qkv_full, dwout, dwin,
    )
    dense, pairs, (small, esum, tiles, cgot) = tail_part(
        (e0, e1, e2, e3), qkv_half, out_half, shares, mine, ada_weight,
        dwin.reshape(NZ, NX * part, hidden), dwout.reshape(NZ, hidden // NZ, width), came_a, came_b, came_w,
    )
    (
        qkv_grad, out_grad, sin_grad, sout_grad, dwin_sum, dwout_sum, ada_grad, adab_grad, qvb_grad, outb_grad,
        sinb_grad, soutb_grad, router_grad, ein_b, eout_b, cond_grad, output, tgrad,
    ) = finish(dense, pairs, small, esum, tiles, cgot, conditioning, output, tgrad, hidden)
    return (
        output[None],
        tgrad[None],
        cond_grad,
        ada_grad,
        adab_grad,
        qkv_grad,
        qvb_grad,
        out_grad,
        outb_grad[0],
        sin_grad,
        sinb_grad,
        sout_grad,
        soutb_grad[0],
        router_grad.T,
        dwin_sum,
        ein_b,
        dwout_sum,
        eout_b,
    )


def layer_norm(rows):
    centred = rows - jnp.mean(rows, axis=-1, keepdims=True)
    return centred * lax.rsqrt(jnp.mean(centred * centred, axis=-1, keepdims=True) + 1e-06)


def modulate(rows, shift, scale):
    return layer_norm(rows) * (1.0 + scale) + shift


def gelu_tanh(values_in):
    return jax.nn.gelu(values_in, approximate=True)


def on_device(
    tokens,
    conditioning,
    routes,
    cotangent,
    ada_weight,
    ada_bias,
    qkv_weight,
    qv_bias,
    out_weight,
    out_bias,
    shared_in,
    shared_in_bias,
    shared_out,
    shared_out_bias,
    router,
    expert_in,
    expert_in_bias,
    expert_out,
    expert_out_bias,
):
    f32 = jnp.float32
    b16 = jnp.bfloat16
    gathered_dense = (
        lax.all_gather(ada_weight, "dp", axis=0, tiled=True),
        lax.all_gather(ada_bias, "dp", axis=0, tiled=True),
        lax.all_gather(qkv_weight, "dp", axis=0, tiled=True),
        lax.all_gather(qv_bias, "dp", axis=1, tiled=True),
        lax.all_gather(out_weight, "dp", axis=0, tiled=True),
        lax.all_gather(out_bias, "dp", axis=0, tiled=True),
        lax.all_gather(shared_in, "dp", axis=0, tiled=True),
        lax.all_gather(shared_in_bias, "dp", axis=0, tiled=True),
        lax.all_gather(shared_out, "dp", axis=0, tiled=True),
        lax.all_gather(shared_out_bias, "dp", axis=0, tiled=True),
        lax.all_gather(router, "dp", axis=0, tiled=True),
    )
    (
        ada_full,
        ada_bias_full,
        qkv_full,
        qv_bias_full,
        out_full,
        out_bias_full,
        shared_in_full,
        shared_in_bias_full,
        shared_out_full,
        shared_out_bias_full,
        router_full,
    ) = gathered_dense
    image_count, length, width = tokens.shape
    row_count = image_count * length
    scaling = HEAD_DIM ** (-0.5)
    head_shape = (image_count, length, HEADS, HEAD_DIM)
    cond_float = conditioning.astype(f32)
    cond_act, silu_back = jax.vjp(jax.nn.silu, cond_float)
    cond_low = cond_act.astype(b16)
    modulation = jnp.dot(cond_low, ada_full, preferred_element_type=f32) + ada_bias_full.astype(f32)
    pieces = [modulation[:, None, index * width : (index + 1) * width] for index in range(6)]
    source = tokens.astype(f32)
    first_norm, first_back = jax.vjp(modulate, source, pieces[0], pieces[1])
    normed = first_norm.astype(b16)
    projected = jnp.einsum("isd,de->ise", normed, qkv_full, preferred_element_type=f32)
    query_heads = (
        (projected[..., :width] + qv_bias_full[0].astype(f32)).astype(b16).reshape(head_shape)
    )
    key_heads = projected[..., width : 2 * width].astype(b16).reshape(head_shape)
    value_heads = (
        (projected[..., 2 * width :] + qv_bias_full[1].astype(f32)).astype(b16).reshape(head_shape)
    )
    scores = (
        jnp.einsum("iqhc,ikhc->ihqk", query_heads, key_heads, preferred_element_type=f32) * scaling
    )
    peak_score = jnp.max(scores, axis=-1, keepdims=True)
    unscaled = jnp.exp(scores - peak_score)
    exp_total = jnp.sum(unscaled, axis=-1, keepdims=True)
    log_total = peak_score + jnp.log(exp_total)
    probs_low = (unscaled / exp_total).astype(b16)
    mixed = (
        jnp.einsum("ihqk,ikhc->iqhc", probs_low, value_heads, preferred_element_type=f32)
        .reshape(image_count, length, width)
        .astype(b16)
    )
    attended = jnp.einsum(
        "isd,de->ise", mixed, out_full, preferred_element_type=f32
    ) + out_bias_full.astype(f32)
    resid = source + pieces[2] * attended
    second_float, second_back = jax.vjp(modulate, resid, pieces[3], pieces[4])
    second = second_float.astype(b16)
    shared_pre = jnp.einsum(
        "isd,df->isf", second, shared_in_full, preferred_element_type=f32
    ) + shared_in_bias_full.astype(f32)
    shared_act, shared_gelu_back = jax.vjp(gelu_tanh, shared_pre)
    shared_low = shared_act.astype(b16)
    shared = jnp.einsum(
        "isf,fd->isd", shared_low, shared_out_full, preferred_element_type=f32
    ) + shared_out_bias_full.astype(f32)
    second_rows = second.reshape(row_count, width)
    logits = jnp.dot(second_rows, router_full, preferred_element_type=f32)
    route_flat = routes.reshape(-1)
    one_hot = (route_flat[:, None] == jnp.arange(E, dtype=jnp.int32)).astype(jnp.int32)
    slot_index = jnp.sum(
        (jnp.cumsum(one_hot, axis=0, dtype=jnp.int32) - one_hot) * one_hot, axis=1, dtype=jnp.int32
    )
    position = jnp.where(slot_index < CAP, route_flat * CAP + slot_index, E * CAP)
    pair_rows = jnp.repeat(second_rows, 2, axis=0)
    buffer = (
        jnp.zeros((E * CAP, width), b16)
        .at[position]
        .set(pair_rows, mode="drop")
        .reshape(E, CAP, width)
    )
    received = lax.all_to_all(buffer, "expert", split_axis=0, concat_axis=1, tiled=True)
    expert_pre = (
        jnp.einsum("erd,edf->erf", received, expert_in, preferred_element_type=f32)
        + expert_in_bias.astype(f32)[:, None, :]
    )
    expert_low = gelu_tanh(expert_pre).astype(b16)
    expert_result = (
        jnp.einsum("erf,efd->erd", expert_low, expert_out, preferred_element_type=f32)
        + expert_out_bias.astype(f32)[:, None, :]
    ).astype(b16)
    returned = lax.all_to_all(
        expert_result, "expert", split_axis=1, concat_axis=0, tiled=True
    ).reshape(E * CAP, width)
    gathered = (
        returned.at[position]
        .get(mode="fill", fill_value=0)
        .reshape(row_count, 2, width)
        .astype(f32)
    )
    pair_mask = one_hot.reshape(row_count, 2, E).astype(f32)
    chosen = jnp.sum(logits[:, None, :] * pair_mask, axis=-1)
    gates = jax.nn.softmax(chosen, axis=-1)
    moe = (shared.reshape(row_count, width) + jnp.sum(gates[..., None] * gathered, axis=1)).reshape(
        image_count, length, width
    )
    output = (resid + pieces[5] * moe).astype(b16)
    ada_back, qkv_back, out_back, shared_in_back, shared_out_back, router_back = (
        ada_full,
        qkv_full,
        out_full,
        shared_in_full,
        shared_out_full,
        router_full,
    )
    grad_out = cotangent.astype(f32)
    gate_two_grad = jnp.sum(grad_out * moe, axis=1, keepdims=True)
    moe_grad = (pieces[5] * grad_out).astype(b16)
    moe_rows_grad = moe_grad.reshape(row_count, width)
    moe_rows_float = moe_rows_grad.astype(f32)
    pair_grad = (
        (gates[..., None] * moe_rows_float[:, None, :]).astype(b16).reshape(2 * row_count, width)
    )
    gate_grad = jnp.sum(moe_rows_float[:, None, :] * gathered, axis=-1)
    chosen_grad = gates * (gate_grad - jnp.sum(gates * gate_grad, axis=-1, keepdims=True))
    logits_grad = jnp.sum(chosen_grad[..., None] * pair_mask, axis=1).astype(b16)
    grad_buffer = (
        jnp.zeros((E * CAP, width), b16)
        .at[position]
        .set(pair_grad, mode="drop")
        .reshape(E, CAP, width)
    )
    result_grad = lax.all_to_all(grad_buffer, "expert", split_axis=0, concat_axis=1, tiled=True)
    pre_again = (
        jnp.einsum("erd,edf->erf", received, expert_in, preferred_element_type=f32)
        + expert_in_bias.astype(f32)[:, None, :]
    )
    act_again, expert_gelu_back = jax.vjp(gelu_tanh, pre_again)
    low_again = act_again.astype(b16)
    expert_out_grad = jnp.einsum("erf,erd->efd", low_again, result_grad, preferred_element_type=f32)
    expert_out_bias_grad = jnp.sum(result_grad.astype(f32), axis=1)
    expert_act_grad = jnp.einsum(
        "erd,efd->erf", result_grad, expert_out, preferred_element_type=f32
    )
    pre_grad = expert_gelu_back(expert_act_grad)[0].astype(b16)
    expert_in_grad = jnp.einsum("erd,erf->edf", received, pre_grad, preferred_element_type=f32)
    expert_in_bias_grad = jnp.sum(pre_grad.astype(f32), axis=1)
    received_grad = jnp.einsum(
        "erf,edf->erd", pre_grad, expert_in, preferred_element_type=f32
    ).astype(b16)
    sent_grad = lax.all_to_all(
        received_grad, "expert", split_axis=1, concat_axis=0, tiled=True
    ).reshape(E * CAP, width)
    dispatch_rows_grad = jnp.sum(
        sent_grad.at[position]
        .get(mode="fill", fill_value=0)
        .reshape(row_count, 2, width)
        .astype(f32),
        axis=1,
    )
    shared_out_grad = jnp.einsum("isf,isd->fd", shared_low, moe_grad, preferred_element_type=f32)
    shared_out_bias_grad = jnp.sum(moe_rows_float, axis=0)
    shared_act_grad = jnp.einsum(
        "isd,fd->isf", moe_grad, shared_out_back, preferred_element_type=f32
    )
    shared_pre_grad = shared_gelu_back(shared_act_grad)[0].astype(b16)
    shared_in_grad = jnp.einsum("isd,isf->df", second, shared_pre_grad, preferred_element_type=f32)
    shared_in_bias_grad = jnp.sum(shared_pre_grad.astype(f32), axis=(0, 1))
    router_grad = jnp.einsum("rd,re->de", second_rows, logits_grad, preferred_element_type=f32)
    second_grad = jnp.einsum(
        "isf,df->isd", shared_pre_grad, shared_in_back, preferred_element_type=f32
    )
    side_grad = dispatch_rows_grad + jnp.einsum(
        "re,de->rd", logits_grad, router_back, preferred_element_type=f32
    )
    second_grad = second_grad + side_grad.reshape(image_count, length, width)
    resid_extra, shift_two_grad, scale_two_grad = second_back(second_grad)
    resid_grad = grad_out + resid_extra
    attended_grad = (pieces[2] * resid_grad).astype(b16)
    gate_one_grad = jnp.sum(resid_grad * attended, axis=1, keepdims=True)
    out_weight_grad = jnp.einsum("isd,ise->de", mixed, attended_grad, preferred_element_type=f32)
    out_bias_grad = jnp.sum(attended_grad.astype(f32), axis=(0, 1))
    mixed_grad = (
        jnp.einsum("ise,de->isd", attended_grad, out_back, preferred_element_type=f32)
        .astype(b16)
        .reshape(head_shape)
    )
    again_scores = (
        jnp.einsum("iqhc,ikhc->ihqk", query_heads, key_heads, preferred_element_type=f32) * scaling
    )
    probs_float = jnp.exp(again_scores - log_total)
    again_low = probs_float.astype(b16)
    probs_grad = jnp.einsum("iqhc,ikhc->ihqk", mixed_grad, value_heads, preferred_element_type=f32)
    values_grad = jnp.einsum(
        "ihqk,iqhc->ikhc", again_low, mixed_grad, preferred_element_type=f32
    ).astype(b16)
    scores_grad = (
        probs_float * (probs_grad - jnp.sum(probs_float * probs_grad, axis=-1, keepdims=True))
    ).astype(b16)
    query_grad = (
        jnp.einsum("ihqk,ikhc->iqhc", scores_grad, key_heads, preferred_element_type=f32) * scaling
    ).astype(b16)
    keys_grad = (
        jnp.einsum("ihqk,iqhc->ikhc", scores_grad, query_heads, preferred_element_type=f32)
        * scaling
    ).astype(b16)
    flat_shape = (image_count, length, width)
    projected_grad = jnp.concatenate(
        [
            query_grad.reshape(flat_shape),
            keys_grad.reshape(flat_shape),
            values_grad.reshape(flat_shape),
        ],
        axis=-1,
    )
    qkv_weight_grad = jnp.einsum("isd,ise->de", normed, projected_grad, preferred_element_type=f32)
    qv_bias_grad = jnp.stack(
        [
            jnp.sum(query_grad.astype(f32), axis=(0, 1)).reshape(width),
            jnp.sum(values_grad.astype(f32), axis=(0, 1)).reshape(width),
        ]
    )
    normed_grad = jnp.einsum("ise,de->isd", projected_grad, qkv_back, preferred_element_type=f32)
    token_extra, shift_one_grad, scale_one_grad = first_back(normed_grad)
    tokens_grad = resid_grad + token_extra
    modulation_grad = jnp.concatenate(
        [
            shift_one_grad,
            scale_one_grad,
            gate_one_grad,
            shift_two_grad,
            scale_two_grad,
            gate_two_grad,
        ],
        axis=-1,
    )[:, 0, :].astype(b16)
    ada_weight_grad = jnp.einsum("id,ie->de", cond_low, modulation_grad, preferred_element_type=f32)
    ada_bias_grad = jnp.sum(modulation_grad.astype(f32), axis=0)
    cond_act_grad = jnp.einsum("ie,de->id", modulation_grad, ada_back, preferred_element_type=f32)
    conditioning_grad = silu_back(cond_act_grad)[0]
    expert_sums = (
        lax.psum_scatter(
            expert_in_grad.astype(jnp.bfloat16), "dp", scatter_dimension=1, tiled=True
        ).astype(jnp.float32),
        lax.psum_scatter(
            expert_in_bias_grad.astype(jnp.bfloat16), "dp", scatter_dimension=1, tiled=True
        ).astype(jnp.float32),
        lax.psum_scatter(
            expert_out_grad.astype(jnp.bfloat16), "dp", scatter_dimension=1, tiled=True
        ).astype(jnp.float32),
        lax.psum_scatter(
            expert_out_bias_grad.astype(jnp.bfloat16), "dp", scatter_dimension=1, tiled=True
        ).astype(jnp.float32),
    )
    dense_parts = (
        lax.psum_scatter(
            ada_weight_grad.astype(jnp.bfloat16), "dp", scatter_dimension=0, tiled=True
        ).astype(jnp.float32),
        lax.psum_scatter(
            ada_bias_grad.astype(jnp.bfloat16), "dp", scatter_dimension=0, tiled=True
        ).astype(jnp.float32),
        lax.psum_scatter(
            qkv_weight_grad.astype(jnp.bfloat16), "dp", scatter_dimension=0, tiled=True
        ).astype(jnp.float32),
        lax.psum_scatter(
            qv_bias_grad.astype(jnp.bfloat16), "dp", scatter_dimension=1, tiled=True
        ).astype(jnp.float32),
        lax.psum_scatter(
            out_weight_grad.astype(jnp.bfloat16), "dp", scatter_dimension=0, tiled=True
        ).astype(jnp.float32),
        lax.psum_scatter(
            out_bias_grad.astype(jnp.bfloat16), "dp", scatter_dimension=0, tiled=True
        ).astype(jnp.float32),
        lax.psum_scatter(
            shared_in_grad.astype(jnp.bfloat16), "dp", scatter_dimension=0, tiled=True
        ).astype(jnp.float32),
        lax.psum_scatter(
            shared_in_bias_grad.astype(jnp.bfloat16), "dp", scatter_dimension=0, tiled=True
        ).astype(jnp.float32),
        lax.psum_scatter(
            shared_out_grad.astype(jnp.bfloat16), "dp", scatter_dimension=0, tiled=True
        ).astype(jnp.float32),
        lax.psum_scatter(
            shared_out_bias_grad.astype(jnp.bfloat16), "dp", scatter_dimension=0, tiled=True
        ).astype(jnp.float32),
        lax.psum_scatter(
            router_grad.astype(jnp.bfloat16), "dp", scatter_dimension=0, tiled=True
        ).astype(jnp.float32),
    )
    dense_sums = lax.psum(
        (
            dense_parts[0],
            dense_parts[1],
            dense_parts[2],
            dense_parts[3],
            dense_parts[4],
            dense_parts[5],
            dense_parts[6],
            dense_parts[7],
            dense_parts[8],
            dense_parts[9],
            dense_parts[10],
        ),
        "expert",
    )
    return (
        output,
        tokens_grad,
        conditioning_grad,
        dense_sums[0],
        dense_sums[1],
        dense_sums[2],
        dense_sums[3],
        dense_sums[4],
        dense_sums[5],
        dense_sums[6],
        dense_sums[7],
        dense_sums[8],
        dense_sums[9],
        dense_sums[10],
        expert_sums[0],
        expert_sums[1],
        expert_sums[2],
        expert_sums[3],
    )


def solution(mesh):
    in_specs = (
        P(("dp", "expert"), None, None),
        P(("dp", "expert"), None),
        P(("dp", "expert"), None, None),
        P(("dp", "expert"), None, None),
        P("dp", None),
        P("dp"),
        P("dp", None),
        P(None, "dp"),
        P("dp", None),
        P("dp"),
        P("dp", None),
        P("dp"),
        P("dp", None),
        P("dp"),
        P("dp", None),
        P("expert", None, None),
        P("expert", None),
        P("expert", None, None),
        P("expert", None),
    )
    out_specs = (
        P(("dp", "expert"), None, None),
        P(("dp", "expert"), None, None),
        P(("dp", "expert"), None),
        P("dp", None),
        P("dp"),
        P("dp", None),
        P(None, "dp"),
        P("dp", None),
        P("dp"),
        P("dp", None),
        P("dp"),
        P("dp", None),
        P("dp"),
        P("dp", None),
        P("expert", "dp", None),
        P("expert", "dp"),
        P("expert", "dp", None),
        P("expert", "dp"),
    )
    body = on_device
    if dict(mesh.shape) == {"dp": NZ * NX, "expert": 4}:
        body = on_block
    return jax.shard_map(
        body, mesh=mesh, in_specs=in_specs, out_specs=out_specs, check_vma=False
    )
```
